128 devices in a mesh: section: 2 (over core), ctx: 16 (over y, x), fsdp: 4 (over z).
Axes of the slice: x: 4, y: 4, z: 4, core: 2. Of those that a mesh axis runs over, the one named last changes fastest.
Arguments:
- inputs: bfloat16 [2, 8192, 576], P(None, ('ctx', 'fsdp')), may hold values from -6 to 6
- positions: int32 [2, 8192], replicated, may hold values from 0 to 8191, as said below
- attn_gain: float32 [2, 576], P('section'), may hold values from 0.5 to 1.5
- w_qkv: bfloat16 [2, 576, 960], P('section', None, 'fsdp'), may hold values from -0.25 to 0.25
- w_out: bfloat16 [2, 576, 576], P('section', None, 'fsdp'), may hold values from -0.5 to 0.5
- ffn_gain: float32 [2, 576], P('section'), may hold values from 0.5 to 1.5
- w_gate_up: bfloat16 [2, 576, 3072], P('section', None, 'fsdp'), may hold values from -0.25 to 0.25
- w_down: bfloat16 [2, 1536, 576], P('section', None, 'fsdp'), may hold values from -0.15625 to 0.15625
- cotangent: bfloat16 [2, 8192, 576], P(None, ('ctx', 'fsdp')), may hold values from -6 to 6
Outputs:
- ends: float32 [2, 2, 8192, 576], P('section', None, ('ctx', 'fsdp'))
- grad_attn_gain: float32 [2, 576], P('section', ('ctx', 'fsdp'))
- grad_qkv: float32 [2, 576, 960], P('section', ('ctx', 'fsdp'))
- grad_out: float32 [2, 576, 576], P('section', ('ctx', 'fsdp'))
- grad_ffn_gain: float32 [2, 576], P('section', ('ctx', 'fsdp'))
- grad_gate_up: float32 [2, 576, 3072], P('section', ('ctx', 'fsdp'))
- grad_down: float32 [2, 1536, 576], P('section', None, ('ctx', 'fsdp'))
The draws below stay inside these ranges and needn't reach their ends.
Inputs may be any that keep to these rules, and one draw needn't show every extreme that they name: Each row is an ordering of 0 to 8191. The positions fall into 32 blocks of 256; the tokens of index r of ctx are one block b and block 31 - b (b differs by r and micro-batch), and index f of fsdp holds the f-th of 4 equal consecutive parts of each of the two, in increasing order.
All inputs are finite; a program needn't handle non-finite values.
Results may differ from the reference program's by a relative error of at most 0.022.
Values may be sent and summed in bfloat16 or wider, within the bound.
A program may use at most 384 MiB of HBM per device.

```python
import math
import jax
import jax.numpy as jnp
from jax import lax

D = 576
HEADS = 9
KV_HEADS = 3
HEAD_DIM = 64
FF = 1536
MICRO = 2
SEQ = 8192
QKV = 960
N_CTX = 16
N_FSDP = 4


def draw_positions(key, part):
    key = jax.random.fold_in(key, 11)
    block = SEQ // (2 * N_CTX)
    share = block // N_FSDP
    orders = jnp.stack([jax.random.permutation(jax.random.fold_in(key, index), N_CTX) for index in range(MICRO)])
    lower = orders[:, :, None, None]
    shard = jnp.arange(N_FSDP)[None, None, :, None]
    offset = jnp.arange(2 * share)[None, None, None, :]
    chosen = jnp.where(offset < share, lower, 2 * N_CTX - 1 - lower)
    spots = chosen * block + shard * share + offset % share
    return spots.reshape(MICRO, SEQ).astype(jnp.int32)


def block_scale(stream_key, dims, cuts, low, top_value):
    def one(axis_at, shards_of):
        heights = jax.random.uniform(jax.random.fold_in(jax.random.fold_in(stream_key, 6), axis_at), (shards_of,), jnp.float32, low / len(cuts), top_value / len(cuts))
        return jnp.repeat(jnp.exp(heights), dims[axis_at] // shards_of).reshape((-1,) + (1,) * (len(dims) - axis_at - 1))

    loudness = one(*cuts[0])
    for cut in cuts[1:]:
        loudness = loudness * one(*cut)
    return loudness


def noise(rng, dims, deviation, limit, shards=(), held_as=jnp.bfloat16):
    drawn = jax.random.normal(rng, dims, jnp.float32) * deviation
    if len(shards) > 0:
        drawn = block_scale(rng, dims, shards, -0.22, 0.18) * drawn
    return jnp.clip(drawn, min=-limit, max=limit).astype(held_as)


def setup_inputs(seed: int = 0) -> dict:
    keys = jax.random.split(jax.random.key(seed), 10)
    inputs = noise(keys[0], (MICRO, SEQ, D), 1.0, 6.0, ((1, 64),))
    positions = draw_positions(jax.random.fold_in(keys[9], 71), 0)
    attn_gain = jnp.clip(1.0 + 0.1 * jax.random.normal(keys[2], (2, D), jnp.float32), 0.5, 1.5)
    w_qkv = noise(keys[3], (2, D, QKV), D ** -0.5, 0.25, ((0, 2), (2, 4)))
    w_out = noise(keys[4], (2, D, D), (D // 4) ** -0.5, 0.5, ((0, 2), (2, 4)))
    ffn_gain = jnp.clip(1.0 + 0.1 * jax.random.normal(keys[5], (2, D), jnp.float32), 0.5, 1.5)
    w_gate_up = noise(keys[6], (2, D, 2 * FF), D ** -0.5, 0.25, ((0, 2), (2, 4)))
    w_down = noise(keys[7], (2, FF, D), FF ** -0.5, 0.15625, ((0, 2), (2, 4)))
    cotangent = noise(keys[8], (MICRO, SEQ, D), 1.0, 6.0, ((1, 64),))
    return {"inputs": inputs, "positions": positions, "attn_gain": attn_gain, "w_qkv": w_qkv, "w_out": w_out, "ffn_gain": ffn_gain, "w_gate_up": w_gate_up, "w_down": w_down, "cotangent": cotangent}


@jax.custom_vjp
def low(v):
    return lax.optimization_barrier(v.astype(jnp.bfloat16)).astype(jnp.float32)

@jax.custom_vjp
def low_back(v):
    return v

def low_keep(v):
    return (low(v), None)

def low_pass(kept, grad):
    return (grad,)

def back_keep(v):
    return (v, None)

def back_low(kept, grad):
    return (low(grad),)
low.defvjp(low_keep, low_pass)
low_back.defvjp(back_keep, back_low)
epsilon = 1e-05
rope_base = 100000.0
HIGHEST = lax.Precision.HIGHEST

def matmul(left, right):
    return jnp.dot(left, right, preferred_element_type=jnp.float32, precision=HIGHEST)

def rope_tables(spots):
    half = HEAD_DIM // 2
    frequency = rope_base ** (-(jnp.arange(half, dtype=jnp.float32) * 2.0 / HEAD_DIM))
    angle = spots.astype(jnp.float32)[:, None] * frequency[None, :]
    return (jnp.cos(angle), jnp.sin(angle))

def rotate(heads, cosine, sine):
    half = HEAD_DIM // 2
    first, second = (heads[..., :half], heads[..., half:])
    cosine, sine = (cosine[:, None, :], sine[:, None, :])
    return jnp.concatenate([first * cosine - second * sine, second * cosine + first * sine], axis=-1)

def rms_norm(values, gain):
    return values * lax.rsqrt(lax.optimization_barrier(jnp.mean(values * values, axis=-1, keepdims=True)) + epsilon) * gain

def attention(query, key, value, spots):
    block = math.gcd(SEQ, 512)
    scale = HEAD_DIM ** (-0.5)

    def one_block(start, query, key, value, spots):
        rows_q = lax.dynamic_slice_in_dim(query, start, block, 0)
        spots_q = lax.dynamic_slice_in_dim(spots, start, block, 0)
        scores = low_back(jnp.einsum('tghd,sgd->ghts', rows_q, key, precision=HIGHEST) * scale)
        allowed = spots_q[:, None] >= spots[None, :]
        scores = jnp.where(allowed[None, None], scores, -1e+30)
        highest = lax.optimization_barrier(jnp.max(scores, axis=-1, keepdims=True))
        exponent = jnp.exp(scores - highest)
        probs = low(exponent / lax.optimization_barrier(jnp.sum(exponent, axis=-1, keepdims=True)))
        mixed = jnp.einsum('ghts,sgd->tghd', probs, value, precision=HIGHEST)
        return mixed.reshape(block, D)
    saved = jax.checkpoint(one_block)
    starts = jnp.arange(SEQ // block, dtype=jnp.int32) * block
    return lax.map(lambda start: saved(start, query, key, value, spots), starts).reshape(SEQ, D)

def layer(weights, sequence, spots):
    attn_gain, w_qkv, w_out, ffn_gain, w_gate_up, w_down = weights
    key_width = KV_HEADS * HEAD_DIM
    group = HEADS // KV_HEADS
    cosine, sine = rope_tables(spots)
    normed = low(rms_norm(sequence, attn_gain))
    projected = low_back(matmul(normed, w_qkv))
    query = projected[:, :D].reshape(SEQ, HEADS, HEAD_DIM)
    key = projected[:, D:D + key_width].reshape(SEQ, KV_HEADS, HEAD_DIM)
    value = low(projected[:, D + key_width:].reshape(SEQ, KV_HEADS, HEAD_DIM))
    query = low(rotate(query, cosine, sine)).reshape(SEQ, KV_HEADS, group, HEAD_DIM)
    key = low(rotate(key, cosine, sine))
    mixed = low_back(low(attention(query, key, value, spots)))
    hidden = sequence + low_back(matmul(mixed, w_out))
    normed_two = low(rms_norm(hidden, ffn_gain))
    both = low_back(matmul(normed_two, w_gate_up))
    act = low(jax.nn.silu(both[:, :FF]) * both[:, FF:])
    return hidden + low_back(matmul(act, w_down))

def forward(params, sequences, positions):
    first = tuple((item[0] for item in params))
    second = tuple((item[1] for item in params))

    def one_sequence(pair):
        sequence, spots = pair
        middle = layer(first, sequence, spots)
        return layer(second, middle, spots)
    return lax.map(one_sequence, (sequences, positions))

def reference(inputs, positions, attn_gain, w_qkv, w_out, ffn_gain, w_gate_up, w_down, cotangent):
    params = tuple((item.astype(jnp.float32) for item in (attn_gain, w_qkv, w_out, ffn_gain, w_gate_up, w_down)))
    outputs, pullback = jax.vjp(lambda weights, sequences: forward(weights, sequences, positions), params, inputs.astype(jnp.float32))
    grad_params, grad_inputs = pullback(cotangent.astype(jnp.float32))
    ends = jnp.stack([grad_inputs, outputs])
    return (ends, grad_params[0], grad_params[1], grad_params[2], grad_params[3], grad_params[4], grad_params[5])
```

```python
import functools

import jax
import jax.numpy as jnp
from jax import lax
from jax.experimental import pallas as pl
from jax.experimental.pallas import tpu as pltpu
from jax.sharding import PartitionSpec as P

HEADS = 9
KV_HEADS = 3
GROUP = 3
HEAD_DIM = 64
FF = 1536
CHUNK = 64
BLOCK = 512
PER = BLOCK // CHUNK
MESH = pl.DeviceIdType.MESH
VMEM_LIMIT = 56 * 1024 * 1024

epsilon = 1e-05
rope_base = 100000.0
contract_last = (((1,), (1,)), ((), ()))
contract_first = (((0,), (0,)), ((), ()))

ORDERS = ((2, 0, 1), (0, 1, 2), (1, 2, 0))
SIDE = 4


def here():
    ctx = lax.axis_index("ctx")
    return (lax.axis_index("section"), (ctx // SIDE, lax.rem(ctx, SIDE), lax.axis_index("fsdp")))


def shifted(at, axis, step):
    return lax.rem(at[axis] + (step + SIDE), SIDE)


def device_at(section, at, axis, step):
    moved = list(at)
    moved[axis] = shifted(at, axis, step)
    return (section, moved[0] * SIDE + moved[1], moved[2])


def enter(section, at):
    barrier = pltpu.get_barrier_semaphore()
    for axis in range(3):
        for step in (1, -1):
            pl.semaphore_signal(
                barrier, inc=1, device_id=device_at(section, at, axis, step), device_id_type=MESH
            )
    pl.semaphore_wait(barrier, 6)


def slab(ref, part, axes, fixed, rows):
    return ref.at[(part,) + tuple(fixed.get(axis, slice(None)) for axis in axes) + (rows,)]


def gather_kernel(split, local_ref, out_ref, send, recv, kept):
    rows = local_ref.shape[1]
    halves = (pl.ds(0, split), pl.ds(split, rows - split))
    section, at = here()
    enter(section, at)
    own = pltpu.make_async_copy(local_ref, out_ref.at[:, at[0], at[1], at[2]], kept)
    own.start()
    every = (0, 1, 2)

    def message(phase, part, way, number, target, coordinate, half):
        order = ORDERS[part]
        axis = order[phase]
        fixed = {later: at[later] for later in order[phase + 1 :]}
        fixed[axis] = coordinate
        place = slab(out_ref, part, every, fixed, halves[half])
        source = place
        if phase == 0 and number < 2:
            source = local_ref.at[part, halves[half]]
        return pltpu.make_async_remote_copy(
            src_ref=source,
            dst_ref=place,
            send_sem=send.at[phase, part, way, number],
            recv_sem=recv.at[phase, part, way, number],
            device_id=device_at(section, at, axis, target),
            device_id_type=MESH,
        )

    for phase in range(3):
        flying = {}
        for number in range(2):
            for part in range(3):
                axis = ORDERS[part][phase]
                for way, step in enumerate((1, -1)):
                    copy = message(phase, part, way, number, step, at[axis], (number + way) % 2)
                    copy.start()
                    flying[part, way, number] = copy
        for part in range(3):
            axis = ORDERS[part][phase]
            for way, step in enumerate((1, -1)):
                flying[part, way, 0].wait_recv()
                copy = message(phase, part, way, 2, step, shifted(at, axis, -step), way)
                copy.start()
                flying[part, way, 2] = copy
        for part in range(3):
            for way in range(2):
                flying[part, way, 0].wait_send()
                flying[part, way, 1].wait()
                flying[part, way, 2].wait()
        if phase == 0:
            own.wait()


def gather_all(local, collective_id):
    parts, rows, lanes = local.shape
    return pl.pallas_call(
        functools.partial(gather_kernel, rows // 2),
        out_shape=jax.ShapeDtypeStruct((parts, SIDE, SIDE, SIDE, rows, lanes), local.dtype),
        in_specs=[pl.BlockSpec(memory_space=pltpu.VMEM)],
        out_specs=pl.BlockSpec(memory_space=pl.ANY),
        scratch_shapes=[
            pltpu.SemaphoreType.DMA((3, 3, 2, 3)),
            pltpu.SemaphoreType.DMA((3, 3, 2, 3)),
            pltpu.SemaphoreType.DMA,
        ],
        compiler_params=pltpu.CompilerParams(
            collective_id=collective_id, has_side_effects=True, vmem_limit_bytes=VMEM_LIMIT
        ),
        cost_estimate=pl.CostEstimate(flops=0, bytes_accessed=2 * 64 * local.size, transcendentals=0),
    )(local)


def scatter_kernel(split, terms_ref, out_ref, sum_one, sum_two, near_one, far_one, near_two, far_two, near_three, far_three, send, recv):
    rows = terms_ref.shape[-2]
    halves = (pl.ds(0, split), pl.ds(split, rows - split))
    section, at = here()
    enter(section, at)
    sums = (terms_ref, sum_one, sum_two, out_ref)
    landing = ((near_one, far_one), (near_two, far_two), (near_three, far_three))

    def remaining(part, phase):
        return tuple(sorted(ORDERS[part][: 3 - phase]))

    def axis_of(part, phase):
        return ORDERS[part][2 - phase]

    def landed(phase, part, way, number):
        half = (number + way) % 2
        slot = {(0, 0): 0, (0, 2): 1, (1, 1): 2, (0, 1): 0, (1, 0): 1, (1, 2): 2}[way, number]
        return landing[phase][half].at[slot, part]

    def message(phase, part, way, number, step, source):
        axis = axis_of(part, phase)
        return pltpu.make_async_remote_copy(
            src_ref=source,
            dst_ref=landed(phase, part, way, number),
            send_sem=send.at[phase, part, way, number],
            recv_sem=recv.at[phase, part, way, number],
            device_id=device_at(section, at, axis, step),
            device_id_type=MESH,
        )

    def own(phase, part, coordinate, half):
        return slab(sums[phase], part, remaining(part, phase), {axis_of(part, phase): coordinate}, halves[half])

    def add(phase, target, terms):
        outer = target.shape[:-2]
        count = 1
        for size in outer:
            count *= size

        def one(index):
            total = terms[0][index].astype(jnp.float32)
            for term in terms[1:]:
                total = total + term[index].astype(jnp.float32)
            target[index] = total.astype(target.dtype)

        if count == 1:
            one((slice(None),) * 2)
            return

        @pl.loop(0, count)
        def _(step):
            if len(outer) == 1:
                one((step,))
            else:
                one((step // SIDE, lax.rem(step, SIDE)))

    for phase in range(3):
        flying = {}
        for number in range(2):
            for part in range(3):
                axis = axis_of(part, phase)
                for way, step in enumerate((1, -1)):
                    coordinate = shifted(at, axis, 2 * step if number == 0 else step)
                    copy = message(phase, part, way, number, step, own(phase, part, coordinate, (number + way) % 2))
                    copy.start()
                    flying[part, way, number] = copy
        for part in range(3):
            axis = axis_of(part, phase)
            for way, step in enumerate((1, -1)):
                flying[part, way, 0].wait_recv()
                passing = landed(phase, part, way, 0)
                add(phase, passing, (passing, own(phase, part, shifted(at, axis, step), way)))
                copy = message(phase, part, way, 2, step, passing)
                copy.start()
                flying[part, way, 2] = copy
        for part in range(3):
            axis = axis_of(part, phase)
            for way in range(2):
                flying[part, way, 1].wait_recv()
                flying[part, way, 2].wait_recv()
            for half in range(2):
                target = sums[phase + 1].at[(part,) + (slice(None),) * (2 - phase) + (halves[half],)]
                add(
                    phase,
                    target,
                    (
                        own(phase, part, at[axis], half),
                        landed(phase, part, half, 2),
                        landed(phase, part, 1 - half, 1),
                    ),
                )
        for part in range(3):
            for way in range(2):
                for number in range(3):
                    flying[part, way, number].wait_send()


def scatter_all(terms, split, collective_id):
    parts, rows, lanes = terms.shape[0], terms.shape[-2], terms.shape[-1]
    kind = terms.dtype
    near, far = split, rows - split
    return pl.pallas_call(
        functools.partial(scatter_kernel, split),
        out_shape=jax.ShapeDtypeStruct((parts, rows, lanes), jnp.float32),
        in_specs=[pl.BlockSpec(memory_space=pltpu.VMEM)],
        out_specs=pl.BlockSpec(memory_space=pltpu.VMEM),
        scratch_shapes=[
            pltpu.VMEM((parts, SIDE, SIDE, rows, lanes), kind),
            pltpu.VMEM((parts, SIDE, rows, lanes), kind),
            pltpu.VMEM((3, parts, SIDE, SIDE, near, lanes), kind),
            pltpu.VMEM((3, parts, SIDE, SIDE, far, lanes), kind),
            pltpu.VMEM((3, parts, SIDE, near, lanes), kind),
            pltpu.VMEM((3, parts, SIDE, far, lanes), kind),
            pltpu.VMEM((3, parts, near, lanes), kind),
            pltpu.VMEM((3, parts, far, lanes), kind),
            pltpu.SemaphoreType.DMA((3, 3, 2, 3)),
            pltpu.SemaphoreType.DMA((3, 3, 2, 3)),
        ],
        compiler_params=pltpu.CompilerParams(
            collective_id=collective_id, has_side_effects=True, vmem_limit_bytes=VMEM_LIMIT
        ),
        cost_estimate=pl.CostEstimate(flops=terms.size, bytes_accessed=2 * terms.size, transcendentals=0),
    )(terms)


def fetch_sorted(inverse_ref, source_ref, keys, sems):
    @pl.loop(0, inverse_ref.shape[0])
    def _(chunk):
        pltpu.make_async_copy(
            source_ref.at[:, inverse_ref[chunk]],
            keys.at[:, pl.ds(pl.multiple_of(chunk * CHUNK, CHUNK), CHUNK)],
            sems.at[chunk // PER],
        ).start()


def wait_block(keys, sems, block):
    rows = keys.at[:, pl.ds(pl.multiple_of(block * BLOCK, BLOCK), BLOCK)]
    pltpu.make_async_copy(rows, rows, sems.at[block]).wait()


def visible(shape, chunk, block):
    row = lax.broadcasted_iota(jnp.int32, shape, 0)
    column = lax.broadcasted_iota(jnp.int32, shape, 1)
    return block * BLOCK + column <= chunk * CHUNK + lax.rem(row, CHUNK)


def attend_kernel(inverse_ref, spots_ref, query_ref, source_ref, mixed_ref, logsum_ref, keys, sems):
    rows = query_ref.shape[2]
    blocks = keys.shape[1] // BLOCK
    fetch_sorted(inverse_ref, source_ref, keys, sems)
    ready = jnp.int32(0)
    for half in range(2):
        chunk = spots_ref[half]
        whole = chunk // PER

        def step(block, carry, masked, half=half, chunk=chunk, ready=ready):
            @pl.when(block >= ready)
            def _():
                wait_block(keys, sems, block)

            start = pl.multiple_of(block * BLOCK, BLOCK)
            result = []
            for group in range(KV_HEADS):
                highest, total, mixed = carry[3 * group : 3 * group + 3]
                both = keys[group, pl.ds(start, BLOCK), :]
                scores = lax.dot_general(
                    query_ref[group, half], both, contract_last, preferred_element_type=jnp.float32
                )
                if masked:
                    scores = jnp.where(visible(scores.shape, chunk, block), scores, -1e30)
                higher = jnp.maximum(highest, jnp.max(scores, axis=-1, keepdims=True))
                exponent = jnp.exp(scores - higher)
                shrink = jnp.exp(highest - higher)
                total = total * shrink + jnp.sum(exponent, axis=-1, keepdims=True)
                mixed = mixed * shrink + jnp.dot(
                    exponent.astype(jnp.bfloat16), both, preferred_element_type=jnp.float32
                )
                result += [higher, total, mixed]
            return tuple(result)

        carry = ()
        for group in range(KV_HEADS):
            carry += (
                jnp.full((rows, 1), -1e30, jnp.float32),
                jnp.zeros((rows, 1), jnp.float32),
                jnp.zeros((rows, 2 * HEAD_DIM), jnp.float32),
            )
        carry = lax.fori_loop(0, whole, functools.partial(step, masked=False), carry)
        carry = step(whole, carry, masked=True)
        ready = jnp.maximum(ready, whole + 1)
        for group in range(KV_HEADS):
            highest, total, mixed = carry[3 * group : 3 * group + 3]
            mixed_ref[group, half] = mixed / total
            logsum_ref[group, half] = highest + jnp.log(total)

    @pl.loop(ready, blocks)
    def _(block):
        wait_block(keys, sems, block)


def attend(inverse, spots, query, both):
    groups, halves, rows, lanes = query.shape
    chunks = both.shape[1]
    scores = rows * halves * groups * (chunks * CHUNK // 2)
    return pl.pallas_call(
        attend_kernel,
        out_shape=(
            jax.ShapeDtypeStruct((groups, halves, rows, lanes), jnp.float32),
            jax.ShapeDtypeStruct((groups, halves, rows, 1), jnp.float32),
        ),
        in_specs=[
            pl.BlockSpec(memory_space=pltpu.SMEM),
            pl.BlockSpec(memory_space=pltpu.SMEM),
            pl.BlockSpec(memory_space=pltpu.VMEM),
            pl.BlockSpec(memory_space=pl.ANY),
        ],
        out_specs=(pl.BlockSpec(memory_space=pltpu.VMEM), pl.BlockSpec(memory_space=pltpu.VMEM)),
        scratch_shapes=[
            pltpu.VMEM((groups, chunks * CHUNK, lanes), jnp.bfloat16),
            pltpu.SemaphoreType.DMA((chunks // PER,)),
        ],
        compiler_params=pltpu.CompilerParams(vmem_limit_bytes=VMEM_LIMIT),
        cost_estimate=pl.CostEstimate(flops=4 * scores * lanes, bytes_accessed=4 * both.size, transcendentals=scores),
    )(inverse, spots, query, both)


def attend_back_kernel(
    inverse_ref, spots_ref, query_ref, grad_ref, logsum_ref, inner_ref, source_ref,
    grad_query_ref, out_ref, keys, totals, rounded, sems, out_sem,
):
    rows = query_ref.shape[2]
    blocks = keys.shape[1] // BLOCK
    fetch_sorted(inverse_ref, source_ref, keys, sems)

    @pl.loop(0, blocks)
    def _(block):
        totals[:, pl.ds(pl.multiple_of(block * BLOCK, BLOCK), BLOCK), :] = jnp.zeros(
            (KV_HEADS, BLOCK, 2 * HEAD_DIM), jnp.float32
        )

    ready = jnp.int32(0)
    for half in range(2):
        chunk = spots_ref[half]
        whole = chunk // PER

        def step(block, carry, masked, half=half, chunk=chunk, ready=ready):
            @pl.when(block >= ready)
            def _():
                wait_block(keys, sems, block)

            start = pl.multiple_of(block * BLOCK, BLOCK)
            result = []
            for group in range(KV_HEADS):
                both = keys[group, pl.ds(start, BLOCK), :]
                query = query_ref[group, half]
                grad = grad_ref[group, half]
                scores = lax.dot_general(query, both, contract_last, preferred_element_type=jnp.float32)
                probs = jnp.exp(scores - logsum_ref[group, half])
                if masked:
                    probs = jnp.where(visible(scores.shape, chunk, block), probs, 0.0)
                grad_weights = lax.dot_general(grad, both, contract_last, preferred_element_type=jnp.float32)
                grad_scores = (probs * (grad_weights - inner_ref[group, half])).astype(jnp.bfloat16)
                weights = probs.astype(jnp.bfloat16)
                result.append(
                    carry[group] + jnp.dot(grad_scores, both, preferred_element_type=jnp.float32)
                )
                totals[group, pl.ds(start, BLOCK), :] += lax.dot_general(
                    jnp.concatenate([weights, grad_scores], axis=0),
                    jnp.concatenate([grad, query], axis=0),
                    contract_first,
                    preferred_element_type=jnp.float32,
                )
            return tuple(result)

        carry = tuple(jnp.zeros((rows, 2 * HEAD_DIM), jnp.float32) for _ in range(KV_HEADS))
        carry = lax.fori_loop(0, whole, functools.partial(step, masked=False), carry)
        carry = step(whole, carry, masked=True)
        ready = jnp.maximum(ready, whole + 1)
        for group in range(KV_HEADS):
            grad_query_ref[group, half] = carry[group]

    @pl.loop(ready, blocks)
    def _(block):
        wait_block(keys, sems, block)

    @pl.loop(0, blocks * PER)
    def _(chunk):
        place = pl.ds(pl.multiple_of(chunk * CHUNK, CHUNK), CHUNK)
        rounded[:, place, :] = totals[:, place, :].astype(jnp.bfloat16)
        pltpu.make_async_copy(rounded.at[:, place], out_ref.at[:, inverse_ref[chunk]], out_sem).start()

    pltpu.make_async_copy(rounded, rounded, out_sem).wait()


def attend_back(inverse, spots, query, grad, logsum, inner, both):
    groups, halves, rows, lanes = query.shape
    chunks = both.shape[1]
    scores = rows * halves * groups * (chunks * CHUNK // 2)
    vmem = pl.BlockSpec(memory_space=pltpu.VMEM)
    smem = pl.BlockSpec(memory_space=pltpu.SMEM)
    return pl.pallas_call(
        attend_back_kernel,
        out_shape=(
            jax.ShapeDtypeStruct((groups, halves, rows, lanes), jnp.float32),
            jax.ShapeDtypeStruct(both.shape, jnp.bfloat16),
        ),
        in_specs=[smem, smem, vmem, vmem, vmem, vmem, pl.BlockSpec(memory_space=pl.ANY)],
        out_specs=(vmem, pl.BlockSpec(memory_space=pl.ANY)),
        scratch_shapes=[
            pltpu.VMEM((groups, chunks * CHUNK, lanes), jnp.bfloat16),
            pltpu.VMEM((groups, chunks * CHUNK, lanes), jnp.float32),
            pltpu.VMEM((groups, chunks * CHUNK, lanes), jnp.bfloat16),
            pltpu.SemaphoreType.DMA((chunks // PER,)),
            pltpu.SemaphoreType.DMA,
        ],
        compiler_params=pltpu.CompilerParams(vmem_limit_bytes=VMEM_LIMIT),
        cost_estimate=pl.CostEstimate(flops=10 * scores * lanes, bytes_accessed=4 * both.size, transcendentals=scores),
    )(inverse, spots, query, grad, logsum, inner, both)


def rope_tables(spots):
    half = HEAD_DIM // 2
    frequency = rope_base ** (-(jnp.arange(half, dtype=jnp.float32) * 2.0 / HEAD_DIM))
    angle = spots.astype(jnp.float32)[:, None] * frequency[None, :]
    return (jnp.cos(angle), jnp.sin(angle))


def rotate(heads, cosine, sine):
    half = HEAD_DIM // 2
    first, second = (heads[..., :half], heads[..., half:])
    cosine, sine = (cosine[:, None, :], sine[:, None, :])
    return jnp.concatenate(
        [first * cosine - second * sine, second * cosine + first * sine], axis=-1
    )


def unrotate(grads, cosine, sine):
    return rotate(grads, cosine, -sine)


def normalize(values):
    factor = lax.rsqrt(jnp.mean(values * values, axis=-1, keepdims=True) + epsilon)
    return (values * factor, factor)


def norm_back(grad_unit, unit, factor):
    return factor * (grad_unit - unit * jnp.mean(grad_unit * unit, axis=-1, keepdims=True))


def product(left, right):
    return jnp.dot(left, right, preferred_element_type=jnp.float32)


def product_back(grads, weight):
    return lax.dot_general(grads, weight, contract_last, preferred_element_type=jnp.float32)


def by_group(heads):
    rows = heads.shape[0] // 2
    split = heads.reshape(2, rows, KV_HEADS, GROUP, HEAD_DIM)
    return split.transpose(2, 0, 3, 1, 4).reshape(KV_HEADS, 2, GROUP * rows, HEAD_DIM)


def by_token(grouped):
    rows = grouped.shape[2] // GROUP
    split = grouped.reshape(KV_HEADS, 2, GROUP, rows, HEAD_DIM)
    return split.transpose(1, 3, 0, 2, 4).reshape(2 * rows, HEADS * HEAD_DIM)


def lower_lanes(grouped):
    return jnp.pad(grouped, ((0, 0), (0, 0), (0, 0), (0, HEAD_DIM)))


def upper_lanes(grouped):
    return jnp.pad(grouped, ((0, 0), (0, 0), (0, 0), (HEAD_DIM, 0)))


def layer_forward(weights, layer_in, tables, inverse, spots):
    gain_one, qkv, out, gain_two, gate_up, down = weights
    rows, width = layer_in.shape
    key_width = KV_HEADS * HEAD_DIM
    cosine, sine = tables
    unit, _ = normalize(layer_in)
    normed = (unit * gain_one).astype(jnp.bfloat16)
    projected = product(normed, qkv)
    key = rotate(projected[:, width : width + key_width].reshape(rows, KV_HEADS, HEAD_DIM), cosine, sine)
    value = projected[:, width + key_width :].reshape(rows, KV_HEADS, HEAD_DIM)
    local = jnp.concatenate([key, value], axis=-1).astype(jnp.bfloat16).transpose(1, 0, 2)
    both = gather_all(local, 0).reshape(KV_HEADS, -1, CHUNK, 2 * HEAD_DIM)
    query = rotate(projected[:, :width].reshape(rows, HEADS, HEAD_DIM), cosine, sine)
    query = lower_lanes(by_group(query.astype(jnp.bfloat16)) * HEAD_DIM ** (-0.5))
    mixed_wide, logsum = attend(inverse, spots, query, both)
    mixed_wide = mixed_wide[..., HEAD_DIM:]
    mixed = by_token(mixed_wide.astype(jnp.bfloat16))
    hidden = layer_in + product(mixed, out)
    unit, _ = normalize(hidden)
    normed_two = (unit * gain_two).astype(jnp.bfloat16)
    pair = product(normed_two, gate_up)
    act = (jax.nn.silu(pair[:, :FF]) * pair[:, FF:]).astype(jnp.bfloat16)
    result = hidden + product(act, down)
    return result, (layer_in, normed, both, query, mixed_wide, logsum, mixed, hidden, normed_two, pair, act)


def layer_backward(weights, saved, grad_out, tables, inverse, spots):
    gain_one, qkv, out, gain_two, gate_up, down = weights
    layer_in, normed, both, query, mixed_wide, logsum, mixed, hidden, normed_two, pair, act = saved
    rows, width = layer_in.shape
    cosine, sine = tables
    gate, upward = pair[:, :FF], pair[:, FF:]
    squashed = jax.nn.sigmoid(gate)
    grad_branch = grad_out.astype(jnp.bfloat16)
    grad_act = product_back(grad_branch, down)
    grad_gate = grad_act * upward * squashed * (1.0 + gate * (1.0 - squashed))
    grad_upward = grad_act * (gate * squashed)
    grad_pair = jnp.concatenate([grad_gate, grad_upward], axis=1).astype(jnp.bfloat16)
    grad_normed_two = product_back(grad_pair, gate_up)
    unit_two, factor_two = normalize(hidden)
    grad_hidden = grad_out + norm_back(grad_normed_two * gain_two, unit_two, factor_two)
    grad_attn = grad_hidden.astype(jnp.bfloat16)
    grad_mixed = by_group(product_back(grad_attn, out).astype(jnp.bfloat16).reshape(rows, HEADS, HEAD_DIM))
    inner = jnp.sum(grad_mixed.astype(jnp.float32) * mixed_wide, axis=-1, keepdims=True)
    grad_query, grad_both = attend_back(
        inverse, spots, query, upper_lanes(grad_mixed), logsum, inner, both
    )
    grad_local = scatter_all(
        grad_both.reshape(KV_HEADS, SIDE, SIDE, SIDE, rows, 2 * HEAD_DIM), rows // 2, 1
    ).transpose(1, 0, 2)
    grad_query = by_token(grad_query[..., :HEAD_DIM]) * HEAD_DIM ** (-0.5)
    grad_query = unrotate(grad_query.reshape(rows, HEADS, HEAD_DIM), cosine, sine).reshape(rows, width)
    grad_key = unrotate(grad_local[..., :HEAD_DIM], cosine, sine).reshape(rows, -1)
    grad_value = grad_local[..., HEAD_DIM:].reshape(rows, -1)
    grad_projected = jnp.concatenate([grad_query, grad_key, grad_value], axis=1).astype(jnp.bfloat16)
    grad_normed = product_back(grad_projected, qkv)
    unit, factor = normalize(layer_in)
    grad_in = grad_hidden + norm_back(grad_normed * gain_one, unit, factor)
    terms = (normed, grad_projected, mixed, grad_attn, normed_two, grad_pair, grad_branch, act)
    gains = jnp.stack(
        [jnp.sum(grad_normed * unit, axis=0), jnp.sum(grad_normed_two * unit_two, axis=0)]
    )
    return grad_in, terms, gains


def whole_weight(local):
    _, rows, columns = local.shape
    parts = lax.all_gather(local[0], ("section", "fsdp"), axis=0, tiled=False)
    return parts.reshape(2, SIDE, rows, columns).transpose(0, 2, 1, 3).reshape(2, rows, SIDE * columns)


def on_device(inputs, positions, attn_gain, w_qkv, w_out, ffn_gain, w_gate_up, w_down, cotangent):
    _, rows, width = inputs.shape
    section = lax.axis_index("section")
    place = lax.axis_index(("ctx", "fsdp"))
    swap = [(0, 1), (1, 0)]

    spots_k = lax.dynamic_index_in_dim(positions, section, 0, keepdims=False)
    spots_q = lax.dynamic_slice_in_dim(spots_k, place * rows, rows, 0)
    chunk_of = spots_k[::CHUNK] // CHUNK
    inverse = jnp.zeros_like(chunk_of).at[chunk_of].set(jnp.arange(chunk_of.shape[0], dtype=jnp.int32))
    spots = lax.dynamic_slice_in_dim(chunk_of, place * 2, 2, 0)
    tables = rope_tables(spots_q)

    gains = lax.all_gather(jnp.stack([attn_gain[0], ffn_gain[0]]), "section", axis=0, tiled=False)
    qkv, out, gate_up, down = (whole_weight(item) for item in (w_qkv, w_out, w_gate_up, w_down))
    layers = [(gains[l, 0], qkv[l], out[l], gains[l, 1], gate_up[l], down[l]) for l in range(2)]

    current = lax.dynamic_index_in_dim(inputs, section, 0, keepdims=False).astype(jnp.float32)
    middle, saved_one = layer_forward(layers[0], current, tables, inverse, spots)
    result, saved_two = layer_forward(layers[1], middle, tables, inverse, spots)
    grad = lax.dynamic_index_in_dim(cotangent, section, 0, keepdims=False).astype(jnp.float32)
    grad, terms_two, gains_two = layer_backward(layers[1], saved_two, grad, tables, inverse, spots)
    grad, terms_one, gains_one = layer_backward(layers[0], saved_one, grad, tables, inverse, spots)

    first = section == 0
    mine = [jnp.where(first, one, two) for one, two in zip(terms_one, terms_two)]
    theirs = [jnp.where(first, two, one) for one, two in zip(terms_one, terms_two)]
    theirs = lax.ppermute(jnp.concatenate(theirs, axis=1), "section", swap)
    starts = [0]
    for term in mine:
        starts.append(starts[-1] + term.shape[1])
    stacked = [
        jnp.concatenate([term, theirs[:, low:high]], axis=0)
        for term, low, high in zip(mine, starts, starts[1:])
    ]
    normed, grad_projected, mixed, grad_attn, normed_two, grad_pair, grad_branch, act = stacked
    blocks = SIDE * SIDE * SIDE
    each = width // blocks

    def weight_term(left, right):
        term = lax.dot_general(left, right, contract_first, preferred_element_type=jnp.float32)
        return term.astype(jnp.bfloat16)

    pieces = [
        weight_term(normed, grad_projected),
        weight_term(mixed, grad_attn),
        weight_term(normed_two, grad_pair),
        weight_term(grad_branch, act),
    ]
    term = jnp.concatenate(pieces, axis=1)
    columns = term.shape[1]
    tiles = columns // 128
    term = term.reshape(blocks, 3, each // 3, tiles, 128).transpose(1, 0, 2, 3, 4)
    term = term.reshape(3, SIDE, SIDE, SIDE, (each // 3) * tiles, 128)
    summed = scatter_all(term, 80, 2).reshape(each, columns)
    grad_qkv = summed[:, :960]
    grad_out_weight = summed[:, 960:1536]
    grad_gate_up = summed[:, 1536:4608]
    grad_down = summed[:, 4608:].T

    gain_sums = lax.psum(jnp.stack([gains_one, gains_two]), ("section", "ctx", "fsdp"))
    gain_sums = lax.dynamic_index_in_dim(gain_sums, section, 0, keepdims=False)
    gain_sums = lax.dynamic_slice_in_dim(gain_sums, place * each, each, 1)

    kept = jnp.where(first, grad, result)
    sent = lax.ppermute(jnp.where(first, result, grad), "section", swap)
    ends = jnp.where(first, jnp.stack([kept, sent]), jnp.stack([sent, kept]))
    return (
        ends[None],
        gain_sums[0][None],
        grad_qkv[None],
        grad_out_weight[None],
        gain_sums[1][None],
        grad_gate_up[None],
        grad_down[None],
    )


def solution(mesh):
    placed = (
        P(None, ("ctx", "fsdp"), None),
        P(),
        P("section", None),
        P("section", None, "fsdp"),
        P("section", None, "fsdp"),
        P("section", None),
        P("section", None, "fsdp"),
        P("section", None, "fsdp"),
        P(None, ("ctx", "fsdp"), None),
    )
    return jax.shard_map(
        on_device,
        mesh=mesh,
        in_specs=placed,
        out_specs=(
            P("section", None, ("ctx", "fsdp"), None),
            P("section", ("ctx", "fsdp")),
            P("section", ("ctx", "fsdp"), None),
            P("section", ("ctx", "fsdp"), None),
            P("section", ("ctx", "fsdp")),
            P("section", ("ctx", "fsdp"), None),
            P("section", None, ("ctx", "fsdp")),
        ),
        check_vma=False,
    )
```

```python
import functools

import jax
import jax.numpy as jnp
from jax import lax
from jax.experimental import pallas as pl
from jax.experimental.pallas import tpu as pltpu
from jax.sharding import PartitionSpec as P

HEADS = 9
KV_HEADS = 3
GROUP = 3
HEAD_DIM = 64
FF = 1536
CHUNK = 64
BLOCK = 512
PER = BLOCK // CHUNK
MESH = pl.DeviceIdType.MESH
VMEM_LIMIT = 56 * 1024 * 1024

epsilon = 1e-05
rope_base = 100000.0
contract_last = (((1,), (1,)), ((), ()))
contract_first = (((0,), (0,)), ((), ()))

ORDERS = ((2, 0, 1), (0, 1, 2), (1, 2, 0))
SIDE = 4


def here():
    ctx = lax.axis_index("ctx")
    return (lax.axis_index("section"), (ctx // SIDE, lax.rem(ctx, SIDE), lax.axis_index("fsdp")))


def shifted(at, axis, step):
    return lax.rem(at[axis] + (step + SIDE), SIDE)


def device_at(section, at, axis, step):
    moved = list(at)
    moved[axis] = shifted(at, axis, step)
    return (section, moved[0] * SIDE + moved[1], moved[2])


def enter(section, at):
    barrier = pltpu.get_barrier_semaphore()
    for axis in range(3):
        for step in (1, -1):
            pl.semaphore_signal(
                barrier, inc=1, device_id=device_at(section, at, axis, step), device_id_type=MESH
            )
    pl.semaphore_wait(barrier, 6)


def slab(ref, part, axes, fixed, rows):
    return ref.at[(part,) + tuple(fixed.get(axis, slice(None)) for axis in axes) + (rows,)]


def gather_kernel(split, local_ref, out_ref, send, recv, kept):
    rows = local_ref.shape[1]
    halves = (pl.ds(0, split), pl.ds(split, rows - split))
    section, at = here()
    enter(section, at)
    own = pltpu.make_async_copy(local_ref, out_ref.at[:, at[0], at[1], at[2]], kept)
    own.start()
    every = (0, 1, 2)

    def message(phase, part, way, number, target, coordinate, half):
        order = ORDERS[part]
        axis = order[phase]
        fixed = {later: at[later] for later in order[phase + 1 :]}
        fixed[axis] = coordinate
        place = slab(out_ref, part, every, fixed, halves[half])
        source = place
        if phase == 0 and number < 2:
            source = local_ref.at[part, halves[half]]
        return pltpu.make_async_remote_copy(
            src_ref=source,
            dst_ref=place,
            send_sem=send.at[phase, part, way, number],
            recv_sem=recv.at[phase, part, way, number],
            device_id=device_at(section, at, axis, target),
            device_id_type=MESH,
        )

    for phase in range(3):
        flying = {}
        for number in range(2):
            for part in range(3):
                axis = ORDERS[part][phase]
                for way, step in enumerate((1, -1)):
                    copy = message(phase, part, way, number, step, at[axis], (number + way) % 2)
                    copy.start()
                    flying[part, way, number] = copy
        for part in range(3):
            axis = ORDERS[part][phase]
            for way, step in enumerate((1, -1)):
                flying[part, way, 0].wait_recv()
                copy = message(phase, part, way, 2, step, shifted(at, axis, -step), way)
                copy.start()
                flying[part, way, 2] = copy
        for part in range(3):
            for way in range(2):
                flying[part, way, 0].wait_send()
                flying[part, way, 1].wait()
                flying[part, way, 2].wait()
        if phase == 0:
            own.wait()


def gather_all(local, collective_id):
    parts, rows, lanes = local.shape
    return pl.pallas_call(
        functools.partial(gather_kernel, rows // 2),
        out_shape=jax.ShapeDtypeStruct((parts, SIDE, SIDE, SIDE, rows, lanes), local.dtype),
        in_specs=[pl.BlockSpec(memory_space=pltpu.VMEM)],
        out_specs=pl.BlockSpec(memory_space=pl.ANY),
        scratch_shapes=[
            pltpu.SemaphoreType.DMA((3, 3, 2, 3)),
            pltpu.SemaphoreType.DMA((3, 3, 2, 3)),
            pltpu.SemaphoreType.DMA,
        ],
        compiler_params=pltpu.CompilerParams(
            collective_id=collective_id, has_side_effects=True, vmem_limit_bytes=VMEM_LIMIT
        ),
        cost_estimate=pl.CostEstimate(flops=0, bytes_accessed=2 * 64 * local.size, transcendentals=0),
    )(local)


def scatter_kernel(split, terms_ref, out_ref, sum_one, sum_two, near_one, far_one, near_two, far_two, near_three, far_three, send, recv):
    rows = terms_ref.shape[-2]
    halves = (pl.ds(0, split), pl.ds(split, rows - split))
    section, at = here()
    enter(section, at)
    sums = (terms_ref, sum_one, sum_two, out_ref)
    landing = ((near_one, far_one), (near_two, far_two), (near_three, far_three))

    def remaining(part, phase):
        return tuple(sorted(ORDERS[part][: 3 - phase]))

    def axis_of(part, phase):
        return ORDERS[part][2 - phase]

    def landed(phase, part, way, number):
        half = (number + way) % 2
        slot = {(0, 0): 0, (0, 2): 1, (1, 1): 2, (0, 1): 0, (1, 0): 1, (1, 2): 2}[way, number]
        return landing[phase][half].at[slot, part]

    def message(phase, part, way, number, step, source):
        axis = axis_of(part, phase)
        return pltpu.make_async_remote_copy(
            src_ref=source,
            dst_ref=landed(phase, part, way, number),
            send_sem=send.at[phase, part, way, number],
            recv_sem=recv.at[phase, part, way, number],
            device_id=device_at(section, at, axis, step),
            device_id_type=MESH,
        )

    def own(phase, part, coordinate, half):
        return slab(sums[phase], part, remaining(part, phase), {axis_of(part, phase): coordinate}, halves[half])

    def add(phase, target, terms):
        outer = target.shape[:-2]
        count = 1
        for size in outer:
            count *= size

        def one(index):
            total = terms[0][index].astype(jnp.float32)
            for term in terms[1:]:
                total = total + term[index].astype(jnp.float32)
            target[index] = total.astype(target.dtype)

        if count == 1:
            one((slice(None),) * 2)
            return

        @pl.loop(0, count)
        def _(step):
            if len(outer) == 1:
                one((step,))
            else:
                one((step // SIDE, lax.rem(step, SIDE)))

    for phase in range(3):
        flying = {}
        for number in range(2):
            for part in range(3):
                axis = axis_of(part, phase)
                for way, step in enumerate((1, -1)):
                    coordinate = shifted(at, axis, 2 * step if number == 0 else step)
                    copy = message(phase, part, way, number, step, own(phase, part, coordinate, (number + way) % 2))
                    copy.start()
                    flying[part, way, number] = copy
        for part in range(3):
            axis = axis_of(part, phase)
            for way, step in enumerate((1, -1)):
                flying[part, way, 0].wait_recv()
                passing = landed(phase, part, way, 0)
                add(phase, passing, (passing, own(phase, part, shifted(at, axis, step), way)))
                copy = message(phase, part, way, 2, step, passing)
                copy.start()
                flying[part, way, 2] = copy
        for part in range(3):
            axis = axis_of(part, phase)
            for way in range(2):
                flying[part, way, 1].wait_recv()
                flying[part, way, 2].wait_recv()
            for half in range(2):
                target = sums[phase + 1].at[(part,) + (slice(None),) * (2 - phase) + (halves[half],)]
                add(
                    phase,
                    target,
                    (
                        own(phase, part, at[axis], half),
                        landed(phase, part, half, 2),
                        landed(phase, part, 1 - half, 1),
                    ),
                )
        for part in range(3):
            for way in range(2):
                for number in range(3):
                    flying[part, way, number].wait_send()


def scatter_all(terms, split, collective_id):
    parts, rows, lanes = terms.shape[0], terms.shape[-2], terms.shape[-1]
    kind = terms.dtype
    near, far = split, rows - split
    return pl.pallas_call(
        functools.partial(scatter_kernel, split),
        out_shape=jax.ShapeDtypeStruct((parts, rows, lanes), jnp.float32),
        in_specs=[pl.BlockSpec(memory_space=pltpu.VMEM)],
        out_specs=pl.BlockSpec(memory_space=pltpu.VMEM),
        scratch_shapes=[
            pltpu.VMEM((parts, SIDE, SIDE, rows, lanes), kind),
            pltpu.VMEM((parts, SIDE, rows, lanes), kind),
            pltpu.VMEM((3, parts, SIDE, SIDE, near, lanes), kind),
            pltpu.VMEM((3, parts, SIDE, SIDE, far, lanes), kind),
            pltpu.VMEM((3, parts, SIDE, near, lanes), kind),
            pltpu.VMEM((3, parts, SIDE, far, lanes), kind),
            pltpu.VMEM((3, parts, near, lanes), kind),
            pltpu.VMEM((3, parts, far, lanes), kind),
            pltpu.SemaphoreType.DMA((3, 3, 2, 3)),
            pltpu.SemaphoreType.DMA((3, 3, 2, 3)),
        ],
        compiler_params=pltpu.CompilerParams(
            collective_id=collective_id, has_side_effects=True, vmem_limit_bytes=VMEM_LIMIT
        ),
        cost_estimate=pl.CostEstimate(flops=terms.size, bytes_accessed=2 * terms.size, transcendentals=0),
    )(terms)


def fetch_sorted(inverse_ref, source_ref, keys, sems):
    @pl.loop(0, inverse_ref.shape[0])
    def _(chunk):
        pltpu.make_async_copy(
            source_ref.at[:, inverse_ref[chunk]],
            keys.at[:, pl.ds(pl.multiple_of(chunk * CHUNK, CHUNK), CHUNK)],
            sems.at[chunk // PER],
        ).start()


def wait_block(keys, sems, block):
    rows = keys.at[:, pl.ds(pl.multiple_of(block * BLOCK, BLOCK), BLOCK)]
    pltpu.make_async_copy(rows, rows, sems.at[block]).wait()


def visible(shape, chunk, block):
    row = lax.broadcasted_iota(jnp.int32, shape, 0)
    column = lax.broadcasted_iota(jnp.int32, shape, 1)
    return block * BLOCK + column <= chunk * CHUNK + lax.rem(row, CHUNK)


def attend_kernel(inverse_ref, spots_ref, query_ref, source_ref, mixed_ref, logsum_ref, keys, sems):
    rows = query_ref.shape[2]
    blocks = keys.shape[1] // BLOCK
    fetch_sorted(inverse_ref, source_ref, keys, sems)
    ready = jnp.int32(0)
    for half in range(2):
        chunk = spots_ref[half]
        whole = chunk // PER

        def step(block, carry, masked, half=half, chunk=chunk, ready=ready):
            @pl.when(block >= ready)
            def _():
                wait_block(keys, sems, block)

            start = pl.multiple_of(block * BLOCK, BLOCK)
            result = []
            for group in range(KV_HEADS):
                highest, total, mixed = carry[3 * group : 3 * group + 3]
                both = keys[group, pl.ds(start, BLOCK), :]
                scores = lax.dot_general(
                    query_ref[group, half], both, contract_last, preferred_element_type=jnp.float32
                )
                if masked:
                    scores = jnp.where(visible(scores.shape, chunk, block), scores, -1e30)
                higher = jnp.maximum(highest, jnp.max(scores, axis=-1, keepdims=True))
                exponent = jnp.exp(scores - higher)
                shrink = jnp.exp(highest - higher)
                total = total * shrink + jnp.sum(exponent, axis=-1, keepdims=True)
                mixed = mixed * shrink + jnp.dot(
                    exponent.astype(jnp.bfloat16), both, preferred_element_type=jnp.float32
                )
                result += [higher, total, mixed]
            return tuple(result)

        carry = ()
        for group in range(KV_HEADS):
            carry += (
                jnp.full((rows, 1), -1e30, jnp.float32),
                jnp.zeros((rows, 1), jnp.float32),
                jnp.zeros((rows, 2 * HEAD_DIM), jnp.float32),
            )
        carry = lax.fori_loop(0, whole, functools.partial(step, masked=False), carry)
        carry = step(whole, carry, masked=True)
        ready = jnp.maximum(ready, whole + 1)
        for group in range(KV_HEADS):
            highest, total, mixed = carry[3 * group : 3 * group + 3]
            mixed_ref[group, half] = mixed / total
            logsum_ref[group, half] = highest + jnp.log(total)

    @pl.loop(ready, blocks)
    def _(block):
        wait_block(keys, sems, block)


def attend(inverse, spots, query, both):
    groups, halves, rows, lanes = query.shape
    chunks = both.shape[1]
    scores = rows * halves * groups * (chunks * CHUNK // 2)
    return pl.pallas_call(
        attend_kernel,
        out_shape=(
            jax.ShapeDtypeStruct((groups, halves, rows, lanes), jnp.float32),
            jax.ShapeDtypeStruct((groups, halves, rows, 1), jnp.float32),
        ),
        in_specs=[
            pl.BlockSpec(memory_space=pltpu.SMEM),
            pl.BlockSpec(memory_space=pltpu.SMEM),
            pl.BlockSpec(memory_space=pltpu.VMEM),
            pl.BlockSpec(memory_space=pl.ANY),
        ],
        out_specs=(pl.BlockSpec(memory_space=pltpu.VMEM), pl.BlockSpec(memory_space=pltpu.VMEM)),
        scratch_shapes=[
            pltpu.VMEM((groups, chunks * CHUNK, lanes), jnp.bfloat16),
            pltpu.SemaphoreType.DMA((chunks // PER,)),
        ],
        compiler_params=pltpu.CompilerParams(vmem_limit_bytes=VMEM_LIMIT),
        cost_estimate=pl.CostEstimate(flops=4 * scores * lanes, bytes_accessed=4 * both.size, transcendentals=scores),
    )(inverse, spots, query, both)


def attend_back_kernel(
    inverse_ref, spots_ref, query_ref, grad_ref, logsum_ref, inner_ref, source_ref,
    grad_query_ref, out_ref, keys, totals, rounded, sems, out_sem,
):
    rows = query_ref.shape[2]
    blocks = keys.shape[1] // BLOCK
    fetch_sorted(inverse_ref, source_ref, keys, sems)

    @pl.loop(0, blocks)
    def _(block):
        totals[:, pl.ds(pl.multiple_of(block * BLOCK, BLOCK), BLOCK), :] = jnp.zeros(
            (KV_HEADS, BLOCK, 2 * HEAD_DIM), jnp.float32
        )

    ready = jnp.int32(0)
    for half in range(2):
        chunk = spots_ref[half]
        whole = chunk // PER

        def step(block, carry, masked, half=half, chunk=chunk, ready=ready):
            @pl.when(block >= ready)
            def _():
                wait_block(keys, sems, block)

            start = pl.multiple_of(block * BLOCK, BLOCK)
            result = []
            for group in range(KV_HEADS):
                both = keys[group, pl.ds(start, BLOCK), :]
                query = query_ref[group, half]
                grad = grad_ref[group, half]
                scores = lax.dot_general(query, both, contract_last, preferred_element_type=jnp.float32)
                probs = jnp.exp(scores - logsum_ref[group, half])
                if masked:
                    probs = jnp.where(visible(scores.shape, chunk, block), probs, 0.0)
                grad_weights = lax.dot_general(grad, both, contract_last, preferred_element_type=jnp.float32)
                grad_scores = (probs * (grad_weights - inner_ref[group, half])).astype(jnp.bfloat16)
                weights = probs.astype(jnp.bfloat16)
                result.append(
                    carry[group] + jnp.dot(grad_scores, both, preferred_element_type=jnp.float32)
                )
                totals[group, pl.ds(start, BLOCK), :] += lax.dot_general(
                    jnp.concatenate([weights, grad_scores], axis=0),
                    jnp.concatenate([grad, query], axis=0),
                    contract_first,
                    preferred_element_type=jnp.float32,
                )
            return tuple(result)

        carry = tuple(jnp.zeros((rows, 2 * HEAD_DIM), jnp.float32) for _ in range(KV_HEADS))
        carry = lax.fori_loop(0, whole, functools.partial(step, masked=False), carry)
        carry = step(whole, carry, masked=True)
        ready = jnp.maximum(ready, whole + 1)
        for group in range(KV_HEADS):
            grad_query_ref[group, half] = carry[group]

    @pl.loop(ready, blocks)
    def _(block):
        wait_block(keys, sems, block)

    @pl.loop(0, blocks * PER)
    def _(chunk):
        place = pl.ds(pl.multiple_of(chunk * CHUNK, CHUNK), CHUNK)
        rounded[:, place, :] = totals[:, place, :].astype(jnp.bfloat16)
        pltpu.make_async_copy(rounded.at[:, place], out_ref.at[:, inverse_ref[chunk]], out_sem).start()

    pltpu.make_async_copy(rounded, rounded, out_sem).wait()


def attend_back(inverse, spots, query, grad, logsum, inner, both):
    groups, halves, rows, lanes = query.shape
    chunks = both.shape[1]
    scores = rows * halves * groups * (chunks * CHUNK // 2)
    vmem = pl.BlockSpec(memory_space=pltpu.VMEM)
    smem = pl.BlockSpec(memory_space=pltpu.SMEM)
    return pl.pallas_call(
        attend_back_kernel,
        out_shape=(
            jax.ShapeDtypeStruct((groups, halves, rows, lanes), jnp.float32),
            jax.ShapeDtypeStruct(both.shape, jnp.bfloat16),
        ),
        in_specs=[smem, smem, vmem, vmem, vmem, vmem, pl.BlockSpec(memory_space=pl.ANY)],
        out_specs=(vmem, pl.BlockSpec(memory_space=pl.ANY)),
        scratch_shapes=[
            pltpu.VMEM((groups, chunks * CHUNK, lanes), jnp.bfloat16),
            pltpu.VMEM((groups, chunks * CHUNK, lanes), jnp.float32),
            pltpu.VMEM((groups, chunks * CHUNK, lanes), jnp.bfloat16),
            pltpu.SemaphoreType.DMA((chunks // PER,)),
            pltpu.SemaphoreType.DMA,
        ],
        compiler_params=pltpu.CompilerParams(vmem_limit_bytes=VMEM_LIMIT),
        cost_estimate=pl.CostEstimate(flops=10 * scores * lanes, bytes_accessed=4 * both.size, transcendentals=scores),
    )(inverse, spots, query, grad, logsum, inner, both)


def first_weight_kernel(local_ref, gains_ref, out_ref, gains_out_ref, send, recv, side_send, side_recv, gain_send, gain_recv, kept):
    rows = local_ref.shape[0]
    halves = (pl.ds(0, 128), pl.ds(128, rows - 128))
    section, at = here()
    place = at[2]
    beside = (1 - section, at[0] * SIDE + at[1], place)
    barrier = pltpu.get_barrier_semaphore()
    for device in (device_at(section, at, 2, 1), device_at(section, at, 2, -1), beside):
        pl.semaphore_signal(barrier, inc=1, device_id=device, device_id_type=MESH)
    pl.semaphore_wait(barrier, 3)
    own_gains = pltpu.make_async_copy(gains_ref, gains_out_ref.at[section], kept.at[0])
    own_gains.start()
    other_gains = pltpu.make_async_remote_copy(
        src_ref=gains_ref,
        dst_ref=gains_out_ref.at[section],
        send_sem=gain_send,
        recv_sem=gain_recv,
        device_id=beside,
        device_id_type=MESH,
    )
    other_gains.start()

    def aside(number, source):
        index = lax.rem(place + (0, 3, 1, 2)[number], SIDE)
        return pltpu.make_async_remote_copy(
            src_ref=out_ref.at[index] if source is None else source,
            dst_ref=out_ref.at[index],
            send_sem=side_send.at[number],
            recv_sem=side_recv.at[number],
            device_id=beside,
            device_id_type=MESH,
        )

    def message(way, number, step, index, half, source):
        spot = out_ref.at[index, halves[half]]
        return pltpu.make_async_remote_copy(
            src_ref=spot if source is None else source.at[halves[half]],
            dst_ref=spot,
            send_sem=send.at[way, number],
            recv_sem=recv.at[way, number],
            device_id=device_at(section, at, 2, step),
            device_id_type=MESH,
        )

    @pl.when(section == 0)
    def _():
        own = pltpu.make_async_copy(local_ref, out_ref.at[place], kept.at[1])
        own.start()
        flying = {}
        for number in range(2):
            for way, step in enumerate((1, -1)):
                flying[way, number] = message(way, number, step, place, (number + way) % 2, local_ref)
                flying[way, number].start()
        sides = [aside(0, local_ref)]
        sides[0].start()
        for way, step in enumerate((1, -1)):
            flying[way, 0].wait_recv()
            flying[way, 2] = message(way, 2, step, shifted(at, 2, -step), way, None)
            flying[way, 2].start()
        for way in range(2):
            flying[way, 1].wait_recv()
            sides.append(aside(1 + way, None))
            sides[-1].start()
        for way in range(2):
            flying[way, 2].wait_recv()
        sides.append(aside(3, None))
        sides[-1].start()
        for side in sides:
            side.wait_send()
        for way in range(2):
            for number in range(3):
                flying[way, number].wait_send()
        own.wait()

    @pl.when(section == 1)
    def _():
        for number in range(4):
            aside(number, None).wait_recv()

    own_gains.wait()
    other_gains.wait()


def first_weight(local, gains):
    rows, columns = local.shape
    any_space = pl.BlockSpec(memory_space=pl.ANY)
    return pl.pallas_call(
        first_weight_kernel,
        out_shape=(
            jax.ShapeDtypeStruct((SIDE, rows, columns), local.dtype),
            jax.ShapeDtypeStruct((2,) + gains.shape, gains.dtype),
        ),
        in_specs=[any_space, any_space],
        out_specs=(any_space, any_space),
        scratch_shapes=[
            pltpu.SemaphoreType.DMA((2, 3)),
            pltpu.SemaphoreType.DMA((2, 3)),
            pltpu.SemaphoreType.DMA((4,)),
            pltpu.SemaphoreType.DMA((4,)),
            pltpu.SemaphoreType.DMA,
            pltpu.SemaphoreType.DMA,
            pltpu.SemaphoreType.DMA((2,)),
        ],
        compiler_params=pltpu.CompilerParams(collective_id=3, has_side_effects=True),
        cost_estimate=pl.CostEstimate(flops=0, bytes_accessed=8 * local.size, transcendentals=0),
    )(local, gains)


def normalize(values):
    factor = lax.rsqrt(jnp.mean(values * values, axis=-1, keepdims=True) + epsilon)
    return (values * factor, factor)


def norm_back(grad_unit, unit, factor):
    return factor * (grad_unit - unit * jnp.mean(grad_unit * unit, axis=-1, keepdims=True))


def product(left, right):
    return jnp.dot(left, right, preferred_element_type=jnp.float32)


def product_turned(left, right):
    return lax.dot_general(left, right, contract_last, preferred_element_type=jnp.float32)


def is_lower(shape):
    return lax.broadcasted_iota(jnp.int32, shape, len(shape) - 1) < HEAD_DIM


def turned(tile, cosine, sine):
    half = HEAD_DIM // 2
    lane = lax.broadcasted_iota(jnp.int32, tile.shape, 1)
    other = jnp.where(
        lax.rem(lane, HEAD_DIM) < half, pltpu.roll(tile, 128 - half, 1), pltpu.roll(tile, half, 1)
    )
    return tile * cosine + other * sine


def swapped(tile):
    return pltpu.roll(tile, HEAD_DIM, 1)


def head_rows(ref, head):
    group, index = head // GROUP, head % GROUP
    rows = slice(index * CHUNK, (index + 1) * CHUNK)
    return jnp.concatenate([ref[group, 0, rows, :], ref[group, 1, rows, :]], axis=0)


def put_head(ref, head, tile):
    group, index = head // GROUP, head % GROUP
    rows = slice(index * CHUNK, (index + 1) * CHUNK)
    ref[group, 0, rows, :] = tile[:CHUNK]
    ref[group, 1, rows, :] = tile[CHUNK:]


def widen(wide, qkv):
    for head in range(HEADS):
        wide[128 * head : 128 * head + 64, :] = qkv[64 * head : 64 * head + 64, :]
        wide[128 * head + 64 : 128 * head + 128, :] = jnp.zeros((64, wide.shape[1]), wide.dtype)
    for group in range(KV_HEADS):
        start = 128 * (HEADS + group)
        wide[start : start + 64, :] = qkv[576 + 64 * group : 640 + 64 * group, :]
        wide[start + 64 : start + 128, :] = qkv[768 + 64 * group : 832 + 64 * group, :]


def project(current, gain, wide, cosine, sine, query_ref, local_ref):
    unit, _ = normalize(current)
    projected = product_turned((unit * gain).astype(jnp.bfloat16), wide[...])
    for head in range(HEADS):
        tile = turned(projected[:, 128 * head : 128 * head + 128], cosine, sine) * HEAD_DIM ** (-0.5)
        put_head(query_ref, head, tile.astype(jnp.bfloat16))
    for group in range(KV_HEADS):
        start = 128 * (HEADS + group)
        local_ref[group] = turned(projected[:, start : start + 128], cosine, sine).astype(jnp.bfloat16)


def project_back(grad_query_ref, grad_local_ref, current, grad_hidden, gain, wide, cosine, sine, terms_ref):
    lower = is_lower((2 * CHUNK, 128))
    tiles = []
    for head in range(HEADS):
        tile = jnp.where(lower, head_rows(grad_query_ref, head), 0.0)
        tiles.append(turned(tile, cosine, -sine) * HEAD_DIM ** (-0.5))
    for group in range(KV_HEADS):
        tiles.append(turned(grad_local_ref[group], cosine, -sine))
    grad_normed = product(
        jnp.concatenate([tile.astype(jnp.bfloat16) for tile in tiles], axis=1), wide[...]
    )
    unit, factor = normalize(current)
    key = tiles[HEADS:]
    pairs = [(tiles[2 * index], swapped(tiles[2 * index + 1])) for index in range(4)]
    pairs += [
        (tiles[8], swapped(key[0])),
        (key[1], swapped(key[2])),
        (swapped(key[0]), key[1]),
        (swapped(key[2]), jnp.zeros_like(key[2])),
    ]
    width = current.shape[1]
    terms_ref[:, :width] = (unit * gain).astype(jnp.bfloat16)
    for index, (low, high) in enumerate(pairs):
        terms_ref[:, 640 + 128 * index : 768 + 128 * index] = jnp.where(lower, low, high).astype(jnp.bfloat16)
    return grad_hidden + norm_back(grad_normed * gain, unit, factor)


def heads_mixed(mixed_ref):
    lower = is_lower((2 * CHUNK, 128))
    tiles = [head_rows(mixed_ref, head) for head in range(HEADS)]
    pairs = [jnp.where(lower, swapped(tiles[2 * i]), tiles[2 * i + 1]) for i in range(4)]
    pairs.append(swapped(tiles[8])[:, :HEAD_DIM])
    return jnp.concatenate([tile.astype(jnp.bfloat16) for tile in pairs], axis=1)


def feed_forward(current, mixed, out, gain, gate_up, down, waits):
    waits[0]()
    hidden = current + product_turned(mixed, out[...])
    unit, _ = normalize(hidden)
    normed = (unit * gain).astype(jnp.bfloat16)
    waits[1]()
    pair = [product(normed, gate_up[index]) for index in range(4)]
    act = [(pair[k] * jax.nn.sigmoid(pair[k]) * pair[k + 2]).astype(jnp.bfloat16) for k in range(2)]
    part = FF // 2
    waits[2]()
    result = hidden + (product_turned(act[0], down[:, :part]) + product_turned(act[1], down[:, part:]))
    return hidden, pair, result


def feed_back(grad_out, hidden, pair, mixed, mixed_ref, out, gain, gate_up, down, waits, terms_ref, grad_ref, inner_ref):
    part = FF // 2
    width = hidden.shape[1]
    branch = grad_out.astype(jnp.bfloat16)
    waits[2]()
    grad_act = product(branch, down[...])
    waits[1]()
    grad_normed = None
    for k in range(2):
        gate, upward = pair(k), pair(k + 2)
        squashed = jax.nn.sigmoid(gate)
        grad = grad_act[:, k * part : (k + 1) * part]
        grad_gate = (grad * upward * squashed * (1.0 + gate * (1.0 - squashed))).astype(jnp.bfloat16)
        grad_upward = (grad * (gate * squashed)).astype(jnp.bfloat16)
        terms_ref[:, 2560 + k * part : 2560 + (k + 1) * part] = grad_gate
        terms_ref[:, 2560 + (k + 2) * part : 2560 + (k + 3) * part] = grad_upward
        terms_ref[:, 5632 + k * part : 5632 + (k + 1) * part] = (gate * squashed * upward).astype(jnp.bfloat16)
        term = product_turned(grad_gate, gate_up[k]) + product_turned(grad_upward, gate_up[k + 2])
        grad_normed = term if grad_normed is None else grad_normed + term
    unit, factor = normalize(hidden)
    terms_ref[:, :width] = mixed
    terms_ref[:, 640 : 640 + width] = (unit * gain).astype(jnp.bfloat16)
    terms_ref[:, 1280 : 1280 + width] = branch
    grad_hidden = grad_out + norm_back(grad_normed * gain, unit, factor)
    grad_attn = grad_hidden.astype(jnp.bfloat16)
    terms_ref[:, 1920:2560] = jnp.concatenate(
        [jnp.zeros((2 * CHUNK, HEAD_DIM), jnp.float32), grad_hidden], axis=1
    ).astype(jnp.bfloat16)
    waits[0]()
    grad_mixed = product(grad_attn, out[...])
    lower = is_lower((2 * CHUNK, 128))
    for head in range(HEADS):
        start = 128 * (head // 2)
        if head == HEADS - 1:
            tile = jnp.concatenate([jnp.zeros((2 * CHUNK, HEAD_DIM), jnp.float32), grad_mixed[:, start:]], axis=1)
        else:
            tile = grad_mixed[:, start : start + 128]
            tile = jnp.where(lower, 0.0, tile if head % 2 else swapped(tile))
        tile = tile.astype(jnp.bfloat16)
        put_head(grad_ref, head, tile)
        inner = jnp.sum(tile.astype(jnp.float32) * head_rows(mixed_ref, head), axis=-1, keepdims=True)
        put_head(inner_ref, head, inner)
    return grad_hidden


def brought(pairs, sems):
    waits = []
    for index, (source, target) in enumerate(pairs):
        copy = pltpu.make_async_copy(source, target, sems.at[index])
        copy.start()
        waits.append(copy.wait)
    return waits


def once(waits):
    return [functools.lru_cache(wait) for wait in waits]


def enter_kernel(current_ref, gain_ref, cosine_ref, sine_ref, qkv_ref, query_ref, local_ref, wide):
    widen(wide, qkv_ref)
    project(
        current_ref[...].astype(jnp.float32), gain_ref[...], wide, cosine_ref[...], sine_ref[...], query_ref, local_ref
    )


def between_kernel(
    mixed_ref, current_ref, gain_ref, next_gain_ref, cosine_ref, sine_ref, out_ref, gate_up_ref, down_ref, qkv_ref,
    hidden_ref, pair_ref, next_ref, query_ref, local_ref,
    out, gate_up, down, qkv, wide, sems,
):
    *waits, wait_qkv = brought(
        [(out_ref, out), (gate_up_ref, gate_up), (down_ref, down), (qkv_ref, qkv)], sems
    )
    mixed = heads_mixed(mixed_ref)
    hidden, pair, result = feed_forward(
        current_ref[...].astype(jnp.float32), mixed, out, gain_ref[...], gate_up, down, waits
    )
    hidden_ref[...] = hidden
    for index in range(4):
        pair_ref[index] = pair[index]
    next_ref[...] = result
    wait_qkv()
    widen(wide, qkv)
    project(result, next_gain_ref[...], wide, cosine_ref[...], sine_ref[...], query_ref, local_ref)


def top_kernel(
    mixed_ref, current_ref, cotangent_ref, gain_ref, out_ref, gate_up_ref, down_ref,
    result_ref, grad_hidden_ref, terms_ref, grad_ref, inner_ref,
    out, gate_up, down, sems,
):
    waits = once(brought([(out_ref, out), (gate_up_ref, gate_up), (down_ref, down)], sems))
    mixed = heads_mixed(mixed_ref)
    gain = gain_ref[...]
    hidden, pair, result = feed_forward(current_ref[...], mixed, out, gain, gate_up, down, waits)
    result_ref[...] = result
    grad_hidden_ref[...] = feed_back(
        cotangent_ref[...].astype(jnp.float32), hidden, lambda index: pair[index], mixed, mixed_ref,
        out, gain, gate_up, down, waits, terms_ref, grad_ref, inner_ref,
    )


def descend_kernel(
    grad_query_ref, grad_local_ref, upper_ref, upper_grad_ref, upper_gain_ref, cosine_ref, sine_ref, qkv_ref,
    mixed_ref, hidden_in_ref, pair_ref, gain_ref, out_ref, gate_up_ref, down_ref,
    upper_terms_ref, grad_hidden_ref, terms_ref, grad_ref, inner_ref,
    out, gate_up, down, wide, sems,
):
    waits = brought([(out_ref, out), (gate_up_ref, gate_up), (down_ref, down)], sems)
    widen(wide, qkv_ref)
    grad = project_back(
        grad_query_ref, grad_local_ref, upper_ref[...], upper_grad_ref[...], upper_gain_ref[...], wide,
        cosine_ref[...], sine_ref[...], upper_terms_ref,
    )
    grad_hidden_ref[...] = feed_back(
        grad, hidden_in_ref[...], lambda index: pair_ref[index], heads_mixed(mixed_ref), mixed_ref,
        out, gain_ref[...], gate_up, down, waits, terms_ref, grad_ref, inner_ref,
    )


def leave_kernel(
    grad_query_ref, grad_local_ref, current_ref, grad_hidden_ref, gain_ref, cosine_ref, sine_ref, qkv_ref,
    grad_in_ref, terms_ref, wide,
):
    widen(wide, qkv_ref)
    grad_in_ref[...] = project_back(
        grad_query_ref, grad_local_ref, current_ref[...].astype(jnp.float32), grad_hidden_ref[...], gain_ref[...], wide,
        cosine_ref[...], sine_ref[...], terms_ref,
    )


def weight_kernel(order_ref, low_ref, low_other_ref, high_ref, high_other_ref, out_ref, gathered):
    width = order_ref.shape[0]
    tiles = 6144 // 128
    blocks = 64

    def both(ref, other_ref, start, size):
        return jnp.concatenate([ref[:, start : start + size], other_ref[:, start : start + size]], axis=0)

    def left(ref, other_ref, start):
        columns = both(ref, other_ref, start, width)
        return product_turned(order_ref[...], columns).astype(jnp.bfloat16)

    def put(term, tile):
        for index in range(width // blocks):
            part, row = index // 3, (index % 3) * tiles + tile
            gathered[part, pl.ds(row, blocks, stride=3 * tiles), :] = term[index * blocks : (index + 1) * blocks]

    normed_one = left(low_ref, low_other_ref, 0)
    mixed = left(high_ref, high_other_ref, 0)
    first = product(normed_one, both(low_ref, low_other_ref, 640, 1024))
    second = product(mixed, both(high_ref, high_other_ref, 1920, 640))
    for tile in range(7):
        put(first[:, 128 * tile : 128 * tile + 128], tile)
    put(first[:, 896:] + second[:, :128], 7)
    for tile in range(1, 5):
        put(second[:, 128 * tile : 128 * tile + 128], 7 + tile)
    normed_two = left(high_ref, high_other_ref, 640)
    for step in range(6):
        third = product(normed_two, both(high_ref, high_other_ref, 2560 + 512 * step, 512))
        for tile in range(4):
            put(third[:, 128 * tile : 128 * tile + 128], 12 + 4 * step + tile)
    branch = left(high_ref, high_other_ref, 1280)
    for step in range(3):
        fourth = product(branch, both(high_ref, high_other_ref, 5632 + 512 * step, 512))
        for tile in range(4):
            put(fourth[:, 128 * tile : 128 * tile + 128], 36 + 4 * step + tile)

    for part in range(3):

        @pl.loop(0, blocks)
        def _(block, part=part):
            start = pl.multiple_of(block * (3 * tiles), 3 * tiles)
            out_ref[part, block] = gathered[part, pl.ds(start, 3 * tiles), :].astype(jnp.bfloat16)


TERMS_LOW = 1664
TERMS_HIGH = 7168


def dense(kernel, arguments, hbm, results, scratch, flops):
    vmem = pl.BlockSpec(memory_space=pltpu.VMEM)
    kept = [vmem] * (len(arguments) - hbm) + [pl.BlockSpec(memory_space=pl.ANY)] * hbm
    size = sum(item.size * item.dtype.itemsize for item in arguments)
    return pl.pallas_call(
        kernel,
        out_shape=tuple(jax.ShapeDtypeStruct(shape, kind) for shape, kind in results),
        in_specs=kept,
        out_specs=tuple(vmem for _ in results),
        scratch_shapes=scratch,
        compiler_params=pltpu.CompilerParams(vmem_limit_bytes=VMEM_LIMIT),
        cost_estimate=pl.CostEstimate(flops=flops, bytes_accessed=size, transcendentals=0),
    )(*arguments)


def on_device(inputs, positions, attn_gain, w_qkv, w_out, ffn_gain, w_gate_up, w_down, cotangent):
    _, rows, width = inputs.shape
    section = lax.axis_index("section")
    place = lax.axis_index(("ctx", "fsdp"))
    swap = [(0, 1), (1, 0)]
    half_kind, kind = jnp.bfloat16, jnp.float32
    lanes = 2 * HEAD_DIM
    columns = w_qkv.shape[2] * SIDE
    wide_rows = 128 * (HEADS + KV_HEADS)

    spots_k = lax.dynamic_index_in_dim(positions, section, 0, keepdims=False)
    spots_q = lax.dynamic_slice_in_dim(spots_k, place * rows, rows, 0)
    chunk_of = spots_k[::CHUNK] // CHUNK
    inverse = jnp.zeros_like(chunk_of).at[chunk_of].set(jnp.arange(chunk_of.shape[0], dtype=jnp.int32))
    spots = lax.dynamic_slice_in_dim(chunk_of, place * 2, 2, 0)
    frequency = rope_base ** (-(jnp.arange(HEAD_DIM // 2, dtype=kind) * 2.0 / HEAD_DIM))
    angle = spots_q.astype(kind)[:, None] * frequency[None, :]
    cosine, sine = jnp.cos(angle), jnp.sin(angle)
    rest = jnp.ones((rows, HEAD_DIM), kind)
    cosine = jnp.concatenate([cosine, cosine, rest], axis=1)
    sine = jnp.concatenate([-sine, sine, 0.0 * rest], axis=1)

    local_gains = jnp.pad(jnp.concatenate([attn_gain, ffn_gain], axis=0), ((0, 6), (0, 0)))
    qkv_turned = w_qkv[0].T
    qkv_first, gains = first_weight(qkv_turned, local_gains)
    qkv_first = qkv_first.reshape(columns, width)

    def gathered(local):
        return lax.all_gather(local, ("section", "fsdp"), axis=0, tiled=False)

    out = gathered(w_out[0].T).reshape(2, width, width)
    gate_up = gathered(w_gate_up[0]).reshape(2, SIDE, width, w_gate_up.shape[2])
    down = gathered(w_down[0].T).reshape(2, width, FF)
    qkv_second = gathered(qkv_turned).reshape(2, columns, width)[1]
    gain_one = [gains[l, 0:1] for l in range(2)]
    gain_two = [gains[l, 1:2] for l in range(2)]

    current = lax.dynamic_index_in_dim(inputs, section, 0, keepdims=False)
    given = lax.dynamic_index_in_dim(cotangent, section, 0, keepdims=False)

    query_like = ((KV_HEADS, 2, GROUP * CHUNK, lanes), half_kind)
    inner_like = ((KV_HEADS, 2, GROUP * CHUNK, 1), kind)
    local_like = ((KV_HEADS, rows, lanes), half_kind)
    state_like = ((rows, width), kind)
    pair_like = ((SIDE, rows, 2 * FF // SIDE), kind)
    low_like = ((rows, TERMS_LOW), half_kind)
    high_like = ((rows, TERMS_HIGH), half_kind)
    wide_scratch = pltpu.VMEM((wide_rows, width), half_kind)
    qkv_scratch = pltpu.VMEM((columns, width), half_kind)
    ffn_scratch = [
        pltpu.VMEM((width, width), half_kind),
        pltpu.VMEM((SIDE, width, 2 * FF // SIDE), half_kind),
        pltpu.VMEM((width, FF), half_kind),
    ]
    sems = pltpu.SemaphoreType.DMA((4,))
    qkv_flops = 2 * rows * width * wide_rows
    ffn_flops = 2 * rows * width * (width + 3 * FF)

    def attention(query, local):
        both = gather_all(local, 0).reshape(KV_HEADS, -1, CHUNK, lanes)
        mixed, logsum = attend(inverse, spots, query, both)
        return both, mixed, logsum

    def attention_back(query, grad, logsum, inner, both):
        grad_query, grad_both = attend_back(inverse, spots, query, grad, logsum, inner, both)
        grad_both = grad_both.reshape(KV_HEADS, SIDE, SIDE, SIDE, rows, lanes)
        return grad_query, scatter_all(grad_both, rows // 2, 1)

    query_one, local = dense(
        enter_kernel, (current, gain_one[0], cosine, sine, qkv_first), 0, (query_like, local_like), [wide_scratch], qkv_flops
    )
    both_one, mixed_one, logsum_one = attention(query_one, local)
    hidden, pair, middle, query_two, local = dense(
        between_kernel,
        (mixed_one, current, gain_two[0], gain_one[1], cosine, sine, out[0], gate_up[0], down[0], qkv_second),
        4,
        (state_like, pair_like, state_like, query_like, local_like),
        ffn_scratch + [qkv_scratch, wide_scratch, sems],
        ffn_flops + qkv_flops,
    )
    both_two, mixed_two, logsum_two = attention(query_two, local)
    result, grad_hidden, high_two, grad, inner = dense(
        top_kernel,
        (mixed_two, middle, given, gain_two[1], out[1], gate_up[1], down[1]),
        3,
        (state_like, state_like, high_like, query_like, inner_like),
        ffn_scratch + [sems],
        2 * ffn_flops,
    )
    grad_query, grad_local = attention_back(query_two, grad, logsum_two, inner, both_two)
    low_two, grad_hidden, high_one, grad, inner = dense(
        descend_kernel,
        (
            grad_query, grad_local, middle, grad_hidden, gain_one[1], cosine, sine, qkv_second,
            mixed_one, hidden, pair, gain_two[0], out[0], gate_up[0], down[0],
        ),
        3,
        (low_like, state_like, high_like, query_like, inner_like),
        ffn_scratch + [wide_scratch, sems],
        ffn_flops + qkv_flops,
    )
    grad_query, grad_local = attention_back(query_one, grad, logsum_one, inner, both_one)
    grad_in, low_one = dense(
        leave_kernel,
        (grad_query, grad_local, current, grad_hidden, gain_one[0], cosine, sine, qkv_first),
        0,
        (state_like, low_like),
        [wide_scratch],
        qkv_flops,
    )

    first = section == 0
    low, low_other = jnp.where(first, low_one, low_two), jnp.where(first, low_two, low_one)
    high, high_other = jnp.where(first, high_one, high_two), jnp.where(first, high_two, high_one)
    low_other = lax.ppermute(low_other, "section", swap)
    high_other = lax.ppermute(high_other, "section", swap)
    blocks = SIDE * SIDE * SIDE
    each = width // blocks
    total = columns + width + 3 * FF
    line = jnp.arange(width)
    order = (line[:, None] % blocks * each + line[:, None] // blocks == line[None, :]).astype(half_kind)
    (term,) = dense(
        weight_kernel,
        (order, low, low_other, high, high_other),
        0,
        (((3, blocks, 3 * total // 128, 128), half_kind),),
        [pltpu.VMEM((3, blocks * 3 * total // 128, 128), kind)],
        4 * rows * width * total,
    )
    term = term.reshape(3, SIDE, SIDE, SIDE, 3 * total // 128, 128)
    summed = scatter_all(term, 80, 2).reshape(each, total)
    grad_qkv = summed[:, :columns]
    grad_out_weight = summed[:, columns : columns + width]
    grad_gate_up = summed[:, columns + width : columns + width + 2 * FF]
    grad_down = summed[:, columns + width + 2 * FF :].T

    qkv_own = jnp.where(first, qkv_first, qkv_second)
    qkv_own = lax.dynamic_slice_in_dim(qkv_own, place * each, each, 1).astype(kind).T
    gate_up_own = lax.dynamic_index_in_dim(gate_up, section, 0, keepdims=False)
    gate_up_own = lax.dynamic_slice_in_dim(gate_up_own, place * each, each, 1).astype(kind)
    split = grad_gate_up.reshape(each, SIDE, -1).transpose(1, 0, 2)
    grad_gain_one = jnp.sum(qkv_own * grad_qkv, axis=1) / lax.dynamic_slice_in_dim(attn_gain[0], place * each, each, 0)
    grad_gain_two = jnp.sum(gate_up_own * split, axis=(0, 2)) / lax.dynamic_slice_in_dim(
        ffn_gain[0], place * each, each, 0
    )

    kept = jnp.where(first, grad_in, result)
    sent = lax.ppermute(jnp.where(first, result, grad_in), "section", swap)
    ends = jnp.where(first, jnp.stack([kept, sent]), jnp.stack([sent, kept]))
    return (
        ends[None],
        grad_gain_one[None],
        grad_qkv[None],
        grad_out_weight[None],
        grad_gain_two[None],
        grad_gate_up[None],
        grad_down[None],
    )


def solution(mesh):
    placed = (
        P(None, ("ctx", "fsdp"), None),
        P(),
        P("section", None),
        P("section", None, "fsdp"),
        P("section", None, "fsdp"),
        P("section", None),
        P("section", None, "fsdp"),
        P("section", None, "fsdp"),
        P(None, ("ctx", "fsdp"), None),
    )
    return jax.shard_map(
        on_device,
        mesh=mesh,
        in_specs=placed,
        out_specs=(
            P("section", None, ("ctx", "fsdp"), None),
            P("section", ("ctx", "fsdp")),
            P("section", ("ctx", "fsdp"), None),
            P("section", ("ctx", "fsdp"), None),
            P("section", ("ctx", "fsdp")),
            P("section", ("ctx", "fsdp"), None),
            P("section", None, ("ctx", "fsdp")),
        ),
        check_vma=False,
    )
```

```python
import functools

import jax
import jax.numpy as jnp
from jax import lax
from jax.experimental import pallas as pl
from jax.experimental.pallas import tpu as pltpu
from jax.sharding import PartitionSpec as P

HEADS = 9
KV_HEADS = 3
GROUP = 3
HEAD_DIM = 64
FF = 1536
CHUNK = 64
BLOCK = 512
PER = BLOCK // CHUNK
MESH = pl.DeviceIdType.MESH
VMEM_LIMIT = 56 * 1024 * 1024

epsilon = 1e-05
rope_base = 100000.0
contract_last = (((1,), (1,)), ((), ()))
contract_first = (((0,), (0,)), ((), ()))

ORDERS = ((2, 0, 1), (0, 1, 2), (1, 2, 0))
SIDE = 4


def here():
    ctx = lax.axis_index("ctx")
    return (lax.axis_index("section"), (ctx // SIDE, lax.rem(ctx, SIDE), lax.axis_index("fsdp")))


def shifted(at, axis, step):
    return lax.rem(at[axis] + (step + SIDE), SIDE)


def device_at(section, at, axis, step):
    moved = list(at)
    moved[axis] = shifted(at, axis, step)
    return (section, moved[0] * SIDE + moved[1], moved[2])


def enter(section, at):
    barrier = pltpu.get_barrier_semaphore()
    for axis in range(3):
        for step in (1, -1):
            pl.semaphore_signal(
                barrier, inc=1, device_id=device_at(section, at, axis, step), device_id_type=MESH
            )
    pl.semaphore_wait(barrier, 6)


def slab(ref, part, axes, fixed, rows):
    return ref.at[(part,) + tuple(fixed.get(axis, slice(None)) for axis in axes) + (rows,)]


def pair_step(at):
    return 1 - 2 * lax.rem(at[2], 2)


class Team:
    def __init__(self):
        self.section, self.at = here()
        w = lax.rem(self.at[2], 2)
        h = self.at[2] // 2
        self.h = lax.rem(h + self.section, 2)
        self.spot = (self.at[0], self.at[1], lax.rem(w + self.section, 2))

    def beside(self):
        return (1 - self.section, self.at[0] * SIDE + self.at[1], self.at[2])

    def device(self, axis, step):
        if axis == 2:
            return (self.section, self.at[0] * SIDE + self.at[1], self.at[2] + pair_step(self.at))
        return device_at(self.section, self.at, axis, step)

    def shifted(self, axis, step):
        return lax.rem(self.spot[axis] + (step + SIDE), 2 if axis == 2 else SIDE)

    def enter(self):
        barrier = pltpu.get_barrier_semaphore()
        devices = [self.device(axis, step) for axis in range(2) for step in (1, -1)]
        devices += [self.device(2, 1), self.beside()]
        for device in devices:
            pl.semaphore_signal(barrier, inc=1, device_id=device, device_id_type=MESH)
        pl.semaphore_wait(barrier, len(devices))


def ring(axis):
    return axis != 2


UNITS = ((0, 0, 64, 128, (2, 0, 1)), (1, 0, 64, 128, (2, 1, 0)), (2, 0, 64, 128, (0, 1, 2)))


def gather_kernel(units, local_ref, out_ref, send, recv, side_send, side_recv, kept):
    team = Team()
    team.enter()
    spot, h = team.spot, team.h
    own = pltpu.make_async_copy(local_ref, out_ref.at[:, spot[0], spot[1], h, spot[2]], kept)
    own.start()

    def slab(unit, phase, coordinate, half):
        part, start, split, stop, order = units[unit]
        low, high = ((start, split), (split, stop), (start, stop))[half]
        fixed = {later: spot[later] for later in order[phase + 1 :]}
        fixed[order[phase]] = coordinate
        y, x, w = (fixed.get(axis, slice(None)) for axis in range(3))
        return out_ref.at[part, y, x, h, w, pl.ds(low, high - low)]

    def message(unit, phase, way, number, step, coordinate, half):
        part, start, split, stop, order = units[unit]
        place = slab(unit, phase, coordinate, half)
        source = place
        if phase == 0 and number < 2:
            low, high = ((start, split), (split, stop), (start, stop))[half]
            source = local_ref.at[part, pl.ds(low, high - low)]
        copy = pltpu.make_async_remote_copy(
            src_ref=source,
            dst_ref=place,
            send_sem=send.at[unit, phase, way, number],
            recv_sem=recv.at[unit, phase, way, number],
            device_id=team.device(order[phase], step),
            device_id_type=MESH,
        )
        copy.start()
        return copy

    sides = []

    def aside(unit, slot, coordinate):
        place = slab(unit, 2, coordinate, 2)
        copy = pltpu.make_async_remote_copy(
            src_ref=place,
            dst_ref=place,
            send_sem=side_send.at[unit, slot],
            recv_sem=side_recv.at[unit, slot],
            device_id=team.beside(),
            device_id_type=MESH,
        )
        copy.start()
        sides.append(copy)

    every = range(len(units))
    steps = tuple(enumerate((1, -1)))
    for phase in range(3):
        axes = [units[unit][4][phase] for unit in every]
        flying = {}
        for number in range(2):
            for unit in every:
                axis = axes[unit]
                if ring(axis):
                    for way, step in steps:
                        flying[unit, way, number] = message(
                            unit, phase, way, number, step, spot[axis], (number + way) % 2
                        )
                elif number == 0:
                    flying[unit, 0, 0] = message(unit, phase, 0, 0, 1, spot[axis], 2)
        if phase == 2:
            for unit in every:
                aside(unit, 0, spot[axes[unit]])
        for unit in every:
            axis = axes[unit]
            if ring(axis):
                for way, step in steps:
                    flying[unit, way, 0].wait_recv()
                    flying[unit, way, 2] = message(unit, phase, way, 2, step, team.shifted(axis, -step), way)
        for unit in every:
            axis = axes[unit]
            if ring(axis):
                for way, step in steps:
                    flying[unit, way, 1].wait_recv()
                    if phase == 2:
                        aside(unit, 1 + way, team.shifted(axis, -step))
            else:
                flying[unit, 0, 0].wait_recv()
                if phase == 2:
                    aside(unit, 1, team.shifted(axis, 1))
        for unit in every:
            axis = axes[unit]
            if ring(axis):
                for way, _ in steps:
                    flying[unit, way, 2].wait_recv()
                if phase == 2:
                    aside(unit, 3, team.shifted(axis, 2))
        for copy in flying.values():
            copy.wait_send()
        if phase == 0:
            own.wait()
    for copy in sides:
        copy.wait()


def gather_all(local, collective_id):
    parts, rows, lanes = local.shape
    count = len(UNITS)
    return pl.pallas_call(
        functools.partial(gather_kernel, UNITS),
        out_shape=jax.ShapeDtypeStruct((parts, SIDE, SIDE, 2, 2, rows, lanes), local.dtype),
        in_specs=[pl.BlockSpec(memory_space=pltpu.VMEM)],
        out_specs=pl.BlockSpec(memory_space=pl.ANY),
        scratch_shapes=[
            pltpu.SemaphoreType.DMA((count, 3, 2, 3)),
            pltpu.SemaphoreType.DMA((count, 3, 2, 3)),
            pltpu.SemaphoreType.DMA((count, 4)),
            pltpu.SemaphoreType.DMA((count, 4)),
            pltpu.SemaphoreType.DMA,
        ],
        compiler_params=pltpu.CompilerParams(
            collective_id=collective_id, has_side_effects=True, vmem_limit_bytes=VMEM_LIMIT
        ),
        cost_estimate=pl.CostEstimate(flops=0, bytes_accessed=2 * 64 * local.size, transcendentals=0),
    )(local)


def add_blocks(target, terms):
    outer = target.shape[:-2]
    count = 1
    for size in outer:
        count *= size

    def one(index):
        total = terms[0][index].astype(jnp.float32)
        for term in terms[1:]:
            total = total + term[index].astype(jnp.float32)
        target[index] = total.astype(target.dtype)

    if count == 1:
        one(tuple(0 for _ in outer) + (slice(None),) * 2)
        return

    @pl.loop(0, count)
    def _(step):
        index = ()
        for size in reversed(outer):
            index = (lax.rem(step, size),) + index
            step = step // size
        one(index)


EXTENT = (SIDE, SIDE, 2)


def combine_shapes(units, kind):
    shapes = []
    for _, start, split, stop, order in units:
        shapes.append(pltpu.VMEM(EXTENT + (stop - start, 128), kind))
        for phase in range(3):
            rest = tuple(EXTENT[axis] for axis in sorted(order[: 2 - phase]))
            if ring(order[2 - phase]):
                shapes.append(pltpu.VMEM((3,) + rest + (split - start, 128), kind))
                shapes.append(pltpu.VMEM((3,) + rest + (stop - split, 128), kind))
            else:
                shapes.append(pltpu.VMEM(rest + (stop - start, 128), kind))
                shapes.append(pltpu.VMEM((8, 128), kind))
            if phase < 2:
                shapes.append(pltpu.VMEM(rest + (stop - start, 128), kind))
    return shapes


def combine_kernel(units, terms_ref, out_ref, *refs):
    count = len(units)
    buffers = [refs[9 * unit : 9 * unit + 9] for unit in range(count)]
    send, recv, side_send, side_recv = refs[9 * count :]
    team = Team()
    team.enter()
    spot = team.spot
    every = range(count)
    steps = tuple(enumerate((1, -1)))

    def sums(unit, phase):
        return buffers[unit][(0, 3, 6)[phase]]

    def rows_of(unit, half):
        _, start, split, stop, _ = units[unit]
        low, high = ((0, split - start), (split - start, stop - start), (0, stop - start))[half]
        return pl.ds(low, high - low)

    def axis_of(unit, phase):
        return units[unit][4][2 - phase]

    def own(unit, phase, coordinate, half):
        axes = sorted(units[unit][4][: 3 - phase])
        axis = axis_of(unit, phase)
        index = tuple(coordinate if other == axis else slice(None) for other in axes)
        return sums(unit, phase).at[index + (rows_of(unit, half),)]

    def landed(unit, phase, way, number):
        if not ring(axis_of(unit, phase)):
            return buffers[unit][3 * phase + 1]
        half = (number + way) % 2
        slot = {(0, 0): 0, (0, 2): 1, (1, 1): 2, (0, 1): 0, (1, 0): 1, (1, 2): 2}[way, number]
        return buffers[unit][3 * phase + 1 + half].at[slot]

    def message(unit, phase, way, number, step, source):
        copy = pltpu.make_async_remote_copy(
            src_ref=source,
            dst_ref=landed(unit, phase, way, number),
            send_sem=send.at[unit, phase, way, number],
            recv_sem=recv.at[unit, phase, way, number],
            device_id=team.device(axis_of(unit, phase), step),
            device_id_type=MESH,
        )
        copy.start()
        return copy

    def given(unit, slot, leaving):
        part, start, _, stop, _ = units[unit]
        axis = axis_of(unit, 0)
        h = 1 - team.h if leaving else team.h
        if ring(axis):
            coordinate = team.shifted(axis, (2, 1, -1, 0)[slot])
        else:
            coordinate = team.shifted(axis, slot if leaving else 1 - slot)
        y, x, w = (coordinate if other == axis else slice(None) for other in range(3))
        return terms_ref.at[part, y, x, h, w, pl.ds(start, stop - start)], coordinate

    def slots(unit):
        return 4 if ring(axis_of(unit, 0)) else 2

    sides = {}
    for slot in range(4):
        for unit in every:
            if slot < slots(unit):
                source, coordinate = given(unit, slot, True)
                copy = pltpu.make_async_remote_copy(
                    src_ref=source,
                    dst_ref=own(unit, 0, coordinate, 2),
                    send_sem=side_send.at[unit, slot],
                    recv_sem=side_recv.at[unit, slot],
                    device_id=team.beside(),
                    device_id_type=MESH,
                )
                copy.start()
                sides[unit, slot] = copy

    def join(unit, slot):
        sides[unit, slot].wait_recv()
        source, coordinate = given(unit, slot, False)
        target = own(unit, 0, coordinate, 2)
        add_blocks(target, (target, source))

    sent = []
    for phase in range(3):
        flying = {}
        for number in range(2):
            for unit in every:
                axis = axis_of(unit, phase)
                if not ring(axis):
                    if number == 0:
                        if phase == 0:
                            join(unit, 0)
                        flying[unit, 0, 0] = message(
                            unit, phase, 0, 0, 1, own(unit, phase, team.shifted(axis, 1), 2)
                        )
                    continue
                if phase == 0 and number == 0:
                    join(unit, 0)
                for way, step in steps:
                    if phase == 0 and number == 1:
                        join(unit, 1 + way)
                    coordinate = team.shifted(axis, 2 * step if number == 0 else step)
                    flying[unit, way, number] = message(
                        unit, phase, way, number, step, own(unit, phase, coordinate, (number + way) % 2)
                    )
        for unit in every:
            axis = axis_of(unit, phase)
            if ring(axis):
                for way, step in steps:
                    flying[unit, way, 0].wait_recv()
                    passing = landed(unit, phase, way, 0)
                    add_blocks(passing, (passing, own(unit, phase, team.shifted(axis, step), way)))
                    flying[unit, way, 2] = message(unit, phase, way, 2, step, passing)
        if phase == 0:
            for unit in every:
                join(unit, slots(unit) - 1)
        for unit in every:
            axis = axis_of(unit, phase)
            part, start, split, stop, _ = units[unit]

            def target(half, unit=unit, phase=phase, part=part, start=start):
                low, size = rows_of(unit, half).start, rows_of(unit, half).size
                if phase == 2:
                    return out_ref.at[part, pl.ds(start + low, size)]
                outer = len(sums(unit, phase + 1).shape) - 2
                return sums(unit, phase + 1).at[(slice(None),) * outer + (pl.ds(low, size),)]

            if ring(axis):
                for way, _ in steps:
                    flying[unit, way, 1].wait_recv()
                    flying[unit, way, 2].wait_recv()
                for half in range(2):
                    add_blocks(
                        target(half),
                        (
                            own(unit, phase, spot[axis], half),
                            landed(unit, phase, half, 2),
                            landed(unit, phase, 1 - half, 1),
                        ),
                    )
            else:
                flying[unit, 0, 0].wait_recv()
                add_blocks(target(2), (own(unit, phase, spot[axis], 2), landed(unit, phase, 0, 0)))
        sent += flying.values()
    for copy in sent:
        copy.wait_send()
    for copy in sides.values():
        copy.wait_send()


def combine_all(terms, collective_id):
    parts, rows, lanes = terms.shape[0], terms.shape[-2], terms.shape[-1]
    count = len(UNITS)
    return pl.pallas_call(
        functools.partial(combine_kernel, UNITS),
        out_shape=jax.ShapeDtypeStruct((parts, rows, lanes), jnp.float32),
        in_specs=[pl.BlockSpec(memory_space=pltpu.VMEM)],
        out_specs=pl.BlockSpec(memory_space=pltpu.VMEM),
        scratch_shapes=combine_shapes(UNITS, terms.dtype)
        + [
            pltpu.SemaphoreType.DMA((count, 3, 2, 3)),
            pltpu.SemaphoreType.DMA((count, 3, 2, 3)),
            pltpu.SemaphoreType.DMA((count, 4)),
            pltpu.SemaphoreType.DMA((count, 4)),
        ],
        compiler_params=pltpu.CompilerParams(
            collective_id=collective_id, has_side_effects=True, vmem_limit_bytes=VMEM_LIMIT
        ),
        cost_estimate=pl.CostEstimate(flops=terms.size, bytes_accessed=2 * terms.size, transcendentals=0),
    )(terms)


def scatter_kernel(split, terms_ref, out_ref, sum_one, sum_two, near_one, far_one, near_two, far_two, near_three, far_three, send, recv):
    rows = terms_ref.shape[-2]
    halves = (pl.ds(0, split), pl.ds(split, rows - split))
    section, at = here()
    enter(section, at)
    sums = (terms_ref, sum_one, sum_two, out_ref)
    landing = ((near_one, far_one), (near_two, far_two), (near_three, far_three))

    def remaining(part, phase):
        return tuple(sorted(ORDERS[part][: 3 - phase]))

    def axis_of(part, phase):
        return ORDERS[part][2 - phase]

    def landed(phase, part, way, number):
        half = (number + way) % 2
        slot = {(0, 0): 0, (0, 2): 1, (1, 1): 2, (0, 1): 0, (1, 0): 1, (1, 2): 2}[way, number]
        return landing[phase][half].at[slot, part]

    def message(phase, part, way, number, step, source):
        axis = axis_of(part, phase)
        return pltpu.make_async_remote_copy(
            src_ref=source,
            dst_ref=landed(phase, part, way, number),
            send_sem=send.at[phase, part, way, number],
            recv_sem=recv.at[phase, part, way, number],
            device_id=device_at(section, at, axis, step),
            device_id_type=MESH,
        )

    def own(phase, part, coordinate, half):
        return slab(sums[phase], part, remaining(part, phase), {axis_of(part, phase): coordinate}, halves[half])

    def add(phase, target, terms):
        outer = target.shape[:-2]
        count = 1
        for size in outer:
            count *= size

        def one(index):
            total = terms[0][index].astype(jnp.float32)
            for term in terms[1:]:
                total = total + term[index].astype(jnp.float32)
            target[index] = total.astype(target.dtype)

        if count == 1:
            one((slice(None),) * 2)
            return

        @pl.loop(0, count)
        def _(step):
            if len(outer) == 1:
                one((step,))
            else:
                one((step // SIDE, lax.rem(step, SIDE)))

    for phase in range(3):
        flying = {}
        for number in range(2):
            for part in range(3):
                axis = axis_of(part, phase)
                for way, step in enumerate((1, -1)):
                    coordinate = shifted(at, axis, 2 * step if number == 0 else step)
                    copy = message(phase, part, way, number, step, own(phase, part, coordinate, (number + way) % 2))
                    copy.start()
                    flying[part, way, number] = copy
        for part in range(3):
            axis = axis_of(part, phase)
            for way, step in enumerate((1, -1)):
                flying[part, way, 0].wait_recv()
                passing = landed(phase, part, way, 0)
                add(phase, passing, (passing, own(phase, part, shifted(at, axis, step), way)))
                copy = message(phase, part, way, 2, step, passing)
                copy.start()
                flying[part, way, 2] = copy
        for part in range(3):
            axis = axis_of(part, phase)
            for way in range(2):
                flying[part, way, 1].wait_recv()
                flying[part, way, 2].wait_recv()
            for half in range(2):
                target = sums[phase + 1].at[(part,) + (slice(None),) * (2 - phase) + (halves[half],)]
                add(
                    phase,
                    target,
                    (
                        own(phase, part, at[axis], half),
                        landed(phase, part, half, 2),
                        landed(phase, part, 1 - half, 1),
                    ),
                )
        for part in range(3):
            for way in range(2):
                for number in range(3):
                    flying[part, way, number].wait_send()


def scatter_all(terms, split, collective_id):
    parts, rows, lanes = terms.shape[0], terms.shape[-2], terms.shape[-1]
    kind = terms.dtype
    near, far = split, rows - split
    return pl.pallas_call(
        functools.partial(scatter_kernel, split),
        out_shape=jax.ShapeDtypeStruct((parts, rows, lanes), jnp.float32),
        in_specs=[pl.BlockSpec(memory_space=pltpu.VMEM)],
        out_specs=pl.BlockSpec(memory_space=pltpu.VMEM),
        scratch_shapes=[
            pltpu.VMEM((parts, SIDE, SIDE, rows, lanes), kind),
            pltpu.VMEM((parts, SIDE, rows, lanes), kind),
            pltpu.VMEM((3, parts, SIDE, SIDE, near, lanes), kind),
            pltpu.VMEM((3, parts, SIDE, SIDE, far, lanes), kind),
            pltpu.VMEM((3, parts, SIDE, near, lanes), kind),
            pltpu.VMEM((3, parts, SIDE, far, lanes), kind),
            pltpu.VMEM((3, parts, near, lanes), kind),
            pltpu.VMEM((3, parts, far, lanes), kind),
            pltpu.SemaphoreType.DMA((3, 3, 2, 3)),
            pltpu.SemaphoreType.DMA((3, 3, 2, 3)),
        ],
        compiler_params=pltpu.CompilerParams(
            collective_id=collective_id, has_side_effects=True, vmem_limit_bytes=VMEM_LIMIT
        ),
        cost_estimate=pl.CostEstimate(flops=terms.size, bytes_accessed=2 * terms.size, transcendentals=0),
    )(terms)


def fetch_sorted(inverse_ref, source_ref, keys, sems):
    @pl.loop(0, inverse_ref.shape[0])
    def _(chunk):
        pltpu.make_async_copy(
            source_ref.at[:, inverse_ref[chunk]],
            keys.at[:, pl.ds(pl.multiple_of(chunk * CHUNK, CHUNK), CHUNK)],
            sems.at[chunk // PER],
        ).start()


def wait_block(keys, sems, block):
    rows = keys.at[:, pl.ds(pl.multiple_of(block * BLOCK, BLOCK), BLOCK)]
    pltpu.make_async_copy(rows, rows, sems.at[block]).wait()


def visible(shape, chunk, block):
    row = lax.broadcasted_iota(jnp.int32, shape, 0)
    column = lax.broadcasted_iota(jnp.int32, shape, 1)
    return block * BLOCK + column <= chunk * CHUNK + lax.rem(row, CHUNK)


def attend_kernel(inverse_ref, spots_ref, query_ref, source_ref, mixed_ref, logsum_ref, keys, sems):
    rows = query_ref.shape[2]
    blocks = keys.shape[1] // BLOCK
    fetch_sorted(inverse_ref, source_ref, keys, sems)
    ready = jnp.int32(0)
    for half in range(2):
        chunk = spots_ref[half]
        whole = chunk // PER

        def step(block, carry, masked, half=half, chunk=chunk, ready=ready):
            @pl.when(block >= ready)
            def _():
                wait_block(keys, sems, block)

            start = pl.multiple_of(block * BLOCK, BLOCK)
            result = []
            for group in range(KV_HEADS):
                highest, total, mixed = carry[3 * group : 3 * group + 3]
                both = keys[group, pl.ds(start, BLOCK), :]
                scores = lax.dot_general(
                    query_ref[group, half], both, contract_last, preferred_element_type=jnp.float32
                )
                if masked:
                    scores = jnp.where(visible(scores.shape, chunk, block), scores, -1e30)
                higher = jnp.maximum(highest, jnp.max(scores, axis=-1, keepdims=True))
                exponent = jnp.exp(scores - higher)
                shrink = jnp.exp(highest - higher)
                total = total * shrink + jnp.sum(exponent, axis=-1, keepdims=True)
                mixed = mixed * shrink + jnp.dot(
                    exponent.astype(jnp.bfloat16), both, preferred_element_type=jnp.float32
                )
                result += [higher, total, mixed]
            return tuple(result)

        carry = ()
        for group in range(KV_HEADS):
            carry += (
                jnp.full((rows, 1), -1e30, jnp.float32),
                jnp.zeros((rows, 1), jnp.float32),
                jnp.zeros((rows, 2 * HEAD_DIM), jnp.float32),
            )
        carry = lax.fori_loop(0, whole, functools.partial(step, masked=False), carry)
        carry = step(whole, carry, masked=True)
        ready = jnp.maximum(ready, whole + 1)
        for group in range(KV_HEADS):
            highest, total, mixed = carry[3 * group : 3 * group + 3]
            mixed_ref[group, half] = mixed / total
            logsum_ref[group, half] = highest + jnp.log(total)

    @pl.loop(ready, blocks)
    def _(block):
        wait_block(keys, sems, block)


def attend(inverse, spots, query, both):
    groups, halves, rows, lanes = query.shape
    chunks = both.shape[1]
    scores = rows * halves * groups * (chunks * CHUNK // 2)
    return pl.pallas_call(
        attend_kernel,
        out_shape=(
            jax.ShapeDtypeStruct((groups, halves, rows, lanes), jnp.float32),
            jax.ShapeDtypeStruct((groups, halves, rows, 1), jnp.float32),
        ),
        in_specs=[
            pl.BlockSpec(memory_space=pltpu.SMEM),
            pl.BlockSpec(memory_space=pltpu.SMEM),
            pl.BlockSpec(memory_space=pltpu.VMEM),
            pl.BlockSpec(memory_space=pl.ANY),
        ],
        out_specs=(pl.BlockSpec(memory_space=pltpu.VMEM), pl.BlockSpec(memory_space=pltpu.VMEM)),
        scratch_shapes=[
            pltpu.VMEM((groups, chunks * CHUNK, lanes), jnp.bfloat16),
            pltpu.SemaphoreType.DMA((chunks // PER,)),
        ],
        compiler_params=pltpu.CompilerParams(vmem_limit_bytes=VMEM_LIMIT),
        cost_estimate=pl.CostEstimate(flops=4 * scores * lanes, bytes_accessed=4 * both.size, transcendentals=scores),
    )(inverse, spots, query, both)


def attend_back_kernel(
    inverse_ref, spots_ref, query_ref, grad_ref, logsum_ref, inner_ref, source_ref,
    grad_query_ref, out_ref, keys, totals, rounded, sems, out_sem,
):
    rows = query_ref.shape[2]
    blocks = keys.shape[1] // BLOCK
    fetch_sorted(inverse_ref, source_ref, keys, sems)

    @pl.loop(0, blocks)
    def _(block):
        totals[:, pl.ds(pl.multiple_of(block * BLOCK, BLOCK), BLOCK), :] = jnp.zeros(
            (KV_HEADS, BLOCK, 2 * HEAD_DIM), jnp.float32
        )

    ready = jnp.int32(0)
    for half in range(2):
        chunk = spots_ref[half]
        whole = chunk // PER

        def step(block, carry, masked, half=half, chunk=chunk, ready=ready):
            @pl.when(block >= ready)
            def _():
                wait_block(keys, sems, block)

            start = pl.multiple_of(block * BLOCK, BLOCK)
            result = []
            for group in range(KV_HEADS):
                both = keys[group, pl.ds(start, BLOCK), :]
                query = query_ref[group, half]
                grad = grad_ref[group, half]
                scores = lax.dot_general(query, both, contract_last, preferred_element_type=jnp.float32)
                probs = jnp.exp(scores - logsum_ref[group, half])
                if masked:
                    probs = jnp.where(visible(scores.shape, chunk, block), probs, 0.0)
                grad_weights = lax.dot_general(grad, both, contract_last, preferred_element_type=jnp.float32)
                grad_scores = (probs * (grad_weights - inner_ref[group, half])).astype(jnp.bfloat16)
                weights = probs.astype(jnp.bfloat16)
                result.append(
                    carry[group] + jnp.dot(grad_scores, both, preferred_element_type=jnp.float32)
                )
                totals[group, pl.ds(start, BLOCK), :] += lax.dot_general(
                    jnp.concatenate([weights, grad_scores], axis=0),
                    jnp.concatenate([grad, query], axis=0),
                    contract_first,
                    preferred_element_type=jnp.float32,
                )
            return tuple(result)

        carry = tuple(jnp.zeros((rows, 2 * HEAD_DIM), jnp.float32) for _ in range(KV_HEADS))
        carry = lax.fori_loop(0, whole, functools.partial(step, masked=False), carry)
        carry = step(whole, carry, masked=True)
        ready = jnp.maximum(ready, whole + 1)
        for group in range(KV_HEADS):
            grad_query_ref[group, half] = carry[group]

    @pl.loop(ready, blocks)
    def _(block):
        wait_block(keys, sems, block)

    @pl.loop(0, blocks * PER)
    def _(chunk):
        place = pl.ds(pl.multiple_of(chunk * CHUNK, CHUNK), CHUNK)
        rounded[:, place, :] = totals[:, place, :].astype(jnp.bfloat16)
        pltpu.make_async_copy(rounded.at[:, place], out_ref.at[:, inverse_ref[chunk]], out_sem).start()

    pltpu.make_async_copy(rounded, rounded, out_sem).wait()


def attend_back(inverse, spots, query, grad, logsum, inner, both):
    groups, halves, rows, lanes = query.shape
    chunks = both.shape[1]
    scores = rows * halves * groups * (chunks * CHUNK // 2)
    vmem = pl.BlockSpec(memory_space=pltpu.VMEM)
    smem = pl.BlockSpec(memory_space=pltpu.SMEM)
    return pl.pallas_call(
        attend_back_kernel,
        out_shape=(
            jax.ShapeDtypeStruct((groups, halves, rows, lanes), jnp.float32),
            jax.ShapeDtypeStruct(both.shape, jnp.bfloat16),
        ),
        in_specs=[smem, smem, vmem, vmem, vmem, vmem, pl.BlockSpec(memory_space=pl.ANY)],
        out_specs=(vmem, pl.BlockSpec(memory_space=pl.ANY)),
        scratch_shapes=[
            pltpu.VMEM((groups, chunks * CHUNK, lanes), jnp.bfloat16),
            pltpu.VMEM((groups, chunks * CHUNK, lanes), jnp.float32),
            pltpu.VMEM((groups, chunks * CHUNK, lanes), jnp.bfloat16),
            pltpu.SemaphoreType.DMA((chunks // PER,)),
            pltpu.SemaphoreType.DMA,
        ],
        compiler_params=pltpu.CompilerParams(vmem_limit_bytes=VMEM_LIMIT),
        cost_estimate=pl.CostEstimate(flops=10 * scores * lanes, bytes_accessed=4 * both.size, transcendentals=scores),
    )(inverse, spots, query, grad, logsum, inner, both)


def first_weight_kernel(
    local_ref, gains_ref, inputs_ref, cotangent_ref, out_ref, gains_out_ref, current_ref, given_ref,
    send, recv, side_send, side_recv, gain_send, gain_recv, token_send, token_recv, kept,
):
    rows = local_ref.shape[0]
    halves = (pl.ds(0, 128), pl.ds(128, rows - 128))
    section, at = here()
    place = at[2]
    beside = (1 - section, at[0] * SIDE + at[1], place)
    barrier = pltpu.get_barrier_semaphore()
    for device in (device_at(section, at, 2, 1), device_at(section, at, 2, -1), beside):
        pl.semaphore_signal(barrier, inc=1, device_id=device, device_id_type=MESH)
    pl.semaphore_wait(barrier, 3)
    own_gains = pltpu.make_async_copy(gains_ref, gains_out_ref.at[section], kept.at[0])
    own_gains.start()
    other_gains = pltpu.make_async_remote_copy(
        src_ref=gains_ref,
        dst_ref=gains_out_ref.at[section],
        send_sem=gain_send,
        recv_sem=gain_recv,
        device_id=beside,
        device_id_type=MESH,
    )
    other_gains.start()

    batch = place // 2
    partner = (section, at[0] * SIDE + at[1], SIDE - 1 - place)
    tokens = ((inputs_ref, current_ref), (cotangent_ref, given_ref))

    def crossing(number):
        source, target = tokens[number]
        return pltpu.make_async_remote_copy(
            src_ref=source.at[1 - batch],
            dst_ref=target,
            send_sem=token_send.at[number],
            recv_sem=token_recv.at[number],
            device_id=partner,
            device_id_type=MESH,
        )

    def staying(number):
        source, target = tokens[number]
        return pltpu.make_async_copy(source.at[batch], target, kept.at[2 + number])

    def aside(number, source):
        index = lax.rem(place + (0, 3, 1, 2)[number], SIDE)
        return pltpu.make_async_remote_copy(
            src_ref=out_ref.at[index] if source is None else source,
            dst_ref=out_ref.at[index],
            send_sem=side_send.at[number],
            recv_sem=side_recv.at[number],
            device_id=beside,
            device_id_type=MESH,
        )

    def message(way, number, step, index, half, source):
        spot = out_ref.at[index, halves[half]]
        return pltpu.make_async_remote_copy(
            src_ref=spot if source is None else source.at[halves[half]],
            dst_ref=spot,
            send_sem=send.at[way, number],
            recv_sem=recv.at[way, number],
            device_id=device_at(section, at, 2, step),
            device_id_type=MESH,
        )

    @pl.when(section == 0)
    def _():
        own = pltpu.make_async_copy(local_ref, out_ref.at[place], kept.at[1])
        own.start()
        for number in range(2):
            staying(number).start()
        flying = {}
        for number in range(2):
            for way, step in enumerate((1, -1)):
                flying[way, number] = message(way, number, step, place, (number + way) % 2, local_ref)
                flying[way, number].start()
        sides = [aside(0, local_ref)]
        sides[0].start()
        for way, step in enumerate((1, -1)):
            flying[way, 0].wait_recv()
            flying[way, 2] = message(way, 2, step, shifted(at, 2, -step), way, None)
            flying[way, 2].start()
        for way in range(2):
            flying[way, 1].wait_recv()
            sides.append(aside(1 + way, None))
            sides[-1].start()
        for way in range(2):
            flying[way, 2].wait_recv()
        sides.append(aside(3, None))
        sides[-1].start()
        for side in sides:
            side.wait_send()
        for way in range(2):
            for number in range(3):
                flying[way, number].wait_send()
        own.wait()
        for number in range(2):
            staying(number).wait()

    @pl.when(section == 1)
    def _():
        for number in range(2):
            crossing(number).start()
        for number in range(2):
            crossing(number).wait()
        for number in range(4):
            aside(number, None).wait_recv()

    own_gains.wait()
    other_gains.wait()


def first_weight(local, gains, inputs, cotangent):
    rows, columns = local.shape
    any_space = pl.BlockSpec(memory_space=pl.ANY)
    return pl.pallas_call(
        first_weight_kernel,
        out_shape=(
            jax.ShapeDtypeStruct((SIDE, rows, columns), local.dtype),
            jax.ShapeDtypeStruct((2,) + gains.shape, gains.dtype),
            jax.ShapeDtypeStruct(inputs.shape[1:], inputs.dtype),
            jax.ShapeDtypeStruct(cotangent.shape[1:], cotangent.dtype),
        ),
        in_specs=[any_space] * 4,
        out_specs=(any_space,) * 4,
        scratch_shapes=[
            pltpu.SemaphoreType.DMA((2, 3)),
            pltpu.SemaphoreType.DMA((2, 3)),
            pltpu.SemaphoreType.DMA((4,)),
            pltpu.SemaphoreType.DMA((4,)),
            pltpu.SemaphoreType.DMA,
            pltpu.SemaphoreType.DMA,
            pltpu.SemaphoreType.DMA((2,)),
            pltpu.SemaphoreType.DMA((2,)),
            pltpu.SemaphoreType.DMA((4,)),
        ],
        compiler_params=pltpu.CompilerParams(collective_id=3, has_side_effects=True),
        cost_estimate=pl.CostEstimate(flops=0, bytes_accessed=8 * local.size, transcendentals=0),
    )(local, gains, inputs, cotangent)


def normalize(values):
    factor = lax.rsqrt(jnp.mean(values * values, axis=-1, keepdims=True) + epsilon)
    return (values * factor, factor)


def norm_back(grad_unit, unit, factor):
    return factor * (grad_unit - unit * jnp.mean(grad_unit * unit, axis=-1, keepdims=True))


def product(left, right):
    return jnp.dot(left, right, preferred_element_type=jnp.float32)


def product_turned(left, right):
    return lax.dot_general(left, right, contract_last, preferred_element_type=jnp.float32)


def is_lower(shape):
    return lax.broadcasted_iota(jnp.int32, shape, len(shape) - 1) < HEAD_DIM


def turned(tile, cosine, sine):
    half = HEAD_DIM // 2
    lane = lax.broadcasted_iota(jnp.int32, tile.shape, 1)
    other = jnp.where(
        lax.rem(lane, HEAD_DIM) < half, pltpu.roll(tile, 128 - half, 1), pltpu.roll(tile, half, 1)
    )
    return tile * cosine + other * sine


def swapped(tile):
    return pltpu.roll(tile, HEAD_DIM, 1)


def head_rows(ref, head):
    group, index = head // GROUP, head % GROUP
    rows = slice(index * CHUNK, (index + 1) * CHUNK)
    return jnp.concatenate([ref[group, 0, rows, :], ref[group, 1, rows, :]], axis=0)


def put_head(ref, head, tile):
    group, index = head // GROUP, head % GROUP
    rows = slice(index * CHUNK, (index + 1) * CHUNK)
    ref[group, 0, rows, :] = tile[:CHUNK]
    ref[group, 1, rows, :] = tile[CHUNK:]


def widen(wide, qkv):
    for head in range(HEADS):
        wide[128 * head : 128 * head + 64, :] = qkv[64 * head : 64 * head + 64, :]
        wide[128 * head + 64 : 128 * head + 128, :] = jnp.zeros((64, wide.shape[1]), wide.dtype)
    for group in range(KV_HEADS):
        start = 128 * (HEADS + group)
        wide[start : start + 64, :] = qkv[576 + 64 * group : 640 + 64 * group, :]
        wide[start + 64 : start + 128, :] = qkv[768 + 64 * group : 832 + 64 * group, :]


def project(current, gain, wide, cosine, sine, query_ref, local_ref):
    unit, _ = normalize(current)
    projected = product_turned((unit * gain).astype(jnp.bfloat16), wide[...])
    for head in range(HEADS):
        tile = turned(projected[:, 128 * head : 128 * head + 128], cosine, sine) * HEAD_DIM ** (-0.5)
        put_head(query_ref, head, tile.astype(jnp.bfloat16))
    for group in range(KV_HEADS):
        start = 128 * (HEADS + group)
        local_ref[group] = turned(projected[:, start : start + 128], cosine, sine).astype(jnp.bfloat16)


def project_back(grad_query_ref, grad_local_ref, current, grad_hidden, gain, wide, cosine, sine, terms_ref):
    lower = is_lower((2 * CHUNK, 128))
    tiles = []
    for head in range(HEADS):
        tile = jnp.where(lower, head_rows(grad_query_ref, head), 0.0)
        tiles.append(turned(tile, cosine, -sine) * HEAD_DIM ** (-0.5))
    for group in range(KV_HEADS):
        tiles.append(turned(grad_local_ref[group], cosine, -sine))
    grad_normed = product(
        jnp.concatenate([tile.astype(jnp.bfloat16) for tile in tiles], axis=1), wide[...]
    )
    unit, factor = normalize(current)
    key = tiles[HEADS:]
    pairs = [(tiles[2 * index], swapped(tiles[2 * index + 1])) for index in range(4)]
    pairs += [
        (tiles[8], swapped(key[0])),
        (key[1], swapped(key[2])),
        (swapped(key[0]), key[1]),
        (swapped(key[2]), jnp.zeros_like(key[2])),
    ]
    width = current.shape[1]
    terms_ref[:, :width] = (unit * gain).astype(jnp.bfloat16)
    for index, (low, high) in enumerate(pairs):
        terms_ref[:, 640 + 128 * index : 768 + 128 * index] = jnp.where(lower, low, high).astype(jnp.bfloat16)
    return grad_hidden + norm_back(grad_normed * gain, unit, factor)


def heads_mixed(mixed_ref):
    lower = is_lower((2 * CHUNK, 128))
    tiles = [head_rows(mixed_ref, head) for head in range(HEADS)]
    pairs = [jnp.where(lower, swapped(tiles[2 * i]), tiles[2 * i + 1]) for i in range(4)]
    pairs.append(swapped(tiles[8])[:, :HEAD_DIM])
    return jnp.concatenate([tile.astype(jnp.bfloat16) for tile in pairs], axis=1)


def feed_forward(current, mixed, out, gain, gate_up, down, waits):
    waits[0]()
    hidden = current + product_turned(mixed, out[...])
    unit, _ = normalize(hidden)
    normed = (unit * gain).astype(jnp.bfloat16)
    waits[1]()
    pair = [product(normed, gate_up[index]) for index in range(4)]
    act = [(pair[k] * jax.nn.sigmoid(pair[k]) * pair[k + 2]).astype(jnp.bfloat16) for k in range(2)]
    part = FF // 2
    waits[2]()
    result = hidden + (product_turned(act[0], down[:, :part]) + product_turned(act[1], down[:, part:]))
    return hidden, pair, result


def feed_back(grad_out, hidden, pair, mixed, mixed_ref, out, gain, gate_up, down, waits, terms_ref, grad_ref, inner_ref):
    part = FF // 2
    width = hidden.shape[1]
    branch = grad_out.astype(jnp.bfloat16)
    waits[2]()
    grad_act = product(branch, down[...])
    waits[1]()
    grad_normed = None
    for k in range(2):
        gate, upward = pair(k), pair(k + 2)
        squashed = jax.nn.sigmoid(gate)
        grad = grad_act[:, k * part : (k + 1) * part]
        grad_gate = (grad * upward * squashed * (1.0 + gate * (1.0 - squashed))).astype(jnp.bfloat16)
        grad_upward = (grad * (gate * squashed)).astype(jnp.bfloat16)
        terms_ref[:, 2560 + k * part : 2560 + (k + 1) * part] = grad_gate
        terms_ref[:, 2560 + (k + 2) * part : 2560 + (k + 3) * part] = grad_upward
        terms_ref[:, 5632 + k * part : 5632 + (k + 1) * part] = (gate * squashed * upward).astype(jnp.bfloat16)
        term = product_turned(grad_gate, gate_up[k]) + product_turned(grad_upward, gate_up[k + 2])
        grad_normed = term if grad_normed is None else grad_normed + term
    unit, factor = normalize(hidden)
    terms_ref[:, :width] = mixed
    terms_ref[:, 640 : 640 + width] = (unit * gain).astype(jnp.bfloat16)
    terms_ref[:, 1280 : 1280 + width] = branch
    grad_hidden = grad_out + norm_back(grad_normed * gain, unit, factor)
    grad_attn = grad_hidden.astype(jnp.bfloat16)
    terms_ref[:, 1920:2560] = jnp.concatenate(
        [jnp.zeros((2 * CHUNK, HEAD_DIM), jnp.float32), grad_hidden], axis=1
    ).astype(jnp.bfloat16)
    waits[0]()
    grad_mixed = product(grad_attn, out[...])
    lower = is_lower((2 * CHUNK, 128))
    for head in range(HEADS):
        start = 128 * (head // 2)
        if head == HEADS - 1:
            tile = jnp.concatenate([jnp.zeros((2 * CHUNK, HEAD_DIM), jnp.float32), grad_mixed[:, start:]], axis=1)
        else:
            tile = grad_mixed[:, start : start + 128]
            tile = jnp.where(lower, 0.0, tile if head % 2 else swapped(tile))
        tile = tile.astype(jnp.bfloat16)
        put_head(grad_ref, head, tile)
        inner = jnp.sum(tile.astype(jnp.float32) * head_rows(mixed_ref, head), axis=-1, keepdims=True)
        put_head(inner_ref, head, inner)
    return grad_hidden


def layer_weights(layer, small_ref, large_ref, out, gate_up, down):
    narrow, deep = w_out_rows(small_ref), gate_up.shape[1] // 2
    lists = ([], [], [])
    for shard in range(SIDE):
        small, large = small_ref.at[layer, shard], large_ref.at[layer, shard]
        rows = pl.ds(shard * narrow, narrow)
        lists[0].append((small.at[pl.ds(0, narrow)], out.at[rows]))
        for half in range(2):
            lists[1].append(
                (
                    large.at[pl.ds(0, deep), pl.ds(half * gate_up.shape[2], gate_up.shape[2])],
                    gate_up.at[shard, pl.ds(half * deep, deep)],
                )
            )
        lists[2].append((large.at[pl.ds(deep, narrow)], down.at[rows]))
    return list(lists)


def w_out_rows(small_ref):
    return small_ref.shape[3] // SIDE


def second_qkv(small_ref, qkv):
    narrow = w_out_rows(small_ref)
    rows = small_ref.shape[2] - narrow
    return [
        (small_ref.at[1, shard, pl.ds(narrow, rows)], qkv.at[pl.ds(shard * rows, rows)]) for shard in range(SIDE)
    ]


def brought(lists, sems):
    waits = []
    number = 0
    for pairs in lists:
        copies = []
        for source, target in pairs:
            copies.append(pltpu.make_async_copy(source, target, sems.at[number]))
            copies[-1].start()
            number += 1

        def wait(copies=tuple(copies)):
            for copy in copies:
                copy.wait()

        waits.append(wait)
    return waits


def once(waits):
    def first_only(wait):
        pending = [wait]

        def run():
            if pending:
                pending.pop()()

        return run

    return [first_only(wait) for wait in waits]


def enter_kernel(current_ref, gain_ref, cosine_ref, sine_ref, qkv_ref, query_ref, local_ref, wide):
    widen(wide, qkv_ref)
    project(
        current_ref[...].astype(jnp.float32), gain_ref[...], wide, cosine_ref[...], sine_ref[...], query_ref, local_ref
    )


def between_kernel(
    mixed_ref, current_ref, gain_ref, next_gain_ref, cosine_ref, sine_ref, small_ref, large_ref,
    hidden_ref, pair_ref, next_ref, query_ref, local_ref,
    out, gate_up, down, qkv, wide, sems,
):
    *waits, wait_qkv = brought(
        layer_weights(0, small_ref, large_ref, out, gate_up, down) + [second_qkv(small_ref, qkv)], sems
    )
    mixed = heads_mixed(mixed_ref)
    hidden, pair, result = feed_forward(
        current_ref[...].astype(jnp.float32), mixed, out, gain_ref[...], gate_up, down, waits
    )
    hidden_ref[...] = hidden
    for index in range(4):
        pair_ref[index] = pair[index]
    next_ref[...] = result
    wait_qkv()
    widen(wide, qkv)
    project(result, next_gain_ref[...], wide, cosine_ref[...], sine_ref[...], query_ref, local_ref)


def top_kernel(
    mixed_ref, current_ref, cotangent_ref, gain_ref, small_ref, large_ref,
    result_ref, grad_hidden_ref, terms_ref, grad_ref, inner_ref,
    out, gate_up, down, sems,
):
    waits = once(brought(layer_weights(1, small_ref, large_ref, out, gate_up, down), sems))
    mixed = heads_mixed(mixed_ref)
    gain = gain_ref[...]
    hidden, pair, result = feed_forward(current_ref[...], mixed, out, gain, gate_up, down, waits)
    result_ref[...] = result
    grad_hidden_ref[...] = feed_back(
        cotangent_ref[...].astype(jnp.float32), hidden, lambda index: pair[index], mixed, mixed_ref,
        out, gain, gate_up, down, waits, terms_ref, grad_ref, inner_ref,
    )


def descend_kernel(
    grad_query_ref, grad_local_ref, upper_ref, upper_grad_ref, upper_gain_ref, cosine_ref, sine_ref,
    mixed_ref, hidden_in_ref, pair_ref, gain_ref, small_ref, large_ref,
    upper_terms_ref, grad_hidden_ref, terms_ref, grad_ref, inner_ref,
    out, gate_up, down, qkv, wide, sems,
):
    wait_qkv, *waits = brought(
        [second_qkv(small_ref, qkv)] + layer_weights(0, small_ref, large_ref, out, gate_up, down), sems
    )
    wait_qkv()
    widen(wide, qkv)
    grad = project_back(
        grad_query_ref, grad_local_ref, upper_ref[...], upper_grad_ref[...], upper_gain_ref[...], wide,
        cosine_ref[...], sine_ref[...], upper_terms_ref,
    )
    grad_hidden_ref[...] = feed_back(
        grad, hidden_in_ref[...], lambda index: pair_ref[index], heads_mixed(mixed_ref), mixed_ref,
        out, gain_ref[...], gate_up, down, waits, terms_ref, grad_ref, inner_ref,
    )


def leave_kernel(
    grad_query_ref, grad_local_ref, current_ref, grad_hidden_ref, gain_ref, cosine_ref, sine_ref, qkv_ref,
    grad_in_ref, terms_ref, wide,
):
    widen(wide, qkv_ref)
    grad_in_ref[...] = project_back(
        grad_query_ref, grad_local_ref, current_ref[...].astype(jnp.float32), grad_hidden_ref[...], gain_ref[...], wide,
        cosine_ref[...], sine_ref[...], terms_ref,
    )


def weight_kernel(order_ref, low_ref, low_other_ref, high_ref, high_other_ref, out_ref, gathered):
    width = order_ref.shape[0]
    tiles = 6144 // 128
    blocks = 64

    def both(ref, other_ref, start, size):
        return jnp.concatenate([ref[:, start : start + size], other_ref[:, start : start + size]], axis=0)

    def left(ref, other_ref, start):
        columns = both(ref, other_ref, start, width)
        return product_turned(order_ref[...], columns).astype(jnp.bfloat16)

    def put(term, tile):
        for index in range(width // blocks):
            part, row = index // 3, (index % 3) * tiles + tile
            gathered[part, pl.ds(row, blocks, stride=3 * tiles), :] = term[index * blocks : (index + 1) * blocks]

    normed_one = left(low_ref, low_other_ref, 0)
    mixed = left(high_ref, high_other_ref, 0)
    first = product(normed_one, both(low_ref, low_other_ref, 640, 1024))
    second = product(mixed, both(high_ref, high_other_ref, 1920, 640))
    for tile in range(7):
        put(first[:, 128 * tile : 128 * tile + 128], tile)
    put(first[:, 896:] + second[:, :128], 7)
    for tile in range(1, 5):
        put(second[:, 128 * tile : 128 * tile + 128], 7 + tile)
    normed_two = left(high_ref, high_other_ref, 640)
    for step in range(6):
        third = product(normed_two, both(high_ref, high_other_ref, 2560 + 512 * step, 512))
        for tile in range(4):
            put(third[:, 128 * tile : 128 * tile + 128], 12 + 4 * step + tile)
    branch = left(high_ref, high_other_ref, 1280)
    for step in range(3):
        fourth = product(branch, both(high_ref, high_other_ref, 5632 + 512 * step, 512))
        for tile in range(4):
            put(fourth[:, 128 * tile : 128 * tile + 128], 36 + 4 * step + tile)

    for part in range(3):

        @pl.loop(0, blocks)
        def _(block, part=part):
            start = pl.multiple_of(block * (3 * tiles), 3 * tiles)
            out_ref[part, block] = gathered[part, pl.ds(start, 3 * tiles), :].astype(jnp.bfloat16)


TERMS_LOW = 1664
TERMS_HIGH = 7168


def dense(kernel, arguments, hbm, results, scratch, flops):
    vmem = pl.BlockSpec(memory_space=pltpu.VMEM)
    kept = [vmem] * (len(arguments) - hbm) + [pl.BlockSpec(memory_space=pl.ANY)] * hbm
    size = sum(item.size * item.dtype.itemsize for item in arguments)
    return pl.pallas_call(
        kernel,
        out_shape=tuple(jax.ShapeDtypeStruct(shape, kind) for shape, kind in results),
        in_specs=kept,
        out_specs=tuple(vmem for _ in results),
        scratch_shapes=scratch,
        compiler_params=pltpu.CompilerParams(vmem_limit_bytes=VMEM_LIMIT),
        cost_estimate=pl.CostEstimate(flops=flops, bytes_accessed=size, transcendentals=0),
    )(*arguments)


def on_device(inputs, positions, attn_gain, w_qkv, w_out, ffn_gain, w_gate_up, w_down, cotangent):
    _, rows, width = inputs.shape
    section = lax.axis_index("section")
    place = lax.axis_index(("ctx", "fsdp"))
    swap = [(0, 1), (1, 0)]
    half_kind, kind = jnp.bfloat16, jnp.float32
    lanes = 2 * HEAD_DIM
    columns = w_qkv.shape[2] * SIDE
    wide_rows = 128 * (HEADS + KV_HEADS)

    depth = lax.axis_index("fsdp")
    batch = depth // 2
    worked = place + section * (SIDE - 1 - 2 * depth)
    spots_k = lax.dynamic_index_in_dim(positions, batch, 0, keepdims=False)
    spots_q = lax.dynamic_slice_in_dim(spots_k, worked * rows, rows, 0)
    chunk_of = spots_k[::CHUNK] // CHUNK
    inverse = jnp.zeros_like(chunk_of).at[chunk_of].set(jnp.arange(chunk_of.shape[0], dtype=jnp.int32))
    spots = lax.dynamic_slice_in_dim(chunk_of, worked * 2, 2, 0)
    frequency = rope_base ** (-(jnp.arange(HEAD_DIM // 2, dtype=kind) * 2.0 / HEAD_DIM))
    angle = spots_q.astype(kind)[:, None] * frequency[None, :]
    cosine, sine = jnp.cos(angle), jnp.sin(angle)
    rest = jnp.ones((rows, HEAD_DIM), kind)
    cosine = jnp.concatenate([cosine, cosine, rest], axis=1)
    sine = jnp.concatenate([-sine, sine, 0.0 * rest], axis=1)

    local_gains = jnp.pad(jnp.concatenate([attn_gain, ffn_gain], axis=0), ((0, 6), (0, 0)))
    qkv_turned = w_qkv[0].T
    qkv_first, gains, current, given = first_weight(qkv_turned, local_gains, inputs, cotangent)
    qkv_first = qkv_first.reshape(columns, width)

    def gathered(local):
        return lax.all_gather(local, ("section", "fsdp"), axis=0, tiled=False)

    deep = width // 2
    small = gathered(jnp.concatenate([w_out[0].T, qkv_turned], axis=0))
    large = gathered(
        jnp.concatenate(
            [jnp.concatenate([w_gate_up[0][:deep], w_gate_up[0][deep:]], axis=1), w_down[0].T], axis=0
        )
    )
    small = small.reshape((2, SIDE) + small.shape[1:])
    large = large.reshape((2, SIDE) + large.shape[1:])
    gain_one = [gains[l, 0:1] for l in range(2)]
    gain_two = [gains[l, 1:2] for l in range(2)]

    query_like = ((KV_HEADS, 2, GROUP * CHUNK, lanes), half_kind)
    inner_like = ((KV_HEADS, 2, GROUP * CHUNK, 1), kind)
    local_like = ((KV_HEADS, rows, lanes), half_kind)
    state_like = ((rows, width), kind)
    pair_like = ((SIDE, rows, 2 * FF // SIDE), kind)
    low_like = ((rows, TERMS_LOW), half_kind)
    high_like = ((rows, TERMS_HIGH), half_kind)
    wide_scratch = pltpu.VMEM((wide_rows, width), half_kind)
    qkv_scratch = pltpu.VMEM((columns, width), half_kind)
    ffn_scratch = [
        pltpu.VMEM((width, width), half_kind),
        pltpu.VMEM((SIDE, width, 2 * FF // SIDE), half_kind),
        pltpu.VMEM((width, FF), half_kind),
    ]
    sems = pltpu.SemaphoreType.DMA((24,))
    qkv_flops = 2 * rows * width * wide_rows
    ffn_flops = 2 * rows * width * (width + 3 * FF)

    def attention(query, local):
        both = gather_all(local, 0).reshape(KV_HEADS, -1, CHUNK, lanes)
        mixed, logsum = attend(inverse, spots, query, both)
        return both, mixed, logsum

    def attention_back(query, grad, logsum, inner, both):
        grad_query, grad_both = attend_back(inverse, spots, query, grad, logsum, inner, both)
        grad_both = grad_both.reshape(KV_HEADS, SIDE, SIDE, 2, 2, rows, lanes)
        return grad_query, combine_all(grad_both, 1)

    query_one, local = dense(
        enter_kernel, (current, gain_one[0], cosine, sine, qkv_first), 0, (query_like, local_like), [wide_scratch], qkv_flops
    )
    both_one, mixed_one, logsum_one = attention(query_one, local)
    hidden, pair, middle, query_two, local = dense(
        between_kernel,
        (mixed_one, current, gain_two[0], gain_one[1], cosine, sine, small, large),
        2,
        (state_like, pair_like, state_like, query_like, local_like),
        ffn_scratch + [qkv_scratch, wide_scratch, sems],
        ffn_flops + qkv_flops,
    )
    both_two, mixed_two, logsum_two = attention(query_two, local)
    result, grad_hidden, high_two, grad, inner = dense(
        top_kernel,
        (mixed_two, middle, given, gain_two[1], small, large),
        2,
        (state_like, state_like, high_like, query_like, inner_like),
        ffn_scratch + [sems],
        2 * ffn_flops,
    )
    earlier = lax.ppermute(
        result,
        ("section", "ctx", "fsdp"),
        [(64 + 4 * ctx + z, 64 + 4 * ctx + 3 - z) for ctx in range(16) for z in range(4)],
    )
    grad_query, grad_local = attention_back(query_two, grad, logsum_two, inner, both_two)
    low_two, grad_hidden, high_one, grad, inner = dense(
        descend_kernel,
        (
            grad_query, grad_local, middle, grad_hidden, gain_one[1], cosine, sine,
            mixed_one, hidden, pair, gain_two[0], small, large,
        ),
        2,
        (low_like, state_like, high_like, query_like, inner_like),
        ffn_scratch + [qkv_scratch, wide_scratch, sems],
        ffn_flops + qkv_flops,
    )
    grad_query, grad_local = attention_back(query_one, grad, logsum_one, inner, both_one)
    grad_in, low_one = dense(
        leave_kernel,
        (grad_query, grad_local, current, grad_hidden, gain_one[0], cosine, sine, qkv_first),
        0,
        (state_like, low_like),
        [wide_scratch],
        qkv_flops,
    )

    first = section == 0
    low, low_other = jnp.where(first, low_one, low_two), jnp.where(first, low_two, low_one)
    high, high_other = jnp.where(first, high_one, high_two), jnp.where(first, high_two, high_one)
    low_other = lax.ppermute(low_other, "section", swap)
    high_other = lax.ppermute(high_other, "section", swap)
    blocks = SIDE * SIDE * SIDE
    each = width // blocks
    total = columns + width + 3 * FF
    line = jnp.arange(width)
    order = (line[:, None] % blocks * each + line[:, None] // blocks == line[None, :]).astype(half_kind)
    (term,) = dense(
        weight_kernel,
        (order, low, low_other, high, high_other),
        0,
        (((3, blocks, 3 * total // 128, 128), half_kind),),
        [pltpu.VMEM((3, blocks * 3 * total // 128, 128), kind)],
        4 * rows * width * total,
    )
    term = term.reshape(3, SIDE, SIDE, SIDE, 3 * total // 128, 128)
    summed = scatter_all(term, 80, 2).reshape(each, total)
    grad_qkv = summed[:, :columns]
    grad_out_weight = summed[:, columns : columns + width]
    grad_gate_up = summed[:, columns + width : columns + width + 2 * FF]
    grad_down = summed[:, columns + width + 2 * FF :].T

    own_layer = lax.dynamic_index_in_dim(small, section, 0, keepdims=False)[:, width // SIDE :]
    qkv_own = lax.dynamic_slice_in_dim(own_layer, place * each, each, 2).astype(kind)
    qkv_own = qkv_own.transpose(2, 0, 1).reshape(each, columns)
    half_place = lax.rem(place, blocks // 2)
    gate_up_own = lax.dynamic_slice(
        large,
        (section, 0, half_place * each, (place // (blocks // 2)) * w_gate_up.shape[2]),
        (1, SIDE, each, w_gate_up.shape[2]),
    )[0].astype(kind)
    split = grad_gate_up.reshape(each, SIDE, -1).transpose(1, 0, 2)
    grad_gain_one = jnp.sum(qkv_own * grad_qkv, axis=1) / lax.dynamic_slice_in_dim(attn_gain[0], place * each, each, 0)
    grad_gain_two = jnp.sum(gate_up_own * split, axis=(0, 2)) / lax.dynamic_slice_in_dim(
        ffn_gain[0], place * each, each, 0
    )

    def index_of(core, ctx, z):
        return (core * SIDE * SIDE + ctx) * SIDE + z

    places = [(ctx, z) for ctx in range(SIDE * SIDE) for z in range(SIDE)]
    axes = ("section", "ctx", "fsdp")
    later = lax.ppermute(
        jnp.where(first, result, grad_in),
        axes,
        [(index_of(0, ctx, z), index_of(1, ctx, z)) for ctx, z in places]
        + [(index_of(1, ctx, z), index_of(0, ctx, SIDE - 1 - z)) for ctx, z in places],
    )
    mine = jnp.where(first, grad_in, later)
    other = jnp.where(first, later, earlier)
    ends = jnp.where(batch == 0, jnp.stack([mine, other]), jnp.stack([other, mine]))
    return (
        ends[None],
        grad_gain_one[None],
        grad_qkv[None],
        grad_out_weight[None],
        grad_gain_two[None],
        grad_gate_up[None],
        grad_down[None],
    )


def solution(mesh):
    placed = (
        P(None, ("ctx", "fsdp"), None),
        P(),
        P("section", None),
        P("section", None, "fsdp"),
        P("section", None, "fsdp"),
        P("section", None),
        P("section", None, "fsdp"),
        P("section", None, "fsdp"),
        P(None, ("ctx", "fsdp"), None),
    )
    return jax.shard_map(
        on_device,
        mesh=mesh,
        in_specs=placed,
        out_specs=(
            P("section", None, ("ctx", "fsdp"), None),
            P("section", ("ctx", "fsdp")),
            P("section", ("ctx", "fsdp"), None),
            P("section", ("ctx", "fsdp"), None),
            P("section", ("ctx", "fsdp")),
            P("section", ("ctx", "fsdp"), None),
            P("section", None, ("ctx", "fsdp")),
        ),
        check_vma=False,
    )
```

```python
import functools

import jax
import jax.numpy as jnp
from jax import lax
from jax.experimental import pallas as pl
from jax.experimental.pallas import tpu as pltpu
from jax.sharding import PartitionSpec as P

HEADS = 9
KV_HEADS = 3
GROUP = 3
HEAD_DIM = 64
FF = 1536
CHUNK = 64
BLOCK = 512
PER = BLOCK // CHUNK
MESH = pl.DeviceIdType.MESH
VMEM_LIMIT = 56 * 1024 * 1024

epsilon = 1e-05
rope_base = 100000.0
contract_last = (((1,), (1,)), ((), ()))
contract_first = (((0,), (0,)), ((), ()))

ORDERS = ((2, 0, 1), (0, 1, 2), (1, 2, 0))
SIDE = 4


def here():
    ctx = lax.axis_index("ctx")
    return (lax.axis_index("section"), (ctx // SIDE, lax.rem(ctx, SIDE), lax.axis_index("fsdp")))


def shifted(at, axis, step):
    return lax.rem(at[axis] + (step + SIDE), SIDE)


def device_at(section, at, axis, step):
    moved = list(at)
    moved[axis] = shifted(at, axis, step)
    return (section, moved[0] * SIDE + moved[1], moved[2])


def enter(section, at):
    barrier = pltpu.get_barrier_semaphore()
    for axis in range(3):
        for step in (1, -1):
            pl.semaphore_signal(
                barrier, inc=1, device_id=device_at(section, at, axis, step), device_id_type=MESH
            )
    pl.semaphore_wait(barrier, 6)


def slab(ref, part, axes, fixed, rows):
    return ref.at[(part,) + tuple(fixed.get(axis, slice(None)) for axis in axes) + (rows,)]


def pair_step(at):
    return 1 - 2 * lax.rem(at[2], 2)


def ring(axis):
    return axis != 2


UNITS = ((0, 48, 0), (48, 96, 1), (96, 128, 2))
EXTENT = (SIDE, SIDE, 2)
STEPS = ((0, 1), (1, -1))


def across(last):
    first, second = [axis for axis in range(3) if axis != last]
    plane = [(a, b) for a in range(EXTENT[first]) for b in range(EXTENT[second])]
    result = []
    for a, b in plane[1:]:
        steps = [0, 0, 0]
        steps[first], steps[second] = a, b
        result.append(tuple(steps))
    return result


class Team:
    def __init__(self):
        self.section, self.at = here()
        w = lax.rem(self.at[2], 2)
        h = self.at[2] // 2
        self.h = lax.rem(h + self.section, 2)
        self.spot = (self.at[0], self.at[1], lax.rem(w + self.section, 2))

    def beside(self):
        return (1 - self.section, self.at[0] * SIDE + self.at[1], self.at[2])

    def shifted(self, axis, step):
        return lax.rem(self.spot[axis] + (step + SIDE), EXTENT[axis])

    def moved(self, steps):
        y, x = (lax.rem(self.at[axis] + (steps[axis] + SIDE), SIDE) for axis in range(2))
        z = self.at[2] + (pair_step(self.at) if steps[2] % 2 else 0)
        return (self.section, y * SIDE + x, z)

    def device(self, axis, step):
        return self.moved(tuple(step if other == axis else 0 for other in range(3)))

    def enter(self):
        barrier = pltpu.get_barrier_semaphore()
        known = sorted({steps for last in range(3) for steps in across(last)})
        for device in [self.moved(steps) for steps in known] + [self.beside()]:
            pl.semaphore_signal(barrier, inc=1, device_id=device, device_id_type=MESH)
        pl.semaphore_wait(barrier, len(known) + 1)


PEERS = 15


def gather_kernel(local_ref, out_ref, near_send, near_recv, send, recv, side_send, side_recv, kept):
    team = Team()
    team.enter()
    spot, h = team.spot, team.h
    own = pltpu.make_async_copy(local_ref, out_ref.at[:, spot[0], spot[1], h, spot[2]], kept)
    own.start()
    every = range(len(UNITS))

    def remote(source, target, send_sem, recv_sem, device):
        copy = pltpu.make_async_remote_copy(
            src_ref=source, dst_ref=target, send_sem=send_sem, recv_sem=recv_sem, device_id=device, device_id_type=MESH
        )
        copy.start()
        return copy

    def slab(unit, coordinate, w=slice(None)):
        start, stop, last = UNITS[unit]
        fixed = {2: w, last: coordinate}
        y, x, w = (fixed.get(axis, slice(None)) for axis in range(3))
        return out_ref.at[:, y, x, h, w, pl.ds(start, stop - start)]

    nears = []
    for unit in every:
        start, stop, last = UNITS[unit]
        rows = pl.ds(start, stop - start)
        for number, steps in enumerate(across(last)):
            nears.append(
                remote(
                    local_ref.at[:, rows],
                    out_ref.at[:, spot[0], spot[1], h, spot[2], rows],
                    near_send.at[unit, number],
                    near_recv.at[unit, number],
                    team.moved(steps),
                )
            )

    def message(unit, way, number, step, coordinate, w):
        place = slab(unit, coordinate, w)
        return remote(
            place, place, send.at[unit, way, number], recv.at[unit, way, number], team.device(UNITS[unit][2], step)
        )

    def aside(unit, slot, coordinate):
        place = slab(unit, coordinate)
        return remote(place, place, side_send.at[unit, slot], side_recv.at[unit, slot], team.beside())

    own.wait()
    for copy in nears:
        copy.wait_recv()
    flying, sides = {}, []
    for number in range(2):
        for unit in every:
            axis = UNITS[unit][2]
            if ring(axis):
                for way, step in STEPS:
                    flying[unit, way, number] = message(unit, way, number, step, spot[axis], (number + way) % 2)
            elif number == 0:
                flying[unit, 0, 0] = message(unit, 0, 0, 1, spot[axis], spot[axis])
    for unit in every:
        sides.append(aside(unit, 0, spot[UNITS[unit][2]]))
    for unit in every:
        axis = UNITS[unit][2]
        if ring(axis):
            for way, step in STEPS:
                flying[unit, way, 0].wait_recv()
                flying[unit, way, 2] = message(unit, way, 2, step, team.shifted(axis, -step), way)
    for unit in every:
        axis = UNITS[unit][2]
        if ring(axis):
            for way, step in STEPS:
                flying[unit, way, 1].wait_recv()
                sides.append(aside(unit, 1 + way, team.shifted(axis, -step)))
    for unit in every:
        axis = UNITS[unit][2]
        if ring(axis):
            for way, _ in STEPS:
                flying[unit, way, 2].wait_recv()
            sides.append(aside(unit, 3, team.shifted(axis, 2)))
        else:
            flying[unit, 0, 0].wait_recv()
            sides.append(aside(unit, 1, team.shifted(axis, 1)))
    for copy in nears + list(flying.values()):
        copy.wait_send()
    for copy in sides:
        copy.wait()


def transfer_sems():
    count = len(UNITS)
    shapes = ((count, PEERS), (count, 2, 3), (count, 4))
    return [pltpu.SemaphoreType.DMA(shape) for shape in shapes for _ in range(2)]


def gather_all(local, collective_id):
    parts, rows, lanes = local.shape
    return pl.pallas_call(
        gather_kernel,
        out_shape=jax.ShapeDtypeStruct((parts, SIDE, SIDE, 2, 2, rows, lanes), local.dtype),
        in_specs=[pl.BlockSpec(memory_space=pltpu.VMEM)],
        out_specs=pl.BlockSpec(memory_space=pl.ANY),
        scratch_shapes=transfer_sems() + [pltpu.SemaphoreType.DMA],
        compiler_params=pltpu.CompilerParams(
            collective_id=collective_id, has_side_effects=True, vmem_limit_bytes=VMEM_LIMIT
        ),
        cost_estimate=pl.CostEstimate(flops=0, bytes_accessed=2 * 64 * local.size, transcendentals=0),
    )(local)


def add_blocks(target, terms):
    outer = target.shape[:-2]
    count = 1
    for size in outer:
        count *= size

    def one(index):
        total = terms[0][index].astype(jnp.float32)
        for term in terms[1:]:
            total = total + term[index].astype(jnp.float32)
        target[index] = total.astype(target.dtype)

    @pl.loop(0, count)
    def _(step):
        index = ()
        for size in reversed(outer):
            index = (lax.rem(step, size),) + index
            step = step // size
        one(index)


PARTS = 3


def combine_shapes(kind):
    shapes = []
    for start, stop, last in UNITS:
        block = (stop - start, 128)
        plane = tuple(EXTENT[axis] for axis in range(3) if axis != last)
        shapes.append(pltpu.VMEM((PARTS,) + EXTENT + block, kind))
        if ring(last):
            shapes.append(pltpu.VMEM((6, PARTS, SIDE) + block, kind))
        else:
            shapes.append(pltpu.VMEM((PARTS,) + plane + block, kind))
        shapes.append(pltpu.VMEM((PARTS,) + plane + block, kind))
        shapes.append(pltpu.VMEM((len(across(last)), PARTS) + block, kind))
    return shapes


def combine_kernel(terms_ref, out_ref, *refs):
    count = len(UNITS)
    every = range(count)
    joined = [refs[4 * unit] for unit in every]
    landing = [refs[4 * unit + 1] for unit in every]
    sums = [refs[4 * unit + 2] for unit in every]
    final = [refs[4 * unit + 3] for unit in every]
    near_send, near_recv, send, recv, side_send, side_recv = refs[4 * count :]
    team = Team()
    team.enter()
    spot = team.spot

    def remote(source, target, send_sem, recv_sem, device):
        copy = pltpu.make_async_remote_copy(
            src_ref=source, dst_ref=target, send_sem=send_sem, recv_sem=recv_sem, device_id=device, device_id_type=MESH
        )
        copy.start()
        return copy

    def cut(unit, coordinate, w=slice(None)):
        fixed = {2: w, UNITS[unit][2]: coordinate}
        return tuple(fixed.get(axis, slice(None)) for axis in range(3))

    def own(unit, coordinate, w=slice(None)):
        return joined[unit].at[(slice(None),) + cut(unit, coordinate, w)]

    def given(unit, slot, leaving):
        start, stop, axis = UNITS[unit]
        h = 1 - team.h if leaving else team.h
        if ring(axis):
            coordinate = team.shifted(axis, (2, 1, -1, 0)[slot])
        else:
            coordinate = team.shifted(axis, slot if leaving else 1 - slot)
        w = coordinate if axis == 2 else slice(None)
        y, x, w = cut(unit, coordinate, w)
        return terms_ref.at[:, y, x, h, w, pl.ds(start, stop - start)], own(unit, coordinate, w)

    def slots(unit):
        return 4 if ring(UNITS[unit][2]) else 2

    sides = {}
    for slot in range(4):
        for unit in every:
            if slot < slots(unit):
                source, target = given(unit, slot, True)
                sides[unit, slot] = remote(
                    source, target, side_send.at[unit, slot], side_recv.at[unit, slot], team.beside()
                )

    def join(unit, slot):
        sides[unit, slot].wait_recv()
        source, target = given(unit, slot, False)
        add_blocks(target, (target, source))

    def message(unit, way, number, step, source):
        target = landing[unit].at[3 * way + number] if ring(UNITS[unit][2]) else landing[unit]
        return remote(
            source, target, send.at[unit, way, number], recv.at[unit, way, number], team.device(UNITS[unit][2], step)
        )

    flying = {}
    for number in range(2):
        for unit in every:
            axis = UNITS[unit][2]
            if not ring(axis):
                if number == 0:
                    join(unit, 0)
                    coordinate = team.shifted(axis, 1)
                    flying[unit, 0, 0] = message(unit, 0, 0, 1, own(unit, coordinate, coordinate))
                continue
            if number == 0:
                join(unit, 0)
            for way, step in STEPS:
                if number == 1:
                    join(unit, 1 + way)
                coordinate = team.shifted(axis, 2 * step if number == 0 else step)
                flying[unit, way, number] = message(
                    unit, way, number, step, own(unit, coordinate, (number + way) % 2)
                )
    for unit in every:
        axis = UNITS[unit][2]
        if ring(axis):
            for way, step in STEPS:
                flying[unit, way, 0].wait_recv()
                passing = landing[unit].at[3 * way]
                add_blocks(passing, (passing, own(unit, team.shifted(axis, step), way)))
                flying[unit, way, 2] = message(unit, way, 2, step, passing)
    for unit in every:
        join(unit, slots(unit) - 1)
    nears = {}
    for unit in every:
        start, stop, axis = UNITS[unit]
        if ring(axis):
            for way, _ in STEPS:
                flying[unit, way, 1].wait_recv()
                flying[unit, way, 2].wait_recv()
            for w in range(2):
                add_blocks(
                    sums[unit].at[:, :, w],
                    (own(unit, spot[axis], w), landing[unit].at[3 * w + 2], landing[unit].at[3 * (1 - w) + 1]),
                )
        else:
            flying[unit, 0, 0].wait_recv()
            add_blocks(sums[unit], (own(unit, spot[axis], spot[axis]), landing[unit]))
        first, second = [other for other in range(3) if other != axis]
        for number, steps in enumerate(across(axis)):
            nears[unit, number] = remote(
                sums[unit].at[:, team.shifted(first, steps[first]), team.shifted(second, steps[second])],
                final[unit].at[number],
                near_send.at[unit, number],
                near_recv.at[unit, number],
                team.moved(steps),
            )
    for unit in every:
        start, stop, axis = UNITS[unit]
        first, second = [other for other in range(3) if other != axis]
        peers = len(across(axis))
        for number in range(peers):
            nears[unit, number].wait_recv()

        @pl.loop(0, PARTS)
        def _(part, unit=unit, start=start, stop=stop, first=first, second=second, peers=peers):
            total = sums[unit][part, spot[first], spot[second]].astype(jnp.float32)
            for number in range(peers):
                total = total + final[unit][number, part].astype(jnp.float32)
            out_ref[part, pl.ds(start, stop - start), :] = total
    for copies in (flying, sides, nears):
        for copy in copies.values():
            copy.wait_send()


def combine_all(terms, collective_id):
    parts, rows, lanes = terms.shape[0], terms.shape[-2], terms.shape[-1]
    return pl.pallas_call(
        combine_kernel,
        out_shape=jax.ShapeDtypeStruct((parts, rows, lanes), jnp.float32),
        in_specs=[pl.BlockSpec(memory_space=pltpu.VMEM)],
        out_specs=pl.BlockSpec(memory_space=pltpu.VMEM),
        scratch_shapes=combine_shapes(terms.dtype) + transfer_sems(),
        compiler_params=pltpu.CompilerParams(
            collective_id=collective_id, has_side_effects=True, vmem_limit_bytes=VMEM_LIMIT
        ),
        cost_estimate=pl.CostEstimate(flops=terms.size, bytes_accessed=2 * terms.size, transcendentals=0),
    )(terms)


def scatter_kernel(split, terms_ref, out_ref, sum_one, sum_two, near_one, far_one, near_two, far_two, near_three, far_three, send, recv):
    rows = terms_ref.shape[-2]
    halves = (pl.ds(0, split), pl.ds(split, rows - split))
    section, at = here()
    enter(section, at)
    sums = (terms_ref, sum_one, sum_two, out_ref)
    landing = ((near_one, far_one), (near_two, far_two), (near_three, far_three))

    def remaining(part, phase):
        return tuple(sorted(ORDERS[part][: 3 - phase]))

    def axis_of(part, phase):
        return ORDERS[part][2 - phase]

    def landed(phase, part, way, number):
        half = (number + way) % 2
        slot = {(0, 0): 0, (0, 2): 1, (1, 1): 2, (0, 1): 0, (1, 0): 1, (1, 2): 2}[way, number]
        return landing[phase][half].at[slot, part]

    def message(phase, part, way, number, step, source):
        axis = axis_of(part, phase)
        return pltpu.make_async_remote_copy(
            src_ref=source,
            dst_ref=landed(phase, part, way, number),
            send_sem=send.at[phase, part, way, number],
            recv_sem=recv.at[phase, part, way, number],
            device_id=device_at(section, at, axis, step),
            device_id_type=MESH,
        )

    def own(phase, part, coordinate, half):
        return slab(sums[phase], part, remaining(part, phase), {axis_of(part, phase): coordinate}, halves[half])

    def add(phase, target, terms):
        outer = target.shape[:-2]
        count = 1
        for size in outer:
            count *= size

        def one(index):
            total = terms[0][index].astype(jnp.float32)
            for term in terms[1:]:
                total = total + term[index].astype(jnp.float32)
            target[index] = total.astype(target.dtype)

        if count == 1:
            one((slice(None),) * 2)
            return

        @pl.loop(0, count)
        def _(step):
            if len(outer) == 1:
                one((step,))
            else:
                one((step // SIDE, lax.rem(step, SIDE)))

    for phase in range(3):
        flying = {}
        for number in range(2):
            for part in range(3):
                axis = axis_of(part, phase)
                for way, step in enumerate((1, -1)):
                    coordinate = shifted(at, axis, 2 * step if number == 0 else step)
                    copy = message(phase, part, way, number, step, own(phase, part, coordinate, (number + way) % 2))
                    copy.start()
                    flying[part, way, number] = copy
        for part in range(3):
            axis = axis_of(part, phase)
            for way, step in enumerate((1, -1)):
                flying[part, way, 0].wait_recv()
                passing = landed(phase, part, way, 0)
                add(phase, passing, (passing, own(phase, part, shifted(at, axis, step), way)))
                copy = message(phase, part, way, 2, step, passing)
                copy.start()
                flying[part, way, 2] = copy
        for part in range(3):
            axis = axis_of(part, phase)
            for way in range(2):
                flying[part, way, 1].wait_recv()
                flying[part, way, 2].wait_recv()
            for half in range(2):
                target = sums[phase + 1].at[(part,) + (slice(None),) * (2 - phase) + (halves[half],)]
                add(
                    phase,
                    target,
                    (
                        own(phase, part, at[axis], half),
                        landed(phase, part, half, 2),
                        landed(phase, part, 1 - half, 1),
                    ),
                )
        for part in range(3):
            for way in range(2):
                for number in range(3):
                    flying[part, way, number].wait_send()


def scatter_all(terms, split, collective_id):
    parts, rows, lanes = terms.shape[0], terms.shape[-2], terms.shape[-1]
    kind = terms.dtype
    near, far = split, rows - split
    return pl.pallas_call(
        functools.partial(scatter_kernel, split),
        out_shape=jax.ShapeDtypeStruct((parts, rows, lanes), jnp.float32),
        in_specs=[pl.BlockSpec(memory_space=pltpu.VMEM)],
        out_specs=pl.BlockSpec(memory_space=pltpu.VMEM),
        scratch_shapes=[
            pltpu.VMEM((parts, SIDE, SIDE, rows, lanes), kind),
            pltpu.VMEM((parts, SIDE, rows, lanes), kind),
            pltpu.VMEM((3, parts, SIDE, SIDE, near, lanes), kind),
            pltpu.VMEM((3, parts, SIDE, SIDE, far, lanes), kind),
            pltpu.VMEM((3, parts, SIDE, near, lanes), kind),
            pltpu.VMEM((3, parts, SIDE, far, lanes), kind),
            pltpu.VMEM((3, parts, near, lanes), kind),
            pltpu.VMEM((3, parts, far, lanes), kind),
            pltpu.SemaphoreType.DMA((3, 3, 2, 3)),
            pltpu.SemaphoreType.DMA((3, 3, 2, 3)),
        ],
        compiler_params=pltpu.CompilerParams(
            collective_id=collective_id, has_side_effects=True, vmem_limit_bytes=VMEM_LIMIT
        ),
        cost_estimate=pl.CostEstimate(flops=terms.size, bytes_accessed=2 * terms.size, transcendentals=0),
    )(terms)


def fetch_sorted(inverse_ref, source_ref, keys, sems):
    @pl.loop(0, inverse_ref.shape[0])
    def _(chunk):
        pltpu.make_async_copy(
            source_ref.at[:, inverse_ref[chunk]],
            keys.at[:, pl.ds(pl.multiple_of(chunk * CHUNK, CHUNK), CHUNK)],
            sems.at[chunk // PER],
        ).start()


def wait_block(keys, sems, block):
    rows = keys.at[:, pl.ds(pl.multiple_of(block * BLOCK, BLOCK), BLOCK)]
    pltpu.make_async_copy(rows, rows, sems.at[block]).wait()


def visible(shape, chunk, block):
    row = lax.broadcasted_iota(jnp.int32, shape, 0)
    column = lax.broadcasted_iota(jnp.int32, shape, 1)
    return block * BLOCK + column <= chunk * CHUNK + lax.rem(row, CHUNK)


def attend_kernel(inverse_ref, spots_ref, query_ref, source_ref, mixed_ref, logsum_ref, keys, sems):
    rows = query_ref.shape[2]
    blocks = keys.shape[1] // BLOCK
    fetch_sorted(inverse_ref, source_ref, keys, sems)
    ready = jnp.int32(0)
    for half in range(2):
        chunk = spots_ref[half]
        whole = chunk // PER

        def step(block, carry, masked, half=half, chunk=chunk, ready=ready):
            @pl.when(block >= ready)
            def _():
                wait_block(keys, sems, block)

            start = pl.multiple_of(block * BLOCK, BLOCK)
            result = []
            for group in range(KV_HEADS):
                highest, total, mixed = carry[3 * group : 3 * group + 3]
                both = keys[group, pl.ds(start, BLOCK), :]
                scores = lax.dot_general(
                    query_ref[group, half], both, contract_last, preferred_element_type=jnp.float32
                )
                if masked:
                    scores = jnp.where(visible(scores.shape, chunk, block), scores, -1e30)
                higher = jnp.maximum(highest, jnp.max(scores, axis=-1, keepdims=True))
                exponent = jnp.exp(scores - higher)
                shrink = jnp.exp(highest - higher)
                total = total * shrink + jnp.sum(exponent, axis=-1, keepdims=True)
                mixed = mixed * shrink + jnp.dot(
                    exponent.astype(jnp.bfloat16), both, preferred_element_type=jnp.float32
                )
                result += [higher, total, mixed]
            return tuple(result)

        carry = ()
        for group in range(KV_HEADS):
            carry += (
                jnp.full((rows, 1), -1e30, jnp.float32),
                jnp.zeros((rows, 1), jnp.float32),
                jnp.zeros((rows, 2 * HEAD_DIM), jnp.float32),
            )
        carry = lax.fori_loop(0, whole, functools.partial(step, masked=False), carry)
        carry = step(whole, carry, masked=True)
        ready = jnp.maximum(ready, whole + 1)
        for group in range(KV_HEADS):
            highest, total, mixed = carry[3 * group : 3 * group + 3]
            mixed_ref[group, half] = mixed / total
            logsum_ref[group, half] = highest + jnp.log(total)

    @pl.loop(ready, blocks)
    def _(block):
        wait_block(keys, sems, block)


def attend(inverse, spots, query, both):
    groups, halves, rows, lanes = query.shape
    chunks = both.shape[1]
    scores = rows * halves * groups * (chunks * CHUNK // 2)
    return pl.pallas_call(
        attend_kernel,
        out_shape=(
            jax.ShapeDtypeStruct((groups, halves, rows, lanes), jnp.float32),
            jax.ShapeDtypeStruct((groups, halves, rows, 1), jnp.float32),
        ),
        in_specs=[
            pl.BlockSpec(memory_space=pltpu.SMEM),
            pl.BlockSpec(memory_space=pltpu.SMEM),
            pl.BlockSpec(memory_space=pltpu.VMEM),
            pl.BlockSpec(memory_space=pl.ANY),
        ],
        out_specs=(pl.BlockSpec(memory_space=pltpu.VMEM), pl.BlockSpec(memory_space=pltpu.VMEM)),
        scratch_shapes=[
            pltpu.VMEM((groups, chunks * CHUNK, lanes), jnp.bfloat16),
            pltpu.SemaphoreType.DMA((chunks // PER,)),
        ],
        compiler_params=pltpu.CompilerParams(vmem_limit_bytes=VMEM_LIMIT),
        cost_estimate=pl.CostEstimate(flops=4 * scores * lanes, bytes_accessed=4 * both.size, transcendentals=scores),
    )(inverse, spots, query, both)


def attend_back_kernel(
    inverse_ref, spots_ref, query_ref, grad_ref, logsum_ref, inner_ref, source_ref,
    grad_query_ref, out_ref, keys, totals, rounded, sems, out_sem,
):
    rows = query_ref.shape[2]
    blocks = keys.shape[1] // BLOCK
    fetch_sorted(inverse_ref, source_ref, keys, sems)

    @pl.loop(0, blocks)
    def _(block):
        totals[:, pl.ds(pl.multiple_of(block * BLOCK, BLOCK), BLOCK), :] = jnp.zeros(
            (KV_HEADS, BLOCK, 2 * HEAD_DIM), jnp.float32
        )

    ready = jnp.int32(0)
    for half in range(2):
        chunk = spots_ref[half]
        whole = chunk // PER

        def step(block, carry, masked, half=half, chunk=chunk, ready=ready):
            @pl.when(block >= ready)
            def _():
                wait_block(keys, sems, block)

            start = pl.multiple_of(block * BLOCK, BLOCK)
            result = []
            for group in range(KV_HEADS):
                both = keys[group, pl.ds(start, BLOCK), :]
                query = query_ref[group, half]
                grad = grad_ref[group, half]
                scores = lax.dot_general(query, both, contract_last, preferred_element_type=jnp.float32)
                probs = jnp.exp(scores - logsum_ref[group, half])
                if masked:
                    probs = jnp.where(visible(scores.shape, chunk, block), probs, 0.0)
                grad_weights = lax.dot_general(grad, both, contract_last, preferred_element_type=jnp.float32)
                grad_scores = (probs * (grad_weights - inner_ref[group, half])).astype(jnp.bfloat16)
                weights = probs.astype(jnp.bfloat16)
                result.append(
                    carry[group] + jnp.dot(grad_scores, both, preferred_element_type=jnp.float32)
                )
                totals[group, pl.ds(start, BLOCK), :] += lax.dot_general(
                    jnp.concatenate([weights, grad_scores], axis=0),
                    jnp.concatenate([grad, query], axis=0),
                    contract_first,
                    preferred_element_type=jnp.float32,
                )
            return tuple(result)

        carry = tuple(jnp.zeros((rows, 2 * HEAD_DIM), jnp.float32) for _ in range(KV_HEADS))
        carry = lax.fori_loop(0, whole, functools.partial(step, masked=False), carry)
        carry = step(whole, carry, masked=True)
        ready = jnp.maximum(ready, whole + 1)
        for group in range(KV_HEADS):
            grad_query_ref[group, half] = carry[group]

    @pl.loop(ready, blocks)
    def _(block):
        wait_block(keys, sems, block)

    @pl.loop(0, blocks * PER)
    def _(chunk):
        place = pl.ds(pl.multiple_of(chunk * CHUNK, CHUNK), CHUNK)
        rounded[:, place, :] = totals[:, place, :].astype(jnp.bfloat16)
        pltpu.make_async_copy(rounded.at[:, place], out_ref.at[:, inverse_ref[chunk]], out_sem).start()

    pltpu.make_async_copy(rounded, rounded, out_sem).wait()


def attend_back(inverse, spots, query, grad, logsum, inner, both):
    groups, halves, rows, lanes = query.shape
    chunks = both.shape[1]
    scores = rows * halves * groups * (chunks * CHUNK // 2)
    vmem = pl.BlockSpec(memory_space=pltpu.VMEM)
    smem = pl.BlockSpec(memory_space=pltpu.SMEM)
    return pl.pallas_call(
        attend_back_kernel,
        out_shape=(
            jax.ShapeDtypeStruct((groups, halves, rows, lanes), jnp.float32),
            jax.ShapeDtypeStruct(both.shape, jnp.bfloat16),
        ),
        in_specs=[smem, smem, vmem, vmem, vmem, vmem, pl.BlockSpec(memory_space=pl.ANY)],
        out_specs=(vmem, pl.BlockSpec(memory_space=pl.ANY)),
        scratch_shapes=[
            pltpu.VMEM((groups, chunks * CHUNK, lanes), jnp.bfloat16),
            pltpu.VMEM((groups, chunks * CHUNK, lanes), jnp.float32),
            pltpu.VMEM((groups, chunks * CHUNK, lanes), jnp.bfloat16),
            pltpu.SemaphoreType.DMA((chunks // PER,)),
            pltpu.SemaphoreType.DMA,
        ],
        compiler_params=pltpu.CompilerParams(vmem_limit_bytes=VMEM_LIMIT),
        cost_estimate=pl.CostEstimate(flops=10 * scores * lanes, bytes_accessed=4 * both.size, transcendentals=scores),
    )(inverse, spots, query, grad, logsum, inner, both)


def first_weight_kernel(
    local_ref, gains_ref, inputs_ref, cotangent_ref, out_ref, gains_out_ref, current_ref, given_ref,
    send, recv, side_send, side_recv, gain_send, gain_recv, token_send, token_recv, kept,
):
    rows = local_ref.shape[0]
    halves = (pl.ds(0, 128), pl.ds(128, rows - 128))
    section, at = here()
    place = at[2]
    beside = (1 - section, at[0] * SIDE + at[1], place)
    barrier = pltpu.get_barrier_semaphore()
    for device in (device_at(section, at, 2, 1), device_at(section, at, 2, -1), beside):
        pl.semaphore_signal(barrier, inc=1, device_id=device, device_id_type=MESH)
    pl.semaphore_wait(barrier, 3)
    own_gains = pltpu.make_async_copy(gains_ref, gains_out_ref.at[section], kept.at[0])
    own_gains.start()
    other_gains = pltpu.make_async_remote_copy(
        src_ref=gains_ref,
        dst_ref=gains_out_ref.at[section],
        send_sem=gain_send,
        recv_sem=gain_recv,
        device_id=beside,
        device_id_type=MESH,
    )
    other_gains.start()

    batch = place // 2
    partner = (section, at[0] * SIDE + at[1], SIDE - 1 - place)
    tokens = ((inputs_ref, current_ref), (cotangent_ref, given_ref))

    def crossing(number):
        source, target = tokens[number]
        return pltpu.make_async_remote_copy(
            src_ref=source.at[1 - batch],
            dst_ref=target,
            send_sem=token_send.at[number],
            recv_sem=token_recv.at[number],
            device_id=partner,
            device_id_type=MESH,
        )

    def staying(number):
        source, target = tokens[number]
        return pltpu.make_async_copy(source.at[batch], target, kept.at[2 + number])

    def aside(number, source):
        index = lax.rem(place + (0, 3, 1, 2)[number], SIDE)
        return pltpu.make_async_remote_copy(
            src_ref=out_ref.at[index] if source is None else source,
            dst_ref=out_ref.at[index],
            send_sem=side_send.at[number],
            recv_sem=side_recv.at[number],
            device_id=beside,
            device_id_type=MESH,
        )

    def message(way, number, step, index, half, source):
        spot = out_ref.at[index, halves[half]]
        return pltpu.make_async_remote_copy(
            src_ref=spot if source is None else source.at[halves[half]],
            dst_ref=spot,
            send_sem=send.at[way, number],
            recv_sem=recv.at[way, number],
            device_id=device_at(section, at, 2, step),
            device_id_type=MESH,
        )

    @pl.when(section == 0)
    def _():
        own = pltpu.make_async_copy(local_ref, out_ref.at[place], kept.at[1])
        own.start()
        for number in range(2):
            staying(number).start()
        flying = {}
        for number in range(2):
            for way, step in enumerate((1, -1)):
                flying[way, number] = message(way, number, step, place, (number + way) % 2, local_ref)
                flying[way, number].start()
        sides = [aside(0, local_ref)]
        sides[0].start()
        for way, step in enumerate((1, -1)):
            flying[way, 0].wait_recv()
            flying[way, 2] = message(way, 2, step, shifted(at, 2, -step), way, None)
            flying[way, 2].start()
        for way in range(2):
            flying[way, 1].wait_recv()
            sides.append(aside(1 + way, None))
            sides[-1].start()
        for way in range(2):
            flying[way, 2].wait_recv()
        sides.append(aside(3, None))
        sides[-1].start()
        for side in sides:
            side.wait_send()
        for way in range(2):
            for number in range(3):
                flying[way, number].wait_send()
        own.wait()
        for number in range(2):
            staying(number).wait()

    @pl.when(section == 1)
    def _():
        for number in range(2):
            crossing(number).start()
        for number in range(2):
            crossing(number).wait()
        for number in range(4):
            aside(number, None).wait_recv()

    own_gains.wait()
    other_gains.wait()


def first_weight(local, gains, inputs, cotangent):
    rows, columns = local.shape
    any_space = pl.BlockSpec(memory_space=pl.ANY)
    return pl.pallas_call(
        first_weight_kernel,
        out_shape=(
            jax.ShapeDtypeStruct((SIDE, rows, columns), local.dtype),
            jax.ShapeDtypeStruct((2,) + gains.shape, gains.dtype),
            jax.ShapeDtypeStruct(inputs.shape[1:], inputs.dtype),
            jax.ShapeDtypeStruct(cotangent.shape[1:], cotangent.dtype),
        ),
        in_specs=[any_space] * 4,
        out_specs=(any_space,) * 4,
        scratch_shapes=[
            pltpu.SemaphoreType.DMA((2, 3)),
            pltpu.SemaphoreType.DMA((2, 3)),
            pltpu.SemaphoreType.DMA((4,)),
            pltpu.SemaphoreType.DMA((4,)),
            pltpu.SemaphoreType.DMA,
            pltpu.SemaphoreType.DMA,
            pltpu.SemaphoreType.DMA((2,)),
            pltpu.SemaphoreType.DMA((2,)),
            pltpu.SemaphoreType.DMA((4,)),
        ],
        compiler_params=pltpu.CompilerParams(collective_id=3, has_side_effects=True),
        cost_estimate=pl.CostEstimate(flops=0, bytes_accessed=8 * local.size, transcendentals=0),
    )(local, gains, inputs, cotangent)


def normalize(values):
    factor = lax.rsqrt(jnp.mean(values * values, axis=-1, keepdims=True) + epsilon)
    return (values * factor, factor)


def norm_back(grad_unit, unit, factor):
    return factor * (grad_unit - unit * jnp.mean(grad_unit * unit, axis=-1, keepdims=True))


def product(left, right):
    return jnp.dot(left, right, preferred_element_type=jnp.float32)


def product_turned(left, right):
    return lax.dot_general(left, right, contract_last, preferred_element_type=jnp.float32)


def is_lower(shape):
    return lax.broadcasted_iota(jnp.int32, shape, len(shape) - 1) < HEAD_DIM


def turned(tile, cosine, sine):
    half = HEAD_DIM // 2
    lane = lax.broadcasted_iota(jnp.int32, tile.shape, 1)
    other = jnp.where(
        lax.rem(lane, HEAD_DIM) < half, pltpu.roll(tile, 128 - half, 1), pltpu.roll(tile, half, 1)
    )
    return tile * cosine + other * sine


def swapped(tile):
    return pltpu.roll(tile, HEAD_DIM, 1)


def head_rows(ref, head):
    group, index = head // GROUP, head % GROUP
    rows = slice(index * CHUNK, (index + 1) * CHUNK)
    return jnp.concatenate([ref[group, 0, rows, :], ref[group, 1, rows, :]], axis=0)


def put_head(ref, head, tile):
    group, index = head // GROUP, head % GROUP
    rows = slice(index * CHUNK, (index + 1) * CHUNK)
    ref[group, 0, rows, :] = tile[:CHUNK]
    ref[group, 1, rows, :] = tile[CHUNK:]


def widen(wide, qkv):
    for head in range(HEADS):
        wide[128 * head : 128 * head + 64, :] = qkv[64 * head : 64 * head + 64, :]
        wide[128 * head + 64 : 128 * head + 128, :] = jnp.zeros((64, wide.shape[1]), wide.dtype)
    for group in range(KV_HEADS):
        start = 128 * (HEADS + group)
        wide[start : start + 64, :] = qkv[576 + 64 * group : 640 + 64 * group, :]
        wide[start + 64 : start + 128, :] = qkv[768 + 64 * group : 832 + 64 * group, :]


def project(current, gain, wide, cosine, sine, query_ref, local_ref):
    unit, _ = normalize(current)
    projected = product_turned((unit * gain).astype(jnp.bfloat16), wide[...])
    for head in range(HEADS):
        tile = turned(projected[:, 128 * head : 128 * head + 128], cosine, sine) * HEAD_DIM ** (-0.5)
        put_head(query_ref, head, tile.astype(jnp.bfloat16))
    for group in range(KV_HEADS):
        start = 128 * (HEADS + group)
        local_ref[group] = turned(projected[:, start : start + 128], cosine, sine).astype(jnp.bfloat16)


def project_back(grad_query_ref, grad_local_ref, current, grad_hidden, gain, wide, cosine, sine, terms_ref):
    lower = is_lower((2 * CHUNK, 128))
    tiles = []
    for head in range(HEADS):
        tile = jnp.where(lower, head_rows(grad_query_ref, head), 0.0)
        tiles.append(turned(tile, cosine, -sine) * HEAD_DIM ** (-0.5))
    for group in range(KV_HEADS):
        tiles.append(turned(grad_local_ref[group], cosine, -sine))
    grad_normed = product(
        jnp.concatenate([tile.astype(jnp.bfloat16) for tile in tiles], axis=1), wide[...]
    )
    unit, factor = normalize(current)
    key = tiles[HEADS:]
    pairs = [(tiles[2 * index], swapped(tiles[2 * index + 1])) for index in range(4)]
    pairs += [
        (tiles[8], swapped(key[0])),
        (key[1], swapped(key[2])),
        (swapped(key[0]), key[1]),
        (swapped(key[2]), jnp.zeros_like(key[2])),
    ]
    width = current.shape[1]
    terms_ref[:, :width] = (unit * gain).astype(jnp.bfloat16)
    for index, (low, high) in enumerate(pairs):
        terms_ref[:, 640 + 128 * index : 768 + 128 * index] = jnp.where(lower, low, high).astype(jnp.bfloat16)
    return grad_hidden + norm_back(grad_normed * gain, unit, factor)


def heads_mixed(mixed_ref):
    lower = is_lower((2 * CHUNK, 128))
    tiles = [head_rows(mixed_ref, head) for head in range(HEADS)]
    pairs = [jnp.where(lower, swapped(tiles[2 * i]), tiles[2 * i + 1]) for i in range(4)]
    pairs.append(swapped(tiles[8])[:, :HEAD_DIM])
    return jnp.concatenate([tile.astype(jnp.bfloat16) for tile in pairs], axis=1)


def feed_forward(current, mixed, out, gain, gate_up, down, waits):
    waits[0]()
    hidden = current + product_turned(mixed, out[...])
    unit, _ = normalize(hidden)
    normed = (unit * gain).astype(jnp.bfloat16)
    waits[1]()
    pair = [product(normed, gate_up[index]) for index in range(4)]
    act = [(pair[k] * jax.nn.sigmoid(pair[k]) * pair[k + 2]).astype(jnp.bfloat16) for k in range(2)]
    part = FF // 2
    waits[2]()
    result = hidden + (product_turned(act[0], down[:, :part]) + product_turned(act[1], down[:, part:]))
    return hidden, pair, result


def feed_back(grad_out, hidden, pair, mixed, mixed_ref, out, gain, gate_up, down, waits, terms_ref, grad_ref, inner_ref):
    part = FF // 2
    width = hidden.shape[1]
    branch = grad_out.astype(jnp.bfloat16)
    waits[2]()
    grad_act = product(branch, down[...])
    waits[1]()
    grad_normed = None
    for k in range(2):
        gate, upward = pair(k), pair(k + 2)
        squashed = jax.nn.sigmoid(gate)
        grad = grad_act[:, k * part : (k + 1) * part]
        grad_gate = (grad * upward * squashed * (1.0 + gate * (1.0 - squashed))).astype(jnp.bfloat16)
        grad_upward = (grad * (gate * squashed)).astype(jnp.bfloat16)
        terms_ref[:, 2560 + k * part : 2560 + (k + 1) * part] = grad_gate
        terms_ref[:, 2560 + (k + 2) * part : 2560 + (k + 3) * part] = grad_upward
        terms_ref[:, 5632 + k * part : 5632 + (k + 1) * part] = (gate * squashed * upward).astype(jnp.bfloat16)
        term = product_turned(grad_gate, gate_up[k]) + product_turned(grad_upward, gate_up[k + 2])
        grad_normed = term if grad_normed is None else grad_normed + term
    unit, factor = normalize(hidden)
    terms_ref[:, :width] = mixed
    terms_ref[:, 640 : 640 + width] = (unit * gain).astype(jnp.bfloat16)
    terms_ref[:, 1280 : 1280 + width] = branch
    grad_hidden = grad_out + norm_back(grad_normed * gain, unit, factor)
    grad_attn = grad_hidden.astype(jnp.bfloat16)
    terms_ref[:, 1920:2560] = jnp.concatenate(
        [jnp.zeros((2 * CHUNK, HEAD_DIM), jnp.float32), grad_hidden], axis=1
    ).astype(jnp.bfloat16)
    waits[0]()
    grad_mixed = product(grad_attn, out[...])
    lower = is_lower((2 * CHUNK, 128))
    for head in range(HEADS):
        start = 128 * (head // 2)
        if head == HEADS - 1:
            tile = jnp.concatenate([jnp.zeros((2 * CHUNK, HEAD_DIM), jnp.float32), grad_mixed[:, start:]], axis=1)
        else:
            tile = grad_mixed[:, start : start + 128]
            tile = jnp.where(lower, 0.0, tile if head % 2 else swapped(tile))
        tile = tile.astype(jnp.bfloat16)
        put_head(grad_ref, head, tile)
        inner = jnp.sum(tile.astype(jnp.float32) * head_rows(mixed_ref, head), axis=-1, keepdims=True)
        put_head(inner_ref, head, inner)
    return grad_hidden


def layer_weights(layer, gathered, out, gate_up, down):
    deep = gate_up.shape[1] // 2
    narrow = out.shape[0] // SIDE
    lists = ([], [], [])
    for shard in range(SIDE):
        small, large = ([refs[kind].at[shard] for refs in gathered] for kind in range(2))
        rows = pl.ds(shard * narrow, narrow)
        lists[0].append(([ref.at[pl.ds(0, narrow)] for ref in small], out.at[rows]))
        for half in range(2):
            columns = pl.ds(half * gate_up.shape[2], gate_up.shape[2])
            lists[1].append(
                (
                    [ref.at[pl.ds(0, deep), columns] for ref in large],
                    gate_up.at[shard, pl.ds(half * deep, deep)],
                )
            )
        lists[2].append(([ref.at[pl.ds(deep, narrow)] for ref in large], down.at[rows]))
    return [(layer, pairs) for pairs in lists]


def second_qkv(gathered, qkv):
    rows = qkv.shape[0] // SIDE
    narrow = qkv.shape[1] // SIDE
    return (
        1,
        [
            ([refs[0].at[shard, pl.ds(narrow, rows)] for refs in gathered], qkv.at[pl.ds(shard * rows, rows)])
            for shard in range(SIDE)
        ],
    )


def brought(lists, sems):
    section = lax.axis_index("section")
    numbered = []
    for layer, pairs in lists:
        start = sum(len(copies) for copies in numbered)
        copies = [
            [pltpu.make_async_copy(source, target, sems.at[start + number]) for source in sources]
            for number, (sources, target) in enumerate(pairs)
        ]
        numbered.append(copies)
        for which in range(2):

            @pl.when(section == (layer if which == 0 else 1 - layer))
            def _(copies=copies, which=which):
                for choice in copies:
                    choice[which].start()

    def waiter(copies):
        def wait():
            for choice in copies:
                choice[0].wait()

        return wait

    return [waiter(copies) for copies in numbered]


def once(waits):
    def first_only(wait):
        pending = [wait]

        def run():
            if pending:
                pending.pop()()

        return run

    return [first_only(wait) for wait in waits]


def enter_kernel(current_ref, gain_ref, cosine_ref, sine_ref, qkv_ref, query_ref, local_ref, wide):
    widen(wide, qkv_ref)
    project(
        current_ref[...].astype(jnp.float32), gain_ref[...], wide, cosine_ref[...], sine_ref[...], query_ref, local_ref
    )


def between_kernel(
    mixed_ref, current_ref, gain_ref, next_gain_ref, cosine_ref, sine_ref, small_ref, large_ref, small_other_ref, large_other_ref,
    hidden_ref, pair_ref, next_ref, query_ref, local_ref,
    out, gate_up, down, qkv, wide, sems,
):
    weights = ((small_ref, large_ref), (small_other_ref, large_other_ref))
    *waits, wait_qkv = brought(
        layer_weights(0, weights, out, gate_up, down) + [second_qkv(weights, qkv)], sems
    )
    mixed = heads_mixed(mixed_ref)
    hidden, pair, result = feed_forward(
        current_ref[...].astype(jnp.float32), mixed, out, gain_ref[...], gate_up, down, waits
    )
    hidden_ref[...] = hidden
    for index in range(4):
        pair_ref[index] = pair[index]
    next_ref[...] = result
    wait_qkv()
    widen(wide, qkv)
    project(result, next_gain_ref[...], wide, cosine_ref[...], sine_ref[...], query_ref, local_ref)


def top_kernel(
    mixed_ref, current_ref, cotangent_ref, gain_ref, small_ref, large_ref, small_other_ref, large_other_ref,
    result_ref, grad_hidden_ref, terms_ref, grad_ref, inner_ref,
    out, gate_up, down, sems,
):
    weights = ((small_ref, large_ref), (small_other_ref, large_other_ref))
    waits = once(brought(layer_weights(1, weights, out, gate_up, down), sems))
    mixed = heads_mixed(mixed_ref)
    gain = gain_ref[...]
    hidden, pair, result = feed_forward(current_ref[...], mixed, out, gain, gate_up, down, waits)
    result_ref[...] = result
    grad_hidden_ref[...] = feed_back(
        cotangent_ref[...].astype(jnp.float32), hidden, lambda index: pair[index], mixed, mixed_ref,
        out, gain, gate_up, down, waits, terms_ref, grad_ref, inner_ref,
    )


def descend_kernel(
    grad_query_ref, grad_local_ref, upper_ref, upper_grad_ref, upper_gain_ref, cosine_ref, sine_ref,
    mixed_ref, hidden_in_ref, pair_ref, gain_ref, small_ref, large_ref, small_other_ref, large_other_ref,
    upper_terms_ref, grad_hidden_ref, terms_ref, grad_ref, inner_ref,
    out, gate_up, down, qkv, wide, sems,
):
    weights = ((small_ref, large_ref), (small_other_ref, large_other_ref))
    wait_qkv, *waits = brought(
        [second_qkv(weights, qkv)] + layer_weights(0, weights, out, gate_up, down), sems
    )
    wait_qkv()
    widen(wide, qkv)
    grad = project_back(
        grad_query_ref, grad_local_ref, upper_ref[...], upper_grad_ref[...], upper_gain_ref[...], wide,
        cosine_ref[...], sine_ref[...], upper_terms_ref,
    )
    grad_hidden_ref[...] = feed_back(
        grad, hidden_in_ref[...], lambda index: pair_ref[index], heads_mixed(mixed_ref), mixed_ref,
        out, gain_ref[...], gate_up, down, waits, terms_ref, grad_ref, inner_ref,
    )


def leave_kernel(
    grad_query_ref, grad_local_ref, current_ref, grad_hidden_ref, gain_ref, cosine_ref, sine_ref, qkv_ref,
    grad_in_ref, terms_ref, wide,
):
    widen(wide, qkv_ref)
    grad_in_ref[...] = project_back(
        grad_query_ref, grad_local_ref, current_ref[...].astype(jnp.float32), grad_hidden_ref[...], gain_ref[...], wide,
        cosine_ref[...], sine_ref[...], terms_ref,
    )


def weight_kernel(order_ref, low_ref, low_other_ref, high_ref, high_other_ref, out_ref, gathered):
    width = order_ref.shape[0]
    tiles = 6144 // 128
    blocks = 64

    def both(ref, other_ref, start, size):
        return jnp.concatenate([ref[:, start : start + size], other_ref[:, start : start + size]], axis=0)

    def left(ref, other_ref, start):
        columns = both(ref, other_ref, start, width)
        return product_turned(order_ref[...], columns).astype(jnp.bfloat16)

    def put(term, tile):
        for index in range(width // blocks):
            part, row = index // 3, (index % 3) * tiles + tile
            gathered[part, pl.ds(row, blocks, stride=3 * tiles), :] = term[index * blocks : (index + 1) * blocks]

    normed_one = left(low_ref, low_other_ref, 0)
    mixed = left(high_ref, high_other_ref, 0)
    first = product(normed_one, both(low_ref, low_other_ref, 640, 1024))
    second = product(mixed, both(high_ref, high_other_ref, 1920, 640))
    for tile in range(7):
        put(first[:, 128 * tile : 128 * tile + 128], tile)
    put(first[:, 896:] + second[:, :128], 7)
    for tile in range(1, 5):
        put(second[:, 128 * tile : 128 * tile + 128], 7 + tile)
    normed_two = left(high_ref, high_other_ref, 640)
    for step in range(6):
        third = product(normed_two, both(high_ref, high_other_ref, 2560 + 512 * step, 512))
        for tile in range(4):
            put(third[:, 128 * tile : 128 * tile + 128], 12 + 4 * step + tile)
    branch = left(high_ref, high_other_ref, 1280)
    for step in range(3):
        fourth = product(branch, both(high_ref, high_other_ref, 5632 + 512 * step, 512))
        for tile in range(4):
            put(fourth[:, 128 * tile : 128 * tile + 128], 36 + 4 * step + tile)

    for part in range(3):

        @pl.loop(0, blocks)
        def _(block, part=part):
            start = pl.multiple_of(block * (3 * tiles), 3 * tiles)
            out_ref[part, block] = gathered[part, pl.ds(start, 3 * tiles), :].astype(jnp.bfloat16)


TERMS_LOW = 1664
TERMS_HIGH = 7168


def dense(kernel, arguments, hbm, results, scratch, flops):
    vmem = pl.BlockSpec(memory_space=pltpu.VMEM)
    kept = [vmem] * (len(arguments) - hbm) + [pl.BlockSpec(memory_space=pl.ANY)] * hbm
    size = sum(item.size * item.dtype.itemsize for item in arguments)
    return pl.pallas_call(
        kernel,
        out_shape=tuple(jax.ShapeDtypeStruct(shape, kind) for shape, kind in results),
        in_specs=kept,
        out_specs=tuple(vmem for _ in results),
        scratch_shapes=scratch,
        compiler_params=pltpu.CompilerParams(vmem_limit_bytes=VMEM_LIMIT),
        cost_estimate=pl.CostEstimate(flops=flops, bytes_accessed=size, transcendentals=0),
    )(*arguments)


def on_device(inputs, positions, attn_gain, w_qkv, w_out, ffn_gain, w_gate_up, w_down, cotangent):
    _, rows, width = inputs.shape
    section = lax.axis_index("section")
    place = lax.axis_index(("ctx", "fsdp"))
    swap = [(0, 1), (1, 0)]
    half_kind, kind = jnp.bfloat16, jnp.float32
    lanes = 2 * HEAD_DIM
    columns = w_qkv.shape[2] * SIDE
    wide_rows = 128 * (HEADS + KV_HEADS)

    depth = lax.axis_index("fsdp")
    batch = depth // 2
    worked = place + section * (SIDE - 1 - 2 * depth)
    spots_k = lax.dynamic_index_in_dim(positions, batch, 0, keepdims=False)
    spots_q = lax.dynamic_slice_in_dim(spots_k, worked * rows, rows, 0)
    chunk_of = spots_k[::CHUNK] // CHUNK
    inverse = jnp.zeros_like(chunk_of).at[chunk_of].set(jnp.arange(chunk_of.shape[0], dtype=jnp.int32))
    spots = lax.dynamic_slice_in_dim(chunk_of, worked * 2, 2, 0)
    frequency = rope_base ** (-(jnp.arange(HEAD_DIM // 2, dtype=kind) * 2.0 / HEAD_DIM))
    angle = spots_q.astype(kind)[:, None] * frequency[None, :]
    cosine, sine = jnp.cos(angle), jnp.sin(angle)
    rest = jnp.ones((rows, HEAD_DIM), kind)
    cosine = jnp.concatenate([cosine, cosine, rest], axis=1)
    sine = jnp.concatenate([-sine, sine, 0.0 * rest], axis=1)

    local_gains = jnp.pad(jnp.concatenate([attn_gain, ffn_gain], axis=0), ((0, 6), (0, 0)))
    qkv_turned = w_qkv[0].T
    qkv_first, gains, current, given = first_weight(qkv_turned, local_gains, inputs, cotangent)
    qkv_first = qkv_first.reshape(columns, width)

    def gathered(local):
        return lax.all_gather(local, "fsdp", axis=0, tiled=False)

    deep = width // 2
    small = gathered(jnp.concatenate([w_out[0].T, qkv_turned], axis=0))
    large = gathered(
        jnp.concatenate(
            [jnp.concatenate([w_gate_up[0][:deep], w_gate_up[0][deep:]], axis=1), w_down[0].T], axis=0
        )
    )
    small_other = lax.ppermute(small, "section", swap)
    large_other = lax.ppermute(large, "section", swap)
    gain_one = [gains[l, 0:1] for l in range(2)]
    gain_two = [gains[l, 1:2] for l in range(2)]

    query_like = ((KV_HEADS, 2, GROUP * CHUNK, lanes), half_kind)
    inner_like = ((KV_HEADS, 2, GROUP * CHUNK, 1), kind)
    local_like = ((KV_HEADS, rows, lanes), half_kind)
    state_like = ((rows, width), kind)
    pair_like = ((SIDE, rows, 2 * FF // SIDE), kind)
    low_like = ((rows, TERMS_LOW), half_kind)
    high_like = ((rows, TERMS_HIGH), half_kind)
    wide_scratch = pltpu.VMEM((wide_rows, width), half_kind)
    qkv_scratch = pltpu.VMEM((columns, width), half_kind)
    ffn_scratch = [
        pltpu.VMEM((width, width), half_kind),
        pltpu.VMEM((SIDE, width, 2 * FF // SIDE), half_kind),
        pltpu.VMEM((width, FF), half_kind),
    ]
    sems = pltpu.SemaphoreType.DMA((24,))
    qkv_flops = 2 * rows * width * wide_rows
    ffn_flops = 2 * rows * width * (width + 3 * FF)

    def attention(query, local):
        both = gather_all(local, 0).reshape(KV_HEADS, -1, CHUNK, lanes)
        mixed, logsum = attend(inverse, spots, query, both)
        return both, mixed, logsum

    def attention_back(query, grad, logsum, inner, both):
        grad_query, grad_both = attend_back(inverse, spots, query, grad, logsum, inner, both)
        grad_both = grad_both.reshape(KV_HEADS, SIDE, SIDE, 2, 2, rows, lanes)
        return grad_query, combine_all(grad_both, 1)

    query_one, local = dense(
        enter_kernel, (current, gain_one[0], cosine, sine, qkv_first), 0, (query_like, local_like), [wide_scratch], qkv_flops
    )
    both_one, mixed_one, logsum_one = attention(query_one, local)
    hidden, pair, middle, query_two, local = dense(
        between_kernel,
        (mixed_one, current, gain_two[0], gain_one[1], cosine, sine, small, large, small_other, large_other),
        4,
        (state_like, pair_like, state_like, query_like, local_like),
        ffn_scratch + [qkv_scratch, wide_scratch, sems],
        ffn_flops + qkv_flops,
    )
    both_two, mixed_two, logsum_two = attention(query_two, local)
    result, grad_hidden, high_two, grad, inner = dense(
        top_kernel,
        (mixed_two, middle, given, gain_two[1], small, large, small_other, large_other),
        4,
        (state_like, state_like, high_like, query_like, inner_like),
        ffn_scratch + [sems],
        2 * ffn_flops,
    )
    earlier = lax.ppermute(
        result,
        ("section", "ctx", "fsdp"),
        [(64 + 4 * ctx + z, 64 + 4 * ctx + 3 - z) for ctx in range(16) for z in range(4)],
    )
    grad_query, grad_local = attention_back(query_two, grad, logsum_two, inner, both_two)
    low_two, grad_hidden, high_one, grad, inner = dense(
        descend_kernel,
        (
            grad_query, grad_local, middle, grad_hidden, gain_one[1], cosine, sine,
            mixed_one, hidden, pair, gain_two[0], small, large, small_other, large_other,
        ),
        4,
        (low_like, state_like, high_like, query_like, inner_like),
        ffn_scratch + [qkv_scratch, wide_scratch, sems],
        ffn_flops + qkv_flops,
    )
    grad_query, grad_local = attention_back(query_one, grad, logsum_one, inner, both_one)
    grad_in, low_one = dense(
        leave_kernel,
        (grad_query, grad_local, current, grad_hidden, gain_one[0], cosine, sine, qkv_first),
        0,
        (state_like, low_like),
        [wide_scratch],
        qkv_flops,
    )

    first = section == 0
    low, low_other = jnp.where(first, low_one, low_two), jnp.where(first, low_two, low_one)
    high, high_other = jnp.where(first, high_one, high_two), jnp.where(first, high_two, high_one)
    low_other = lax.ppermute(low_other, "section", swap)
    high_other = lax.ppermute(high_other, "section", swap)
    blocks = SIDE * SIDE * SIDE
    each = width // blocks
    total = columns + width + 3 * FF
    line = jnp.arange(width)
    order = (line[:, None] % blocks * each + line[:, None] // blocks == line[None, :]).astype(half_kind)
    (term,) = dense(
        weight_kernel,
        (order, low, low_other, high, high_other),
        0,
        (((3, blocks, 3 * total // 128, 128), half_kind),),
        [pltpu.VMEM((3, blocks * 3 * total // 128, 128), kind)],
        4 * rows * width * total,
    )
    term = term.reshape(3, SIDE, SIDE, SIDE, 3 * total // 128, 128)
    summed = scatter_all(term, 80, 2).reshape(each, total)
    grad_qkv = summed[:, :columns]
    grad_out_weight = summed[:, columns : columns + width]
    grad_gate_up = summed[:, columns + width : columns + width + 2 * FF]
    grad_down = summed[:, columns + width + 2 * FF :].T

    qkv_own = lax.dynamic_slice_in_dim(small[:, width // SIDE :], place * each, each, 2).astype(kind)
    qkv_own = qkv_own.transpose(2, 0, 1).reshape(each, columns)
    half_place = lax.rem(place, blocks // 2)
    gate_up_own = lax.dynamic_slice(
        large,
        (0, half_place * each, (place // (blocks // 2)) * w_gate_up.shape[2]),
        (SIDE, each, w_gate_up.shape[2]),
    ).astype(kind)
    split = grad_gate_up.reshape(each, SIDE, -1).transpose(1, 0, 2)
    grad_gain_one = jnp.sum(qkv_own * grad_qkv, axis=1) / lax.dynamic_slice_in_dim(attn_gain[0], place * each, each, 0)
    grad_gain_two = jnp.sum(gate_up_own * split, axis=(0, 2)) / lax.dynamic_slice_in_dim(
        ffn_gain[0], place * each, each, 0
    )

    def index_of(core, ctx, z):
        return (core * SIDE * SIDE + ctx) * SIDE + z

    places = [(ctx, z) for ctx in range(SIDE * SIDE) for z in range(SIDE)]
    axes = ("section", "ctx", "fsdp")
    later = lax.ppermute(
        jnp.where(first, result, grad_in),
        axes,
        [(index_of(0, ctx, z), index_of(1, ctx, z)) for ctx, z in places]
        + [(index_of(1, ctx, z), index_of(0, ctx, SIDE - 1 - z)) for ctx, z in places],
    )
    mine = jnp.where(first, grad_in, later)
    other = jnp.where(first, later, earlier)
    ends = jnp.where(batch == 0, jnp.stack([mine, other]), jnp.stack([other, mine]))
    return (
        ends[None],
        grad_gain_one[None],
        grad_qkv[None],
        grad_out_weight[None],
        grad_gain_two[None],
        grad_gate_up[None],
        grad_down[None],
    )


def solution(mesh):
    placed = (
        P(None, ("ctx", "fsdp"), None),
        P(),
        P("section", None),
        P("section", None, "fsdp"),
        P("section", None, "fsdp"),
        P("section", None),
        P("section", None, "fsdp"),
        P("section", None, "fsdp"),
        P(None, ("ctx", "fsdp"), None),
    )
    return jax.shard_map(
        on_device,
        mesh=mesh,
        in_specs=placed,
        out_specs=(
            P("section", None, ("ctx", "fsdp"), None),
            P("section", ("ctx", "fsdp")),
            P("section", ("ctx", "fsdp"), None),
            P("section", ("ctx", "fsdp"), None),
            P("section", ("ctx", "fsdp")),
            P("section", ("ctx", "fsdp"), None),
            P("section", None, ("ctx", "fsdp")),
        ),
        check_vma=False,
    )
```

```python
import functools

import jax
import jax.numpy as jnp
from jax import lax
from jax.experimental import pallas as pl
from jax.experimental.pallas import tpu as pltpu
from jax.sharding import PartitionSpec as P

HEADS = 9
KV_HEADS = 3
GROUP = 3
HEAD_DIM = 64
FF = 1536
CHUNK = 64
BLOCK = 512
PER = BLOCK // CHUNK
MESH = pl.DeviceIdType.MESH
VMEM_LIMIT = 56 * 1024 * 1024

epsilon = 1e-05
rope_base = 100000.0
contract_last = (((1,), (1,)), ((), ()))
contract_first = (((0,), (0,)), ((), ()))

ORDERS = ((2, 0, 1), (0, 1, 2), (1, 2, 0))
SIDE = 4


def here():
    ctx = lax.axis_index("ctx")
    return (lax.axis_index("section"), (ctx // SIDE, lax.rem(ctx, SIDE), lax.axis_index("fsdp")))


def shifted(at, axis, step):
    return lax.rem(at[axis] + (step + SIDE), SIDE)


def device_at(section, at, axis, step):
    moved = list(at)
    moved[axis] = shifted(at, axis, step)
    return (section, moved[0] * SIDE + moved[1], moved[2])


def enter(section, at):
    barrier = pltpu.get_barrier_semaphore()
    for axis in range(3):
        for step in (1, -1):
            pl.semaphore_signal(
                barrier, inc=1, device_id=device_at(section, at, axis, step), device_id_type=MESH
            )
    pl.semaphore_wait(barrier, 6)


def slab(ref, part, axes, fixed, rows):
    return ref.at[(part,) + tuple(fixed.get(axis, slice(None)) for axis in axes) + (rows,)]


def pair_step(at):
    return 1 - 2 * lax.rem(at[2], 2)


def ring(axis):
    return axis != 2


UNITS = ((0, 64, 0), (64, 128, 1))
EXTENT = (SIDE, SIDE, 2)
STEPS = ((0, 1), (1, -1))


def across(last):
    first, second = [axis for axis in range(3) if axis != last]
    plane = [(a, b) for a in range(EXTENT[first]) for b in range(EXTENT[second])]
    result = []
    for a, b in plane[1:]:
        steps = [0, 0, 0]
        steps[first], steps[second] = a, b
        result.append(tuple(steps))
    return result


class Team:
    def __init__(self):
        self.section, self.at = here()
        w = lax.rem(self.at[2], 2)
        h = self.at[2] // 2
        self.h = lax.rem(h + self.section, 2)
        self.spot = (self.at[0], self.at[1], lax.rem(w + self.section, 2))

    def beside(self):
        return (1 - self.section, self.at[0] * SIDE + self.at[1], self.at[2])

    def shifted(self, axis, step):
        return lax.rem(self.spot[axis] + (step + SIDE), EXTENT[axis])

    def moved(self, steps):
        y, x = (lax.rem(self.at[axis] + (steps[axis] + SIDE), SIDE) for axis in range(2))
        z = self.at[2] + (pair_step(self.at) if steps[2] % 2 else 0)
        return (self.section, y * SIDE + x, z)

    def device(self, axis, step):
        return self.moved(tuple(step if other == axis else 0 for other in range(3)))

    def enter(self, known=None):
        barrier = pltpu.get_barrier_semaphore()
        known = known or sorted({steps for _, _, last in UNITS for steps in across(last)})
        devices = [self.moved(steps) for steps in known] + [self.beside()]
        if known is STRAIGHT:
            devices.append(device_at(self.section, self.at, 2, -pair_step(self.at)))
        for device in devices:
            pl.semaphore_signal(barrier, inc=1, device_id=device, device_id_type=MESH)
        pl.semaphore_wait(barrier, len(devices))


PEERS = 7


def transfer_sems():
    count = len(UNITS)
    shapes = ((count, PEERS), (count, 2, 3), (count, 4))
    return [pltpu.SemaphoreType.DMA(shape) for shape in shapes for _ in range(2)]


def add_blocks(target, terms):
    outer = target.shape[:-2]
    count = 1
    for size in outer:
        count *= size

    def one(index):
        total = terms[0][index].astype(jnp.float32)
        for term in terms[1:]:
            total = total + term[index].astype(jnp.float32)
        target[index] = total.astype(target.dtype)

    @pl.loop(0, count)
    def _(step):
        index = ()
        for size in reversed(outer):
            index = (lax.rem(step, size),) + index
            step = step // size
        one(index)


PARTS = 3


def combine_shapes(kind):
    shapes = []
    for start, stop, last in UNITS:
        block = (stop - start, 128)
        plane = tuple(EXTENT[axis] for axis in range(3) if axis != last)
        shapes.append(pltpu.VMEM((PARTS,) + EXTENT + block, kind))
        if ring(last):
            shapes.append(pltpu.VMEM((6, PARTS, SIDE) + block, kind))
        else:
            shapes.append(pltpu.VMEM((PARTS,) + plane + block, kind))
        shapes.append(pltpu.VMEM((PARTS,) + plane + block, kind))
        shapes.append(pltpu.VMEM((len(across(last)), PARTS) + block, kind))
    return shapes


def combine_kernel(terms_ref, out_ref, *refs):
    count = len(UNITS)
    every = range(count)
    joined = [refs[4 * unit] for unit in every]
    landing = [refs[4 * unit + 1] for unit in every]
    sums = [refs[4 * unit + 2] for unit in every]
    final = [refs[4 * unit + 3] for unit in every]
    near_send, near_recv, send, recv, side_send, side_recv = refs[4 * count :]
    team = Team()
    team.enter()
    spot = team.spot

    def remote(source, target, send_sem, recv_sem, device):
        copy = pltpu.make_async_remote_copy(
            src_ref=source, dst_ref=target, send_sem=send_sem, recv_sem=recv_sem, device_id=device, device_id_type=MESH
        )
        copy.start()
        return copy

    def cut(unit, coordinate, w=slice(None)):
        fixed = {2: w, UNITS[unit][2]: coordinate}
        return tuple(fixed.get(axis, slice(None)) for axis in range(3))

    def own(unit, coordinate, w=slice(None)):
        return joined[unit].at[(slice(None),) + cut(unit, coordinate, w)]

    def given(unit, slot, leaving):
        start, stop, axis = UNITS[unit]
        h = 1 - team.h if leaving else team.h
        if ring(axis):
            coordinate = team.shifted(axis, (2, 1, -1, 0)[slot])
        else:
            coordinate = team.shifted(axis, slot if leaving else 1 - slot)
        w = coordinate if axis == 2 else slice(None)
        y, x, w = cut(unit, coordinate, w)
        return terms_ref.at[:, y, x, h, w, pl.ds(start, stop - start)], own(unit, coordinate, w)

    def slots(unit):
        return 4 if ring(UNITS[unit][2]) else 2

    sides = {}
    for slot in range(4):
        for unit in every:
            if slot < slots(unit):
                source, target = given(unit, slot, True)
                sides[unit, slot] = remote(
                    source, target, side_send.at[unit, slot], side_recv.at[unit, slot], team.beside()
                )

    def join(unit, slot):
        sides[unit, slot].wait_recv()
        source, target = given(unit, slot, False)
        add_blocks(target, (target, source))

    def message(unit, way, number, step, source):
        target = landing[unit].at[3 * way + number] if ring(UNITS[unit][2]) else landing[unit]
        return remote(
            source, target, send.at[unit, way, number], recv.at[unit, way, number], team.device(UNITS[unit][2], step)
        )

    flying = {}
    for number in range(2):
        for unit in every:
            axis = UNITS[unit][2]
            if not ring(axis):
                if number == 0:
                    join(unit, 0)
                    coordinate = team.shifted(axis, 1)
                    flying[unit, 0, 0] = message(unit, 0, 0, 1, own(unit, coordinate, coordinate))
                continue
            if number == 0:
                join(unit, 0)
            for way, step in STEPS:
                if number == 1:
                    join(unit, 1 + way)
                coordinate = team.shifted(axis, 2 * step if number == 0 else step)
                flying[unit, way, number] = message(
                    unit, way, number, step, own(unit, coordinate, (number + way) % 2)
                )
    for unit in every:
        axis = UNITS[unit][2]
        if ring(axis):
            for way, step in STEPS:
                flying[unit, way, 0].wait_recv()
                passing = landing[unit].at[3 * way]
                add_blocks(passing, (passing, own(unit, team.shifted(axis, step), way)))
                flying[unit, way, 2] = message(unit, way, 2, step, passing)
    for unit in every:
        join(unit, slots(unit) - 1)
    nears = {}
    for unit in every:
        start, stop, axis = UNITS[unit]
        if ring(axis):
            for way, _ in STEPS:
                flying[unit, way, 1].wait_recv()
                flying[unit, way, 2].wait_recv()
            for w in range(2):
                add_blocks(
                    sums[unit].at[:, :, w],
                    (own(unit, spot[axis], w), landing[unit].at[3 * w + 2], landing[unit].at[3 * (1 - w) + 1]),
                )
        else:
            flying[unit, 0, 0].wait_recv()
            add_blocks(sums[unit], (own(unit, spot[axis], spot[axis]), landing[unit]))
        first, second = [other for other in range(3) if other != axis]
        for number, steps in enumerate(across(axis)):
            nears[unit, number] = remote(
                sums[unit].at[:, team.shifted(first, steps[first]), team.shifted(second, steps[second])],
                final[unit].at[number],
                near_send.at[unit, number],
                near_recv.at[unit, number],
                team.moved(steps),
            )
    for unit in every:
        start, stop, axis = UNITS[unit]
        first, second = [other for other in range(3) if other != axis]
        peers = len(across(axis))
        for number in range(peers):
            nears[unit, number].wait_recv()

        @pl.loop(0, PARTS)
        def _(part, unit=unit, start=start, stop=stop, first=first, second=second, peers=peers):
            total = sums[unit][part, spot[first], spot[second]].astype(jnp.float32)
            for number in range(peers):
                total = total + final[unit][number, part].astype(jnp.float32)
            out_ref[part, pl.ds(start, stop - start), :] = total
    for copies in (flying, sides, nears):
        for copy in copies.values():
            copy.wait_send()


def combine_all(terms, collective_id):
    parts, rows, lanes = terms.shape[0], terms.shape[-2], terms.shape[-1]
    return pl.pallas_call(
        combine_kernel,
        out_shape=jax.ShapeDtypeStruct((parts, rows, lanes), jnp.float32),
        in_specs=[pl.BlockSpec(memory_space=pltpu.VMEM)],
        out_specs=pl.BlockSpec(memory_space=pltpu.VMEM),
        scratch_shapes=combine_shapes(terms.dtype) + transfer_sems(),
        compiler_params=pltpu.CompilerParams(
            collective_id=collective_id, has_side_effects=True, vmem_limit_bytes=VMEM_LIMIT
        ),
        cost_estimate=pl.CostEstimate(flops=terms.size, bytes_accessed=2 * terms.size, transcendentals=0),
    )(terms)


def scatter_kernel(split, terms_ref, out_ref, sum_one, sum_two, near_one, far_one, near_two, far_two, near_three, far_three, send, recv):
    rows = terms_ref.shape[-2]
    halves = (pl.ds(0, split), pl.ds(split, rows - split))
    section, at = here()
    enter(section, at)
    sums = (terms_ref, sum_one, sum_two, out_ref)
    landing = ((near_one, far_one), (near_two, far_two), (near_three, far_three))

    def remaining(part, phase):
        return tuple(sorted(ORDERS[part][: 3 - phase]))

    def axis_of(part, phase):
        return ORDERS[part][2 - phase]

    def landed(phase, part, way, number):
        half = (number + way) % 2
        slot = {(0, 0): 0, (0, 2): 1, (1, 1): 2, (0, 1): 0, (1, 0): 1, (1, 2): 2}[way, number]
        return landing[phase][half].at[slot, part]

    def message(phase, part, way, number, step, source):
        axis = axis_of(part, phase)
        return pltpu.make_async_remote_copy(
            src_ref=source,
            dst_ref=landed(phase, part, way, number),
            send_sem=send.at[phase, part, way, number],
            recv_sem=recv.at[phase, part, way, number],
            device_id=device_at(section, at, axis, step),
            device_id_type=MESH,
        )

    def own(phase, part, coordinate, half):
        return slab(sums[phase], part, remaining(part, phase), {axis_of(part, phase): coordinate}, halves[half])

    def add(phase, target, terms):
        outer = target.shape[:-2]
        count = 1
        for size in outer:
            count *= size

        def one(index):
            total = terms[0][index].astype(jnp.float32)
            for term in terms[1:]:
                total = total + term[index].astype(jnp.float32)
            target[index] = total.astype(target.dtype)

        if count == 1:
            one((slice(None),) * 2)
            return

        @pl.loop(0, count)
        def _(step):
            if len(outer) == 1:
                one((step,))
            else:
                one((step // SIDE, lax.rem(step, SIDE)))

    for phase in range(3):
        flying = {}
        for number in range(2):
            for part in range(3):
                axis = axis_of(part, phase)
                for way, step in enumerate((1, -1)):
                    coordinate = shifted(at, axis, 2 * step if number == 0 else step)
                    copy = message(phase, part, way, number, step, own(phase, part, coordinate, (number + way) % 2))
                    copy.start()
                    flying[part, way, number] = copy
        for part in range(3):
            axis = axis_of(part, phase)
            for way, step in enumerate((1, -1)):
                flying[part, way, 0].wait_recv()
                passing = landed(phase, part, way, 0)
                add(phase, passing, (passing, own(phase, part, shifted(at, axis, step), way)))
                copy = message(phase, part, way, 2, step, passing)
                copy.start()
                flying[part, way, 2] = copy
        for part in range(3):
            axis = axis_of(part, phase)
            for way in range(2):
                flying[part, way, 1].wait_recv()
                flying[part, way, 2].wait_recv()
            for half in range(2):
                target = sums[phase + 1].at[(part,) + (slice(None),) * (2 - phase) + (halves[half],)]
                add(
                    phase,
                    target,
                    (
                        own(phase, part, at[axis], half),
                        landed(phase, part, half, 2),
                        landed(phase, part, 1 - half, 1),
                    ),
                )
        for part in range(3):
            for way in range(2):
                for number in range(3):
                    flying[part, way, number].wait_send()


def scatter_all(terms, split, collective_id):
    parts, rows, lanes = terms.shape[0], terms.shape[-2], terms.shape[-1]
    kind = terms.dtype
    near, far = split, rows - split
    return pl.pallas_call(
        functools.partial(scatter_kernel, split),
        out_shape=jax.ShapeDtypeStruct((parts, rows, lanes), jnp.float32),
        in_specs=[pl.BlockSpec(memory_space=pltpu.VMEM)],
        out_specs=pl.BlockSpec(memory_space=pltpu.VMEM),
        scratch_shapes=[
            pltpu.VMEM((parts, SIDE, SIDE, rows, lanes), kind),
            pltpu.VMEM((parts, SIDE, rows, lanes), kind),
            pltpu.VMEM((3, parts, SIDE, SIDE, near, lanes), kind),
            pltpu.VMEM((3, parts, SIDE, SIDE, far, lanes), kind),
            pltpu.VMEM((3, parts, SIDE, near, lanes), kind),
            pltpu.VMEM((3, parts, SIDE, far, lanes), kind),
            pltpu.VMEM((3, parts, near, lanes), kind),
            pltpu.VMEM((3, parts, far, lanes), kind),
            pltpu.SemaphoreType.DMA((3, 3, 2, 3)),
            pltpu.SemaphoreType.DMA((3, 3, 2, 3)),
        ],
        compiler_params=pltpu.CompilerParams(
            collective_id=collective_id, has_side_effects=True, vmem_limit_bytes=VMEM_LIMIT
        ),
        cost_estimate=pl.CostEstimate(flops=terms.size, bytes_accessed=2 * terms.size, transcendentals=0),
    )(terms)


def fetch_sorted(inverse_ref, source_ref, keys, sems):
    @pl.loop(0, inverse_ref.shape[0])
    def _(chunk):
        pltpu.make_async_copy(
            source_ref.at[:, inverse_ref[chunk]],
            keys.at[:, pl.ds(pl.multiple_of(chunk * CHUNK, CHUNK), CHUNK)],
            sems.at[chunk // PER],
        ).start()


def wait_block(keys, sems, block):
    rows = keys.at[:, pl.ds(pl.multiple_of(block * BLOCK, BLOCK), BLOCK)]
    pltpu.make_async_copy(rows, rows, sems.at[block]).wait()


def visible(shape, chunk, block):
    row = lax.broadcasted_iota(jnp.int32, shape, 0)
    column = lax.broadcasted_iota(jnp.int32, shape, 1)
    return block * BLOCK + column <= chunk * CHUNK + lax.rem(row, CHUNK)


STEPS_UNMASKED = 15


STRAIGHT = ((1, 0, 0), (2, 0, 0), (3, 0, 0), (0, 1, 0), (0, 2, 0), (0, 3, 0), (0, 0, 1))


class Exchange:
    def __init__(self, team, sems):
        self.team, self.sems = team, sems

    def send(self, source, target, device, kind, *index):
        send, recv = self.sems[kind]
        copy = pltpu.make_async_remote_copy(
            src_ref=source,
            dst_ref=target,
            send_sem=send.at[index],
            recv_sem=recv.at[index],
            device_id=device,
            device_id_type=MESH,
        )
        copy.start()
        return copy


class PartGather:
    def __init__(self, part, exchange, local_ref, keys):
        self.part, self.exchange, self.team = part, exchange, exchange.team
        self.local_ref, self.keys = local_ref, keys
        self.near, self.ring, self.side = [], {}, []

    def slab(self, unit, coordinate, w=slice(None)):
        y, x = (coordinate, slice(None)) if unit == 0 else (slice(None), coordinate)
        return self.keys.at[y, x, self.team.h, w, unit]

    def start_near(self):
        spot = self.team.spot
        for unit in range(2):
            for step in range(1, SIDE):
                steps = (0, step, 0) if unit == 0 else (step, 0, 0)
                place = self.keys.at[spot[0], spot[1], self.team.h, :, unit]
                self.near.append(
                    self.exchange.send(place, place, self.team.moved(steps), "near", self.part, unit, step - 1)
                )

    def message(self, unit, way, number, coordinate, w):
        place = self.slab(unit, coordinate, w)
        self.ring[unit, way, number] = self.exchange.send(
            place, place, self.team.device(unit, STEPS[way][1]), "ring", self.part, unit, way, number
        )

    def aside(self, unit, slot, coordinate):
        place = self.slab(unit, coordinate)
        self.side.append(
            self.exchange.send(place, place, self.team.beside(), "side", self.part, unit, slot)
        )

    def start_ring(self):
        for copy in self.near:
            copy.wait_recv()
        for number in range(2):
            for unit in range(2):
                for way, _ in STEPS:
                    self.message(unit, way, number, self.team.spot[unit], (number + way) % 2)
        for unit in range(2):
            self.aside(unit, 0, self.team.spot[unit])

    def pass_on(self):
        for unit in range(2):
            for way, step in STEPS:
                self.ring[unit, way, 0].wait_recv()
                self.message(unit, way, 2, self.team.shifted(unit, -step), way)

    def share(self):
        for unit in range(2):
            for way, step in STEPS:
                self.ring[unit, way, 1].wait_recv()
                self.aside(unit, 1 + way, self.team.shifted(unit, -step))
        for unit in range(2):
            for way, _ in STEPS:
                self.ring[unit, way, 2].wait_recv()
            self.aside(unit, 3, self.team.shifted(unit, 2))

    def finish(self):
        for copy in self.side:
            copy.wait_recv()

    def drain(self):
        for copy in self.near + list(self.ring.values()) + self.side:
            copy.wait_send()


class WeightGather:
    def __init__(self, owner, number, exchange, local_ref, out_ref):
        self.owner, self.number, self.exchange, self.team = owner, number, exchange, exchange.team
        self.local_ref, self.out_ref = local_ref, out_ref
        rows = local_ref.shape[0]
        split = rows // 32 * 16
        self.halves = (pl.ds(0, split), pl.ds(split, rows - split))
        self.copies = []

    def here(self):
        return self.team.section == self.owner

    def index(self, step):
        return lax.rem(self.team.at[2] + (step + SIDE), SIDE)

    def message(self, way, number, index, half, start=True):
        spot = self.out_ref.at[index, self.halves[half]]
        source = self.local_ref.at[self.halves[half]] if number < 2 else spot
        return self.copy(source, spot, device_at(self.team.section, self.team.at, 2, STEPS[way][1]), "weight_ring", start, way, number)

    def aside(self, slot, start=True):
        spot = self.out_ref.at[self.index((0, -1, 1, 2)[slot])]
        source = self.local_ref if slot == 0 else spot
        return self.copy(source, spot, self.team.beside(), "weight_side", start, slot)

    def copy(self, source, target, device, kind, start, *index):
        send, recv = self.exchange.sems[kind]
        place = (self.number,) + index
        copy = pltpu.make_async_remote_copy(
            src_ref=source, dst_ref=target, send_sem=send.at[place], recv_sem=recv.at[place],
            device_id=device, device_id_type=MESH,
        )
        if start:
            copy.start()
        return copy

    def own(self):
        return pltpu.make_async_copy(self.local_ref, self.out_ref.at[self.team.at[2]], self.exchange.sems["weight_own"].at[self.number])

    def start(self):
        @pl.when(self.here())
        def _():
            self.own().start()
            for number in range(2):
                for way, _ in STEPS:
                    self.message(way, number, self.team.at[2], (number + way) % 2)

    def pass_on(self):
        @pl.when(self.here())
        def _():
            self.aside(0)
            for way, step in STEPS:
                self.message(way, 0, self.team.at[2], way, False).wait_recv()
                self.message(way, 2, self.index(-step), way)
            for way, step in STEPS:
                self.message(way, 1, self.team.at[2], 1 - way, False).wait_recv()
                self.aside(1 + way)

    def share(self):
        @pl.when(self.here())
        def _():
            for way, step in STEPS:
                self.message(way, 2, self.index(-step), way, False).wait_recv()
            self.aside(3)

    def finish(self):
        @pl.when(self.here())
        def _():
            self.own().wait()
            for way, step in STEPS:
                for number in range(3):
                    index = self.team.at[2] if number < 2 else self.index(-step)
                    self.message(way, number, index, (number + way) % 2, False).wait_send()
            for slot in range(4):
                self.aside(slot, False).wait_send()

        @pl.when(jnp.logical_not(self.here()))
        def _():
            for slot in range(4):
                self.aside(slot, False).wait_recv()


EXP = jnp.exp


def key_block(inverse_ref, keys, block):
    pieces = []
    for index in range(PER):
        place = inverse_ref[block * PER + index]
        y = lax.div(place, 32)
        x = lax.rem(lax.div(place, 8), SIDE)
        h = lax.rem(lax.div(place, 4), 2)
        w = lax.rem(lax.div(place, 2), 2)
        pieces.append(keys[y, x, h, w, lax.rem(place, 2)])
    return jnp.concatenate(pieces, axis=0)


def schedule(spots_ref):
    return lax.div(spots_ref[0], PER), lax.div(spots_ref[1], PER)


def attend_all_kernel(
    owner, inverse_ref, spots_ref, local_ref, query_ref, *refs
):
    count = 4 if owner == 0 else 3
    shard_refs, refs = refs[:count], refs[count:]
    (mixed_ref, logsum_ref, both_ref), refs = refs[:3], refs[3:]
    whole_refs, refs = refs[:count], refs[count:]
    keys, (highest_at, mixed_at), refs = refs[:3], refs[3:5], refs[5:]
    sems = {
        "near": refs[0:2], "ring": refs[2:4], "side": refs[4:6],
        "weight_ring": refs[6:8], "weight_side": refs[8:10], "pair": refs[10:12], "weight_own": refs[12],
    }
    kept = refs[13]
    team = Team()
    team.enter(STRAIGHT)
    exchange = Exchange(team, sems)
    spot, h = team.spot, team.h
    parts = [PartGather(part, exchange, local_ref, keys[part]) for part in range(KV_HEADS)]
    weights = [
        WeightGather(owner if number < 3 else 1 - owner, number, exchange, shard_refs[number], whole_refs[number])
        for number in range(count)
    ]
    own = [
        pltpu.make_async_copy(local_ref.at[part], keys[part].at[spot[0], spot[1], h, spot[2]], kept.at[part])
        for part in range(KV_HEADS)
    ]
    saved = [
        pltpu.make_async_copy(keys[part], both_ref.at[part], kept.at[KV_HEADS + part]) for part in range(KV_HEADS)
    ]
    ends = schedule(spots_ref)

    def attend_scores(part, half, block):
        both = key_block(inverse_ref, keys[part], block)
        return lax.dot_general(
            query_ref[part, half], both, contract_last, preferred_element_type=jnp.float32
        )

    def attend_rest(part, scores, block, highest, mixed):
        both = key_block(inverse_ref, keys[part], block)
        higher = jnp.maximum(highest, jnp.broadcast_to(jnp.max(scores, axis=-1, keepdims=True), highest.shape))
        exponent = EXP(scores - jnp.concatenate([higher] * (BLOCK // 128), axis=1)).astype(jnp.bfloat16)
        values = jnp.where(is_lower(both.shape), jnp.bfloat16(1.0), both)
        return higher, jnp.dot(exponent, values, preferred_element_type=jnp.float32) + EXP(highest - higher) * mixed

    def attend_first(part):
        for half in range(2):
            scores = attend_scores(part, half, ends[half])
            scores = jnp.where(visible(scores.shape, spots_ref[half], ends[half]), scores, -1e30)
            highest, mixed = attend_rest(
                part, scores, ends[half], jnp.full((scores.shape[0], 128), -1e30, jnp.float32), jnp.zeros((scores.shape[0], 128), jnp.float32)
            )
            highest_at[half] = highest
            mixed_at[half] = mixed

    def attend_some(part, low, high):
        if True:
            size = high - low
            steps = [low + index for index in range(size)]
            halves = [jnp.where(step >= ends[0], 1, 0) for step in steps]
            blocks = [step - half * ends[0] for step, half in zip(steps, halves)]
            befores = [jnp.where(step == ends[0], 1, jnp.where(step == 0, 0, step + 1)) for step in steps]
            scores = attend_scores(part, halves[0], blocks[0])
            for index in range(size):
                later = attend_scores(part, halves[index + 1], blocks[index + 1]) if index + 1 < size else None
                before = befores[index]
                highest, mixed = attend_rest(part, scores, blocks[index], highest_at[before], mixed_at[before])
                highest_at[steps[index] + 2] = highest
                mixed_at[steps[index] + 2] = mixed
                scores = later

    def attend_last(part):
        last = (
            jnp.where(ends[0] == 0, 0, ends[0] + 1),
            jnp.where(ends[0] == STEPS_UNMASKED, 1, STEPS_UNMASKED + 1),
        )
        for half in range(2):
            mixed = mixed_at[last[half]]
            total = mixed[:, :1]
            mixed_ref[part, half] = mixed / total
            logsum_ref[part, half] = highest_at[last[half]][:, :1] + jnp.log(total)

    pairs = [
        exchange.send(
            local_ref.at[part], keys[part].at[spot[0], spot[1], h, spot[2]], team.device(2, 1), "pair", part
        )
        for part in range(KV_HEADS)
    ]
    for copy in own:
        copy.start()
    for weight in weights:
        weight.start()
    for part in range(KV_HEADS):
        own[part].wait()
        pairs[part].wait_recv()
        parts[part].start_near()
    for part in parts:
        part.start_ring()
    parts[0].pass_on()
    parts[1].pass_on()
    parts[0].share()
    parts[2].pass_on()
    parts[0].finish()
    saved[0].start()
    attend_first(0)
    attend_some(0, 0, 7)
    parts[1].share()
    attend_some(0, 7, 15)
    for weight in weights:
        weight.pass_on()
    attend_last(0)
    parts[1].finish()
    saved[1].start()
    attend_first(1)
    attend_some(1, 0, 7)
    parts[2].share()
    attend_some(1, 7, 15)
    attend_last(1)
    parts[2].finish()
    saved[2].start()
    attend_first(2)
    attend_some(2, 0, 7)
    for weight in weights:
        weight.share()
    attend_some(2, 7, 15)
    attend_last(2)
    for copy in pairs:
        copy.wait_send()
    for part in parts:
        part.drain()
    for weight in weights:
        weight.finish()
    for copy in saved:
        copy.wait()


def attend_all(owner, inverse, spots, local, query, shards, collective_id):
    groups, halves, rows, lanes = query.shape
    count = len(shards)
    keys = (SIDE, SIDE, 2, 2, 2, CHUNK, lanes)
    vmem, smem, held = (pl.BlockSpec(memory_space=space) for space in (pltpu.VMEM, pltpu.SMEM, pl.ANY))
    slots = STEPS_UNMASKED + 2
    scores = rows * BLOCK * slots * groups
    semaphore = pltpu.SemaphoreType.DMA
    return pl.pallas_call(
        functools.partial(attend_all_kernel, owner),
        out_shape=(
            jax.ShapeDtypeStruct((groups, halves, rows, lanes), jnp.float32),
            jax.ShapeDtypeStruct((groups, halves, rows, 1), jnp.float32),
            jax.ShapeDtypeStruct((groups,) + keys, local.dtype),
        )
        + tuple(jax.ShapeDtypeStruct((SIDE,) + item.shape, item.dtype) for item in shards),
        in_specs=[smem, smem, vmem, vmem] + [held] * count,
        out_specs=(vmem, vmem, held) + (held,) * count,
        scratch_shapes=[pltpu.VMEM(keys, local.dtype) for _ in range(groups)]
        + [
            pltpu.VMEM((slots, rows, lanes), jnp.float32),
            pltpu.VMEM((slots, rows, lanes), jnp.float32),
        ]
        + [semaphore(shape) for shape in ((3, 2, 3), (3, 2, 2, 3), (3, 2, 4), (count, 2, 3), (count, 4), (3,)) for _ in range(2)]
        + [semaphore((count,)), semaphore((2 * groups,))],
        compiler_params=pltpu.CompilerParams(
            collective_id=collective_id, has_side_effects=True, vmem_limit_bytes=VMEM_LIMIT
        ),
        cost_estimate=pl.CostEstimate(flops=4 * scores * lanes, bytes_accessed=128 * local.size, transcendentals=scores),
    )(inverse, spots, local, query, *shards)


def attend_back_kernel(
    inverse_ref, spots_ref, query_ref, grad_ref, logsum_ref, inner_ref, source_ref,
    grad_query_ref, out_ref, keys, totals, rounded, sems, out_sem,
):
    rows = query_ref.shape[2]
    blocks = keys.shape[1] // BLOCK
    fetch_sorted(inverse_ref, source_ref, keys, sems)

    @pl.loop(0, blocks)
    def _(block):
        totals[:, pl.ds(pl.multiple_of(block * BLOCK, BLOCK), BLOCK), :] = jnp.zeros(
            (KV_HEADS, BLOCK, 2 * HEAD_DIM), jnp.float32
        )

    ready = jnp.int32(0)
    for half in range(2):
        chunk = spots_ref[half]
        whole = chunk // PER

        def step(block, carry, masked, half=half, chunk=chunk, ready=ready):
            @pl.when(block >= ready)
            def _():
                wait_block(keys, sems, block)

            start = pl.multiple_of(block * BLOCK, BLOCK)
            result = []
            for group in range(KV_HEADS):
                both = keys[group, pl.ds(start, BLOCK), :]
                query = query_ref[group, half]
                grad = grad_ref[group, half]
                scores = lax.dot_general(query, both, contract_last, preferred_element_type=jnp.float32)
                probs = jnp.exp(scores - logsum_ref[group, half])
                if masked:
                    probs = jnp.where(visible(scores.shape, chunk, block), probs, 0.0)
                grad_weights = lax.dot_general(grad, both, contract_last, preferred_element_type=jnp.float32)
                grad_scores = (probs * (grad_weights - inner_ref[group, half])).astype(jnp.bfloat16)
                weights = probs.astype(jnp.bfloat16)
                result.append(
                    carry[group] + jnp.dot(grad_scores, both, preferred_element_type=jnp.float32)
                )
                totals[group, pl.ds(start, BLOCK), :] += lax.dot_general(
                    jnp.concatenate([weights, grad_scores], axis=0),
                    jnp.concatenate([grad, query], axis=0),
                    contract_first,
                    preferred_element_type=jnp.float32,
                )
            return tuple(result)

        carry = tuple(jnp.zeros((rows, 2 * HEAD_DIM), jnp.float32) for _ in range(KV_HEADS))
        carry = lax.fori_loop(0, whole, functools.partial(step, masked=False), carry)
        carry = step(whole, carry, masked=True)
        ready = jnp.maximum(ready, whole + 1)
        for group in range(KV_HEADS):
            grad_query_ref[group, half] = carry[group]

    @pl.loop(ready, blocks)
    def _(block):
        wait_block(keys, sems, block)

    @pl.loop(0, blocks * PER)
    def _(chunk):
        place = pl.ds(pl.multiple_of(chunk * CHUNK, CHUNK), CHUNK)
        rounded[:, place, :] = totals[:, place, :].astype(jnp.bfloat16)
        pltpu.make_async_copy(rounded.at[:, place], out_ref.at[:, inverse_ref[chunk]], out_sem).start()

    pltpu.make_async_copy(rounded, rounded, out_sem).wait()


def attend_back(inverse, spots, query, grad, logsum, inner, both):
    groups, halves, rows, lanes = query.shape
    chunks = both.shape[1]
    scores = rows * halves * groups * (chunks * CHUNK // 2)
    vmem = pl.BlockSpec(memory_space=pltpu.VMEM)
    smem = pl.BlockSpec(memory_space=pltpu.SMEM)
    return pl.pallas_call(
        attend_back_kernel,
        out_shape=(
            jax.ShapeDtypeStruct((groups, halves, rows, lanes), jnp.float32),
            jax.ShapeDtypeStruct(both.shape, jnp.bfloat16),
        ),
        in_specs=[smem, smem, vmem, vmem, vmem, vmem, pl.BlockSpec(memory_space=pl.ANY)],
        out_specs=(vmem, pl.BlockSpec(memory_space=pl.ANY)),
        scratch_shapes=[
            pltpu.VMEM((groups, chunks * CHUNK, lanes), jnp.bfloat16),
            pltpu.VMEM((groups, chunks * CHUNK, lanes), jnp.float32),
            pltpu.VMEM((groups, chunks * CHUNK, lanes), jnp.bfloat16),
            pltpu.SemaphoreType.DMA((chunks // PER,)),
            pltpu.SemaphoreType.DMA,
        ],
        compiler_params=pltpu.CompilerParams(vmem_limit_bytes=VMEM_LIMIT),
        cost_estimate=pl.CostEstimate(flops=10 * scores * lanes, bytes_accessed=4 * both.size, transcendentals=scores),
    )(inverse, spots, query, grad, logsum, inner, both)


def first_weight_kernel(
    local_ref, gains_ref, inputs_ref, cotangent_ref, out_ref, gains_out_ref, current_ref, given_ref,
    send, recv, side_send, side_recv, gain_send, gain_recv, token_send, token_recv, kept,
):
    rows = local_ref.shape[0]
    halves = (pl.ds(0, 128), pl.ds(128, rows - 128))
    section, at = here()
    place = at[2]
    beside = (1 - section, at[0] * SIDE + at[1], place)
    barrier = pltpu.get_barrier_semaphore()
    for device in (device_at(section, at, 2, 1), device_at(section, at, 2, -1), beside):
        pl.semaphore_signal(barrier, inc=1, device_id=device, device_id_type=MESH)
    pl.semaphore_wait(barrier, 3)
    own_gains = pltpu.make_async_copy(gains_ref, gains_out_ref.at[section], kept.at[0])
    own_gains.start()
    other_gains = pltpu.make_async_remote_copy(
        src_ref=gains_ref,
        dst_ref=gains_out_ref.at[section],
        send_sem=gain_send,
        recv_sem=gain_recv,
        device_id=beside,
        device_id_type=MESH,
    )
    other_gains.start()

    batch = place // 2
    partner = (section, at[0] * SIDE + at[1], SIDE - 1 - place)
    tokens = ((inputs_ref, current_ref), (cotangent_ref, given_ref))

    def crossing(number):
        source, target = tokens[number]
        return pltpu.make_async_remote_copy(
            src_ref=source.at[1 - batch],
            dst_ref=target,
            send_sem=token_send.at[number],
            recv_sem=token_recv.at[number],
            device_id=partner,
            device_id_type=MESH,
        )

    def staying(number):
        source, target = tokens[number]
        return pltpu.make_async_copy(source.at[batch], target, kept.at[2 + number])

    def aside(number, source):
        index = lax.rem(place + (0, 3, 1, 2)[number], SIDE)
        return pltpu.make_async_remote_copy(
            src_ref=out_ref.at[index] if source is None else source,
            dst_ref=out_ref.at[index],
            send_sem=side_send.at[number],
            recv_sem=side_recv.at[number],
            device_id=beside,
            device_id_type=MESH,
        )

    def message(way, number, step, index, half, source):
        spot = out_ref.at[index, halves[half]]
        return pltpu.make_async_remote_copy(
            src_ref=spot if source is None else source.at[halves[half]],
            dst_ref=spot,
            send_sem=send.at[way, number],
            recv_sem=recv.at[way, number],
            device_id=device_at(section, at, 2, step),
            device_id_type=MESH,
        )

    @pl.when(section == 0)
    def _():
        own = pltpu.make_async_copy(local_ref, out_ref.at[place], kept.at[1])
        own.start()
        for number in range(2):
            staying(number).start()
        flying = {}
        for number in range(2):
            for way, step in enumerate((1, -1)):
                flying[way, number] = message(way, number, step, place, (number + way) % 2, local_ref)
                flying[way, number].start()
        sides = [aside(0, local_ref)]
        sides[0].start()
        for way, step in enumerate((1, -1)):
            flying[way, 0].wait_recv()
            flying[way, 2] = message(way, 2, step, shifted(at, 2, -step), way, None)
            flying[way, 2].start()
        for way in range(2):
            flying[way, 1].wait_recv()
            sides.append(aside(1 + way, None))
            sides[-1].start()
        for way in range(2):
            flying[way, 2].wait_recv()
        sides.append(aside(3, None))
        sides[-1].start()
        for side in sides:
            side.wait_send()
        for way in range(2):
            for number in range(3):
                flying[way, number].wait_send()
        own.wait()
        for number in range(2):
            staying(number).wait()

    @pl.when(section == 1)
    def _():
        for number in range(2):
            crossing(number).start()
        for number in range(2):
            crossing(number).wait()
        for number in range(4):
            aside(number, None).wait_recv()

    own_gains.wait()
    other_gains.wait()


def first_weight(local, gains, inputs, cotangent):
    rows, columns = local.shape
    any_space = pl.BlockSpec(memory_space=pl.ANY)
    return pl.pallas_call(
        first_weight_kernel,
        out_shape=(
            jax.ShapeDtypeStruct((SIDE, rows, columns), local.dtype),
            jax.ShapeDtypeStruct((2,) + gains.shape, gains.dtype),
            jax.ShapeDtypeStruct(inputs.shape[1:], inputs.dtype),
            jax.ShapeDtypeStruct(cotangent.shape[1:], cotangent.dtype),
        ),
        in_specs=[any_space] * 4,
        out_specs=(any_space,) * 4,
        scratch_shapes=[
            pltpu.SemaphoreType.DMA((2, 3)),
            pltpu.SemaphoreType.DMA((2, 3)),
            pltpu.SemaphoreType.DMA((4,)),
            pltpu.SemaphoreType.DMA((4,)),
            pltpu.SemaphoreType.DMA,
            pltpu.SemaphoreType.DMA,
            pltpu.SemaphoreType.DMA((2,)),
            pltpu.SemaphoreType.DMA((2,)),
            pltpu.SemaphoreType.DMA((4,)),
        ],
        compiler_params=pltpu.CompilerParams(collective_id=3, has_side_effects=True),
        cost_estimate=pl.CostEstimate(flops=0, bytes_accessed=8 * local.size, transcendentals=0),
    )(local, gains, inputs, cotangent)


def normalize(values):
    factor = lax.rsqrt(jnp.mean(values * values, axis=-1, keepdims=True) + epsilon)
    return (values * factor, factor)


def norm_back(grad_unit, unit, factor):
    return factor * (grad_unit - unit * jnp.mean(grad_unit * unit, axis=-1, keepdims=True))


def product(left, right):
    return jnp.dot(left, right, preferred_element_type=jnp.float32)


def product_turned(left, right):
    return lax.dot_general(left, right, contract_last, preferred_element_type=jnp.float32)


def is_lower(shape):
    return lax.broadcasted_iota(jnp.int32, shape, len(shape) - 1) < HEAD_DIM


def turned(tile, cosine, sine):
    half = HEAD_DIM // 2
    lane = lax.broadcasted_iota(jnp.int32, tile.shape, 1)
    other = jnp.where(
        lax.rem(lane, HEAD_DIM) < half, pltpu.roll(tile, 128 - half, 1), pltpu.roll(tile, half, 1)
    )
    return tile * cosine + other * sine


def swapped(tile):
    return pltpu.roll(tile, HEAD_DIM, 1)


def head_rows(ref, head):
    group, index = head // GROUP, head % GROUP
    rows = slice(index * CHUNK, (index + 1) * CHUNK)
    return jnp.concatenate([ref[group, 0, rows, :], ref[group, 1, rows, :]], axis=0)


def put_head(ref, head, tile):
    group, index = head // GROUP, head % GROUP
    rows = slice(index * CHUNK, (index + 1) * CHUNK)
    ref[group, 0, rows, :] = tile[:CHUNK]
    ref[group, 1, rows, :] = tile[CHUNK:]


def widen(wide, qkv):
    for head in range(HEADS):
        wide[128 * head : 128 * head + 64, :] = qkv[64 * head : 64 * head + 64, :]
        wide[128 * head + 64 : 128 * head + 128, :] = jnp.zeros((64, wide.shape[1]), wide.dtype)
    for group in range(KV_HEADS):
        start = 128 * (HEADS + group)
        wide[start : start + 64, :] = qkv[576 + 64 * group : 640 + 64 * group, :]
        wide[start + 64 : start + 128, :] = qkv[768 + 64 * group : 832 + 64 * group, :]


def project(current, gain, wide, cosine, sine, query_ref, local_ref):
    unit, _ = normalize(current)
    projected = product_turned((unit * gain).astype(jnp.bfloat16), wide[...])
    for head in range(HEADS):
        tile = turned(projected[:, 128 * head : 128 * head + 128], cosine, sine) * HEAD_DIM ** (-0.5)
        put_head(query_ref, head, tile.astype(jnp.bfloat16))
    for group in range(KV_HEADS):
        start = 128 * (HEADS + group)
        tile = turned(projected[:, start : start + 128], cosine, sine).astype(jnp.bfloat16)
        local_ref[group, 0] = tile[:CHUNK]
        local_ref[group, 1] = tile[CHUNK:]


def project_back(grad_query_ref, grad_local_ref, current, grad_hidden, gain, wide, cosine, sine, terms_ref):
    lower = is_lower((2 * CHUNK, 128))
    tiles = []
    for head in range(HEADS):
        tile = jnp.where(lower, head_rows(grad_query_ref, head), 0.0)
        tiles.append(turned(tile, cosine, -sine) * HEAD_DIM ** (-0.5))
    for group in range(KV_HEADS):
        tiles.append(turned(grad_local_ref[group], cosine, -sine))
    grad_normed = product(
        jnp.concatenate([tile.astype(jnp.bfloat16) for tile in tiles], axis=1), wide[...]
    )
    unit, factor = normalize(current)
    key = tiles[HEADS:]
    pairs = [(tiles[2 * index], swapped(tiles[2 * index + 1])) for index in range(4)]
    pairs += [
        (tiles[8], swapped(key[0])),
        (key[1], swapped(key[2])),
        (swapped(key[0]), key[1]),
        (swapped(key[2]), jnp.zeros_like(key[2])),
    ]
    width = current.shape[1]
    terms_ref[:, :width] = (unit * gain).astype(jnp.bfloat16)
    for index, (low, high) in enumerate(pairs):
        terms_ref[:, 640 + 128 * index : 768 + 128 * index] = jnp.where(lower, low, high).astype(jnp.bfloat16)
    return grad_hidden + norm_back(grad_normed * gain, unit, factor)


def heads_mixed(mixed_ref):
    lower = is_lower((2 * CHUNK, 128))
    tiles = [head_rows(mixed_ref, head) for head in range(HEADS)]
    pairs = [jnp.where(lower, swapped(tiles[2 * i]), tiles[2 * i + 1]) for i in range(4)]
    pairs.append(swapped(tiles[8])[:, :HEAD_DIM])
    return jnp.concatenate([tile.astype(jnp.bfloat16) for tile in pairs], axis=1)


def feed_forward(current, mixed, out, gain, gate_up, down, waits):
    waits[0]()
    hidden = current + product_turned(mixed, out[...])
    unit, _ = normalize(hidden)
    normed = (unit * gain).astype(jnp.bfloat16)
    waits[1]()
    pair = [product(normed, gate_up[index]) for index in range(4)]
    act = [(pair[k] * jax.nn.sigmoid(pair[k]) * pair[k + 2]).astype(jnp.bfloat16) for k in range(2)]
    part = FF // 2
    waits[2]()
    result = hidden + (product_turned(act[0], down[:, :part]) + product_turned(act[1], down[:, part:]))
    return hidden, pair, result


def feed_back(grad_out, hidden, pair, mixed, mixed_ref, out, gain, gate_up, down, waits, terms_ref, grad_ref, inner_ref):
    part = FF // 2
    width = hidden.shape[1]
    branch = grad_out.astype(jnp.bfloat16)
    waits[2]()
    grad_act = product(branch, down[...])
    waits[1]()
    grad_normed = None
    for k in range(2):
        gate, upward = pair(k), pair(k + 2)
        squashed = jax.nn.sigmoid(gate)
        grad = grad_act[:, k * part : (k + 1) * part]
        grad_gate = (grad * upward * squashed * (1.0 + gate * (1.0 - squashed))).astype(jnp.bfloat16)
        grad_upward = (grad * (gate * squashed)).astype(jnp.bfloat16)
        terms_ref[:, 2560 + k * part : 2560 + (k + 1) * part] = grad_gate
        terms_ref[:, 2560 + (k + 2) * part : 2560 + (k + 3) * part] = grad_upward
        terms_ref[:, 5632 + k * part : 5632 + (k + 1) * part] = (gate * squashed * upward).astype(jnp.bfloat16)
        term = product_turned(grad_gate, gate_up[k]) + product_turned(grad_upward, gate_up[k + 2])
        grad_normed = term if grad_normed is None else grad_normed + term
    unit, factor = normalize(hidden)
    terms_ref[:, :width] = mixed
    terms_ref[:, 640 : 640 + width] = (unit * gain).astype(jnp.bfloat16)
    terms_ref[:, 1280 : 1280 + width] = branch
    grad_hidden = grad_out + norm_back(grad_normed * gain, unit, factor)
    grad_attn = grad_hidden.astype(jnp.bfloat16)
    terms_ref[:, 1920:2560] = jnp.concatenate(
        [jnp.zeros((2 * CHUNK, HEAD_DIM), jnp.float32), grad_hidden], axis=1
    ).astype(jnp.bfloat16)
    waits[0]()
    grad_mixed = product(grad_attn, out[...])
    lower = is_lower((2 * CHUNK, 128))
    for head in range(HEADS):
        start = 128 * (head // 2)
        if head == HEADS - 1:
            tile = jnp.concatenate([jnp.zeros((2 * CHUNK, HEAD_DIM), jnp.float32), grad_mixed[:, start:]], axis=1)
        else:
            tile = grad_mixed[:, start : start + 128]
            tile = jnp.where(lower, 0.0, tile if head % 2 else swapped(tile))
        tile = tile.astype(jnp.bfloat16)
        put_head(grad_ref, head, tile)
        inner = jnp.sum(tile.astype(jnp.float32) * head_rows(mixed_ref, head), axis=-1, keepdims=True)
        put_head(inner_ref, head, inner)
    return grad_hidden


def brought(pairs, sems):
    waits = []
    for index, (source, target) in enumerate(pairs):
        copy = pltpu.make_async_copy(source, target, sems.at[index])
        copy.start()
        waits.append(copy.wait)
    return waits


def once(waits):
    def first_only(wait):
        pending = [wait]

        def run():
            if pending:
                pending.pop()()

        return run

    return [first_only(wait) for wait in waits]


def enter_kernel(current_ref, gain_ref, cosine_ref, sine_ref, qkv_ref, query_ref, local_ref, wide):
    widen(wide, qkv_ref)
    project(
        current_ref[...].astype(jnp.float32), gain_ref[...], wide, cosine_ref[...], sine_ref[...], query_ref, local_ref
    )


def between_kernel(
    mixed_ref, current_ref, gain_ref, next_gain_ref, cosine_ref, sine_ref, out_ref, gate_up_ref, down_ref, qkv_ref,
    hidden_ref, pair_ref, next_ref, query_ref, local_ref,
    out, gate_up, down, qkv, wide, sems,
):
    *waits, wait_qkv = brought(
        [(out_ref, out), (gate_up_ref, gate_up), (down_ref, down), (qkv_ref, qkv)], sems
    )
    mixed = heads_mixed(mixed_ref)
    hidden, pair, result = feed_forward(
        current_ref[...].astype(jnp.float32), mixed, out, gain_ref[...], gate_up, down, waits
    )
    hidden_ref[...] = hidden
    for index in range(4):
        pair_ref[index] = pair[index]
    next_ref[...] = result
    wait_qkv()
    widen(wide, qkv)
    project(result, next_gain_ref[...], wide, cosine_ref[...], sine_ref[...], query_ref, local_ref)


def top_kernel(
    mixed_ref, current_ref, cotangent_ref, gain_ref, out_ref, gate_up_ref, down_ref,
    result_ref, grad_hidden_ref, terms_ref, grad_ref, inner_ref,
    out, gate_up, down, sems,
):
    waits = once(brought([(out_ref, out), (gate_up_ref, gate_up), (down_ref, down)], sems))
    mixed = heads_mixed(mixed_ref)
    gain = gain_ref[...]
    hidden, pair, result = feed_forward(current_ref[...], mixed, out, gain, gate_up, down, waits)
    result_ref[...] = result
    grad_hidden_ref[...] = feed_back(
        cotangent_ref[...].astype(jnp.float32), hidden, lambda index: pair[index], mixed, mixed_ref,
        out, gain, gate_up, down, waits, terms_ref, grad_ref, inner_ref,
    )


def descend_kernel(
    grad_query_ref, grad_local_ref, upper_ref, upper_grad_ref, upper_gain_ref, cosine_ref, sine_ref,
    mixed_ref, hidden_in_ref, pair_ref, gain_ref, qkv_ref, out_ref, gate_up_ref, down_ref,
    upper_terms_ref, grad_hidden_ref, terms_ref, grad_ref, inner_ref,
    out, gate_up, down, qkv, wide, sems,
):
    wait_qkv, *waits = brought(
        [(qkv_ref, qkv), (out_ref, out), (gate_up_ref, gate_up), (down_ref, down)], sems
    )
    wait_qkv()
    widen(wide, qkv)
    grad = project_back(
        grad_query_ref, grad_local_ref, upper_ref[...], upper_grad_ref[...], upper_gain_ref[...], wide,
        cosine_ref[...], sine_ref[...], upper_terms_ref,
    )
    grad_hidden_ref[...] = feed_back(
        grad, hidden_in_ref[...], lambda index: pair_ref[index], heads_mixed(mixed_ref), mixed_ref,
        out, gain_ref[...], gate_up, down, waits, terms_ref, grad_ref, inner_ref,
    )


def leave_kernel(
    grad_query_ref, grad_local_ref, current_ref, grad_hidden_ref, gain_ref, cosine_ref, sine_ref, qkv_ref,
    grad_in_ref, terms_ref, wide,
):
    widen(wide, qkv_ref)
    grad_in_ref[...] = project_back(
        grad_query_ref, grad_local_ref, current_ref[...].astype(jnp.float32), grad_hidden_ref[...], gain_ref[...], wide,
        cosine_ref[...], sine_ref[...], terms_ref,
    )


def weight_kernel(order_ref, low_ref, low_other_ref, high_ref, high_other_ref, out_ref, gathered):
    width = order_ref.shape[0]
    tiles = 6144 // 128
    blocks = 64

    def both(ref, other_ref, start, size):
        return jnp.concatenate([ref[:, start : start + size], other_ref[:, start : start + size]], axis=0)

    def left(ref, other_ref, start):
        columns = both(ref, other_ref, start, width)
        return product_turned(order_ref[...], columns).astype(jnp.bfloat16)

    def put(term, tile):
        for index in range(width // blocks):
            part, row = index // 3, (index % 3) * tiles + tile
            gathered[part, pl.ds(row, blocks, stride=3 * tiles), :] = term[index * blocks : (index + 1) * blocks]

    normed_one = left(low_ref, low_other_ref, 0)
    mixed = left(high_ref, high_other_ref, 0)
    first = product(normed_one, both(low_ref, low_other_ref, 640, 1024))
    second = product(mixed, both(high_ref, high_other_ref, 1920, 640))
    for tile in range(7):
        put(first[:, 128 * tile : 128 * tile + 128], tile)
    put(first[:, 896:] + second[:, :128], 7)
    for tile in range(1, 5):
        put(second[:, 128 * tile : 128 * tile + 128], 7 + tile)
    normed_two = left(high_ref, high_other_ref, 640)
    for step in range(6):
        third = product(normed_two, both(high_ref, high_other_ref, 2560 + 512 * step, 512))
        for tile in range(4):
            put(third[:, 128 * tile : 128 * tile + 128], 12 + 4 * step + tile)
    branch = left(high_ref, high_other_ref, 1280)
    for step in range(3):
        fourth = product(branch, both(high_ref, high_other_ref, 5632 + 512 * step, 512))
        for tile in range(4):
            put(fourth[:, 128 * tile : 128 * tile + 128], 36 + 4 * step + tile)

    for part in range(3):

        @pl.loop(0, blocks)
        def _(block, part=part):
            start = pl.multiple_of(block * (3 * tiles), 3 * tiles)
            out_ref[part, block] = gathered[part, pl.ds(start, 3 * tiles), :].astype(jnp.bfloat16)


TERMS_LOW = 1664
TERMS_HIGH = 7168


def dense(kernel, arguments, hbm, results, scratch, flops):
    vmem = pl.BlockSpec(memory_space=pltpu.VMEM)
    kept = [vmem] * (len(arguments) - hbm) + [pl.BlockSpec(memory_space=pl.ANY)] * hbm
    size = sum(item.size * item.dtype.itemsize for item in arguments)
    return pl.pallas_call(
        kernel,
        out_shape=tuple(jax.ShapeDtypeStruct(shape, kind) for shape, kind in results),
        in_specs=kept,
        out_specs=tuple(vmem for _ in results),
        scratch_shapes=scratch,
        compiler_params=pltpu.CompilerParams(vmem_limit_bytes=VMEM_LIMIT),
        cost_estimate=pl.CostEstimate(flops=flops, bytes_accessed=size, transcendentals=0),
    )(*arguments)


def on_device(inputs, positions, attn_gain, w_qkv, w_out, ffn_gain, w_gate_up, w_down, cotangent):
    _, rows, width = inputs.shape
    section = lax.axis_index("section")
    place = lax.axis_index(("ctx", "fsdp"))
    swap = [(0, 1), (1, 0)]
    half_kind, kind = jnp.bfloat16, jnp.float32
    lanes = 2 * HEAD_DIM
    columns = w_qkv.shape[2] * SIDE
    wide_rows = 128 * (HEADS + KV_HEADS)

    depth = lax.axis_index("fsdp")
    batch = depth // 2
    worked = place + section * (SIDE - 1 - 2 * depth)
    spots_k = lax.dynamic_index_in_dim(positions, batch, 0, keepdims=False)
    spots_q = lax.dynamic_slice_in_dim(spots_k, worked * rows, rows, 0)
    chunk_of = spots_k[::CHUNK] // CHUNK
    inverse = jnp.zeros_like(chunk_of).at[chunk_of].set(jnp.arange(chunk_of.shape[0], dtype=jnp.int32))
    spots = lax.dynamic_slice_in_dim(chunk_of, worked * 2, 2, 0)
    frequency = rope_base ** (-(jnp.arange(HEAD_DIM // 2, dtype=kind) * 2.0 / HEAD_DIM))
    angle = spots_q.astype(kind)[:, None] * frequency[None, :]
    cosine, sine = jnp.cos(angle), jnp.sin(angle)
    rest = jnp.ones((rows, HEAD_DIM), kind)
    cosine = jnp.concatenate([cosine, cosine, rest], axis=1)
    sine = jnp.concatenate([-sine, sine, 0.0 * rest], axis=1)

    local_gains = jnp.pad(jnp.concatenate([attn_gain, ffn_gain], axis=0), ((0, 6), (0, 0)))
    qkv_turned = w_qkv[0].T
    qkv_first, gains, current, given = first_weight(qkv_turned, local_gains, inputs, cotangent)
    qkv_first = qkv_first.reshape(columns, width)

    shards = [w_out[0].T, w_gate_up[0], w_down[0].T, qkv_turned]
    gain_one = [gains[l, 0:1] for l in range(2)]
    gain_two = [gains[l, 1:2] for l in range(2)]

    query_like = ((KV_HEADS, 2, GROUP * CHUNK, lanes), half_kind)
    inner_like = ((KV_HEADS, 2, GROUP * CHUNK, 1), kind)
    local_like = ((KV_HEADS, 2, CHUNK, lanes), half_kind)
    state_like = ((rows, width), kind)
    pair_like = ((SIDE, rows, 2 * FF // SIDE), kind)
    low_like = ((rows, TERMS_LOW), half_kind)
    high_like = ((rows, TERMS_HIGH), half_kind)
    wide_scratch = pltpu.VMEM((wide_rows, width), half_kind)
    qkv_scratch = pltpu.VMEM((columns, width), half_kind)
    ffn_scratch = [
        pltpu.VMEM((width, width), half_kind),
        pltpu.VMEM((SIDE, width, 2 * FF // SIDE), half_kind),
        pltpu.VMEM((width, FF), half_kind),
    ]
    sems = pltpu.SemaphoreType.DMA((4,))
    qkv_flops = 2 * rows * width * wide_rows
    ffn_flops = 2 * rows * width * (width + 3 * FF)

    def attention(layer, query, local, shards):
        mixed, logsum, both, out, gate_up, down, *rest = attend_all(
            layer, inverse, spots, local, query, shards, layer
        )
        both = both.reshape(KV_HEADS, -1, CHUNK, lanes)
        weights = [out.reshape(width, width), gate_up, down.reshape(width, FF)]
        return both, mixed, logsum, weights, [item.reshape(columns, width) for item in rest]

    def attention_back(query, grad, logsum, inner, both):
        grad_query, grad_both = attend_back(inverse, spots, query, grad, logsum, inner, both)
        grad_both = grad_both.reshape(KV_HEADS, SIDE, SIDE, 2, 2, rows, lanes)
        return grad_query, combine_all(grad_both, 4)

    query_one, local = dense(
        enter_kernel, (current, gain_one[0], cosine, sine, qkv_first), 0, (query_like, local_like), [wide_scratch], qkv_flops
    )
    both_one, mixed_one, logsum_one, weights_one, (qkv_second,) = attention(0, query_one, local, shards)
    hidden, pair, middle, query_two, local = dense(
        between_kernel,
        (mixed_one, current, gain_two[0], gain_one[1], cosine, sine, *weights_one, qkv_second),
        4,
        (state_like, pair_like, state_like, query_like, local_like),
        ffn_scratch + [qkv_scratch, wide_scratch, sems],
        ffn_flops + qkv_flops,
    )
    both_two, mixed_two, logsum_two, weights_two, _ = attention(1, query_two, local, shards[:3])
    result, grad_hidden, high_two, grad, inner = dense(
        top_kernel,
        (mixed_two, middle, given, gain_two[1], *weights_two),
        3,
        (state_like, state_like, high_like, query_like, inner_like),
        ffn_scratch + [sems],
        2 * ffn_flops,
    )
    earlier = lax.ppermute(
        result,
        ("section", "ctx", "fsdp"),
        [(64 + 4 * ctx + z, 64 + 4 * ctx + 3 - z) for ctx in range(16) for z in range(4)],
    )
    grad_query, grad_local = attention_back(query_two, grad, logsum_two, inner, both_two)
    low_two, grad_hidden, high_one, grad, inner = dense(
        descend_kernel,
        (
            grad_query, grad_local, middle, grad_hidden, gain_one[1], cosine, sine,
            mixed_one, hidden, pair, gain_two[0], qkv_second, *weights_one,
        ),
        4,
        (low_like, state_like, high_like, query_like, inner_like),
        ffn_scratch + [qkv_scratch, wide_scratch, sems],
        ffn_flops + qkv_flops,
    )
    grad_query, grad_local = attention_back(query_one, grad, logsum_one, inner, both_one)
    grad_in, low_one = dense(
        leave_kernel,
        (grad_query, grad_local, current, grad_hidden, gain_one[0], cosine, sine, qkv_first),
        0,
        (state_like, low_like),
        [wide_scratch],
        qkv_flops,
    )

    first = section == 0
    low, low_other = jnp.where(first, low_one, low_two), jnp.where(first, low_two, low_one)
    high, high_other = jnp.where(first, high_one, high_two), jnp.where(first, high_two, high_one)
    low_other = lax.ppermute(low_other, "section", swap)
    high_other = lax.ppermute(high_other, "section", swap)
    blocks = SIDE * SIDE * SIDE
    each = width // blocks
    total = columns + width + 3 * FF
    line = jnp.arange(width)
    order = (line[:, None] % blocks * each + line[:, None] // blocks == line[None, :]).astype(half_kind)
    (term,) = dense(
        weight_kernel,
        (order, low, low_other, high, high_other),
        0,
        (((3, blocks, 3 * total // 128, 128), half_kind),),
        [pltpu.VMEM((3, blocks * 3 * total // 128, 128), kind)],
        4 * rows * width * total,
    )
    term = term.reshape(3, SIDE, SIDE, SIDE, 3 * total // 128, 128)
    summed = scatter_all(term, 80, 2).reshape(each, total)
    grad_qkv = summed[:, :columns]
    grad_out_weight = summed[:, columns : columns + width]
    grad_gate_up = summed[:, columns + width : columns + width + 2 * FF]
    grad_down = summed[:, columns + width + 2 * FF :].T

    qkv_own = jnp.where(
        first,
        lax.dynamic_slice_in_dim(qkv_first, place * each, each, 1),
        lax.dynamic_slice_in_dim(qkv_second, place * each, each, 1),
    )
    qkv_own = qkv_own.astype(kind).T
    gate_up_own = jnp.where(
        first,
        lax.dynamic_slice_in_dim(weights_one[1], place * each, each, 1),
        lax.dynamic_slice_in_dim(weights_two[1], place * each, each, 1),
    ).astype(kind)
    split = grad_gate_up.reshape(each, SIDE, -1).transpose(1, 0, 2)
    grad_gain_one = jnp.sum(qkv_own * grad_qkv, axis=1) / lax.dynamic_slice_in_dim(attn_gain[0], place * each, each, 0)
    grad_gain_two = jnp.sum(gate_up_own * split, axis=(0, 2)) / lax.dynamic_slice_in_dim(
        ffn_gain[0], place * each, each, 0
    )

    def index_of(core, ctx, z):
        return (core * SIDE * SIDE + ctx) * SIDE + z

    places = [(ctx, z) for ctx in range(SIDE * SIDE) for z in range(SIDE)]
    axes = ("section", "ctx", "fsdp")
    later = lax.ppermute(
        jnp.where(first, result, grad_in),
        axes,
        [(index_of(0, ctx, z), index_of(1, ctx, z)) for ctx, z in places]
        + [(index_of(1, ctx, z), index_of(0, ctx, SIDE - 1 - z)) for ctx, z in places],
    )
    mine = jnp.where(first, grad_in, later)
    other = jnp.where(first, later, earlier)
    ends = jnp.where(batch == 0, jnp.stack([mine, other]), jnp.stack([other, mine]))
    return (
        ends[None],
        grad_gain_one[None],
        grad_qkv[None],
        grad_out_weight[None],
        grad_gain_two[None],
        grad_gate_up[None],
        grad_down[None],
    )


def solution(mesh):
    placed = (
        P(None, ("ctx", "fsdp"), None),
        P(),
        P("section", None),
        P("section", None, "fsdp"),
        P("section", None, "fsdp"),
        P("section", None),
        P("section", None, "fsdp"),
        P("section", None, "fsdp"),
        P(None, ("ctx", "fsdp"), None),
    )
    return jax.shard_map(
        on_device,
        mesh=mesh,
        in_specs=placed,
        out_specs=(
            P("section", None, ("ctx", "fsdp"), None),
            P("section", ("ctx", "fsdp")),
            P("section", ("ctx", "fsdp"), None),
            P("section", ("ctx", "fsdp"), None),
            P("section", ("ctx", "fsdp")),
            P("section", ("ctx", "fsdp"), None),
            P("section", None, ("ctx", "fsdp")),
        ),
        check_vma=False,
    )
```

```python
import functools

import jax
import jax.numpy as jnp
from jax import lax
from jax.experimental import pallas as pl
from jax.experimental.pallas import tpu as pltpu
from jax.sharding import PartitionSpec as P

HEADS = 9
KV_HEADS = 3
GROUP = 3
HEAD_DIM = 64
FF = 1536
CHUNK = 64
BLOCK = 512
PER = BLOCK // CHUNK
MESH = pl.DeviceIdType.MESH
VMEM_LIMIT = 56 * 1024 * 1024

epsilon = 1e-05
rope_base = 100000.0
contract_last = (((1,), (1,)), ((), ()))
contract_first = (((0,), (0,)), ((), ()))

ORDERS = ((2, 0, 1), (0, 1, 2), (1, 2, 0))
SIDE = 4


def here():
    ctx = lax.axis_index("ctx")
    return (lax.axis_index("section"), (ctx // SIDE, lax.rem(ctx, SIDE), lax.axis_index("fsdp")))


def shifted(at, axis, step):
    return lax.rem(at[axis] + (step + SIDE), SIDE)


def device_at(section, at, axis, step):
    moved = list(at)
    moved[axis] = shifted(at, axis, step)
    return (section, moved[0] * SIDE + moved[1], moved[2])


def enter(section, at):
    barrier = pltpu.get_barrier_semaphore()
    for axis in range(3):
        for step in (1, -1):
            pl.semaphore_signal(
                barrier, inc=1, device_id=device_at(section, at, axis, step), device_id_type=MESH
            )
    pl.semaphore_wait(barrier, 6)


def slab(ref, part, axes, fixed, rows):
    return ref.at[(part,) + tuple(fixed.get(axis, slice(None)) for axis in axes) + (rows,)]


def pair_step(at):
    return 1 - 2 * lax.rem(at[2], 2)


SIDES = (SIDE, SIDE, 2)
STEPS = ((0, 1), (1, -1))


class Team:
    def __init__(self):
        self.section, self.at = here()
        w = lax.rem(self.at[2], 2)
        h = self.at[2] // 2
        self.h = lax.rem(h + self.section, 2)
        self.spot = (self.at[0], self.at[1], lax.rem(w + self.section, 2))

    def beside(self):
        return (1 - self.section, self.at[0] * SIDE + self.at[1], self.at[2])

    def shifted(self, axis, step):
        return lax.rem(self.spot[axis] + (step + SIDE), SIDES[axis])

    def moved(self, steps):
        y, x = (lax.rem(self.at[axis] + (steps[axis] + SIDE), SIDE) for axis in range(2))
        z = self.at[2] + (pair_step(self.at) if steps[2] % 2 else 0)
        return (self.section, y * SIDE + x, z)

    def device(self, axis, step):
        return self.moved(tuple(step if other == axis else 0 for other in range(3)))

    def enter(self):
        barrier = pltpu.get_barrier_semaphore()
        devices = [self.moved(steps) for steps in STRAIGHT]
        devices += [self.beside(), device_at(self.section, self.at, 2, -pair_step(self.at))]
        for device in devices:
            pl.semaphore_signal(barrier, inc=1, device_id=device, device_id_type=MESH)
        pl.semaphore_wait(barrier, len(devices))


def scatter_kernel(split, terms_ref, out_ref, sum_one, sum_two, near_one, far_one, near_two, far_two, near_three, far_three, send, recv):
    rows = terms_ref.shape[-2]
    halves = (pl.ds(0, split), pl.ds(split, rows - split))
    section, at = here()
    enter(section, at)
    sums = (terms_ref, sum_one, sum_two, out_ref)
    landing = ((near_one, far_one), (near_two, far_two), (near_three, far_three))

    def remaining(part, phase):
        return tuple(sorted(ORDERS[part][: 3 - phase]))

    def axis_of(part, phase):
        return ORDERS[part][2 - phase]

    def landed(phase, part, way, number):
        half = (number + way) % 2
        slot = {(0, 0): 0, (0, 2): 1, (1, 1): 2, (0, 1): 0, (1, 0): 1, (1, 2): 2}[way, number]
        return landing[phase][half].at[slot, part]

    def message(phase, part, way, number, step, source):
        axis = axis_of(part, phase)
        return pltpu.make_async_remote_copy(
            src_ref=source,
            dst_ref=landed(phase, part, way, number),
            send_sem=send.at[phase, part, way, number],
            recv_sem=recv.at[phase, part, way, number],
            device_id=device_at(section, at, axis, step),
            device_id_type=MESH,
        )

    def own(phase, part, coordinate, half):
        return slab(sums[phase], part, remaining(part, phase), {axis_of(part, phase): coordinate}, halves[half])

    def add(phase, target, terms):
        outer = target.shape[:-2]
        count = 1
        for size in outer:
            count *= size

        def one(index):
            total = terms[0][index].astype(jnp.float32)
            for term in terms[1:]:
                total = total + term[index].astype(jnp.float32)
            target[index] = total.astype(target.dtype)

        if count == 1:
            one((slice(None),) * 2)
            return

        @pl.loop(0, count)
        def _(step):
            if len(outer) == 1:
                one((step,))
            else:
                one((step // SIDE, lax.rem(step, SIDE)))

    for phase in range(3):
        flying = {}
        for number in range(2):
            for part in range(3):
                axis = axis_of(part, phase)
                for way, step in enumerate((1, -1)):
                    coordinate = shifted(at, axis, 2 * step if number == 0 else step)
                    copy = message(phase, part, way, number, step, own(phase, part, coordinate, (number + way) % 2))
                    copy.start()
                    flying[part, way, number] = copy
        for part in range(3):
            axis = axis_of(part, phase)
            for way, step in enumerate((1, -1)):
                flying[part, way, 0].wait_recv()
                passing = landed(phase, part, way, 0)
                add(phase, passing, (passing, own(phase, part, shifted(at, axis, step), way)))
                copy = message(phase, part, way, 2, step, passing)
                copy.start()
                flying[part, way, 2] = copy
        for part in range(3):
            axis = axis_of(part, phase)
            for way in range(2):
                flying[part, way, 1].wait_recv()
                flying[part, way, 2].wait_recv()
            for half in range(2):
                target = sums[phase + 1].at[(part,) + (slice(None),) * (2 - phase) + (halves[half],)]
                add(
                    phase,
                    target,
                    (
                        own(phase, part, at[axis], half),
                        landed(phase, part, half, 2),
                        landed(phase, part, 1 - half, 1),
                    ),
                )
        for part in range(3):
            for way in range(2):
                for number in range(3):
                    flying[part, way, number].wait_send()


def scatter_all(terms, split, collective_id):
    parts, rows, lanes = terms.shape[0], terms.shape[-2], terms.shape[-1]
    kind = terms.dtype
    near, far = split, rows - split
    return pl.pallas_call(
        functools.partial(scatter_kernel, split),
        out_shape=jax.ShapeDtypeStruct((parts, rows, lanes), jnp.float32),
        in_specs=[pl.BlockSpec(memory_space=pltpu.VMEM)],
        out_specs=pl.BlockSpec(memory_space=pltpu.VMEM),
        scratch_shapes=[
            pltpu.VMEM((parts, SIDE, SIDE, rows, lanes), kind),
            pltpu.VMEM((parts, SIDE, rows, lanes), kind),
            pltpu.VMEM((3, parts, SIDE, SIDE, near, lanes), kind),
            pltpu.VMEM((3, parts, SIDE, SIDE, far, lanes), kind),
            pltpu.VMEM((3, parts, SIDE, near, lanes), kind),
            pltpu.VMEM((3, parts, SIDE, far, lanes), kind),
            pltpu.VMEM((3, parts, near, lanes), kind),
            pltpu.VMEM((3, parts, far, lanes), kind),
            pltpu.SemaphoreType.DMA((3, 3, 2, 3)),
            pltpu.SemaphoreType.DMA((3, 3, 2, 3)),
        ],
        compiler_params=pltpu.CompilerParams(
            collective_id=collective_id, has_side_effects=True, vmem_limit_bytes=VMEM_LIMIT
        ),
        cost_estimate=pl.CostEstimate(flops=terms.size, bytes_accessed=2 * terms.size, transcendentals=0),
    )(terms)


def visible(shape, chunk, block):
    row = lax.broadcasted_iota(jnp.int32, shape, 0)
    column = lax.broadcasted_iota(jnp.int32, shape, 1)
    return block * BLOCK + column <= chunk * CHUNK + lax.rem(row, CHUNK)


STEPS_UNMASKED = 15


STRAIGHT = ((1, 0, 0), (2, 0, 0), (3, 0, 0), (0, 1, 0), (0, 2, 0), (0, 3, 0), (0, 0, 1))


class Exchange:
    def __init__(self, team, sems):
        self.team, self.sems = team, sems

    def send(self, source, target, device, kind, *index):
        send, recv = self.sems[kind]
        copy = pltpu.make_async_remote_copy(
            src_ref=source,
            dst_ref=target,
            send_sem=send.at[index],
            recv_sem=recv.at[index],
            device_id=device,
            device_id_type=MESH,
        )
        copy.start()
        return copy


class PartGather:
    def __init__(self, part, exchange, local_ref, keys):
        self.part, self.exchange, self.team = part, exchange, exchange.team
        self.local_ref, self.keys = local_ref, keys
        self.near, self.ring, self.side = [], {}, []

    def slab(self, unit, coordinate, w=slice(None)):
        y, x = (coordinate, slice(None)) if unit == 0 else (slice(None), coordinate)
        return self.keys.at[y, x, self.team.h, w, unit]

    def start_near(self):
        spot = self.team.spot
        for unit in range(2):
            for step in range(1, SIDE):
                steps = (0, step, 0) if unit == 0 else (step, 0, 0)
                place = self.keys.at[spot[0], spot[1], self.team.h, :, unit]
                self.near.append(
                    self.exchange.send(place, place, self.team.moved(steps), "near", self.part, unit, step - 1)
                )

    def message(self, unit, way, number, coordinate, w):
        place = self.slab(unit, coordinate, w)
        self.ring[unit, way, number] = self.exchange.send(
            place, place, self.team.device(unit, STEPS[way][1]), "ring", self.part, unit, way, number
        )

    def aside(self, unit, slot, coordinate):
        place = self.slab(unit, coordinate)
        self.side.append(
            self.exchange.send(place, place, self.team.beside(), "side", self.part, unit, slot)
        )

    def start_ring(self):
        for copy in self.near:
            copy.wait_recv()
        for number in range(2):
            for unit in range(2):
                for way, _ in STEPS:
                    self.message(unit, way, number, self.team.spot[unit], (number + way) % 2)
        for unit in range(2):
            self.aside(unit, 0, self.team.spot[unit])

    def pass_on(self):
        for unit in range(2):
            for way, step in STEPS:
                self.ring[unit, way, 0].wait_recv()
                self.message(unit, way, 2, self.team.shifted(unit, -step), way)

    def share(self):
        for unit in range(2):
            for way, step in STEPS:
                self.ring[unit, way, 1].wait_recv()
                self.aside(unit, 1 + way, self.team.shifted(unit, -step))
        for unit in range(2):
            for way, _ in STEPS:
                self.ring[unit, way, 2].wait_recv()
            self.aside(unit, 3, self.team.shifted(unit, 2))

    def finish(self):
        for copy in self.side:
            copy.wait_recv()

    def drain(self):
        for copy in self.near + list(self.ring.values()) + self.side:
            copy.wait_send()


class WeightGather:
    def __init__(self, owner, number, exchange, local_ref, out_ref):
        self.owner, self.number, self.exchange, self.team = owner, number, exchange, exchange.team
        self.local_ref, self.out_ref = local_ref, out_ref
        rows = local_ref.shape[0]
        split = rows // 32 * 16
        self.halves = (pl.ds(0, split), pl.ds(split, rows - split))
        self.copies = []

    def here(self):
        return self.team.section == self.owner

    def index(self, step):
        return lax.rem(self.team.at[2] + (step + SIDE), SIDE)

    def message(self, way, number, index, half, start=True):
        spot = self.out_ref.at[index, self.halves[half]]
        source = self.local_ref.at[self.halves[half]] if number < 2 else spot
        return self.copy(source, spot, device_at(self.team.section, self.team.at, 2, STEPS[way][1]), "weight_ring", start, way, number)

    def aside(self, slot, start=True):
        spot = self.out_ref.at[self.index((0, -1, 1, 2)[slot])]
        source = self.local_ref if slot == 0 else spot
        return self.copy(source, spot, self.team.beside(), "weight_side", start, slot)

    def copy(self, source, target, device, kind, start, *index):
        send, recv = self.exchange.sems[kind]
        place = (self.number,) + index
        copy = pltpu.make_async_remote_copy(
            src_ref=source, dst_ref=target, send_sem=send.at[place], recv_sem=recv.at[place],
            device_id=device, device_id_type=MESH,
        )
        if start:
            copy.start()
        return copy

    def own(self):
        return pltpu.make_async_copy(self.local_ref, self.out_ref.at[self.team.at[2]], self.exchange.sems["weight_own"].at[self.number])

    def start(self):
        @pl.when(self.here())
        def _():
            self.own().start()
            for number in range(2):
                for way, _ in STEPS:
                    self.message(way, number, self.team.at[2], (number + way) % 2)
            self.aside(0)

    def pass_on(self):
        @pl.when(self.here())
        def _():
            for way, step in STEPS:
                self.message(way, 0, self.team.at[2], way, False).wait_recv()
                self.message(way, 2, self.index(-step), way)

    def hand(self):
        @pl.when(self.here())
        def _():
            for way, step in STEPS:
                self.message(way, 1, self.team.at[2], 1 - way, False).wait_recv()
                self.aside(1 + way)

    def share(self):
        @pl.when(self.here())
        def _():
            for way, step in STEPS:
                self.message(way, 2, self.index(-step), way, False).wait_recv()
            self.aside(3)

    def finish(self):
        @pl.when(self.here())
        def _():
            self.own().wait()
            for way, step in STEPS:
                for number in range(3):
                    index = self.team.at[2] if number < 2 else self.index(-step)
                    self.message(way, number, index, (number + way) % 2, False).wait_send()
            for slot in range(4):
                self.aside(slot, False).wait_send()

        @pl.when(jnp.logical_not(self.here()))
        def _():
            for slot in range(4):
                self.aside(slot, False).wait_recv()


EXP = jnp.exp


def key_block(inverse_ref, keys, block):
    pieces = []
    for index in range(PER):
        place = inverse_ref[block * PER + index]
        y = lax.shift_right_logical(place, 5)
        x, h, w, half = (
            lax.bitwise_and(lax.shift_right_logical(place, shift), mask) for shift, mask in ((3, 3), (2, 1), (1, 1), (0, 1))
        )
        pieces.append(keys[y, x, h, w, half])
    return jnp.concatenate(pieces, axis=0)


def schedule(spots_ref):
    return lax.shift_right_logical(spots_ref[0], 3), lax.shift_right_logical(spots_ref[1], 3)


def attend_all_kernel(
    owner, inverse_ref, spots_ref, local_ref, query_ref, *refs
):
    count = 4 if owner == 0 else 3
    shard_refs, refs = refs[:count], refs[count:]
    (mixed_ref, logsum_ref, both_ref), refs = refs[:3], refs[3:]
    whole_refs, refs = refs[:count], refs[count:]
    keys, (highest_at, mixed_at), refs = refs[:3], refs[3:5], refs[5:]
    sems = {
        "near": refs[0:2], "ring": refs[2:4], "side": refs[4:6],
        "weight_ring": refs[6:8], "weight_side": refs[8:10], "pair": refs[10:12], "weight_own": refs[12],
    }
    kept = refs[13]
    team = Team()
    team.enter()
    exchange = Exchange(team, sems)
    spot, h = team.spot, team.h
    parts = [PartGather(part, exchange, local_ref, keys[part]) for part in range(KV_HEADS)]
    weights = [
        WeightGather(owner if number < 3 else 1 - owner, number, exchange, shard_refs[number], whole_refs[number])
        for number in range(count)
    ]
    own = [
        pltpu.make_async_copy(local_ref.at[part], keys[part].at[spot[0], spot[1], h, spot[2]], kept.at[part])
        for part in range(KV_HEADS)
    ]
    saved = [
        pltpu.make_async_copy(keys[part], both_ref.at[part], kept.at[KV_HEADS + part]) for part in range(KV_HEADS)
    ]
    ends = schedule(spots_ref)

    def attend_scores(part, half, block):
        both = key_block(inverse_ref, keys[part], block)
        return lax.dot_general(
            query_ref[part, half], both, contract_last, preferred_element_type=jnp.float32
        )

    def attend_rest(part, scores, block, highest, mixed):
        both = key_block(inverse_ref, keys[part], block)
        higher = jnp.maximum(highest, jnp.broadcast_to(jnp.max(scores, axis=-1, keepdims=True), highest.shape))
        exponent = EXP(scores - jnp.concatenate([higher] * (BLOCK // 128), axis=1)).astype(jnp.bfloat16)
        values = jnp.where(is_lower(both.shape), jnp.bfloat16(1.0), both)
        return higher, jnp.dot(exponent, values, preferred_element_type=jnp.float32) + EXP(highest - higher) * mixed

    def attend_first(part):
        for half in range(2):
            scores = attend_scores(part, half, ends[half])
            scores = jnp.where(visible(scores.shape, spots_ref[half], ends[half]), scores, -1e30)
            highest, mixed = attend_rest(
                part, scores, ends[half], jnp.full((scores.shape[0], 128), -1e30, jnp.float32), jnp.zeros((scores.shape[0], 128), jnp.float32)
            )
            highest_at[half] = highest
            mixed_at[half] = mixed

    def attend_some(part, low, high):
        if True:
            size = high - low
            steps = [low + index for index in range(size)]
            halves = [jnp.where(step >= ends[0], 1, 0) for step in steps]
            blocks = [step - half * ends[0] for step, half in zip(steps, halves)]
            befores = [jnp.where(step == ends[0], 1, jnp.where(step == 0, 0, step + 1)) for step in steps]
            scores = attend_scores(part, halves[0], blocks[0])
            for index in range(size):
                later = attend_scores(part, halves[index + 1], blocks[index + 1]) if index + 1 < size else None
                before = befores[index]
                highest, mixed = attend_rest(part, scores, blocks[index], highest_at[before], mixed_at[before])
                highest_at[steps[index] + 2] = highest
                mixed_at[steps[index] + 2] = mixed
                scores = later

    def attend_last(part):
        last = (
            jnp.where(ends[0] == 0, 0, ends[0] + 1),
            jnp.where(ends[0] == STEPS_UNMASKED, 1, STEPS_UNMASKED + 1),
        )
        for half in range(2):
            mixed = mixed_at[last[half]]
            total = mixed[:, :1]
            mixed_ref[part, half] = mixed / total
            logsum_ref[part, half] = highest_at[last[half]][:, :1] + jnp.log(total)

    pairs = [
        exchange.send(
            local_ref.at[part], keys[part].at[spot[0], spot[1], h, spot[2]], team.device(2, 1), "pair", part
        )
        for part in range(KV_HEADS)
    ]
    for copy in own:
        copy.start()
    for weight in weights:
        weight.start()
    for part in range(KV_HEADS):
        own[part].wait()
        pairs[part].wait_recv()
        parts[part].start_near()
    for part in parts:
        part.start_ring()
    parts[0].pass_on()
    parts[1].pass_on()
    parts[0].share()
    parts[2].pass_on()
    parts[0].finish()
    saved[0].start()
    attend_first(0)
    attend_some(0, 0, 7)
    parts[1].share()
    for weight in weights:
        weight.pass_on()
    attend_some(0, 7, 15)
    attend_last(0)
    parts[1].finish()
    saved[1].start()
    attend_first(1)
    attend_some(1, 0, 7)
    parts[2].share()
    for weight in weights:
        weight.hand()
    attend_some(1, 7, 15)
    attend_last(1)
    parts[2].finish()
    saved[2].start()
    attend_first(2)
    for weight in weights:
        weight.share()
    attend_some(2, 0, 15)
    attend_last(2)
    for copy in pairs:
        copy.wait_send()
    for part in parts:
        part.drain()
    for weight in weights:
        weight.finish()
    for copy in saved:
        copy.wait()


def attend_all(owner, inverse, spots, local, query, shards, collective_id):
    groups, halves, rows, lanes = query.shape
    count = len(shards)
    keys = (SIDE, SIDE, 2, 2, 2, CHUNK, lanes)
    vmem, smem, held = (pl.BlockSpec(memory_space=space) for space in (pltpu.VMEM, pltpu.SMEM, pl.ANY))
    slots = STEPS_UNMASKED + 2
    scores = rows * BLOCK * slots * groups
    semaphore = pltpu.SemaphoreType.DMA
    return pl.pallas_call(
        functools.partial(attend_all_kernel, owner),
        out_shape=(
            jax.ShapeDtypeStruct((groups, halves, rows, lanes), jnp.float32),
            jax.ShapeDtypeStruct((groups, halves, rows, 1), jnp.float32),
            jax.ShapeDtypeStruct((groups,) + keys, local.dtype),
        )
        + tuple(jax.ShapeDtypeStruct((SIDE,) + item.shape, item.dtype) for item in shards),
        in_specs=[smem, smem, vmem, vmem] + [held] * count,
        out_specs=(vmem, vmem, held) + (held,) * count,
        scratch_shapes=[pltpu.VMEM(keys, local.dtype) for _ in range(groups)]
        + [
            pltpu.VMEM((slots, rows, lanes), jnp.float32),
            pltpu.VMEM((slots, rows, lanes), jnp.float32),
        ]
        + [semaphore(shape) for shape in ((3, 2, 3), (3, 2, 2, 3), (3, 2, 4), (count, 2, 3), (count, 4), (3,)) for _ in range(2)]
        + [semaphore((count,)), semaphore((2 * groups,))],
        compiler_params=pltpu.CompilerParams(
            collective_id=collective_id, has_side_effects=True, vmem_limit_bytes=VMEM_LIMIT
        ),
        cost_estimate=pl.CostEstimate(flops=4 * scores * lanes, bytes_accessed=128 * local.size, transcendentals=scores),
    )(inverse, spots, local, query, *shards)


class PartScatter:
    def __init__(self, part, exchange, terms, joined, landing, sums, near, pair, out_ref):
        self.part, self.exchange, self.team = part, exchange, exchange.team
        self.terms, self.joined, self.landing, self.sums = terms, joined, landing, sums
        self.near, self.pair, self.out_ref = near, pair, out_ref
        self.sides, self.rings, self.nears, self.pairs = [], [], [], []

    def swap(self):
        for unit in range(2):
            source = self.terms.at[:, :, 1 - self.team.h, :, unit]
            self.sides.append(
                self.exchange.send(source, self.joined.at[unit], self.team.beside(), "side", self.part, unit)
            )

    def send_ring(self):
        for unit in range(2):
            self.sides[unit].wait_recv()

            @pl.loop(0, SIDE * SIDE)
            def _(index, unit=unit):
                y, x = lax.div(index, SIDE), lax.rem(index, SIDE)
                own = self.terms[y, x, self.team.h, :, unit].astype(jnp.float32)
                other = self.joined[unit, y, x].astype(jnp.float32)
                self.joined[unit, y, x] = (own + other).astype(jnp.bfloat16)

            for step in (2, 1, 3):
                coordinate = self.team.shifted(unit, step)
                place = self.joined.at[unit, coordinate] if unit == 0 else self.joined.at[unit, :, coordinate]
                steps = (step, 0, 0) if unit == 0 else (0, step, 0)
                self.rings.append(
                    self.exchange.send(
                        place, self.landing.at[unit, step - 1], self.team.moved(steps), "ring", self.part, unit, step - 1
                    )
                )

    def send_near(self):
        for copy in self.rings:
            copy.wait_recv()
        for unit in range(2):
            mine = self.team.spot[unit]
            for index in range(SIDE):
                place = (unit, mine, index) if unit == 0 else (unit, index, mine)
                total = self.joined[place].astype(jnp.float32)
                for step in range(SIDE - 1):
                    total = total + self.landing[unit, step, index].astype(jnp.float32)
                self.sums[unit, index] = total.astype(jnp.bfloat16)
            for step in range(1, SIDE):
                steps = (0, step, 0) if unit == 0 else (step, 0, 0)
                self.nears.append(
                    self.exchange.send(
                        self.sums.at[unit, self.team.shifted(1 - unit, step)], self.near.at[unit, step - 1],
                        self.team.moved(steps), "near", self.part, unit, step - 1,
                    )
                )

    def send_pair(self):
        for copy in self.nears:
            copy.wait_recv()
        w = self.team.spot[2]
        for unit in range(2):
            mine = self.team.spot[1 - unit]
            for index in range(2):
                place = w if index == 0 else 1 - w
                total = self.sums[unit, mine, place].astype(jnp.float32)
                for step in range(SIDE - 1):
                    total = total + self.near[unit, step, place].astype(jnp.float32)
                if index == 0:
                    self.out_ref[self.part, unit] = total
                else:
                    self.pair[0, unit] = total.astype(jnp.bfloat16)
        self.pairs.append(
            self.exchange.send(self.pair.at[0], self.pair.at[1], self.team.device(2, 1), "pair", self.part)
        )

    def finish(self):
        self.pairs[0].wait_recv()
        for unit in range(2):
            self.out_ref[self.part, unit] = self.out_ref[self.part, unit] + self.pair[1, unit].astype(jnp.float32)
        for copy in self.sides + self.rings + self.nears + self.pairs:
            copy.wait_send()


def attend_back_all_kernel(
    inverse_ref, spots_ref, chunk_ref, query_ref, grad_ref, logsum_ref, inner_ref, both_ref,
    grad_query_ref, out_ref, *refs
):
    keys, refs = refs[:3], refs[3:]
    terms, refs = refs[:3], refs[3:]
    buffers, refs = [refs[5 * part : 5 * part + 5] for part in range(3)], refs[15:]
    logsum_at, inner_at, query_at, grad_at, *refs = refs
    sems = {kind: refs[2 * index : 2 * index + 2] for index, kind in enumerate(("side", "ring", "near", "pair"))}
    kept = refs[8]
    team = Team()
    brought_in = [pltpu.make_async_copy(both_ref.at[part], keys[part], kept.at[part]) for part in range(KV_HEADS)]
    for copy in brought_in:
        copy.start()
    team.enter()
    exchange = Exchange(team, sems)
    parts = [
        PartScatter(part, exchange, terms[part], *buffers[part], out_ref) for part in range(KV_HEADS)
    ]
    ends = schedule(spots_ref)
    for part in range(KV_HEADS):
        for half in range(2):
            logsum_at[part, half] = jnp.broadcast_to(logsum_ref[part, half], logsum_at.shape[2:])
            inner_at[part, half] = jnp.broadcast_to(inner_ref[part, half], inner_at.shape[2:])

    grad_at[STEPS_UNMASKED + 2] = jnp.zeros(grad_at.shape[1:], jnp.float32)

    def products(part, half, block):
        both = key_block(inverse_ref, keys[part], block)
        scores = lax.dot_general(query_ref[part, half], both, contract_last, preferred_element_type=jnp.float32)
        grad_weights = lax.dot_general(grad_ref[part, half], both, contract_last, preferred_element_type=jnp.float32)
        return scores, grad_weights

    def rest(part, slot, half, block, found, masked, before):
        scores, grad_weights = found
        both = key_block(inverse_ref, keys[part], block)
        logsum = jnp.concatenate([logsum_at[part, half]] * (BLOCK // 128), axis=1)
        inner = jnp.concatenate([inner_at[part, half]] * (BLOCK // 128), axis=1)
        probs = EXP(scores - logsum)
        if masked:
            probs = jnp.where(visible(scores.shape, spots_ref[half], block), probs, 0.0)
        grad_scores = (probs * (grad_weights - inner)).astype(jnp.bfloat16)
        grad_query = jnp.dot(grad_scores, both, preferred_element_type=jnp.float32)
        query_at[slot] = grad_query if before is None else grad_query + query_at[before]
        grad_at[slot] = lax.dot_general(
            jnp.concatenate([probs.astype(jnp.bfloat16), grad_scores], axis=0),
            jnp.concatenate([grad_ref[part, half], query_ref[part, half]], axis=0),
            contract_first,
            preferred_element_type=jnp.float32,
        ).reshape(PER, CHUNK, 2 * HEAD_DIM)

    def back_first(part):
        for half in range(2):
            rest(part, half, half, ends[half], products(part, half, ends[half]), True, None)

    def back_some(part, low, high):
        steps = list(range(low, high))
        halves = [jnp.where(step >= ends[0], 1, 0) for step in steps]
        blocks = [step - half * ends[0] for step, half in zip(steps, halves)]
        found = products(part, halves[0], blocks[0])
        for index, step in enumerate(steps):
            later = products(part, halves[index + 1], blocks[index + 1]) if index + 1 < len(steps) else None
            before = jnp.where(step == ends[0], 1, jnp.where(step == 0, 0, step + 1))
            rest(part, step + 2, halves[index], blocks[index], found, False, before)
            found = later

    def back_last(part):
        last = (
            jnp.where(ends[0] == 0, 0, ends[0] + 1),
            jnp.where(ends[0] == STEPS_UNMASKED, 1, STEPS_UNMASKED + 1),
        )
        for half in range(2):
            grad_query_ref[part, half] = query_at[last[half]]

        @pl.loop(0, SIDE * SIDE)
        def _(column):
            y, x = lax.div(column, SIDE), lax.rem(column, SIDE)
            for number in range(8):
                chunk = chunk_ref[8 * column + number]
                row = lax.bitwise_and(chunk, PER - 1)
                block = lax.shift_right_logical(chunk, 3)
                total = None
                for half in range(2):
                    slot = jnp.where(block == ends[half], half, 2 + half * ends[0] + block)
                    term = grad_at[jnp.where(block <= ends[half], slot, STEPS_UNMASKED + 2), row]
                    total = term if total is None else total + term
                terms[part][y, x, number // 4, number // 2 % 2, number % 2] = total.astype(jnp.bfloat16)

    def begin(part):
        brought_in[part].wait()
        back_first(part)
        back_some(part, 0, 5)

    begin(0)
    back_some(0, 5, 15)
    back_last(0)
    parts[0].swap()
    begin(1)
    back_some(1, 5, 10)
    parts[0].send_ring()
    back_some(1, 10, 15)
    back_last(1)
    parts[1].swap()
    begin(2)
    back_some(2, 5, 10)
    parts[1].send_ring()
    back_some(2, 10, 15)
    back_last(2)
    parts[2].swap()
    parts[0].send_near()
    parts[2].send_ring()
    parts[0].send_pair()
    parts[1].send_near()
    parts[0].finish()
    parts[1].send_pair()
    parts[2].send_near()
    parts[1].finish()
    parts[2].send_pair()
    parts[2].finish()


def attend_back_all(inverse, spots, chunk_of, query, grad, logsum, inner, both, collective_id):
    groups, halves, rows, lanes = query.shape
    keys = both.shape[1:]
    kind = both.dtype
    block = (CHUNK, lanes)
    vmem, smem = (pl.BlockSpec(memory_space=space) for space in (pltpu.VMEM, pltpu.SMEM))
    slots = STEPS_UNMASKED + 2
    scores = rows * BLOCK * slots * groups
    semaphore = pltpu.SemaphoreType.DMA
    buffers = [
        pltpu.VMEM((2, SIDE, SIDE, 2) + block, kind),
        pltpu.VMEM((2, 3, SIDE, 2) + block, kind),
        pltpu.VMEM((2, SIDE, 2) + block, kind),
        pltpu.VMEM((2, 3, 2) + block, kind),
        pltpu.VMEM((2, 2) + block, kind),
    ]
    return pl.pallas_call(
        attend_back_all_kernel,
        out_shape=(
            jax.ShapeDtypeStruct((groups, halves, rows, lanes), jnp.float32),
            jax.ShapeDtypeStruct((groups, 2) + block, jnp.float32),
        ),
        in_specs=[smem] * 3 + [vmem] * 4 + [pl.BlockSpec(memory_space=pl.ANY)],
        out_specs=(vmem, vmem),
        scratch_shapes=[pltpu.VMEM(keys, kind) for _ in range(2 * groups)]
        + buffers * groups
        + [
            pltpu.VMEM((groups, halves, rows, lanes), jnp.float32),
            pltpu.VMEM((groups, halves, rows, lanes), jnp.float32),
            pltpu.VMEM((slots, rows, lanes), jnp.float32),
            pltpu.VMEM((slots + 1, PER) + block, jnp.float32),
        ]
        + [semaphore(shape) for shape in ((3, 2), (3, 2, 3), (3, 2, 3), (3,)) for _ in range(2)]
        + [semaphore((groups,))],
        compiler_params=pltpu.CompilerParams(
            collective_id=collective_id, has_side_effects=True, vmem_limit_bytes=VMEM_LIMIT
        ),
        cost_estimate=pl.CostEstimate(flops=10 * scores * lanes, bytes_accessed=4 * both.size, transcendentals=scores),
    )(inverse, spots, chunk_of, query, grad, logsum, inner, both)


def first_weight_kernel(
    local_ref, gains_ref, inputs_ref, cotangent_ref, out_ref, gains_out_ref, current_ref, given_ref,
    send, recv, side_send, side_recv, gain_send, gain_recv, token_send, token_recv, kept,
):
    rows = local_ref.shape[0]
    halves = (pl.ds(0, 128), pl.ds(128, rows - 128))
    section, at = here()
    place = at[2]
    beside = (1 - section, at[0] * SIDE + at[1], place)
    barrier = pltpu.get_barrier_semaphore()
    for device in (device_at(section, at, 2, 1), device_at(section, at, 2, -1), beside):
        pl.semaphore_signal(barrier, inc=1, device_id=device, device_id_type=MESH)
    pl.semaphore_wait(barrier, 3)
    own_gains = pltpu.make_async_copy(gains_ref, gains_out_ref.at[section], kept.at[0])
    own_gains.start()
    other_gains = pltpu.make_async_remote_copy(
        src_ref=gains_ref,
        dst_ref=gains_out_ref.at[section],
        send_sem=gain_send,
        recv_sem=gain_recv,
        device_id=beside,
        device_id_type=MESH,
    )
    other_gains.start()

    batch = place // 2
    partner = (section, at[0] * SIDE + at[1], SIDE - 1 - place)
    tokens = ((inputs_ref, current_ref), (cotangent_ref, given_ref))

    def crossing(number):
        source, target = tokens[number]
        return pltpu.make_async_remote_copy(
            src_ref=source.at[1 - batch],
            dst_ref=target,
            send_sem=token_send.at[number],
            recv_sem=token_recv.at[number],
            device_id=partner,
            device_id_type=MESH,
        )

    def staying(number):
        source, target = tokens[number]
        return pltpu.make_async_copy(source.at[batch], target, kept.at[2 + number])

    def aside(number, source):
        index = lax.rem(place + (0, 3, 1, 2)[number], SIDE)
        return pltpu.make_async_remote_copy(
            src_ref=out_ref.at[index] if source is None else source,
            dst_ref=out_ref.at[index],
            send_sem=side_send.at[number],
            recv_sem=side_recv.at[number],
            device_id=beside,
            device_id_type=MESH,
        )

    def message(way, number, step, index, half, source):
        spot = out_ref.at[index, halves[half]]
        return pltpu.make_async_remote_copy(
            src_ref=spot if source is None else source.at[halves[half]],
            dst_ref=spot,
            send_sem=send.at[way, number],
            recv_sem=recv.at[way, number],
            device_id=device_at(section, at, 2, step),
            device_id_type=MESH,
        )

    @pl.when(section == 0)
    def _():
        own = pltpu.make_async_copy(local_ref, out_ref.at[place], kept.at[1])
        own.start()
        for number in range(2):
            staying(number).start()
        flying = {}
        for number in range(2):
            for way, step in enumerate((1, -1)):
                flying[way, number] = message(way, number, step, place, (number + way) % 2, local_ref)
                flying[way, number].start()
        sides = [aside(0, local_ref)]
        sides[0].start()
        for way, step in enumerate((1, -1)):
            flying[way, 0].wait_recv()
            flying[way, 2] = message(way, 2, step, shifted(at, 2, -step), way, None)
            flying[way, 2].start()
        for way in range(2):
            flying[way, 1].wait_recv()
            sides.append(aside(1 + way, None))
            sides[-1].start()
        for way in range(2):
            flying[way, 2].wait_recv()
        sides.append(aside(3, None))
        sides[-1].start()
        for side in sides:
            side.wait_send()
        for way in range(2):
            for number in range(3):
                flying[way, number].wait_send()
        own.wait()
        for number in range(2):
            staying(number).wait()

    @pl.when(section == 1)
    def _():
        for number in range(2):
            crossing(number).start()
        for number in range(2):
            crossing(number).wait()
        for number in range(4):
            aside(number, None).wait_recv()

    own_gains.wait()
    other_gains.wait()


def first_weight(local, gains, inputs, cotangent):
    rows, columns = local.shape
    any_space = pl.BlockSpec(memory_space=pl.ANY)
    return pl.pallas_call(
        first_weight_kernel,
        out_shape=(
            jax.ShapeDtypeStruct((SIDE, rows, columns), local.dtype),
            jax.ShapeDtypeStruct((2,) + gains.shape, gains.dtype),
            jax.ShapeDtypeStruct(inputs.shape[1:], inputs.dtype),
            jax.ShapeDtypeStruct(cotangent.shape[1:], cotangent.dtype),
        ),
        in_specs=[any_space] * 4,
        out_specs=(any_space,) * 4,
        scratch_shapes=[
            pltpu.SemaphoreType.DMA((2, 3)),
            pltpu.SemaphoreType.DMA((2, 3)),
            pltpu.SemaphoreType.DMA((4,)),
            pltpu.SemaphoreType.DMA((4,)),
            pltpu.SemaphoreType.DMA,
            pltpu.SemaphoreType.DMA,
            pltpu.SemaphoreType.DMA((2,)),
            pltpu.SemaphoreType.DMA((2,)),
            pltpu.SemaphoreType.DMA((4,)),
        ],
        compiler_params=pltpu.CompilerParams(collective_id=3, has_side_effects=True),
        cost_estimate=pl.CostEstimate(flops=0, bytes_accessed=8 * local.size, transcendentals=0),
    )(local, gains, inputs, cotangent)


def normalize(values):
    factor = lax.rsqrt(jnp.mean(values * values, axis=-1, keepdims=True) + epsilon)
    return (values * factor, factor)


def norm_back(grad_unit, unit, factor):
    return factor * (grad_unit - unit * jnp.mean(grad_unit * unit, axis=-1, keepdims=True))


def product(left, right):
    return jnp.dot(left, right, preferred_element_type=jnp.float32)


def product_turned(left, right):
    return lax.dot_general(left, right, contract_last, preferred_element_type=jnp.float32)


def is_lower(shape):
    return lax.broadcasted_iota(jnp.int32, shape, len(shape) - 1) < HEAD_DIM


def turned(tile, cosine, sine):
    half = HEAD_DIM // 2
    lane = lax.broadcasted_iota(jnp.int32, tile.shape, 1)
    other = jnp.where(
        lax.rem(lane, HEAD_DIM) < half, pltpu.roll(tile, 128 - half, 1), pltpu.roll(tile, half, 1)
    )
    return tile * cosine + other * sine


def swapped(tile):
    return pltpu.roll(tile, HEAD_DIM, 1)


def head_rows(ref, head):
    group, index = head // GROUP, head % GROUP
    rows = slice(index * CHUNK, (index + 1) * CHUNK)
    return jnp.concatenate([ref[group, 0, rows, :], ref[group, 1, rows, :]], axis=0)


def put_head(ref, head, tile):
    group, index = head // GROUP, head % GROUP
    rows = slice(index * CHUNK, (index + 1) * CHUNK)
    ref[group, 0, rows, :] = tile[:CHUNK]
    ref[group, 1, rows, :] = tile[CHUNK:]


def widen(wide, qkv):
    for head in range(HEADS):
        wide[128 * head : 128 * head + 64, :] = qkv[64 * head : 64 * head + 64, :]
        wide[128 * head + 64 : 128 * head + 128, :] = jnp.zeros((64, wide.shape[1]), wide.dtype)
    for group in range(KV_HEADS):
        start = 128 * (HEADS + group)
        wide[start : start + 64, :] = qkv[576 + 64 * group : 640 + 64 * group, :]
        wide[start + 64 : start + 128, :] = qkv[768 + 64 * group : 832 + 64 * group, :]


def project(current, gain, wide, cosine, sine, query_ref, local_ref):
    unit, _ = normalize(current)
    projected = product_turned((unit * gain).astype(jnp.bfloat16), wide[...])
    for head in range(HEADS):
        tile = turned(projected[:, 128 * head : 128 * head + 128], cosine, sine) * HEAD_DIM ** (-0.5)
        put_head(query_ref, head, tile.astype(jnp.bfloat16))
    for group in range(KV_HEADS):
        start = 128 * (HEADS + group)
        tile = turned(projected[:, start : start + 128], cosine, sine).astype(jnp.bfloat16)
        local_ref[group, 0] = tile[:CHUNK]
        local_ref[group, 1] = tile[CHUNK:]


def project_back(grad_query_ref, grad_local_ref, current, grad_hidden, gain, wide, cosine, sine, terms_ref):
    lower = is_lower((2 * CHUNK, 128))
    tiles = []
    for head in range(HEADS):
        tile = jnp.where(lower, head_rows(grad_query_ref, head), 0.0)
        tiles.append(turned(tile, cosine, -sine) * HEAD_DIM ** (-0.5))
    for group in range(KV_HEADS):
        tiles.append(turned(grad_local_ref[group], cosine, -sine))
    grad_normed = product(
        jnp.concatenate([tile.astype(jnp.bfloat16) for tile in tiles], axis=1), wide[...]
    )
    unit, factor = normalize(current)
    key = tiles[HEADS:]
    pairs = [(tiles[2 * index], swapped(tiles[2 * index + 1])) for index in range(4)]
    pairs += [
        (tiles[8], swapped(key[0])),
        (key[1], swapped(key[2])),
        (swapped(key[0]), key[1]),
        (swapped(key[2]), jnp.zeros_like(key[2])),
    ]
    width = current.shape[1]
    terms_ref[:, :width] = (unit * gain).astype(jnp.bfloat16)
    for index, (low, high) in enumerate(pairs):
        terms_ref[:, 640 + 128 * index : 768 + 128 * index] = jnp.where(lower, low, high).astype(jnp.bfloat16)
    return grad_hidden + norm_back(grad_normed * gain, unit, factor)


def heads_mixed(mixed_ref):
    lower = is_lower((2 * CHUNK, 128))
    tiles = [head_rows(mixed_ref, head) for head in range(HEADS)]
    pairs = [jnp.where(lower, swapped(tiles[2 * i]), tiles[2 * i + 1]) for i in range(4)]
    pairs.append(swapped(tiles[8])[:, :HEAD_DIM])
    return jnp.concatenate([tile.astype(jnp.bfloat16) for tile in pairs], axis=1)


def feed_forward(current, mixed, out, gain, gate_up, down, waits):
    waits[0]()
    hidden = current + product_turned(mixed, out[...])
    unit, _ = normalize(hidden)
    normed = (unit * gain).astype(jnp.bfloat16)
    waits[1]()
    pair = [product(normed, gate_up[index]) for index in range(4)]
    act = [(pair[k] * jax.nn.sigmoid(pair[k]) * pair[k + 2]).astype(jnp.bfloat16) for k in range(2)]
    part = FF // 2
    waits[2]()
    result = hidden + (product_turned(act[0], down[:, :part]) + product_turned(act[1], down[:, part:]))
    return hidden, pair, result


def feed_back(grad_out, hidden, pair, mixed, mixed_ref, out, gain, gate_up, down, waits, terms_ref, grad_ref, inner_ref):
    part = FF // 2
    width = hidden.shape[1]
    branch = grad_out.astype(jnp.bfloat16)
    waits[2]()
    grad_act = product(branch, down[...])
    waits[1]()
    grad_normed = None
    for k in range(2):
        gate, upward = pair(k), pair(k + 2)
        squashed = jax.nn.sigmoid(gate)
        grad = grad_act[:, k * part : (k + 1) * part]
        grad_gate = (grad * upward * squashed * (1.0 + gate * (1.0 - squashed))).astype(jnp.bfloat16)
        grad_upward = (grad * (gate * squashed)).astype(jnp.bfloat16)
        terms_ref[:, 2560 + k * part : 2560 + (k + 1) * part] = grad_gate
        terms_ref[:, 2560 + (k + 2) * part : 2560 + (k + 3) * part] = grad_upward
        terms_ref[:, 5632 + k * part : 5632 + (k + 1) * part] = (gate * squashed * upward).astype(jnp.bfloat16)
        term = product_turned(grad_gate, gate_up[k]) + product_turned(grad_upward, gate_up[k + 2])
        grad_normed = term if grad_normed is None else grad_normed + term
    unit, factor = normalize(hidden)
    terms_ref[:, :width] = mixed
    terms_ref[:, 640 : 640 + width] = (unit * gain).astype(jnp.bfloat16)
    terms_ref[:, 1280 : 1280 + width] = branch
    grad_hidden = grad_out + norm_back(grad_normed * gain, unit, factor)
    grad_attn = grad_hidden.astype(jnp.bfloat16)
    terms_ref[:, 1920:2560] = jnp.concatenate(
        [jnp.zeros((2 * CHUNK, HEAD_DIM), jnp.float32), grad_hidden], axis=1
    ).astype(jnp.bfloat16)
    waits[0]()
    grad_mixed = product(grad_attn, out[...])
    lower = is_lower((2 * CHUNK, 128))
    for head in range(HEADS):
        start = 128 * (head // 2)
        if head == HEADS - 1:
            tile = jnp.concatenate([jnp.zeros((2 * CHUNK, HEAD_DIM), jnp.float32), grad_mixed[:, start:]], axis=1)
        else:
            tile = grad_mixed[:, start : start + 128]
            tile = jnp.where(lower, 0.0, tile if head % 2 else swapped(tile))
        tile = tile.astype(jnp.bfloat16)
        put_head(grad_ref, head, tile)
        inner = jnp.sum(tile.astype(jnp.float32) * head_rows(mixed_ref, head), axis=-1, keepdims=True)
        put_head(inner_ref, head, inner)
    return grad_hidden


def brought(pairs, sems):
    waits = []
    for index, (source, target) in enumerate(pairs):
        copy = pltpu.make_async_copy(source, target, sems.at[index])
        copy.start()
        waits.append(copy.wait)
    return waits


def once(waits):
    def first_only(wait):
        pending = [wait]

        def run():
            if pending:
                pending.pop()()

        return run

    return [first_only(wait) for wait in waits]


def enter_kernel(current_ref, gain_ref, cosine_ref, sine_ref, qkv_ref, query_ref, local_ref, wide):
    widen(wide, qkv_ref)
    project(
        current_ref[...].astype(jnp.float32).T, gain_ref[...], wide, cosine_ref[...], sine_ref[...], query_ref, local_ref
    )


def between_kernel(
    mixed_ref, current_ref, gain_ref, next_gain_ref, cosine_ref, sine_ref, out_ref, gate_up_ref, down_ref, qkv_ref,
    hidden_ref, pair_ref, next_ref, query_ref, local_ref,
    out, gate_up, down, qkv, wide, sems,
):
    *waits, wait_qkv = brought(
        [(out_ref, out), (gate_up_ref, gate_up), (down_ref, down), (qkv_ref, qkv)], sems
    )
    mixed = heads_mixed(mixed_ref)
    hidden, pair, result = feed_forward(
        current_ref[...].astype(jnp.float32).T, mixed, out, gain_ref[...], gate_up, down, waits
    )
    hidden_ref[...] = hidden
    for index in range(4):
        pair_ref[index] = pair[index]
    next_ref[...] = result
    wait_qkv()
    widen(wide, qkv)
    project(result, next_gain_ref[...], wide, cosine_ref[...], sine_ref[...], query_ref, local_ref)


def top_kernel(
    mixed_ref, current_ref, cotangent_ref, gain_ref, out_ref, gate_up_ref, down_ref,
    result_ref, grad_hidden_ref, terms_ref, grad_ref, inner_ref,
    out, gate_up, down, sems,
):
    waits = once(brought([(out_ref, out), (gate_up_ref, gate_up), (down_ref, down)], sems))
    mixed = heads_mixed(mixed_ref)
    gain = gain_ref[...]
    hidden, pair, result = feed_forward(current_ref[...], mixed, out, gain, gate_up, down, waits)
    result_ref[...] = result
    grad_hidden_ref[...] = feed_back(
        cotangent_ref[...].astype(jnp.float32).T, hidden, lambda index: pair[index], mixed, mixed_ref,
        out, gain, gate_up, down, waits, terms_ref, grad_ref, inner_ref,
    )


def descend_kernel(
    grad_query_ref, grad_local_ref, upper_ref, upper_grad_ref, upper_gain_ref, cosine_ref, sine_ref,
    mixed_ref, hidden_in_ref, pair_ref, gain_ref, qkv_ref, out_ref, gate_up_ref, down_ref,
    upper_terms_ref, grad_hidden_ref, terms_ref, grad_ref, inner_ref,
    out, gate_up, down, qkv, wide, sems,
):
    wait_qkv, *waits = brought(
        [(qkv_ref, qkv), (out_ref, out), (gate_up_ref, gate_up), (down_ref, down)], sems
    )
    wait_qkv()
    widen(wide, qkv)
    grad = project_back(
        grad_query_ref, grad_local_ref, upper_ref[...], upper_grad_ref[...], upper_gain_ref[...], wide,
        cosine_ref[...], sine_ref[...], upper_terms_ref,
    )
    grad_hidden_ref[...] = feed_back(
        grad, hidden_in_ref[...], lambda index: pair_ref[index], heads_mixed(mixed_ref), mixed_ref,
        out, gain_ref[...], gate_up, down, waits, terms_ref, grad_ref, inner_ref,
    )


def leave_kernel(
    grad_query_ref, grad_local_ref, current_ref, grad_hidden_ref, gain_ref, cosine_ref, sine_ref, qkv_ref,
    grad_in_ref, terms_ref, wide,
):
    widen(wide, qkv_ref)
    grad_in_ref[...] = project_back(
        grad_query_ref, grad_local_ref, current_ref[...].astype(jnp.float32).T, grad_hidden_ref[...], gain_ref[...], wide,
        cosine_ref[...], sine_ref[...], terms_ref,
    )


def weight_kernel(order_ref, *refs):
    given, (out_ref, gathered, low, high, sems) = refs[:8], refs[8:]
    width = order_ref.shape[0]
    tiles = 6144 // 128
    blocks = 64
    rows = low.shape[0] // 2
    targets = (low.at[pl.ds(0, rows)], low.at[pl.ds(rows, rows)], high.at[pl.ds(0, rows)], high.at[pl.ds(rows, rows)])
    copies = [
        [pltpu.make_async_copy(given[4 * layer + index], targets[index], sems.at[index]) for index in range(4)]
        for layer in range(2)
    ]
    for layer in range(2):

        @pl.when(lax.axis_index("section") == layer)
        def _(layer=layer):
            for copy in copies[layer]:
                copy.start()

    for copy in copies[0]:
        copy.wait()

    def both(ref, start, size):
        return ref[:, start : start + size]

    def left(ref, start):
        columns = both(ref, start, width)
        return product_turned(order_ref[...], columns).astype(jnp.bfloat16)

    def put(term, tile):
        for index in range(width // blocks):
            part, row = index // 3, (index % 3) * tiles + tile
            gathered[part, pl.ds(row, blocks, stride=3 * tiles), :] = term[index * blocks : (index + 1) * blocks]

    normed_one = left(low, 0)
    mixed = left(high, 0)
    first = product(normed_one, both(low, 640, 1024))
    second = product(mixed, both(high, 1920, 640))
    for tile in range(7):
        put(first[:, 128 * tile : 128 * tile + 128], tile)
    put(first[:, 896:] + second[:, :128], 7)
    for tile in range(1, 5):
        put(second[:, 128 * tile : 128 * tile + 128], 7 + tile)
    normed_two = left(high, 640)
    for step in range(6):
        third = product(normed_two, both(high, 2560 + 512 * step, 512))
        for tile in range(4):
            put(third[:, 128 * tile : 128 * tile + 128], 12 + 4 * step + tile)
    branch = left(high, 1280)
    for step in range(3):
        fourth = product(branch, both(high, 5632 + 512 * step, 512))
        for tile in range(4):
            put(fourth[:, 128 * tile : 128 * tile + 128], 36 + 4 * step + tile)

    for part in range(3):

        @pl.loop(0, blocks)
        def _(block, part=part):
            start = pl.multiple_of(block * (3 * tiles), 3 * tiles)
            out_ref[part, block] = gathered[part, pl.ds(start, 3 * tiles), :].astype(jnp.bfloat16)


TERMS_LOW = 1664
TERMS_HIGH = 7168


def dense(kernel, arguments, hbm, results, scratch, flops):
    vmem = pl.BlockSpec(memory_space=pltpu.VMEM)
    kept = [vmem] * (len(arguments) - hbm) + [pl.BlockSpec(memory_space=pl.ANY)] * hbm
    size = sum(item.size * item.dtype.itemsize for item in arguments)
    return pl.pallas_call(
        kernel,
        out_shape=tuple(jax.ShapeDtypeStruct(shape, kind) for shape, kind in results),
        in_specs=kept,
        out_specs=tuple(vmem for _ in results),
        scratch_shapes=scratch,
        compiler_params=pltpu.CompilerParams(vmem_limit_bytes=VMEM_LIMIT),
        cost_estimate=pl.CostEstimate(flops=flops, bytes_accessed=size, transcendentals=0),
    )(*arguments)


def on_device(inputs, positions, attn_gain, w_qkv, w_out, ffn_gain, w_gate_up, w_down, cotangent):
    _, rows, width = inputs.shape
    section = lax.axis_index("section")
    place = lax.axis_index(("ctx", "fsdp"))
    half_kind, kind = jnp.bfloat16, jnp.float32
    lanes = 2 * HEAD_DIM
    columns = w_qkv.shape[2] * SIDE
    wide_rows = 128 * (HEADS + KV_HEADS)

    depth = lax.axis_index("fsdp")
    batch = depth // 2
    worked = place + section * (SIDE - 1 - 2 * depth)
    spots_k = lax.dynamic_index_in_dim(positions, batch, 0, keepdims=False)
    spots_q = lax.dynamic_slice_in_dim(spots_k, worked * rows, rows, 0)
    chunk_of = spots_k[::CHUNK] // CHUNK
    inverse = jnp.zeros_like(chunk_of).at[chunk_of].set(jnp.arange(chunk_of.shape[0], dtype=jnp.int32))
    spots = lax.dynamic_slice_in_dim(chunk_of, worked * 2, 2, 0)
    frequency = rope_base ** (-(jnp.arange(HEAD_DIM // 2, dtype=kind) * 2.0 / HEAD_DIM))
    angle = spots_q.astype(kind)[:, None] * frequency[None, :]
    cosine, sine = jnp.cos(angle), jnp.sin(angle)
    rest = jnp.ones((rows, HEAD_DIM), kind)
    cosine = jnp.concatenate([cosine, cosine, rest], axis=1)
    sine = jnp.concatenate([-sine, sine, 0.0 * rest], axis=1)

    local_gains = jnp.pad(jnp.concatenate([attn_gain, ffn_gain], axis=0), ((0, 6), (0, 0)))
    qkv_turned = w_qkv[0].T
    qkv_first, gains, current, given = first_weight(
        qkv_turned, local_gains, inputs.transpose(0, 2, 1), cotangent.transpose(0, 2, 1)
    )
    qkv_first = qkv_first.reshape(columns, width)

    shards = [w_out[0].T, w_gate_up[0], w_down[0].T, qkv_turned]
    gain_one = [gains[l, 0:1] for l in range(2)]
    gain_two = [gains[l, 1:2] for l in range(2)]

    query_like = ((KV_HEADS, 2, GROUP * CHUNK, lanes), half_kind)
    inner_like = ((KV_HEADS, 2, GROUP * CHUNK, 1), kind)
    local_like = ((KV_HEADS, 2, CHUNK, lanes), half_kind)
    state_like = ((rows, width), kind)
    pair_like = ((SIDE, rows, 2 * FF // SIDE), kind)
    low_like = ((rows, TERMS_LOW), half_kind)
    high_like = ((rows, TERMS_HIGH), half_kind)
    wide_scratch = pltpu.VMEM((wide_rows, width), half_kind)
    qkv_scratch = pltpu.VMEM((columns, width), half_kind)
    ffn_scratch = [
        pltpu.VMEM((width, width), half_kind),
        pltpu.VMEM((SIDE, width, 2 * FF // SIDE), half_kind),
        pltpu.VMEM((width, FF), half_kind),
    ]
    sems = pltpu.SemaphoreType.DMA((4,))
    qkv_flops = 2 * rows * width * wide_rows
    ffn_flops = 2 * rows * width * (width + 3 * FF)

    def attention(layer, query, local, shards):
        mixed, logsum, both, out, gate_up, down, *rest = attend_all(
            layer, inverse, spots, local, query, shards, layer
        )
        weights = [out.reshape(width, width), gate_up, down.reshape(width, FF)]
        return both, mixed, logsum, weights, [item.reshape(columns, width) for item in rest]

    def attention_back(query, grad, logsum, inner, both):
        grad_query, grad_both = attend_back_all(inverse, spots, chunk_of, query, grad, logsum, inner, both, 4)
        return grad_query, grad_both.reshape(KV_HEADS, rows, lanes)

    query_one, local = dense(
        enter_kernel, (current, gain_one[0], cosine, sine, qkv_first), 0, (query_like, local_like), [wide_scratch], qkv_flops
    )
    both_one, mixed_one, logsum_one, weights_one, (qkv_second,) = attention(0, query_one, local, shards)
    hidden, pair, middle, query_two, local = dense(
        between_kernel,
        (mixed_one, current, gain_two[0], gain_one[1], cosine, sine, *weights_one, qkv_second),
        4,
        (state_like, pair_like, state_like, query_like, local_like),
        ffn_scratch + [qkv_scratch, wide_scratch, sems],
        ffn_flops + qkv_flops,
    )
    both_two, mixed_two, logsum_two, weights_two, _ = attention(1, query_two, local, shards[:3])
    result, grad_hidden, high_two, grad, inner = dense(
        top_kernel,
        (mixed_two, middle, given, gain_two[1], *weights_two),
        3,
        (state_like, state_like, high_like, query_like, inner_like),
        ffn_scratch + [sems],
        2 * ffn_flops,
    )
    earlier = lax.ppermute(
        result,
        ("section", "ctx", "fsdp"),
        [(64 + 4 * ctx + z, 64 + 4 * ctx + 3 - z) for ctx in range(16) for z in range(4)],
    )
    grad_query, grad_local = attention_back(query_two, grad, logsum_two, inner, both_two)
    low_two, grad_hidden, high_one, grad, inner = dense(
        descend_kernel,
        (
            grad_query, grad_local, middle, grad_hidden, gain_one[1], cosine, sine,
            mixed_one, hidden, pair, gain_two[0], qkv_second, *weights_one,
        ),
        4,
        (low_like, state_like, high_like, query_like, inner_like),
        ffn_scratch + [qkv_scratch, wide_scratch, sems],
        ffn_flops + qkv_flops,
    )
    grad_query, grad_local = attention_back(query_one, grad, logsum_one, inner, both_one)
    grad_in, low_one = dense(
        leave_kernel,
        (grad_query, grad_local, current, grad_hidden, gain_one[0], cosine, sine, qkv_first),
        0,
        (state_like, low_like),
        [wide_scratch],
        qkv_flops,
    )

    first = section == 0
    down_pairs, up_pairs = [(0, 1)], [(1, 0)]
    terms = [
        low_one, lax.ppermute(low_one, "section", up_pairs), high_one, lax.ppermute(high_one, "section", up_pairs),
        low_two, lax.ppermute(low_two, "section", down_pairs), high_two, lax.ppermute(high_two, "section", down_pairs),
    ]
    blocks = SIDE * SIDE * SIDE
    each = width // blocks
    total = columns + width + 3 * FF
    line = jnp.arange(width)
    order = (line[:, None] % blocks * each + line[:, None] // blocks == line[None, :]).astype(half_kind)
    (term,) = dense(
        weight_kernel,
        (order, *terms),
        8,
        (((3, blocks, 3 * total // 128, 128), half_kind),),
        [
            pltpu.VMEM((3, blocks * 3 * total // 128, 128), kind),
            pltpu.VMEM((2 * rows, TERMS_LOW), half_kind),
            pltpu.VMEM((2 * rows, TERMS_HIGH), half_kind),
            sems,
        ],
        4 * rows * width * total,
    )
    term = term.reshape(3, SIDE, SIDE, SIDE, 3 * total // 128, 128)
    summed = scatter_all(term, 80, 2).reshape(each, total)
    grad_qkv = summed[:, :columns]
    grad_out_weight = summed[:, columns : columns + width]
    grad_gate_up = summed[:, columns + width : columns + width + 2 * FF]
    grad_down = summed[:, columns + width + 2 * FF :].T

    qkv_own = jnp.where(
        first,
        lax.dynamic_slice_in_dim(qkv_first, place * each, each, 1),
        lax.dynamic_slice_in_dim(qkv_second, place * each, each, 1),
    )
    qkv_own = qkv_own.astype(kind).T
    gate_up_own = jnp.where(
        first,
        lax.dynamic_slice_in_dim(weights_one[1], place * each, each, 1),
        lax.dynamic_slice_in_dim(weights_two[1], place * each, each, 1),
    ).astype(kind)
    split = grad_gate_up.reshape(each, SIDE, -1).transpose(1, 0, 2)
    grad_gain_one = jnp.sum(qkv_own * grad_qkv, axis=1) / lax.dynamic_slice_in_dim(attn_gain[0], place * each, each, 0)
    grad_gain_two = jnp.sum(gate_up_own * split, axis=(0, 2)) / lax.dynamic_slice_in_dim(
        ffn_gain[0], place * each, each, 0
    )

    def index_of(core, ctx, z):
        return (core * SIDE * SIDE + ctx) * SIDE + z

    places = [(ctx, z) for ctx in range(SIDE * SIDE) for z in range(SIDE)]
    axes = ("section", "ctx", "fsdp")
    later = lax.ppermute(
        jnp.where(first, result, grad_in),
        axes,
        [(index_of(0, ctx, z), index_of(1, ctx, z)) for ctx, z in places]
        + [(index_of(1, ctx, z), index_of(0, ctx, SIDE - 1 - z)) for ctx, z in places],
    )
    mine = jnp.where(first, grad_in, later)
    other = jnp.where(first, later, earlier)
    ends = jnp.where(batch == 0, jnp.stack([mine, other]), jnp.stack([other, mine]))
    return (
        ends[None],
        grad_gain_one[None],
        grad_qkv[None],
        grad_out_weight[None],
        grad_gain_two[None],
        grad_gate_up[None],
        grad_down[None],
    )


def solution(mesh):
    placed = (
        P(None, ("ctx", "fsdp"), None),
        P(),
        P("section", None),
        P("section", None, "fsdp"),
        P("section", None, "fsdp"),
        P("section", None),
        P("section", None, "fsdp"),
        P("section", None, "fsdp"),
        P(None, ("ctx", "fsdp"), None),
    )
    return jax.shard_map(
        on_device,
        mesh=mesh,
        in_specs=placed,
        out_specs=(
            P("section", None, ("ctx", "fsdp"), None),
            P("section", ("ctx", "fsdp")),
            P("section", ("ctx", "fsdp"), None),
            P("section", ("ctx", "fsdp"), None),
            P("section", ("ctx", "fsdp")),
            P("section", ("ctx", "fsdp"), None),
            P("section", None, ("ctx", "fsdp")),
        ),
        check_vma=False,
    )
```

```python
import functools

import jax
import jax.numpy as jnp
from jax import lax
from jax.experimental import pallas as pl
from jax.experimental.pallas import tpu as pltpu
from jax.sharding import PartitionSpec as P

HEADS = 9
KV_HEADS = 3
GROUP = 3
HEAD_DIM = 64
FF = 1536
CHUNK = 64
BLOCK = 512
PER = BLOCK // CHUNK
MESH = pl.DeviceIdType.MESH
VMEM_LIMIT = 56 * 1024 * 1024

epsilon = 1e-05
rope_base = 100000.0
contract_last = (((1,), (1,)), ((), ()))
contract_first = (((0,), (0,)), ((), ()))

ORDERS = ((2, 0, 1), (0, 1, 2), (1, 2, 0))
SIDE = 4


def here():
    ctx = lax.axis_index("ctx")
    return (lax.axis_index("section"), (ctx // SIDE, lax.rem(ctx, SIDE), lax.axis_index("fsdp")))


def shifted(at, axis, step):
    return lax.rem(at[axis] + (step + SIDE), SIDE)


def device_at(section, at, axis, step):
    moved = list(at)
    moved[axis] = shifted(at, axis, step)
    return (section, moved[0] * SIDE + moved[1], moved[2])


def enter(section, at):
    barrier = pltpu.get_barrier_semaphore()
    for axis in range(3):
        for step in (1, -1):
            pl.semaphore_signal(
                barrier, inc=1, device_id=device_at(section, at, axis, step), device_id_type=MESH
            )
    pl.semaphore_wait(barrier, 6)


def slab(ref, part, axes, fixed, rows):
    return ref.at[(part,) + tuple(fixed.get(axis, slice(None)) for axis in axes) + (rows,)]


def pair_step(at):
    return 1 - 2 * lax.rem(at[2], 2)


SIDES = (SIDE, SIDE, 2)
STEPS = ((0, 1), (1, -1))


class Team:
    def __init__(self):
        self.section, self.at = here()
        w = lax.rem(self.at[2], 2)
        h = self.at[2] // 2
        self.h = lax.rem(h + self.section, 2)
        self.spot = (self.at[0], self.at[1], lax.rem(w + self.section, 2))

    def beside(self):
        return (1 - self.section, self.at[0] * SIDE + self.at[1], self.at[2])

    def shifted(self, axis, step):
        return lax.rem(self.spot[axis] + (step + SIDE), SIDES[axis])

    def moved(self, steps):
        y, x = (lax.rem(self.at[axis] + (steps[axis] + SIDE), SIDE) for axis in range(2))
        z = self.at[2] + (pair_step(self.at) if steps[2] % 2 else 0)
        return (self.section, y * SIDE + x, z)

    def device(self, axis, step):
        return self.moved(tuple(step if other == axis else 0 for other in range(3)))

    def enter(self):
        barrier = pltpu.get_barrier_semaphore()
        devices = [self.moved(steps) for steps in STRAIGHT]
        devices += [self.beside(), device_at(self.section, self.at, 2, -pair_step(self.at))]
        for device in devices:
            pl.semaphore_signal(barrier, inc=1, device_id=device, device_id_type=MESH)
        pl.semaphore_wait(barrier, len(devices))


def scatter_kernel(split, terms_ref, out_ref, sum_one, sum_two, near_one, far_one, near_two, far_two, near_three, far_three, send, recv):
    rows = terms_ref.shape[-2]
    halves = (pl.ds(0, split), pl.ds(split, rows - split))
    section, at = here()
    enter(section, at)
    sums = (terms_ref, sum_one, sum_two, out_ref)
    landing = ((near_one, far_one), (near_two, far_two), (near_three, far_three))

    def remaining(part, phase):
        return tuple(sorted(ORDERS[part][: 3 - phase]))

    def axis_of(part, phase):
        return ORDERS[part][2 - phase]

    def landed(phase, part, way, number):
        half = (number + way) % 2
        slot = {(0, 0): 0, (0, 2): 1, (1, 1): 2, (0, 1): 0, (1, 0): 1, (1, 2): 2}[way, number]
        return landing[phase][half].at[slot, part]

    def message(phase, part, way, number, step, source):
        axis = axis_of(part, phase)
        return pltpu.make_async_remote_copy(
            src_ref=source,
            dst_ref=landed(phase, part, way, number),
            send_sem=send.at[phase, part, way, number],
            recv_sem=recv.at[phase, part, way, number],
            device_id=device_at(section, at, axis, step),
            device_id_type=MESH,
        )

    def own(phase, part, coordinate, half):
        return slab(sums[phase], part, remaining(part, phase), {axis_of(part, phase): coordinate}, halves[half])

    def add(phase, target, terms):
        outer = target.shape[:-2]
        count = 1
        for size in outer:
            count *= size

        def one(index):
            total = terms[0][index].astype(jnp.float32)
            for term in terms[1:]:
                total = total + term[index].astype(jnp.float32)
            target[index] = total.astype(target.dtype)

        if count == 1:
            one((slice(None),) * 2)
            return

        @pl.loop(0, count)
        def _(step):
            if len(outer) == 1:
                one((step,))
            else:
                one((step // SIDE, lax.rem(step, SIDE)))

    for phase in range(3):
        flying = {}
        for number in range(2):
            for part in range(3):
                axis = axis_of(part, phase)
                for way, step in enumerate((1, -1)):
                    coordinate = shifted(at, axis, 2 * step if number == 0 else step)
                    copy = message(phase, part, way, number, step, own(phase, part, coordinate, (number + way) % 2))
                    copy.start()
                    flying[part, way, number] = copy
        for part in range(3):
            axis = axis_of(part, phase)
            for way, step in enumerate((1, -1)):
                flying[part, way, 0].wait_recv()
                passing = landed(phase, part, way, 0)
                add(phase, passing, (passing, own(phase, part, shifted(at, axis, step), way)))
                copy = message(phase, part, way, 2, step, passing)
                copy.start()
                flying[part, way, 2] = copy
        for part in range(3):
            axis = axis_of(part, phase)
            for way in range(2):
                flying[part, way, 1].wait_recv()
                flying[part, way, 2].wait_recv()
            for half in range(2):
                target = sums[phase + 1].at[(part,) + (slice(None),) * (2 - phase) + (halves[half],)]
                add(
                    phase,
                    target,
                    (
                        own(phase, part, at[axis], half),
                        landed(phase, part, half, 2),
                        landed(phase, part, 1 - half, 1),
                    ),
                )
        for part in range(3):
            for way in range(2):
                for number in range(3):
                    flying[part, way, number].wait_send()


def scatter_all(terms, split, collective_id):
    parts, rows, lanes = terms.shape[0], terms.shape[-2], terms.shape[-1]
    kind = terms.dtype
    near, far = split, rows - split
    return pl.pallas_call(
        functools.partial(scatter_kernel, split),
        out_shape=jax.ShapeDtypeStruct((parts, rows, lanes), jnp.float32),
        in_specs=[pl.BlockSpec(memory_space=pltpu.VMEM)],
        out_specs=pl.BlockSpec(memory_space=pltpu.VMEM),
        scratch_shapes=[
            pltpu.VMEM((parts, SIDE, SIDE, rows, lanes), kind),
            pltpu.VMEM((parts, SIDE, rows, lanes), kind),
            pltpu.VMEM((3, parts, SIDE, SIDE, near, lanes), kind),
            pltpu.VMEM((3, parts, SIDE, SIDE, far, lanes), kind),
            pltpu.VMEM((3, parts, SIDE, near, lanes), kind),
            pltpu.VMEM((3, parts, SIDE, far, lanes), kind),
            pltpu.VMEM((3, parts, near, lanes), kind),
            pltpu.VMEM((3, parts, far, lanes), kind),
            pltpu.SemaphoreType.DMA((3, 3, 2, 3)),
            pltpu.SemaphoreType.DMA((3, 3, 2, 3)),
        ],
        compiler_params=pltpu.CompilerParams(
            collective_id=collective_id, has_side_effects=True, vmem_limit_bytes=VMEM_LIMIT
        ),
        cost_estimate=pl.CostEstimate(flops=terms.size, bytes_accessed=2 * terms.size, transcendentals=0),
    )(terms)


def visible(shape, chunk, block):
    row = lax.broadcasted_iota(jnp.int32, shape, 0)
    column = lax.broadcasted_iota(jnp.int32, shape, 1)
    return block * BLOCK + column <= chunk * CHUNK + lax.rem(row, CHUNK)


STEPS_UNMASKED = 15


STRAIGHT = ((1, 0, 0), (2, 0, 0), (3, 0, 0), (0, 1, 0), (0, 2, 0), (0, 3, 0), (0, 0, 1))


class Exchange:
    def __init__(self, team, sems):
        self.team, self.sems = team, sems

    def send(self, source, target, device, kind, *index):
        send, recv = self.sems[kind]
        copy = pltpu.make_async_remote_copy(
            src_ref=source,
            dst_ref=target,
            send_sem=send.at[index],
            recv_sem=recv.at[index],
            device_id=device,
            device_id_type=MESH,
        )
        copy.start()
        return copy


class PartGather:
    def __init__(self, part, exchange, local_ref, keys):
        self.part, self.exchange, self.team = part, exchange, exchange.team
        self.local_ref, self.keys = local_ref, keys
        self.near, self.ring, self.side = [], {}, []

    def slab(self, unit, coordinate, w=slice(None)):
        y, x = (coordinate, slice(None)) if unit == 0 else (slice(None), coordinate)
        return self.keys.at[y, x, self.team.h, w, unit]

    def start_near(self):
        spot = self.team.spot
        for unit in range(2):
            for step in range(1, SIDE):
                steps = (0, step, 0) if unit == 0 else (step, 0, 0)
                place = self.keys.at[spot[0], spot[1], self.team.h, :, unit]
                self.near.append(
                    self.exchange.send(place, place, self.team.moved(steps), "near", self.part, unit, step - 1)
                )

    def message(self, unit, way, number, coordinate, w):
        place = self.slab(unit, coordinate, w)
        self.ring[unit, way, number] = self.exchange.send(
            place, place, self.team.device(unit, STEPS[way][1]), "ring", self.part, unit, way, number
        )

    def aside(self, unit, slot, coordinate):
        place = self.slab(unit, coordinate)
        self.side.append(
            self.exchange.send(place, place, self.team.beside(), "side", self.part, unit, slot)
        )

    def start_ring(self):
        for copy in self.near:
            copy.wait_recv()
        for number in range(2):
            for unit in range(2):
                for way, _ in STEPS:
                    self.message(unit, way, number, self.team.spot[unit], (number + way) % 2)
        for unit in range(2):
            self.aside(unit, 0, self.team.spot[unit])

    def pass_on(self):
        for unit in range(2):
            for way, step in STEPS:
                self.ring[unit, way, 0].wait_recv()
                self.message(unit, way, 2, self.team.shifted(unit, -step), way)

    def share(self):
        for unit in range(2):
            for way, step in STEPS:
                self.ring[unit, way, 1].wait_recv()
                self.aside(unit, 1 + way, self.team.shifted(unit, -step))
        for unit in range(2):
            for way, _ in STEPS:
                self.ring[unit, way, 2].wait_recv()
            self.aside(unit, 3, self.team.shifted(unit, 2))

    def finish(self):
        for copy in self.side:
            copy.wait_recv()

    def drain(self):
        for copy in self.near + list(self.ring.values()) + self.side:
            copy.wait_send()


class WeightGather:
    def __init__(self, owner, number, exchange, local_ref, out_ref):
        self.owner, self.number, self.exchange, self.team = owner, number, exchange, exchange.team
        self.local_ref, self.out_ref = local_ref, out_ref
        self.place = self.team.at[2]
        rows = local_ref.shape[0]
        middle = rows // 32 * 16
        if number % 2 == 0:
            middle = rows - middle
        self.rows = ((0, middle), (middle, rows))

    def each(self, body, roles=(0, 1)):
        for role in roles:

            @pl.when(self.team.section == (self.owner if role == 0 else 1 - self.owner))
            def _(role=role):
                body(role)

    def index(self, step):
        return lax.rem(self.place + (step + SIDE), SIDE)

    def message(self, role, way, number, start=True):
        low, high = self.rows[role]
        split = low + (high - low + 16) // 32 * 16
        low, high = (low, split) if (number + way) % 2 == 0 else (split, high)
        rows = pl.ds(low, high - low)
        spot = self.out_ref.at[self.place if number < 2 else self.index(-STEPS[way][1]), rows]
        source = self.local_ref.at[rows] if number < 2 and role == 0 else spot
        device = device_at(self.team.section, self.team.at, 2, STEPS[way][1])
        return self.copy(source, spot, device, "weight_ring", start, way, number)

    def aside(self, role, slot, start=True):
        if slot == 0:
            return self.copy(self.local_ref, self.out_ref.at[self.place], self.team.beside(), "weight_side", start, 0)
        low, high = self.rows[role]
        spot = self.out_ref.at[self.index((-1, 1, 2)[slot - 1]), pl.ds(low, high - low)]
        return self.copy(spot, spot, self.team.beside(), "weight_side", start, slot)

    def copy(self, source, target, device, kind, start, *index):
        send, recv = self.exchange.sems[kind]
        place = (self.number,) + index
        copy = pltpu.make_async_remote_copy(
            src_ref=source,
            dst_ref=target,
            send_sem=send.at[place],
            recv_sem=recv.at[place],
            device_id=device,
            device_id_type=MESH,
        )
        if start:
            copy.start()
        return copy

    def own(self):
        return pltpu.make_async_copy(
            self.local_ref, self.out_ref.at[self.place], self.exchange.sems["weight_own"].at[self.number]
        )

    def start_ring(self, role):
        for number in range(2):
            for way in range(2):
                self.message(role, way, number)

    def start(self):
        def body(role):
            self.own().start()
            self.aside(0, 0)
            self.start_ring(0)

        self.each(body, (0,))

    def start_beside(self):
        def body(role):
            self.aside(0, 0, False).wait_recv()
            self.start_ring(1)

        self.each(body, (1,))

    def pass_on(self):
        def body(role):
            for way in range(2):
                self.message(role, way, 0, False).wait_recv()
                self.message(role, way, 2)

        self.each(body)

    def hand(self):
        def body(role):
            for way in range(2):
                self.message(role, way, 1, False).wait_recv()
                self.aside(role, 1 + way)

        self.each(body)

    def share(self):
        def body(role):
            for way in range(2):
                self.message(role, way, 2, False).wait_recv()
            self.aside(role, 3)

        self.each(body)

    def finish(self):
        def body(role):
            for way in range(2):
                for number in range(3):
                    self.message(role, way, number, False).wait_send()
            for slot in range(1, 4):
                self.aside(role, slot, False).wait_send()
                self.aside(1 - role, slot, False).wait_recv()
            if role == 0:
                self.own().wait()
                self.aside(0, 0, False).wait_send()

        self.each(body)


EXP = jnp.exp


def key_block(inverse_ref, keys, block):
    pieces = []
    for index in range(PER):
        place = inverse_ref[block * PER + index]
        y = lax.shift_right_logical(place, 5)
        x, h, w, half = (
            lax.bitwise_and(lax.shift_right_logical(place, shift), mask) for shift, mask in ((3, 3), (2, 1), (1, 1), (0, 1))
        )
        pieces.append(keys[y, x, h, w, half])
    return jnp.concatenate(pieces, axis=0)


def schedule(spots_ref):
    return lax.shift_right_logical(spots_ref[0], 3), lax.shift_right_logical(spots_ref[1], 3)


def attend_all_kernel(
    owner, inverse_ref, spots_ref, local_ref, query_ref, *refs
):
    count = 4 if owner == 0 else 3
    shard_refs, refs = refs[:count], refs[count:]
    (mixed_ref, logsum_ref, both_ref), refs = refs[:3], refs[3:]
    whole_refs, refs = refs[:count], refs[count:]
    keys, (highest_at, mixed_at), refs = refs[:3], refs[3:5], refs[5:]
    sems = {
        "near": refs[0:2], "ring": refs[2:4], "side": refs[4:6],
        "weight_ring": refs[6:8], "weight_side": refs[8:10], "pair": refs[10:12], "weight_own": refs[12],
    }
    kept = refs[13]
    team = Team()
    team.enter()
    exchange = Exchange(team, sems)
    spot, h = team.spot, team.h
    parts = [PartGather(part, exchange, local_ref, keys[part]) for part in range(KV_HEADS)]
    weights = [
        WeightGather(owner if number < 3 else 1 - owner, number, exchange, shard_refs[number], whole_refs[number])
        for number in range(count)
    ]
    own = [
        pltpu.make_async_copy(local_ref.at[part], keys[part].at[spot[0], spot[1], h, spot[2]], kept.at[part])
        for part in range(KV_HEADS)
    ]
    saved = [
        pltpu.make_async_copy(keys[part], both_ref.at[part], kept.at[KV_HEADS + part]) for part in range(KV_HEADS)
    ]
    ends = schedule(spots_ref)

    def attend_scores(part, half, block):
        both = key_block(inverse_ref, keys[part], block)
        return lax.dot_general(
            query_ref[part, half], both, contract_last, preferred_element_type=jnp.float32
        )

    def attend_rest(part, scores, block, highest, mixed):
        both = key_block(inverse_ref, keys[part], block)
        higher = jnp.maximum(highest, jnp.broadcast_to(jnp.max(scores, axis=-1, keepdims=True), highest.shape))
        exponent = EXP(scores - jnp.concatenate([higher] * (BLOCK // 128), axis=1)).astype(jnp.bfloat16)
        values = jnp.where(is_lower(both.shape), jnp.bfloat16(1.0), both)
        return higher, jnp.dot(exponent, values, preferred_element_type=jnp.float32) + EXP(highest - higher) * mixed

    def attend_first(part):
        for half in range(2):
            scores = attend_scores(part, half, ends[half])
            scores = jnp.where(visible(scores.shape, spots_ref[half], ends[half]), scores, -1e30)
            highest, mixed = attend_rest(
                part, scores, ends[half], jnp.full((scores.shape[0], 128), -1e30, jnp.float32), jnp.zeros((scores.shape[0], 128), jnp.float32)
            )
            highest_at[half] = highest
            mixed_at[half] = mixed

    def attend_some(part, low, high):
        if True:
            size = high - low
            steps = [low + index for index in range(size)]
            halves = [jnp.where(step >= ends[0], 1, 0) for step in steps]
            blocks = [step - half * ends[0] for step, half in zip(steps, halves)]
            befores = [jnp.where(step == ends[0], 1, jnp.where(step == 0, 0, step + 1)) for step in steps]
            scores = attend_scores(part, halves[0], blocks[0])
            for index in range(size):
                later = attend_scores(part, halves[index + 1], blocks[index + 1]) if index + 1 < size else None
                before = befores[index]
                highest, mixed = attend_rest(part, scores, blocks[index], highest_at[before], mixed_at[before])
                highest_at[steps[index] + 2] = highest
                mixed_at[steps[index] + 2] = mixed
                scores = later

    def attend_last(part):
        last = (
            jnp.where(ends[0] == 0, 0, ends[0] + 1),
            jnp.where(ends[0] == STEPS_UNMASKED, 1, STEPS_UNMASKED + 1),
        )
        for half in range(2):
            mixed = mixed_at[last[half]]
            total = mixed[:, :1]
            mixed_ref[part, half] = mixed / total
            logsum_ref[part, half] = highest_at[last[half]][:, :1] + jnp.log(total)

    pairs = [
        exchange.send(
            local_ref.at[part], keys[part].at[spot[0], spot[1], h, spot[2]], team.device(2, 1), "pair", part
        )
        for part in range(KV_HEADS)
    ]
    for copy in own:
        copy.start()
    for weight in weights:
        weight.start()
    for part in range(KV_HEADS):
        own[part].wait()
        pairs[part].wait_recv()
        parts[part].start_near()
    for part in parts:
        part.start_ring()
    for weight in weights:
        weight.start_beside()
    parts[0].pass_on()
    parts[1].pass_on()
    parts[0].share()
    parts[2].pass_on()
    parts[0].finish()
    saved[0].start()
    attend_first(0)
    attend_some(0, 0, 7)
    parts[1].share()
    for weight in weights:
        weight.pass_on()
    attend_some(0, 7, 15)
    attend_last(0)
    parts[1].finish()
    saved[1].start()
    attend_first(1)
    attend_some(1, 0, 7)
    parts[2].share()
    for weight in weights:
        weight.hand()
    attend_some(1, 7, 15)
    attend_last(1)
    parts[2].finish()
    saved[2].start()
    attend_first(2)
    for weight in weights:
        weight.share()
    attend_some(2, 0, 15)
    attend_last(2)
    for copy in pairs:
        copy.wait_send()
    for part in parts:
        part.drain()
    for weight in weights:
        weight.finish()
    for copy in saved:
        copy.wait()


def attend_all(owner, inverse, spots, local, query, shards, collective_id):
    groups, halves, rows, lanes = query.shape
    count = len(shards)
    keys = (SIDE, SIDE, 2, 2, 2, CHUNK, lanes)
    vmem, smem, held = (pl.BlockSpec(memory_space=space) for space in (pltpu.VMEM, pltpu.SMEM, pl.ANY))
    slots = STEPS_UNMASKED + 2
    scores = rows * BLOCK * slots * groups
    semaphore = pltpu.SemaphoreType.DMA
    return pl.pallas_call(
        functools.partial(attend_all_kernel, owner),
        out_shape=(
            jax.ShapeDtypeStruct((groups, halves, rows, lanes), jnp.float32),
            jax.ShapeDtypeStruct((groups, halves, rows, 1), jnp.float32),
            jax.ShapeDtypeStruct((groups,) + keys, local.dtype),
        )
        + tuple(jax.ShapeDtypeStruct((SIDE,) + item.shape, item.dtype) for item in shards),
        in_specs=[smem, smem, vmem, vmem] + [vmem] * count,
        out_specs=(vmem, vmem, held) + (held,) * count,
        scratch_shapes=[pltpu.VMEM(keys, local.dtype) for _ in range(groups)]
        + [
            pltpu.VMEM((slots, rows, lanes), jnp.float32),
            pltpu.VMEM((slots, rows, lanes), jnp.float32),
        ]
        + [semaphore(shape) for shape in ((3, 2, 3), (3, 2, 2, 3), (3, 2, 4), (count, 2, 3), (count, 4), (3,)) for _ in range(2)]
        + [semaphore((count,)), semaphore((2 * groups,))],
        compiler_params=pltpu.CompilerParams(
            collective_id=collective_id, has_side_effects=True, vmem_limit_bytes=VMEM_LIMIT
        ),
        cost_estimate=pl.CostEstimate(flops=4 * scores * lanes, bytes_accessed=128 * local.size, transcendentals=scores),
    )(inverse, spots, local, query, *shards)


class PartScatter:
    def __init__(self, part, exchange, terms, joined, landing, sums, near, pair, out_ref):
        self.part, self.exchange, self.team = part, exchange, exchange.team
        self.terms, self.joined, self.landing, self.sums = terms, joined, landing, sums
        self.near, self.pair, self.out_ref = near, pair, out_ref
        self.sides, self.rings, self.nears, self.pairs = [], [], [], []

    def swap(self):
        for unit in range(2):
            source = self.terms.at[:, :, 1 - self.team.h, :, unit]
            self.sides.append(
                self.exchange.send(source, self.joined.at[unit], self.team.beside(), "side", self.part, unit)
            )

    def send_ring(self):
        for unit in range(2):
            self.sides[unit].wait_recv()

            @pl.loop(0, SIDE * SIDE)
            def _(index, unit=unit):
                y, x = lax.div(index, SIDE), lax.rem(index, SIDE)
                own = self.terms[y, x, self.team.h, :, unit].astype(jnp.float32)
                other = self.joined[unit, y, x].astype(jnp.float32)
                self.joined[unit, y, x] = (own + other).astype(jnp.bfloat16)

            for step in (2, 1, 3):
                coordinate = self.team.shifted(unit, step)
                place = self.joined.at[unit, coordinate] if unit == 0 else self.joined.at[unit, :, coordinate]
                steps = (step, 0, 0) if unit == 0 else (0, step, 0)
                self.rings.append(
                    self.exchange.send(
                        place, self.landing.at[unit, step - 1], self.team.moved(steps), "ring", self.part, unit, step - 1
                    )
                )

    def send_near(self):
        for copy in self.rings:
            copy.wait_recv()
        for unit in range(2):
            mine = self.team.spot[unit]
            for index in range(SIDE):
                place = (unit, mine, index) if unit == 0 else (unit, index, mine)
                total = self.joined[place].astype(jnp.float32)
                for step in range(SIDE - 1):
                    total = total + self.landing[unit, step, index].astype(jnp.float32)
                self.sums[unit, index] = total.astype(jnp.bfloat16)
            for step in range(1, SIDE):
                steps = (0, step, 0) if unit == 0 else (step, 0, 0)
                self.nears.append(
                    self.exchange.send(
                        self.sums.at[unit, self.team.shifted(1 - unit, step)], self.near.at[unit, step - 1],
                        self.team.moved(steps), "near", self.part, unit, step - 1,
                    )
                )

    def send_pair(self):
        for copy in self.nears:
            copy.wait_recv()
        w = self.team.spot[2]
        for unit in range(2):
            mine = self.team.spot[1 - unit]
            for index in range(2):
                place = w if index == 0 else 1 - w
                total = self.sums[unit, mine, place].astype(jnp.float32)
                for step in range(SIDE - 1):
                    total = total + self.near[unit, step, place].astype(jnp.float32)
                if index == 0:
                    self.out_ref[self.part, unit] = total
                else:
                    self.pair[0, unit] = total.astype(jnp.bfloat16)
        self.pairs.append(
            self.exchange.send(self.pair.at[0], self.pair.at[1], self.team.device(2, 1), "pair", self.part)
        )

    def finish(self):
        self.pairs[0].wait_recv()
        for unit in range(2):
            self.out_ref[self.part, unit] = self.out_ref[self.part, unit] + self.pair[1, unit].astype(jnp.float32)
        for copy in self.sides + self.rings + self.nears + self.pairs:
            copy.wait_send()


def attend_back_all_kernel(
    inverse_ref, spots_ref, chunk_ref, query_ref, grad_ref, logsum_ref, inner_ref, both_ref,
    grad_query_ref, out_ref, *refs
):
    keys, refs = refs[:3], refs[3:]
    terms, refs = refs[:3], refs[3:]
    buffers, refs = [refs[5 * part : 5 * part + 5] for part in range(3)], refs[15:]
    logsum_at, inner_at, query_at, grad_at, *refs = refs
    sems = {kind: refs[2 * index : 2 * index + 2] for index, kind in enumerate(("side", "ring", "near", "pair"))}
    kept = refs[8]
    team = Team()
    brought_in = [pltpu.make_async_copy(both_ref.at[part], keys[part], kept.at[part]) for part in range(KV_HEADS)]
    for copy in brought_in:
        copy.start()
    team.enter()
    exchange = Exchange(team, sems)
    parts = [
        PartScatter(part, exchange, terms[part], *buffers[part], out_ref) for part in range(KV_HEADS)
    ]
    ends = schedule(spots_ref)
    for part in range(KV_HEADS):
        for half in range(2):
            logsum_at[part, half] = jnp.broadcast_to(logsum_ref[part, half], logsum_at.shape[2:])
            inner_at[part, half] = jnp.broadcast_to(inner_ref[part, half], inner_at.shape[2:])

    grad_at[STEPS_UNMASKED + 2] = jnp.zeros(grad_at.shape[1:], jnp.float32)

    def products(part, half, block):
        both = key_block(inverse_ref, keys[part], block)
        scores = lax.dot_general(query_ref[part, half], both, contract_last, preferred_element_type=jnp.float32)
        grad_weights = lax.dot_general(grad_ref[part, half], both, contract_last, preferred_element_type=jnp.float32)
        return scores, grad_weights

    def rest(part, slot, half, block, found, masked, before):
        scores, grad_weights = found
        both = key_block(inverse_ref, keys[part], block)
        logsum = jnp.concatenate([logsum_at[part, half]] * (BLOCK // 128), axis=1)
        inner = jnp.concatenate([inner_at[part, half]] * (BLOCK // 128), axis=1)
        probs = EXP(scores - logsum)
        if masked:
            probs = jnp.where(visible(scores.shape, spots_ref[half], block), probs, 0.0)
        grad_scores = (probs * (grad_weights - inner)).astype(jnp.bfloat16)
        grad_query = jnp.dot(grad_scores, both, preferred_element_type=jnp.float32)
        query_at[slot] = grad_query if before is None else grad_query + query_at[before]
        grad_at[slot] = lax.dot_general(
            jnp.concatenate([probs.astype(jnp.bfloat16), grad_scores], axis=0),
            jnp.concatenate([grad_ref[part, half], query_ref[part, half]], axis=0),
            contract_first,
            preferred_element_type=jnp.float32,
        ).reshape(PER, CHUNK, 2 * HEAD_DIM)

    def back_first(part):
        for half in range(2):
            rest(part, half, half, ends[half], products(part, half, ends[half]), True, None)

    def back_some(part, low, high):
        steps = list(range(low, high))
        halves = [jnp.where(step >= ends[0], 1, 0) for step in steps]
        blocks = [step - half * ends[0] for step, half in zip(steps, halves)]
        found = products(part, halves[0], blocks[0])
        for index, step in enumerate(steps):
            later = products(part, halves[index + 1], blocks[index + 1]) if index + 1 < len(steps) else None
            before = jnp.where(step == ends[0], 1, jnp.where(step == 0, 0, step + 1))
            rest(part, step + 2, halves[index], blocks[index], found, False, before)
            found = later

    def back_last(part):
        last = (
            jnp.where(ends[0] == 0, 0, ends[0] + 1),
            jnp.where(ends[0] == STEPS_UNMASKED, 1, STEPS_UNMASKED + 1),
        )
        for half in range(2):
            grad_query_ref[part, half] = query_at[last[half]]

        @pl.loop(0, SIDE * SIDE)
        def _(column):
            y, x = lax.div(column, SIDE), lax.rem(column, SIDE)
            for number in range(8):
                chunk = chunk_ref[8 * column + number]
                row = lax.bitwise_and(chunk, PER - 1)
                block = lax.shift_right_logical(chunk, 3)
                total = None
                for half in range(2):
                    slot = jnp.where(block == ends[half], half, 2 + half * ends[0] + block)
                    term = grad_at[jnp.where(block <= ends[half], slot, STEPS_UNMASKED + 2), row]
                    total = term if total is None else total + term
                terms[part][y, x, number // 4, number // 2 % 2, number % 2] = total.astype(jnp.bfloat16)

    def begin(part):
        brought_in[part].wait()
        back_first(part)
        back_some(part, 0, 5)

    begin(0)
    back_some(0, 5, 15)
    back_last(0)
    parts[0].swap()
    begin(1)
    back_some(1, 5, 10)
    parts[0].send_ring()
    back_some(1, 10, 15)
    back_last(1)
    parts[1].swap()
    begin(2)
    back_some(2, 5, 10)
    parts[1].send_ring()
    back_some(2, 10, 15)
    back_last(2)
    parts[2].swap()
    parts[0].send_near()
    parts[2].send_ring()
    parts[0].send_pair()
    parts[1].send_near()
    parts[0].finish()
    parts[1].send_pair()
    parts[2].send_near()
    parts[1].finish()
    parts[2].send_pair()
    parts[2].finish()


def attend_back_all(inverse, spots, chunk_of, query, grad, logsum, inner, both, collective_id):
    groups, halves, rows, lanes = query.shape
    keys = both.shape[1:]
    kind = both.dtype
    block = (CHUNK, lanes)
    vmem, smem = (pl.BlockSpec(memory_space=space) for space in (pltpu.VMEM, pltpu.SMEM))
    slots = STEPS_UNMASKED + 2
    scores = rows * BLOCK * slots * groups
    semaphore = pltpu.SemaphoreType.DMA
    buffers = [
        pltpu.VMEM((2, SIDE, SIDE, 2) + block, kind),
        pltpu.VMEM((2, 3, SIDE, 2) + block, kind),
        pltpu.VMEM((2, SIDE, 2) + block, kind),
        pltpu.VMEM((2, 3, 2) + block, kind),
        pltpu.VMEM((2, 2) + block, kind),
    ]
    return pl.pallas_call(
        attend_back_all_kernel,
        out_shape=(
            jax.ShapeDtypeStruct((groups, halves, rows, lanes), jnp.float32),
            jax.ShapeDtypeStruct((groups, 2) + block, jnp.float32),
        ),
        in_specs=[smem] * 3 + [vmem] * 4 + [pl.BlockSpec(memory_space=pl.ANY)],
        out_specs=(vmem, vmem),
        scratch_shapes=[pltpu.VMEM(keys, kind) for _ in range(2 * groups)]
        + buffers * groups
        + [
            pltpu.VMEM((groups, halves, rows, lanes), jnp.float32),
            pltpu.VMEM((groups, halves, rows, lanes), jnp.float32),
            pltpu.VMEM((slots, rows, lanes), jnp.float32),
            pltpu.VMEM((slots + 1, PER) + block, jnp.float32),
        ]
        + [semaphore(shape) for shape in ((3, 2), (3, 2, 3), (3, 2, 3), (3,)) for _ in range(2)]
        + [semaphore((groups,))],
        compiler_params=pltpu.CompilerParams(
            collective_id=collective_id, has_side_effects=True, vmem_limit_bytes=VMEM_LIMIT
        ),
        cost_estimate=pl.CostEstimate(flops=10 * scores * lanes, bytes_accessed=4 * both.size, transcendentals=scores),
    )(inverse, spots, chunk_of, query, grad, logsum, inner, both)


def first_weight_kernel(
    local_ref, gains_ref, inputs_ref, cotangent_ref, out_ref, gains_out_ref, current_ref, given_ref,
    send, recv, side_send, side_recv, gain_send, gain_recv, token_send, token_recv, kept,
):
    rows = local_ref.shape[0]
    halves = (pl.ds(0, 128), pl.ds(128, rows - 128))
    section, at = here()
    place = at[2]
    beside = (1 - section, at[0] * SIDE + at[1], place)
    barrier = pltpu.get_barrier_semaphore()
    for device in (device_at(section, at, 2, 1), device_at(section, at, 2, -1), beside):
        pl.semaphore_signal(barrier, inc=1, device_id=device, device_id_type=MESH)
    pl.semaphore_wait(barrier, 3)
    own_gains = pltpu.make_async_copy(gains_ref, gains_out_ref.at[section], kept.at[0])
    own_gains.start()
    other_gains = pltpu.make_async_remote_copy(
        src_ref=gains_ref,
        dst_ref=gains_out_ref.at[section],
        send_sem=gain_send,
        recv_sem=gain_recv,
        device_id=beside,
        device_id_type=MESH,
    )
    other_gains.start()

    batch = place // 2
    partner = (section, at[0] * SIDE + at[1], SIDE - 1 - place)
    tokens = ((inputs_ref, current_ref), (cotangent_ref, given_ref))

    def crossing(number):
        source, target = tokens[number]
        return pltpu.make_async_remote_copy(
            src_ref=source.at[1 - batch],
            dst_ref=target,
            send_sem=token_send.at[number],
            recv_sem=token_recv.at[number],
            device_id=partner,
            device_id_type=MESH,
        )

    def staying(number):
        source, target = tokens[number]
        return pltpu.make_async_copy(source.at[batch], target, kept.at[2 + number])

    def aside(number, source):
        index = lax.rem(place + (0, 3, 1, 2)[number], SIDE)
        return pltpu.make_async_remote_copy(
            src_ref=out_ref.at[index] if source is None else source,
            dst_ref=out_ref.at[index],
            send_sem=side_send.at[number],
            recv_sem=side_recv.at[number],
            device_id=beside,
            device_id_type=MESH,
        )

    def message(way, number, step, index, half, source):
        spot = out_ref.at[index, halves[half]]
        return pltpu.make_async_remote_copy(
            src_ref=spot if source is None else source.at[halves[half]],
            dst_ref=spot,
            send_sem=send.at[way, number],
            recv_sem=recv.at[way, number],
            device_id=device_at(section, at, 2, step),
            device_id_type=MESH,
        )

    @pl.when(section == 0)
    def _():
        own = pltpu.make_async_copy(local_ref, out_ref.at[place], kept.at[1])
        own.start()
        for number in range(2):
            staying(number).start()
        flying = {}
        for number in range(2):
            for way, step in enumerate((1, -1)):
                flying[way, number] = message(way, number, step, place, (number + way) % 2, local_ref)
                flying[way, number].start()
        sides = [aside(0, local_ref)]
        sides[0].start()
        for way, step in enumerate((1, -1)):
            flying[way, 0].wait_recv()
            flying[way, 2] = message(way, 2, step, shifted(at, 2, -step), way, None)
            flying[way, 2].start()
        for way in range(2):
            flying[way, 1].wait_recv()
            sides.append(aside(1 + way, None))
            sides[-1].start()
        for way in range(2):
            flying[way, 2].wait_recv()
        sides.append(aside(3, None))
        sides[-1].start()
        for side in sides:
            side.wait_send()
        for way in range(2):
            for number in range(3):
                flying[way, number].wait_send()
        own.wait()
        for number in range(2):
            staying(number).wait()

    @pl.when(section == 1)
    def _():
        for number in range(2):
            crossing(number).start()
        for number in range(2):
            crossing(number).wait()
        for number in range(4):
            aside(number, None).wait_recv()

    own_gains.wait()
    other_gains.wait()


def first_weight(local, gains, inputs, cotangent):
    rows, columns = local.shape
    any_space = pl.BlockSpec(memory_space=pl.ANY)
    return pl.pallas_call(
        first_weight_kernel,
        out_shape=(
            jax.ShapeDtypeStruct((SIDE, rows, columns), local.dtype),
            jax.ShapeDtypeStruct((2,) + gains.shape, gains.dtype),
            jax.ShapeDtypeStruct(inputs.shape[1:], inputs.dtype),
            jax.ShapeDtypeStruct(cotangent.shape[1:], cotangent.dtype),
        ),
        in_specs=[pl.BlockSpec(memory_space=pltpu.VMEM)] * 4,
        out_specs=(any_space,) * 4,
        scratch_shapes=[
            pltpu.SemaphoreType.DMA((2, 3)),
            pltpu.SemaphoreType.DMA((2, 3)),
            pltpu.SemaphoreType.DMA((4,)),
            pltpu.SemaphoreType.DMA((4,)),
            pltpu.SemaphoreType.DMA,
            pltpu.SemaphoreType.DMA,
            pltpu.SemaphoreType.DMA((2,)),
            pltpu.SemaphoreType.DMA((2,)),
            pltpu.SemaphoreType.DMA((4,)),
        ],
        compiler_params=pltpu.CompilerParams(collective_id=3, has_side_effects=True),
        cost_estimate=pl.CostEstimate(flops=0, bytes_accessed=8 * local.size, transcendentals=0),
    )(local, gains, inputs, cotangent)


def normalize(values):
    factor = lax.rsqrt(jnp.mean(values * values, axis=-1, keepdims=True) + epsilon)
    return (values * factor, factor)


def norm_back(grad_unit, unit, factor):
    return factor * (grad_unit - unit * jnp.mean(grad_unit * unit, axis=-1, keepdims=True))


def product(left, right):
    return jnp.dot(left, right, preferred_element_type=jnp.float32)


def product_turned(left, right):
    return lax.dot_general(left, right, contract_last, preferred_element_type=jnp.float32)


def is_lower(shape):
    return lax.broadcasted_iota(jnp.int32, shape, len(shape) - 1) < HEAD_DIM


def turned(tile, cosine, sine):
    half = HEAD_DIM // 2
    lane = lax.broadcasted_iota(jnp.int32, tile.shape, 1)
    other = jnp.where(
        lax.rem(lane, HEAD_DIM) < half, pltpu.roll(tile, 128 - half, 1), pltpu.roll(tile, half, 1)
    )
    return tile * cosine + other * sine


def swapped(tile):
    return pltpu.roll(tile, HEAD_DIM, 1)


def head_rows(ref, head):
    group, index = head // GROUP, head % GROUP
    rows = slice(index * CHUNK, (index + 1) * CHUNK)
    return jnp.concatenate([ref[group, 0, rows, :], ref[group, 1, rows, :]], axis=0)


def put_head(ref, head, tile):
    group, index = head // GROUP, head % GROUP
    rows = slice(index * CHUNK, (index + 1) * CHUNK)
    ref[group, 0, rows, :] = tile[:CHUNK]
    ref[group, 1, rows, :] = tile[CHUNK:]


def widen(wide, qkv):
    for head in range(HEADS):
        wide[128 * head : 128 * head + 64, :] = qkv[64 * head : 64 * head + 64, :]
        wide[128 * head + 64 : 128 * head + 128, :] = jnp.zeros((64, wide.shape[1]), wide.dtype)
    for group in range(KV_HEADS):
        start = 128 * (HEADS + group)
        wide[start : start + 64, :] = qkv[576 + 64 * group : 640 + 64 * group, :]
        wide[start + 64 : start + 128, :] = qkv[768 + 64 * group : 832 + 64 * group, :]


def project(current, gain, wide, cosine, sine, query_ref, local_ref):
    unit, _ = normalize(current)
    projected = product_turned((unit * gain).astype(jnp.bfloat16), wide[...])
    for head in range(HEADS):
        tile = turned(projected[:, 128 * head : 128 * head + 128], cosine, sine) * HEAD_DIM ** (-0.5)
        put_head(query_ref, head, tile.astype(jnp.bfloat16))
    for group in range(KV_HEADS):
        start = 128 * (HEADS + group)
        tile = turned(projected[:, start : start + 128], cosine, sine).astype(jnp.bfloat16)
        local_ref[group, 0] = tile[:CHUNK]
        local_ref[group, 1] = tile[CHUNK:]


def project_back(grad_query_ref, grad_local_ref, current, grad_hidden, gain, wide, cosine, sine, terms_ref):
    lower = is_lower((2 * CHUNK, 128))
    tiles = []
    for head in range(HEADS):
        tile = jnp.where(lower, head_rows(grad_query_ref, head), 0.0)
        tiles.append(turned(tile, cosine, -sine) * HEAD_DIM ** (-0.5))
    for group in range(KV_HEADS):
        tiles.append(turned(grad_local_ref[group], cosine, -sine))
    grad_normed = product(
        jnp.concatenate([tile.astype(jnp.bfloat16) for tile in tiles], axis=1), wide[...]
    )
    unit, factor = normalize(current)
    key = tiles[HEADS:]
    pairs = [(tiles[2 * index], swapped(tiles[2 * index + 1])) for index in range(4)]
    pairs += [
        (tiles[8], swapped(key[0])),
        (key[1], swapped(key[2])),
        (swapped(key[0]), key[1]),
        (swapped(key[2]), jnp.zeros_like(key[2])),
    ]
    width = current.shape[1]
    terms_ref[:, :width] = (unit * gain).astype(jnp.bfloat16)
    for index, (low, high) in enumerate(pairs):
        terms_ref[:, 640 + 128 * index : 768 + 128 * index] = jnp.where(lower, low, high).astype(jnp.bfloat16)
    return grad_hidden + norm_back(grad_normed * gain, unit, factor)


def heads_mixed(mixed_ref):
    lower = is_lower((2 * CHUNK, 128))
    tiles = [head_rows(mixed_ref, head) for head in range(HEADS)]
    pairs = [jnp.where(lower, swapped(tiles[2 * i]), tiles[2 * i + 1]) for i in range(4)]
    pairs.append(swapped(tiles[8])[:, :HEAD_DIM])
    return jnp.concatenate([tile.astype(jnp.bfloat16) for tile in pairs], axis=1)


def feed_forward(current, mixed, out, gain, gate_up, down, waits):
    waits[0]()
    hidden = current + product_turned(mixed, out[...])
    unit, _ = normalize(hidden)
    normed = (unit * gain).astype(jnp.bfloat16)
    waits[1]()
    pair = [product(normed, gate_up[index]) for index in range(4)]
    act = [(pair[k] * jax.nn.sigmoid(pair[k]) * pair[k + 2]).astype(jnp.bfloat16) for k in range(2)]
    part = FF // 2
    waits[2]()
    result = hidden + (product_turned(act[0], down[:, :part]) + product_turned(act[1], down[:, part:]))
    return hidden, pair, result


def feed_back(grad_out, hidden, pair, mixed, mixed_ref, out, gain, gate_up, down, waits, terms_ref, grad_ref, inner_ref):
    part = FF // 2
    width = hidden.shape[1]
    branch = grad_out.astype(jnp.bfloat16)
    waits[2]()
    grad_act = product(branch, down[...])
    waits[1]()
    grad_normed = None
    for k in range(2):
        gate, upward = pair(k), pair(k + 2)
        squashed = jax.nn.sigmoid(gate)
        grad = grad_act[:, k * part : (k + 1) * part]
        grad_gate = (grad * upward * squashed * (1.0 + gate * (1.0 - squashed))).astype(jnp.bfloat16)
        grad_upward = (grad * (gate * squashed)).astype(jnp.bfloat16)
        terms_ref[:, 2560 + k * part : 2560 + (k + 1) * part] = grad_gate
        terms_ref[:, 2560 + (k + 2) * part : 2560 + (k + 3) * part] = grad_upward
        terms_ref[:, 5632 + k * part : 5632 + (k + 1) * part] = (gate * squashed * upward).astype(jnp.bfloat16)
        term = product_turned(grad_gate, gate_up[k]) + product_turned(grad_upward, gate_up[k + 2])
        grad_normed = term if grad_normed is None else grad_normed + term
    unit, factor = normalize(hidden)
    terms_ref[:, :width] = mixed
    terms_ref[:, 640 : 640 + width] = (unit * gain).astype(jnp.bfloat16)
    terms_ref[:, 1280 : 1280 + width] = branch
    grad_hidden = grad_out + norm_back(grad_normed * gain, unit, factor)
    grad_attn = grad_hidden.astype(jnp.bfloat16)
    terms_ref[:, 1920:2560] = jnp.concatenate(
        [jnp.zeros((2 * CHUNK, HEAD_DIM), jnp.float32), grad_hidden], axis=1
    ).astype(jnp.bfloat16)
    waits[0]()
    grad_mixed = product(grad_attn, out[...])
    lower = is_lower((2 * CHUNK, 128))
    for head in range(HEADS):
        start = 128 * (head // 2)
        if head == HEADS - 1:
            tile = jnp.concatenate([jnp.zeros((2 * CHUNK, HEAD_DIM), jnp.float32), grad_mixed[:, start:]], axis=1)
        else:
            tile = grad_mixed[:, start : start + 128]
            tile = jnp.where(lower, 0.0, tile if head % 2 else swapped(tile))
        tile = tile.astype(jnp.bfloat16)
        put_head(grad_ref, head, tile)
        inner = jnp.sum(tile.astype(jnp.float32) * head_rows(mixed_ref, head), axis=-1, keepdims=True)
        put_head(inner_ref, head, inner)
    return grad_hidden


def brought(pairs, sems):
    waits = []
    for index, (source, target) in enumerate(pairs):
        copy = pltpu.make_async_copy(source, target, sems.at[index])
        copy.start()
        waits.append(copy.wait)
    return waits


def once(waits):
    def first_only(wait):
        pending = [wait]

        def run():
            if pending:
                pending.pop()()

        return run

    return [first_only(wait) for wait in waits]


def enter_kernel(current_ref, gain_ref, cosine_ref, sine_ref, qkv_ref, query_ref, local_ref, wide):
    widen(wide, qkv_ref)
    project(
        current_ref[...].astype(jnp.float32).T, gain_ref[...], wide, cosine_ref[...], sine_ref[...], query_ref, local_ref
    )


def between_kernel(
    mixed_ref, current_ref, gain_ref, next_gain_ref, cosine_ref, sine_ref, out_ref, gate_up_ref, down_ref, qkv_ref,
    hidden_ref, pair_ref, next_ref, query_ref, local_ref,
    out, gate_up, down, qkv, wide, sems,
):
    *waits, wait_qkv = brought(
        [(out_ref, out), (gate_up_ref, gate_up), (down_ref, down), (qkv_ref, qkv)], sems
    )
    mixed = heads_mixed(mixed_ref)
    hidden, pair, result = feed_forward(
        current_ref[...].astype(jnp.float32).T, mixed, out, gain_ref[...], gate_up, down, waits
    )
    hidden_ref[...] = hidden
    for index in range(4):
        pair_ref[index] = pair[index]
    next_ref[...] = result
    wait_qkv()
    widen(wide, qkv)
    project(result, next_gain_ref[...], wide, cosine_ref[...], sine_ref[...], query_ref, local_ref)


def top_kernel(
    mixed_ref, current_ref, cotangent_ref, gain_ref, out_ref, gate_up_ref, down_ref,
    result_ref, grad_hidden_ref, terms_ref, grad_ref, inner_ref,
    out, gate_up, down, sems,
):
    waits = once(brought([(out_ref, out), (gate_up_ref, gate_up), (down_ref, down)], sems))
    mixed = heads_mixed(mixed_ref)
    gain = gain_ref[...]
    hidden, pair, result = feed_forward(current_ref[...], mixed, out, gain, gate_up, down, waits)
    result_ref[...] = result
    grad_hidden_ref[...] = feed_back(
        cotangent_ref[...].astype(jnp.float32).T, hidden, lambda index: pair[index], mixed, mixed_ref,
        out, gain, gate_up, down, waits, terms_ref, grad_ref, inner_ref,
    )


def descend_kernel(
    grad_query_ref, grad_local_ref, upper_ref, upper_grad_ref, upper_gain_ref, cosine_ref, sine_ref,
    mixed_ref, hidden_in_ref, pair_ref, gain_ref, qkv_ref, out_ref, gate_up_ref, down_ref,
    upper_terms_ref, grad_hidden_ref, terms_ref, grad_ref, inner_ref,
    out, gate_up, down, qkv, wide, sems,
):
    wait_qkv, *waits = brought(
        [(qkv_ref, qkv), (out_ref, out), (gate_up_ref, gate_up), (down_ref, down)], sems
    )
    wait_qkv()
    widen(wide, qkv)
    grad = project_back(
        grad_query_ref, grad_local_ref, upper_ref[...], upper_grad_ref[...], upper_gain_ref[...], wide,
        cosine_ref[...], sine_ref[...], upper_terms_ref,
    )
    grad_hidden_ref[...] = feed_back(
        grad, hidden_in_ref[...], lambda index: pair_ref[index], heads_mixed(mixed_ref), mixed_ref,
        out, gain_ref[...], gate_up, down, waits, terms_ref, grad_ref, inner_ref,
    )


def leave_kernel(
    grad_query_ref, grad_local_ref, current_ref, grad_hidden_ref, gain_ref, cosine_ref, sine_ref, qkv_ref,
    grad_in_ref, terms_ref, wide,
):
    widen(wide, qkv_ref)
    grad_in_ref[...] = project_back(
        grad_query_ref, grad_local_ref, current_ref[...].astype(jnp.float32).T, grad_hidden_ref[...], gain_ref[...], wide,
        cosine_ref[...], sine_ref[...], terms_ref,
    )


def weight_kernel(order_ref, *refs):
    given, (out_ref, gathered, low, high, sems) = refs[:8], refs[8:]
    width = order_ref.shape[0]
    tiles = 6144 // 128
    blocks = 64
    rows = low.shape[0] // 2
    targets = (low.at[pl.ds(0, rows)], low.at[pl.ds(rows, rows)], high.at[pl.ds(0, rows)], high.at[pl.ds(rows, rows)])
    copies = [
        [pltpu.make_async_copy(given[4 * layer + index], targets[index], sems.at[index]) for index in range(4)]
        for layer in range(2)
    ]
    for layer in range(2):

        @pl.when(lax.axis_index("section") == layer)
        def _(layer=layer):
            for copy in copies[layer]:
                copy.start()

    for copy in copies[0]:
        copy.wait()

    def both(ref, start, size):
        return ref[:, start : start + size]

    def left(ref, start):
        columns = both(ref, start, width)
        return product_turned(order_ref[...], columns).astype(jnp.bfloat16)

    def put(term, tile):
        for index in range(width // blocks):
            part, row = index // 3, (index % 3) * tiles + tile
            gathered[part, pl.ds(row, blocks, stride=3 * tiles), :] = term[index * blocks : (index + 1) * blocks]

    normed_one = left(low, 0)
    mixed = left(high, 0)
    first = product(normed_one, both(low, 640, 1024))
    second = product(mixed, both(high, 1920, 640))
    for tile in range(7):
        put(first[:, 128 * tile : 128 * tile + 128], tile)
    put(first[:, 896:] + second[:, :128], 7)
    for tile in range(1, 5):
        put(second[:, 128 * tile : 128 * tile + 128], 7 + tile)
    normed_two = left(high, 640)
    for step in range(6):
        third = product(normed_two, both(high, 2560 + 512 * step, 512))
        for tile in range(4):
            put(third[:, 128 * tile : 128 * tile + 128], 12 + 4 * step + tile)
    branch = left(high, 1280)
    for step in range(3):
        fourth = product(branch, both(high, 5632 + 512 * step, 512))
        for tile in range(4):
            put(fourth[:, 128 * tile : 128 * tile + 128], 36 + 4 * step + tile)

    for part in range(3):

        @pl.loop(0, blocks)
        def _(block, part=part):
            start = pl.multiple_of(block * (3 * tiles), 3 * tiles)
            out_ref[part, block] = gathered[part, pl.ds(start, 3 * tiles), :].astype(jnp.bfloat16)


TERMS_LOW = 1664
TERMS_HIGH = 7168


def dense(kernel, arguments, hbm, results, scratch, flops):
    vmem = pl.BlockSpec(memory_space=pltpu.VMEM)
    kept = [vmem] * (len(arguments) - hbm) + [pl.BlockSpec(memory_space=pl.ANY)] * hbm
    size = sum(item.size * item.dtype.itemsize for item in arguments)
    return pl.pallas_call(
        kernel,
        out_shape=tuple(jax.ShapeDtypeStruct(shape, kind) for shape, kind in results),
        in_specs=kept,
        out_specs=tuple(vmem for _ in results),
        scratch_shapes=scratch,
        compiler_params=pltpu.CompilerParams(vmem_limit_bytes=VMEM_LIMIT),
        cost_estimate=pl.CostEstimate(flops=flops, bytes_accessed=size, transcendentals=0),
    )(*arguments)


def on_device(inputs, positions, attn_gain, w_qkv, w_out, ffn_gain, w_gate_up, w_down, cotangent):
    _, rows, width = inputs.shape
    section = lax.axis_index("section")
    place = lax.axis_index(("ctx", "fsdp"))
    half_kind, kind = jnp.bfloat16, jnp.float32
    lanes = 2 * HEAD_DIM
    columns = w_qkv.shape[2] * SIDE
    wide_rows = 128 * (HEADS + KV_HEADS)

    depth = lax.axis_index("fsdp")
    batch = depth // 2
    worked = place + section * (SIDE - 1 - 2 * depth)
    spots_k = lax.dynamic_index_in_dim(positions, batch, 0, keepdims=False)
    spots_q = lax.dynamic_slice_in_dim(spots_k, worked * rows, rows, 0)
    chunk_of = spots_k[::CHUNK] // CHUNK
    inverse = jnp.zeros_like(chunk_of).at[chunk_of].set(jnp.arange(chunk_of.shape[0], dtype=jnp.int32))
    spots = lax.dynamic_slice_in_dim(chunk_of, worked * 2, 2, 0)
    frequency = rope_base ** (-(jnp.arange(HEAD_DIM // 2, dtype=kind) * 2.0 / HEAD_DIM))
    angle = spots_q.astype(kind)[:, None] * frequency[None, :]
    cosine, sine = jnp.cos(angle), jnp.sin(angle)
    rest = jnp.ones((rows, HEAD_DIM), kind)
    cosine = jnp.concatenate([cosine, cosine, rest], axis=1)
    sine = jnp.concatenate([-sine, sine, 0.0 * rest], axis=1)

    local_gains = jnp.pad(jnp.concatenate([attn_gain, ffn_gain], axis=0), ((0, 6), (0, 0)))
    qkv_turned = w_qkv[0].T
    qkv_first, gains, current, given = first_weight(
        qkv_turned, local_gains, inputs.transpose(0, 2, 1), cotangent.transpose(0, 2, 1)
    )
    qkv_first = qkv_first.reshape(columns, width)

    shards = [w_out[0].T, w_gate_up[0], w_down[0].T, qkv_turned]
    gain_one = [gains[l, 0:1] for l in range(2)]
    gain_two = [gains[l, 1:2] for l in range(2)]

    query_like = ((KV_HEADS, 2, GROUP * CHUNK, lanes), half_kind)
    inner_like = ((KV_HEADS, 2, GROUP * CHUNK, 1), kind)
    local_like = ((KV_HEADS, 2, CHUNK, lanes), half_kind)
    state_like = ((rows, width), kind)
    pair_like = ((SIDE, rows, 2 * FF // SIDE), kind)
    low_like = ((rows, TERMS_LOW), half_kind)
    high_like = ((rows, TERMS_HIGH), half_kind)
    wide_scratch = pltpu.VMEM((wide_rows, width), half_kind)
    qkv_scratch = pltpu.VMEM((columns, width), half_kind)
    ffn_scratch = [
        pltpu.VMEM((width, width), half_kind),
        pltpu.VMEM((SIDE, width, 2 * FF // SIDE), half_kind),
        pltpu.VMEM((width, FF), half_kind),
    ]
    sems = pltpu.SemaphoreType.DMA((4,))
    qkv_flops = 2 * rows * width * wide_rows
    ffn_flops = 2 * rows * width * (width + 3 * FF)

    def attention(layer, query, local, shards):
        mixed, logsum, both, out, gate_up, down, *rest = attend_all(
            layer, inverse, spots, local, query, shards, layer
        )
        weights = [out.reshape(width, width), gate_up, down.reshape(width, FF)]
        return both, mixed, logsum, weights, [item.reshape(columns, width) for item in rest]

    def attention_back(query, grad, logsum, inner, both):
        grad_query, grad_both = attend_back_all(inverse, spots, chunk_of, query, grad, logsum, inner, both, 4)
        return grad_query, grad_both.reshape(KV_HEADS, rows, lanes)

    query_one, local = dense(
        enter_kernel, (current, gain_one[0], cosine, sine, qkv_first), 0, (query_like, local_like), [wide_scratch], qkv_flops
    )
    both_one, mixed_one, logsum_one, weights_one, (qkv_second,) = attention(0, query_one, local, shards)
    hidden, pair, middle, query_two, local = dense(
        between_kernel,
        (mixed_one, current, gain_two[0], gain_one[1], cosine, sine, *weights_one, qkv_second),
        4,
        (state_like, pair_like, state_like, query_like, local_like),
        ffn_scratch + [qkv_scratch, wide_scratch, sems],
        ffn_flops + qkv_flops,
    )
    both_two, mixed_two, logsum_two, weights_two, _ = attention(1, query_two, local, shards[:3])
    result, grad_hidden, high_two, grad, inner = dense(
        top_kernel,
        (mixed_two, middle, given, gain_two[1], *weights_two),
        3,
        (state_like, state_like, high_like, query_like, inner_like),
        ffn_scratch + [sems],
        2 * ffn_flops,
    )
    earlier = lax.ppermute(
        result,
        ("section", "ctx", "fsdp"),
        [(64 + 4 * ctx + z, 64 + 4 * ctx + 3 - z) for ctx in range(16) for z in range(4)],
    )
    grad_query, grad_local = attention_back(query_two, grad, logsum_two, inner, both_two)
    low_two, grad_hidden, high_one, grad, inner = dense(
        descend_kernel,
        (
            grad_query, grad_local, middle, grad_hidden, gain_one[1], cosine, sine,
            mixed_one, hidden, pair, gain_two[0], qkv_second, *weights_one,
        ),
        4,
        (low_like, state_like, high_like, query_like, inner_like),
        ffn_scratch + [qkv_scratch, wide_scratch, sems],
        ffn_flops + qkv_flops,
    )
    grad_query, grad_local = attention_back(query_one, grad, logsum_one, inner, both_one)
    grad_in, low_one = dense(
        leave_kernel,
        (grad_query, grad_local, current, grad_hidden, gain_one[0], cosine, sine, qkv_first),
        0,
        (state_like, low_like),
        [wide_scratch],
        qkv_flops,
    )

    first = section == 0
    down_pairs, up_pairs = [(0, 1)], [(1, 0)]
    terms = [
        low_one, lax.ppermute(low_one, "section", up_pairs), high_one, lax.ppermute(high_one, "section", up_pairs),
        low_two, lax.ppermute(low_two, "section", down_pairs), high_two, lax.ppermute(high_two, "section", down_pairs),
    ]
    blocks = SIDE * SIDE * SIDE
    each = width // blocks
    total = columns + width + 3 * FF
    line = jnp.arange(width)
    order = (line[:, None] % blocks * each + line[:, None] // blocks == line[None, :]).astype(half_kind)
    (term,) = dense(
        weight_kernel,
        (order, *terms),
        8,
        (((3, blocks, 3 * total // 128, 128), half_kind),),
        [
            pltpu.VMEM((3, blocks * 3 * total // 128, 128), kind),
            pltpu.VMEM((2 * rows, TERMS_LOW), half_kind),
            pltpu.VMEM((2 * rows, TERMS_HIGH), half_kind),
            sems,
        ],
        4 * rows * width * total,
    )
    term = term.reshape(3, SIDE, SIDE, SIDE, 3 * total // 128, 128)
    summed = scatter_all(term, 80, 2).reshape(each, total)
    grad_qkv = summed[:, :columns]
    grad_out_weight = summed[:, columns : columns + width]
    grad_gate_up = summed[:, columns + width : columns + width + 2 * FF]
    grad_down = summed[:, columns + width + 2 * FF :].T

    qkv_own = jnp.where(
        first,
        lax.dynamic_slice_in_dim(qkv_first, place * each, each, 1),
        lax.dynamic_slice_in_dim(qkv_second, place * each, each, 1),
    )
    qkv_own = qkv_own.astype(kind).T
    gate_up_own = jnp.where(
        first,
        lax.dynamic_slice_in_dim(weights_one[1], place * each, each, 1),
        lax.dynamic_slice_in_dim(weights_two[1], place * each, each, 1),
    ).astype(kind)
    split = grad_gate_up.reshape(each, SIDE, -1).transpose(1, 0, 2)
    grad_gain_one = jnp.sum(qkv_own * grad_qkv, axis=1) / lax.dynamic_slice_in_dim(attn_gain[0], place * each, each, 0)
    grad_gain_two = jnp.sum(gate_up_own * split, axis=(0, 2)) / lax.dynamic_slice_in_dim(
        ffn_gain[0], place * each, each, 0
    )

    def index_of(core, ctx, z):
        return (core * SIDE * SIDE + ctx) * SIDE + z

    places = [(ctx, z) for ctx in range(SIDE * SIDE) for z in range(SIDE)]
    axes = ("section", "ctx", "fsdp")
    later = lax.ppermute(
        jnp.where(first, result, grad_in),
        axes,
        [(index_of(0, ctx, z), index_of(1, ctx, z)) for ctx, z in places]
        + [(index_of(1, ctx, z), index_of(0, ctx, SIDE - 1 - z)) for ctx, z in places],
    )
    mine = jnp.where(first, grad_in, later)
    other = jnp.where(first, later, earlier)
    ends = jnp.where(batch == 0, jnp.stack([mine, other]), jnp.stack([other, mine]))
    return (
        ends[None],
        grad_gain_one[None],
        grad_qkv[None],
        grad_out_weight[None],
        grad_gain_two[None],
        grad_gate_up[None],
        grad_down[None],
    )


def solution(mesh):
    placed = (
        P(None, ("ctx", "fsdp"), None),
        P(),
        P("section", None),
        P("section", None, "fsdp"),
        P("section", None, "fsdp"),
        P("section", None),
        P("section", None, "fsdp"),
        P("section", None, "fsdp"),
        P(None, ("ctx", "fsdp"), None),
    )
    return jax.shard_map(
        on_device,
        mesh=mesh,
        in_specs=placed,
        out_specs=(
            P("section", None, ("ctx", "fsdp"), None),
            P("section", ("ctx", "fsdp")),
            P("section", ("ctx", "fsdp"), None),
            P("section", ("ctx", "fsdp"), None),
            P("section", ("ctx", "fsdp")),
            P("section", ("ctx", "fsdp"), None),
            P("section", None, ("ctx", "fsdp")),
        ),
        check_vma=False,
    )
```

```python
import functools

import jax
import jax.numpy as jnp
from jax import lax
from jax.experimental import pallas as pl
from jax.experimental.pallas import tpu as pltpu
from jax.sharding import PartitionSpec as P

HEADS = 9
KV_HEADS = 3
GROUP = 3
HEAD_DIM = 64
FF = 1536
CHUNK = 64
BLOCK = 512
PER = BLOCK // CHUNK
MESH = pl.DeviceIdType.MESH
VMEM_LIMIT = 56 * 1024 * 1024

epsilon = 1e-05
rope_base = 100000.0
contract_last = (((1,), (1,)), ((), ()))
contract_first = (((0,), (0,)), ((), ()))

SIDE = 4


def here():
    ctx = lax.axis_index("ctx")
    return (lax.axis_index("section"), (ctx // SIDE, lax.rem(ctx, SIDE), lax.axis_index("fsdp")))


def shifted(at, axis, step):
    return lax.rem(at[axis] + (step + SIDE), SIDE)


def device_at(section, at, axis, step):
    moved = list(at)
    moved[axis] = shifted(at, axis, step)
    return (section, moved[0] * SIDE + moved[1], moved[2])


def pair_step(at):
    return 1 - 2 * lax.rem(at[2], 2)


SIDES = (SIDE, SIDE, 2)
STEPS = ((0, 1), (1, -1))


class Team:
    def __init__(self):
        self.section, self.at = here()
        w = lax.rem(self.at[2], 2)
        h = self.at[2] // 2
        self.h = lax.rem(h + self.section, 2)
        self.spot = (self.at[0], self.at[1], lax.rem(w + self.section, 2))

    def beside(self):
        return (1 - self.section, self.at[0] * SIDE + self.at[1], self.at[2])

    def shifted(self, axis, step):
        return lax.rem(self.spot[axis] + (step + SIDE), SIDES[axis])

    def moved(self, steps):
        y, x = (lax.rem(self.at[axis] + (steps[axis] + SIDE), SIDE) for axis in range(2))
        z = self.at[2] + (pair_step(self.at) if steps[2] % 2 else 0)
        return (self.section, y * SIDE + x, z)

    def device(self, axis, step):
        return self.moved(tuple(step if other == axis else 0 for other in range(3)))

    def enter(self):
        barrier = pltpu.get_barrier_semaphore()
        devices = [self.moved(steps) for steps in STRAIGHT]
        devices += [self.beside(), device_at(self.section, self.at, 2, -pair_step(self.at))]
        for device in devices:
            pl.semaphore_signal(barrier, inc=1, device_id=device, device_id_type=MESH)
        pl.semaphore_wait(barrier, len(devices))


def visible(shape, chunk, block):
    row = lax.broadcasted_iota(jnp.int32, shape, 0)
    column = lax.broadcasted_iota(jnp.int32, shape, 1)
    return block * BLOCK + column <= chunk * CHUNK + lax.rem(row, CHUNK)


STEPS_UNMASKED = 15


STRAIGHT = ((1, 0, 0), (2, 0, 0), (3, 0, 0), (0, 1, 0), (0, 2, 0), (0, 3, 0), (0, 0, 1))


class Exchange:
    def __init__(self, team, sems):
        self.team, self.sems = team, sems

    def send(self, source, target, device, kind, *index):
        send, recv = self.sems[kind]
        copy = pltpu.make_async_remote_copy(
            src_ref=source,
            dst_ref=target,
            send_sem=send.at[index],
            recv_sem=recv.at[index],
            device_id=device,
            device_id_type=MESH,
        )
        copy.start()
        return copy


class PartGather:
    def __init__(self, part, exchange, local_ref, keys):
        self.part, self.exchange, self.team = part, exchange, exchange.team
        self.local_ref, self.keys = local_ref, keys
        self.near, self.ring, self.side = [], {}, []

    def slab(self, unit, coordinate, w=slice(None)):
        y, x = (coordinate, slice(None)) if unit == 0 else (slice(None), coordinate)
        return self.keys.at[y, x, self.team.h, w, unit]

    def start_near(self):
        spot = self.team.spot
        for unit in range(2):
            for step in range(1, SIDE):
                steps = (0, step, 0) if unit == 0 else (step, 0, 0)
                place = self.keys.at[spot[0], spot[1], self.team.h, :, unit]
                self.near.append(
                    self.exchange.send(place, place, self.team.moved(steps), "near", self.part, unit, step - 1)
                )

    def message(self, unit, way, number, coordinate, w):
        place = self.slab(unit, coordinate, w)
        self.ring[unit, way, number] = self.exchange.send(
            place, place, self.team.device(unit, STEPS[way][1]), "ring", self.part, unit, way, number
        )

    def aside(self, unit, slot, coordinate):
        place = self.slab(unit, coordinate)
        self.side.append(
            self.exchange.send(place, place, self.team.beside(), "side", self.part, unit, slot)
        )

    def start_ring(self):
        for copy in self.near:
            copy.wait_recv()
        for number in range(2):
            for unit in range(2):
                for way, _ in STEPS:
                    self.message(unit, way, number, self.team.spot[unit], (number + way) % 2)
        for unit in range(2):
            self.aside(unit, 0, self.team.spot[unit])

    def pass_on(self):
        for unit in range(2):
            for way, step in STEPS:
                self.ring[unit, way, 0].wait_recv()
                self.message(unit, way, 2, self.team.shifted(unit, -step), way)

    def share(self):
        for unit in range(2):
            for way, step in STEPS:
                self.ring[unit, way, 1].wait_recv()
                self.aside(unit, 1 + way, self.team.shifted(unit, -step))
        for unit in range(2):
            for way, _ in STEPS:
                self.ring[unit, way, 2].wait_recv()
            self.aside(unit, 3, self.team.shifted(unit, 2))

    def finish(self):
        for copy in self.side:
            copy.wait_recv()

    def drain(self):
        for copy in self.near + list(self.ring.values()) + self.side:
            copy.wait_send()


class WeightGather:
    def __init__(self, owner, number, exchange, local_ref, out_ref):
        self.owner, self.number, self.exchange, self.team = owner, number, exchange, exchange.team
        self.local_ref, self.out_ref = local_ref, out_ref
        self.place = self.team.at[2]
        rows = local_ref.shape[0]
        middle = rows // 32 * 16
        if number % 2 == 0:
            middle = rows - middle
        self.rows = ((0, middle), (middle, rows))

    def each(self, body, roles=(0, 1)):
        for role in roles:

            @pl.when(self.team.section == (self.owner if role == 0 else 1 - self.owner))
            def _(role=role):
                body(role)

    def index(self, step):
        return lax.rem(self.place + (step + SIDE), SIDE)

    def message(self, role, way, number, start=True):
        low, high = self.rows[role]
        split = low + (high - low + 16) // 32 * 16
        low, high = (low, split) if (number + way) % 2 == 0 else (split, high)
        rows = pl.ds(low, high - low)
        spot = self.out_ref.at[self.place if number < 2 else self.index(-STEPS[way][1]), rows]
        source = self.local_ref.at[rows] if number < 2 and role == 0 else spot
        device = device_at(self.team.section, self.team.at, 2, STEPS[way][1])
        return self.copy(source, spot, device, "weight_ring", start, way, number)

    def aside(self, role, slot, start=True):
        if slot == 0:
            return self.copy(self.local_ref, self.out_ref.at[self.place], self.team.beside(), "weight_side", start, 0)
        low, high = self.rows[role]
        spot = self.out_ref.at[self.index((-1, 1, 2)[slot - 1]), pl.ds(low, high - low)]
        return self.copy(spot, spot, self.team.beside(), "weight_side", start, slot)

    def copy(self, source, target, device, kind, start, *index):
        send, recv = self.exchange.sems[kind]
        place = (self.number,) + index
        copy = pltpu.make_async_remote_copy(
            src_ref=source,
            dst_ref=target,
            send_sem=send.at[place],
            recv_sem=recv.at[place],
            device_id=device,
            device_id_type=MESH,
        )
        if start:
            copy.start()
        return copy

    def own(self):
        return pltpu.make_async_copy(
            self.local_ref, self.out_ref.at[self.place], self.exchange.sems["weight_own"].at[self.number]
        )

    def start_ring(self, role):
        for number in range(2):
            for way in range(2):
                self.message(role, way, number)

    def start(self):
        def body(role):
            self.own().start()
            self.aside(0, 0)
            self.start_ring(0)

        self.each(body, (0,))

    def start_beside(self):
        def body(role):
            self.aside(0, 0, False).wait_recv()
            self.start_ring(1)

        self.each(body, (1,))

    def pass_on(self):
        def body(role):
            for way in range(2):
                self.message(role, way, 0, False).wait_recv()
                self.message(role, way, 2)

        self.each(body)

    def hand(self):
        def body(role):
            for way in range(2):
                self.message(role, way, 1, False).wait_recv()
                self.aside(role, 1 + way)

        self.each(body)

    def share(self):
        def body(role):
            for way in range(2):
                self.message(role, way, 2, False).wait_recv()
            self.aside(role, 3)

        self.each(body)

    def finish(self):
        def body(role):
            for way in range(2):
                for number in range(3):
                    self.message(role, way, number, False).wait_send()
            for slot in range(1, 4):
                self.aside(role, slot, False).wait_send()
                self.aside(1 - role, slot, False).wait_recv()
            if role == 0:
                self.own().wait()
                self.aside(0, 0, False).wait_send()

        self.each(body)


EXP = jnp.exp


def key_block(inverse_ref, keys, block):
    pieces = []
    for index in range(PER):
        place = inverse_ref[block * PER + index]
        y = lax.shift_right_logical(place, 5)
        x, h, w, half = (
            lax.bitwise_and(lax.shift_right_logical(place, shift), mask) for shift, mask in ((3, 3), (2, 1), (1, 1), (0, 1))
        )
        pieces.append(keys[y, x, h, w, half])
    return jnp.concatenate(pieces, axis=0)


def schedule(spots_ref):
    return lax.shift_right_logical(spots_ref[0], 3), lax.shift_right_logical(spots_ref[1], 3)


def attend_all_kernel(
    owner, inverse_ref, spots_ref, local_ref, query_ref, *refs
):
    count = 4 if owner == 0 else 3
    shard_refs, refs = refs[:count], refs[count:]
    (mixed_ref, logsum_ref, both_ref), refs = refs[:3], refs[3:]
    whole_refs, refs = refs[:count], refs[count:]
    keys, (highest_at, mixed_at), refs = refs[:3], refs[3:5], refs[5:]
    sems = {
        "near": refs[0:2], "ring": refs[2:4], "side": refs[4:6],
        "weight_ring": refs[6:8], "weight_side": refs[8:10], "pair": refs[10:12], "weight_own": refs[12],
    }
    kept = refs[13]
    team = Team()
    team.enter()
    exchange = Exchange(team, sems)
    spot, h = team.spot, team.h
    parts = [PartGather(part, exchange, local_ref, keys[part]) for part in range(KV_HEADS)]
    weights = [
        WeightGather(owner if number < 3 else 1 - owner, number, exchange, shard_refs[number], whole_refs[number])
        for number in range(count)
    ]
    own = [
        pltpu.make_async_copy(local_ref.at[part], keys[part].at[spot[0], spot[1], h, spot[2]], kept.at[part])
        for part in range(KV_HEADS)
    ]
    saved = [
        pltpu.make_async_copy(keys[part], both_ref.at[part], kept.at[KV_HEADS + part]) for part in range(KV_HEADS)
    ]
    ends = schedule(spots_ref)

    def attend_scores(part, half, block):
        both = key_block(inverse_ref, keys[part], block)
        return lax.dot_general(
            query_ref[part, half], both, contract_last, preferred_element_type=jnp.float32
        )

    def attend_rest(part, scores, block, highest, mixed):
        both = key_block(inverse_ref, keys[part], block)
        higher = jnp.maximum(highest, jnp.broadcast_to(jnp.max(scores, axis=-1, keepdims=True), highest.shape))
        exponent = EXP(scores - jnp.concatenate([higher] * (BLOCK // 128), axis=1)).astype(jnp.bfloat16)
        values = jnp.where(is_lower(both.shape), jnp.bfloat16(1.0), both)
        return higher, jnp.dot(exponent, values, preferred_element_type=jnp.float32) + EXP(highest - higher) * mixed

    def attend_first(part):
        for half in range(2):
            scores = attend_scores(part, half, ends[half])
            scores = jnp.where(visible(scores.shape, spots_ref[half], ends[half]), scores, -1e30)
            highest, mixed = attend_rest(
                part, scores, ends[half], jnp.full((scores.shape[0], 128), -1e30, jnp.float32), jnp.zeros((scores.shape[0], 128), jnp.float32)
            )
            highest_at[half] = highest
            mixed_at[half] = mixed

    def attend_some(part, low, high):
        if True:
            size = high - low
            steps = [low + index for index in range(size)]
            halves = [jnp.where(step >= ends[0], 1, 0) for step in steps]
            blocks = [step - half * ends[0] for step, half in zip(steps, halves)]
            befores = [jnp.where(step == ends[0], 1, jnp.where(step == 0, 0, step + 1)) for step in steps]
            scores = attend_scores(part, halves[0], blocks[0])
            for index in range(size):
                later = attend_scores(part, halves[index + 1], blocks[index + 1]) if index + 1 < size else None
                before = befores[index]
                highest, mixed = attend_rest(part, scores, blocks[index], highest_at[before], mixed_at[before])
                highest_at[steps[index] + 2] = highest
                mixed_at[steps[index] + 2] = mixed
                scores = later

    def attend_last(part):
        last = (
            jnp.where(ends[0] == 0, 0, ends[0] + 1),
            jnp.where(ends[0] == STEPS_UNMASKED, 1, STEPS_UNMASKED + 1),
        )
        for half in range(2):
            mixed = mixed_at[last[half]]
            total = mixed[:, :1]
            mixed_ref[part, half] = mixed / total
            logsum_ref[part, half] = highest_at[last[half]][:, :1] + jnp.log(total)

    pairs = [
        exchange.send(
            local_ref.at[part], keys[part].at[spot[0], spot[1], h, spot[2]], team.device(2, 1), "pair", part
        )
        for part in range(KV_HEADS)
    ]
    for copy in own:
        copy.start()
    for weight in weights:
        weight.start()
    for part in range(KV_HEADS):
        own[part].wait()
        pairs[part].wait_recv()
        parts[part].start_near()
    for part in parts:
        part.start_ring()
    for weight in weights:
        weight.start_beside()
    parts[0].pass_on()
    parts[1].pass_on()
    parts[0].share()
    parts[2].pass_on()
    parts[0].finish()
    saved[0].start()
    attend_first(0)
    attend_some(0, 0, 7)
    parts[1].share()
    for weight in weights:
        weight.pass_on()
    attend_some(0, 7, 15)
    attend_last(0)
    parts[1].finish()
    saved[1].start()
    attend_first(1)
    attend_some(1, 0, 7)
    parts[2].share()
    for weight in weights:
        weight.hand()
    attend_some(1, 7, 15)
    attend_last(1)
    parts[2].finish()
    saved[2].start()
    attend_first(2)
    for weight in weights:
        weight.share()
    attend_some(2, 0, 15)
    attend_last(2)
    for copy in pairs:
        copy.wait_send()
    for part in parts:
        part.drain()
    for weight in weights:
        weight.finish()
    for copy in saved:
        copy.wait()


def attend_all(owner, inverse, spots, local, query, shards, collective_id):
    groups, halves, rows, lanes = query.shape
    count = len(shards)
    keys = (SIDE, SIDE, 2, 2, 2, CHUNK, lanes)
    vmem, smem, held = (pl.BlockSpec(memory_space=space) for space in (pltpu.VMEM, pltpu.SMEM, pl.ANY))
    slots = STEPS_UNMASKED + 2
    scores = rows * BLOCK * slots * groups
    semaphore = pltpu.SemaphoreType.DMA
    return pl.pallas_call(
        functools.partial(attend_all_kernel, owner),
        out_shape=(
            jax.ShapeDtypeStruct((groups, halves, rows, lanes), jnp.float32),
            jax.ShapeDtypeStruct((groups, halves, rows, 1), jnp.float32),
            jax.ShapeDtypeStruct((groups,) + keys, local.dtype),
        )
        + tuple(jax.ShapeDtypeStruct((SIDE,) + item.shape, item.dtype) for item in shards),
        in_specs=[smem, smem, vmem, vmem] + [vmem] * count,
        out_specs=(vmem, vmem, held) + (held,) * count,
        scratch_shapes=[pltpu.VMEM(keys, local.dtype) for _ in range(groups)]
        + [
            pltpu.VMEM((slots, rows, lanes), jnp.float32),
            pltpu.VMEM((slots, rows, lanes), jnp.float32),
        ]
        + [semaphore(shape) for shape in ((3, 2, 3), (3, 2, 2, 3), (3, 2, 4), (count, 2, 3), (count, 4), (3,)) for _ in range(2)]
        + [semaphore((count,)), semaphore((2 * groups,))],
        compiler_params=pltpu.CompilerParams(
            collective_id=collective_id, has_side_effects=True, vmem_limit_bytes=VMEM_LIMIT
        ),
        cost_estimate=pl.CostEstimate(flops=4 * scores * lanes, bytes_accessed=128 * local.size, transcendentals=scores),
    )(inverse, spots, local, query, *shards)


class PartScatter:
    def __init__(self, part, exchange, terms, joined, landing, sums, near, pair, out_ref):
        self.part, self.exchange, self.team = part, exchange, exchange.team
        self.terms, self.joined, self.landing, self.sums = terms, joined, landing, sums
        self.near, self.pair, self.out_ref = near, pair, out_ref
        self.sides, self.rings, self.nears, self.pairs = [], [], [], []

    def swap(self):
        for unit in range(2):
            source = self.terms.at[:, :, 1 - self.team.h, :, unit]
            self.sides.append(
                self.exchange.send(source, self.joined.at[unit], self.team.beside(), "side", self.part, unit)
            )

    def send_ring(self):
        for unit in range(2):
            self.sides[unit].wait_recv()

            @pl.loop(0, SIDE * SIDE)
            def _(index, unit=unit):
                y, x = lax.div(index, SIDE), lax.rem(index, SIDE)
                own = self.terms[y, x, self.team.h, :, unit].astype(jnp.float32)
                other = self.joined[unit, y, x].astype(jnp.float32)
                self.joined[unit, y, x] = (own + other).astype(jnp.bfloat16)

            for step in (2, 1, 3):
                coordinate = self.team.shifted(unit, step)
                place = self.joined.at[unit, coordinate] if unit == 0 else self.joined.at[unit, :, coordinate]
                steps = (step, 0, 0) if unit == 0 else (0, step, 0)
                self.rings.append(
                    self.exchange.send(
                        place, self.landing.at[unit, step - 1], self.team.moved(steps), "ring", self.part, unit, step - 1
                    )
                )

    def send_near(self):
        for copy in self.rings:
            copy.wait_recv()
        for unit in range(2):
            mine = self.team.spot[unit]
            for index in range(SIDE):
                place = (unit, mine, index) if unit == 0 else (unit, index, mine)
                total = self.joined[place].astype(jnp.float32)
                for step in range(SIDE - 1):
                    total = total + self.landing[unit, step, index].astype(jnp.float32)
                self.sums[unit, index] = total.astype(jnp.bfloat16)
            for step in range(1, SIDE):
                steps = (0, step, 0) if unit == 0 else (step, 0, 0)
                self.nears.append(
                    self.exchange.send(
                        self.sums.at[unit, self.team.shifted(1 - unit, step)], self.near.at[unit, step - 1],
                        self.team.moved(steps), "near", self.part, unit, step - 1,
                    )
                )

    def send_pair(self):
        for copy in self.nears:
            copy.wait_recv()
        w = self.team.spot[2]
        for unit in range(2):
            mine = self.team.spot[1 - unit]
            for index in range(2):
                place = w if index == 0 else 1 - w
                total = self.sums[unit, mine, place].astype(jnp.float32)
                for step in range(SIDE - 1):
                    total = total + self.near[unit, step, place].astype(jnp.float32)
                if index == 0:
                    self.out_ref[self.part, unit] = total
                else:
                    self.pair[0, unit] = total.astype(jnp.bfloat16)
        self.pairs.append(
            self.exchange.send(self.pair.at[0], self.pair.at[1], self.team.device(2, 1), "pair", self.part)
        )

    def finish(self):
        self.pairs[0].wait_recv()
        for unit in range(2):
            self.out_ref[self.part, unit] = self.out_ref[self.part, unit] + self.pair[1, unit].astype(jnp.float32)
        for copy in self.sides + self.rings + self.nears + self.pairs:
            copy.wait_send()


def attend_back_all_kernel(
    layer, inverse_ref, spots_ref, chunk_ref, query_ref, grad_ref, logsum_ref, inner_ref, both_ref, terms_ref,
    grad_query_ref, out_ref, terms_in_ref, *refs
):
    keys, refs = refs[:3], refs[3:]
    terms, refs = refs[:3], refs[3:]
    buffers, refs = [refs[5 * part : 5 * part + 5] for part in range(3)], refs[15:]
    logsum_at, inner_at, query_at, grad_at, *refs = refs
    sems = {kind: refs[2 * index : 2 * index + 2] for index, kind in enumerate(("side", "ring", "near", "pair"))}
    kept = refs[8]
    terms_send, terms_recv = refs[9:]
    team = Team()
    brought_in = [pltpu.make_async_copy(both_ref.at[part], keys[part], kept.at[part]) for part in range(KV_HEADS)]
    for copy in brought_in:
        copy.start()
    team.enter()
    exchange = Exchange(team, sems)
    parts = [
        PartScatter(part, exchange, terms[part], *buffers[part], out_ref) for part in range(KV_HEADS)
    ]
    ends = schedule(spots_ref)
    for part in range(KV_HEADS):
        for half in range(2):
            logsum_at[part, half] = jnp.broadcast_to(logsum_ref[part, half], logsum_at.shape[2:])
            inner_at[part, half] = jnp.broadcast_to(inner_ref[part, half], inner_at.shape[2:])

    grad_at[STEPS_UNMASKED + 2] = jnp.zeros(grad_at.shape[1:], jnp.float32)

    def products(part, half, block):
        both = key_block(inverse_ref, keys[part], block)
        scores = lax.dot_general(query_ref[part, half], both, contract_last, preferred_element_type=jnp.float32)
        grad_weights = lax.dot_general(grad_ref[part, half], both, contract_last, preferred_element_type=jnp.float32)
        return scores, grad_weights

    def rest(part, slot, half, block, found, masked, before):
        scores, grad_weights = found
        both = key_block(inverse_ref, keys[part], block)
        logsum = jnp.concatenate([logsum_at[part, half]] * (BLOCK // 128), axis=1)
        inner = jnp.concatenate([inner_at[part, half]] * (BLOCK // 128), axis=1)
        probs = EXP(scores - logsum)
        if masked:
            probs = jnp.where(visible(scores.shape, spots_ref[half], block), probs, 0.0)
        grad_scores = (probs * (grad_weights - inner)).astype(jnp.bfloat16)
        grad_query = jnp.dot(grad_scores, both, preferred_element_type=jnp.float32)
        query_at[slot] = grad_query if before is None else grad_query + query_at[before]
        grad_at[slot] = lax.dot_general(
            jnp.concatenate([probs.astype(jnp.bfloat16), grad_scores], axis=0),
            jnp.concatenate([grad_ref[part, half], query_ref[part, half]], axis=0),
            contract_first,
            preferred_element_type=jnp.float32,
        ).reshape(PER, CHUNK, 2 * HEAD_DIM)

    def back_first(part):
        for half in range(2):
            rest(part, half, half, ends[half], products(part, half, ends[half]), True, None)

    def back_some(part, low, high):
        steps = list(range(low, high))
        halves = [jnp.where(step >= ends[0], 1, 0) for step in steps]
        blocks = [step - half * ends[0] for step, half in zip(steps, halves)]
        found = products(part, halves[0], blocks[0])
        for index, step in enumerate(steps):
            later = products(part, halves[index + 1], blocks[index + 1]) if index + 1 < len(steps) else None
            before = jnp.where(step == ends[0], 1, jnp.where(step == 0, 0, step + 1))
            rest(part, step + 2, halves[index], blocks[index], found, False, before)
            found = later

    def back_last(part):
        last = (
            jnp.where(ends[0] == 0, 0, ends[0] + 1),
            jnp.where(ends[0] == STEPS_UNMASKED, 1, STEPS_UNMASKED + 1),
        )
        for half in range(2):
            grad_query_ref[part, half] = query_at[last[half]]

        @pl.loop(0, SIDE * SIDE)
        def _(column):
            y, x = lax.div(column, SIDE), lax.rem(column, SIDE)
            for number in range(8):
                chunk = chunk_ref[8 * column + number]
                row = lax.bitwise_and(chunk, PER - 1)
                block = lax.shift_right_logical(chunk, 3)
                total = None
                for half in range(2):
                    slot = jnp.where(block == ends[half], half, 2 + half * ends[0] + block)
                    term = grad_at[jnp.where(block <= ends[half], slot, STEPS_UNMASKED + 2), row]
                    total = term if total is None else total + term
                terms[part][y, x, number // 4, number // 2 % 2, number % 2] = total.astype(jnp.bfloat16)

    crossing = pltpu.make_async_remote_copy(
        src_ref=terms_ref,
        dst_ref=terms_in_ref,
        send_sem=terms_send,
        recv_sem=terms_recv,
        device_id=team.beside(),
        device_id_type=MESH,
    )

    @pl.when(team.section != layer)
    def _():
        crossing.start()

    def begin(part):
        brought_in[part].wait()
        back_first(part)
        back_some(part, 0, 5)

    begin(0)
    back_some(0, 5, 15)
    back_last(0)
    parts[0].swap()
    begin(1)
    back_some(1, 5, 10)
    parts[0].send_ring()
    back_some(1, 10, 15)
    back_last(1)
    parts[1].swap()
    begin(2)
    back_some(2, 5, 10)
    parts[1].send_ring()
    back_some(2, 10, 15)
    back_last(2)
    parts[2].swap()
    parts[0].send_near()
    parts[2].send_ring()
    parts[0].send_pair()
    parts[1].send_near()
    parts[0].finish()
    parts[1].send_pair()
    parts[2].send_near()
    parts[1].finish()
    parts[2].send_pair()
    parts[2].finish()

    @pl.when(team.section != layer)
    def _():
        crossing.wait_send()

    @pl.when(team.section == layer)
    def _():
        crossing.wait_recv()


def attend_back_all(layer, inverse, spots, chunk_of, query, grad, logsum, inner, both, high, collective_id):
    groups, halves, rows, lanes = query.shape
    keys = both.shape[1:]
    kind = both.dtype
    block = (CHUNK, lanes)
    vmem, smem = (pl.BlockSpec(memory_space=space) for space in (pltpu.VMEM, pltpu.SMEM))
    slots = STEPS_UNMASKED + 2
    scores = rows * BLOCK * slots * groups
    semaphore = pltpu.SemaphoreType.DMA
    buffers = [
        pltpu.VMEM((2, SIDE, SIDE, 2) + block, kind),
        pltpu.VMEM((2, 3, SIDE, 2) + block, kind),
        pltpu.VMEM((2, SIDE, 2) + block, kind),
        pltpu.VMEM((2, 3, 2) + block, kind),
        pltpu.VMEM((2, 2) + block, kind),
    ]
    return pl.pallas_call(
        functools.partial(attend_back_all_kernel, layer),
        out_shape=(
            jax.ShapeDtypeStruct((groups, halves, rows, lanes), jnp.float32),
            jax.ShapeDtypeStruct((groups, 2) + block, jnp.float32),
            jax.ShapeDtypeStruct(high.shape, high.dtype),
        ),
        in_specs=[smem] * 3 + [vmem] * 4 + [pl.BlockSpec(memory_space=pl.ANY)] * 2,
        out_specs=(vmem, vmem, pl.BlockSpec(memory_space=pl.ANY)),
        scratch_shapes=[pltpu.VMEM(keys, kind) for _ in range(2 * groups)]
        + buffers * groups
        + [
            pltpu.VMEM((groups, halves, rows, lanes), jnp.float32),
            pltpu.VMEM((groups, halves, rows, lanes), jnp.float32),
            pltpu.VMEM((slots, rows, lanes), jnp.float32),
            pltpu.VMEM((slots + 1, PER) + block, jnp.float32),
        ]
        + [semaphore(shape) for shape in ((3, 2), (3, 2, 3), (3, 2, 3), (3,)) for _ in range(2)]
        + [semaphore((groups,)), semaphore, semaphore],
        compiler_params=pltpu.CompilerParams(
            collective_id=collective_id, has_side_effects=True, vmem_limit_bytes=VMEM_LIMIT
        ),
        cost_estimate=pl.CostEstimate(flops=10 * scores * lanes, bytes_accessed=4 * both.size, transcendentals=scores),
    )(inverse, spots, chunk_of, query, grad, logsum, inner, both, high)


def first_weight_kernel(
    local_ref, gains_ref, inputs_ref, cotangent_ref, out_ref, gains_out_ref, current_ref, given_ref,
    send, recv, side_send, side_recv, gain_send, gain_recv, token_send, token_recv, kept,
):
    rows = local_ref.shape[0]
    halves = (pl.ds(0, 128), pl.ds(128, rows - 128))
    section, at = here()
    place = at[2]
    beside = (1 - section, at[0] * SIDE + at[1], place)
    barrier = pltpu.get_barrier_semaphore()
    for device in (device_at(section, at, 2, 1), device_at(section, at, 2, -1), beside):
        pl.semaphore_signal(barrier, inc=1, device_id=device, device_id_type=MESH)
    pl.semaphore_wait(barrier, 3)
    own_gains = pltpu.make_async_copy(gains_ref, gains_out_ref.at[section], kept.at[0])
    own_gains.start()
    other_gains = pltpu.make_async_remote_copy(
        src_ref=gains_ref,
        dst_ref=gains_out_ref.at[section],
        send_sem=gain_send,
        recv_sem=gain_recv,
        device_id=beside,
        device_id_type=MESH,
    )
    other_gains.start()

    batch = place // 2
    partner = (section, at[0] * SIDE + at[1], SIDE - 1 - place)
    tokens = ((inputs_ref, current_ref), (cotangent_ref, given_ref))

    def crossing(number):
        source, target = tokens[number]
        return pltpu.make_async_remote_copy(
            src_ref=source.at[1 - batch],
            dst_ref=target,
            send_sem=token_send.at[number],
            recv_sem=token_recv.at[number],
            device_id=partner,
            device_id_type=MESH,
        )

    def staying(number):
        source, target = tokens[number]
        return pltpu.make_async_copy(source.at[batch], target, kept.at[2 + number])

    def aside(number, source):
        index = lax.rem(place + (0, 3, 1, 2)[number], SIDE)
        return pltpu.make_async_remote_copy(
            src_ref=out_ref.at[index] if source is None else source,
            dst_ref=out_ref.at[index],
            send_sem=side_send.at[number],
            recv_sem=side_recv.at[number],
            device_id=beside,
            device_id_type=MESH,
        )

    def message(way, number, step, index, half, source):
        spot = out_ref.at[index, halves[half]]
        return pltpu.make_async_remote_copy(
            src_ref=spot if source is None else source.at[halves[half]],
            dst_ref=spot,
            send_sem=send.at[way, number],
            recv_sem=recv.at[way, number],
            device_id=device_at(section, at, 2, step),
            device_id_type=MESH,
        )

    @pl.when(section == 0)
    def _():
        own = pltpu.make_async_copy(local_ref, out_ref.at[place], kept.at[1])
        own.start()
        for number in range(2):
            staying(number).start()
        flying = {}
        for number in range(2):
            for way, step in enumerate((1, -1)):
                flying[way, number] = message(way, number, step, place, (number + way) % 2, local_ref)
                flying[way, number].start()
        sides = [aside(0, local_ref)]
        sides[0].start()
        for way, step in enumerate((1, -1)):
            flying[way, 0].wait_recv()
            flying[way, 2] = message(way, 2, step, shifted(at, 2, -step), way, None)
            flying[way, 2].start()
        for way in range(2):
            flying[way, 1].wait_recv()
            sides.append(aside(1 + way, None))
            sides[-1].start()
        for way in range(2):
            flying[way, 2].wait_recv()
        sides.append(aside(3, None))
        sides[-1].start()
        for side in sides:
            side.wait_send()
        for way in range(2):
            for number in range(3):
                flying[way, number].wait_send()
        own.wait()
        for number in range(2):
            staying(number).wait()

    @pl.when(section == 1)
    def _():
        for number in range(2):
            crossing(number).start()
        for number in range(2):
            crossing(number).wait()
        for number in range(4):
            aside(number, None).wait_recv()

    own_gains.wait()
    other_gains.wait()


def first_weight(local, gains, inputs, cotangent):
    rows, columns = local.shape
    any_space = pl.BlockSpec(memory_space=pl.ANY)
    return pl.pallas_call(
        first_weight_kernel,
        out_shape=(
            jax.ShapeDtypeStruct((SIDE, rows, columns), local.dtype),
            jax.ShapeDtypeStruct((2,) + gains.shape, gains.dtype),
            jax.ShapeDtypeStruct(inputs.shape[1:], inputs.dtype),
            jax.ShapeDtypeStruct(cotangent.shape[1:], cotangent.dtype),
        ),
        in_specs=[pl.BlockSpec(memory_space=pltpu.VMEM)] * 4,
        out_specs=(any_space,) * 4,
        scratch_shapes=[
            pltpu.SemaphoreType.DMA((2, 3)),
            pltpu.SemaphoreType.DMA((2, 3)),
            pltpu.SemaphoreType.DMA((4,)),
            pltpu.SemaphoreType.DMA((4,)),
            pltpu.SemaphoreType.DMA,
            pltpu.SemaphoreType.DMA,
            pltpu.SemaphoreType.DMA((2,)),
            pltpu.SemaphoreType.DMA((2,)),
            pltpu.SemaphoreType.DMA((4,)),
        ],
        compiler_params=pltpu.CompilerParams(collective_id=3, has_side_effects=True),
        cost_estimate=pl.CostEstimate(flops=0, bytes_accessed=8 * local.size, transcendentals=0),
    )(local, gains, inputs, cotangent)


def normalize(values):
    factor = lax.rsqrt(jnp.mean(values * values, axis=-1, keepdims=True) + epsilon)
    return (values * factor, factor)


def norm_back(grad_unit, unit, factor):
    return factor * (grad_unit - unit * jnp.mean(grad_unit * unit, axis=-1, keepdims=True))


def product(left, right):
    return jnp.dot(left, right, preferred_element_type=jnp.float32)


def product_turned(left, right):
    return lax.dot_general(left, right, contract_last, preferred_element_type=jnp.float32)


def is_lower(shape):
    return lax.broadcasted_iota(jnp.int32, shape, len(shape) - 1) < HEAD_DIM


def turned(tile, cosine, sine):
    half = HEAD_DIM // 2
    lane = lax.broadcasted_iota(jnp.int32, tile.shape, 1)
    other = jnp.where(
        lax.rem(lane, HEAD_DIM) < half, pltpu.roll(tile, 128 - half, 1), pltpu.roll(tile, half, 1)
    )
    return tile * cosine + other * sine


def swapped(tile):
    return pltpu.roll(tile, HEAD_DIM, 1)


def head_rows(ref, head):
    group, index = head // GROUP, head % GROUP
    rows = slice(index * CHUNK, (index + 1) * CHUNK)
    return jnp.concatenate([ref[group, 0, rows, :], ref[group, 1, rows, :]], axis=0)


def put_head(ref, head, tile):
    group, index = head // GROUP, head % GROUP
    rows = slice(index * CHUNK, (index + 1) * CHUNK)
    ref[group, 0, rows, :] = tile[:CHUNK]
    ref[group, 1, rows, :] = tile[CHUNK:]


def widen(wide, qkv):
    for head in range(HEADS):
        wide[128 * head : 128 * head + 64, :] = qkv[64 * head : 64 * head + 64, :]
        wide[128 * head + 64 : 128 * head + 128, :] = jnp.zeros((64, wide.shape[1]), wide.dtype)
    for group in range(KV_HEADS):
        start = 128 * (HEADS + group)
        wide[start : start + 64, :] = qkv[576 + 64 * group : 640 + 64 * group, :]
        wide[start + 64 : start + 128, :] = qkv[768 + 64 * group : 832 + 64 * group, :]


def project(current, gain, wide, cosine, sine, query_ref, local_ref):
    unit, _ = normalize(current)
    projected = product_turned((unit * gain).astype(jnp.bfloat16), wide[...])
    for head in range(HEADS):
        tile = turned(projected[:, 128 * head : 128 * head + 128], cosine, sine) * HEAD_DIM ** (-0.5)
        put_head(query_ref, head, tile.astype(jnp.bfloat16))
    for group in range(KV_HEADS):
        start = 128 * (HEADS + group)
        tile = turned(projected[:, start : start + 128], cosine, sine).astype(jnp.bfloat16)
        local_ref[group, 0] = tile[:CHUNK]
        local_ref[group, 1] = tile[CHUNK:]


def project_back(grad_query_ref, grad_local_ref, current, grad_hidden, gain, wide, cosine, sine, terms_ref):
    lower = is_lower((2 * CHUNK, 128))
    tiles = []
    for head in range(HEADS):
        tile = jnp.where(lower, head_rows(grad_query_ref, head), 0.0)
        tiles.append(turned(tile, cosine, -sine) * HEAD_DIM ** (-0.5))
    for group in range(KV_HEADS):
        tiles.append(turned(grad_local_ref[group], cosine, -sine))
    grad_normed = product(
        jnp.concatenate([tile.astype(jnp.bfloat16) for tile in tiles], axis=1), wide[...]
    )
    unit, factor = normalize(current)
    key = tiles[HEADS:]
    pairs = [(tiles[2 * index], swapped(tiles[2 * index + 1])) for index in range(4)]
    pairs += [
        (tiles[8], swapped(key[0])),
        (key[1], swapped(key[2])),
        (swapped(key[0]), key[1]),
        (swapped(key[2]), jnp.zeros_like(key[2])),
    ]
    width = current.shape[1]
    terms_ref[:, :width] = (unit * gain).astype(jnp.bfloat16)
    for index, (low, high) in enumerate(pairs):
        terms_ref[:, 640 + 128 * index : 768 + 128 * index] = jnp.where(lower, low, high).astype(jnp.bfloat16)
    return grad_hidden + norm_back(grad_normed * gain, unit, factor)


def heads_mixed(mixed_ref):
    lower = is_lower((2 * CHUNK, 128))
    tiles = [head_rows(mixed_ref, head) for head in range(HEADS)]
    pairs = [jnp.where(lower, swapped(tiles[2 * i]), tiles[2 * i + 1]) for i in range(4)]
    pairs.append(swapped(tiles[8])[:, :HEAD_DIM])
    return jnp.concatenate([tile.astype(jnp.bfloat16) for tile in pairs], axis=1)


def feed_forward(current, mixed, out, gain, gate_up, down, waits):
    waits[0]()
    hidden = current + product_turned(mixed, out[...])
    unit, _ = normalize(hidden)
    normed = (unit * gain).astype(jnp.bfloat16)
    waits[1]()
    pair = [product(normed, gate_up[index]) for index in range(4)]
    act = [(pair[k] * jax.nn.sigmoid(pair[k]) * pair[k + 2]).astype(jnp.bfloat16) for k in range(2)]
    part = FF // 2
    waits[2]()
    result = hidden + (product_turned(act[0], down[:, :part]) + product_turned(act[1], down[:, part:]))
    return hidden, pair, result


def feed_back(grad_out, hidden, pair, mixed, mixed_ref, out, gain, gate_up, down, waits, terms_ref, grad_ref, inner_ref):
    part = FF // 2
    width = hidden.shape[1]
    branch = grad_out.astype(jnp.bfloat16)
    waits[2]()
    grad_act = product(branch, down[...])
    waits[1]()
    grad_normed = None
    for k in range(2):
        gate, upward = pair(k), pair(k + 2)
        squashed = jax.nn.sigmoid(gate)
        grad = grad_act[:, k * part : (k + 1) * part]
        grad_gate = (grad * upward * squashed * (1.0 + gate * (1.0 - squashed))).astype(jnp.bfloat16)
        grad_upward = (grad * (gate * squashed)).astype(jnp.bfloat16)
        terms_ref[:, 2560 + k * part : 2560 + (k + 1) * part] = grad_gate
        terms_ref[:, 2560 + (k + 2) * part : 2560 + (k + 3) * part] = grad_upward
        terms_ref[:, 5632 + k * part : 5632 + (k + 1) * part] = (gate * squashed * upward).astype(jnp.bfloat16)
        term = product_turned(grad_gate, gate_up[k]) + product_turned(grad_upward, gate_up[k + 2])
        grad_normed = term if grad_normed is None else grad_normed + term
    unit, factor = normalize(hidden)
    terms_ref[:, :width] = mixed
    terms_ref[:, 640 : 640 + width] = (unit * gain).astype(jnp.bfloat16)
    terms_ref[:, 1280 : 1280 + width] = branch
    grad_hidden = grad_out + norm_back(grad_normed * gain, unit, factor)
    grad_attn = grad_hidden.astype(jnp.bfloat16)
    terms_ref[:, 1920:2560] = jnp.concatenate(
        [jnp.zeros((2 * CHUNK, HEAD_DIM), jnp.float32), grad_hidden], axis=1
    ).astype(jnp.bfloat16)
    waits[0]()
    grad_mixed = product(grad_attn, out[...])
    lower = is_lower((2 * CHUNK, 128))
    for head in range(HEADS):
        start = 128 * (head // 2)
        if head == HEADS - 1:
            tile = jnp.concatenate([jnp.zeros((2 * CHUNK, HEAD_DIM), jnp.float32), grad_mixed[:, start:]], axis=1)
        else:
            tile = grad_mixed[:, start : start + 128]
            tile = jnp.where(lower, 0.0, tile if head % 2 else swapped(tile))
        tile = tile.astype(jnp.bfloat16)
        put_head(grad_ref, head, tile)
        inner = jnp.sum(tile.astype(jnp.float32) * head_rows(mixed_ref, head), axis=-1, keepdims=True)
        put_head(inner_ref, head, inner)
    return grad_hidden


def brought(pairs, sems):
    waits = []
    for index, (source, target) in enumerate(pairs):
        copy = pltpu.make_async_copy(source, target, sems.at[index])
        copy.start()
        waits.append(copy.wait)
    return waits


def once(waits):
    def first_only(wait):
        pending = [wait]

        def run():
            if pending:
                pending.pop()()

        return run

    return [first_only(wait) for wait in waits]


def enter_kernel(current_ref, gain_ref, cosine_ref, sine_ref, qkv_ref, query_ref, local_ref, wide):
    widen(wide, qkv_ref)
    project(
        current_ref[...].astype(jnp.float32).T, gain_ref[...], wide, cosine_ref[...], sine_ref[...], query_ref, local_ref
    )


def between_kernel(
    mixed_ref, current_ref, gain_ref, next_gain_ref, cosine_ref, sine_ref, out_ref, gate_up_ref, down_ref, qkv_ref,
    hidden_ref, pair_ref, next_ref, query_ref, local_ref,
    out, gate_up, down, qkv, wide, sems,
):
    *waits, wait_qkv = brought(
        [(out_ref, out), (gate_up_ref, gate_up), (down_ref, down), (qkv_ref, qkv)], sems
    )
    mixed = heads_mixed(mixed_ref)
    hidden, pair, result = feed_forward(
        current_ref[...].astype(jnp.float32).T, mixed, out, gain_ref[...], gate_up, down, waits
    )
    hidden_ref[...] = hidden
    for index in range(4):
        pair_ref[index] = pair[index]
    next_ref[...] = result
    wait_qkv()
    widen(wide, qkv)
    project(result, next_gain_ref[...], wide, cosine_ref[...], sine_ref[...], query_ref, local_ref)


def top_kernel(
    mixed_ref, current_ref, cotangent_ref, gain_ref, out_ref, gate_up_ref, down_ref,
    result_ref, grad_hidden_ref, terms_ref, grad_ref, inner_ref,
    out, gate_up, down, sems,
):
    waits = once(brought([(out_ref, out), (gate_up_ref, gate_up), (down_ref, down)], sems))
    mixed = heads_mixed(mixed_ref)
    gain = gain_ref[...]
    hidden, pair, result = feed_forward(current_ref[...], mixed, out, gain, gate_up, down, waits)
    result_ref[...] = result
    grad_hidden_ref[...] = feed_back(
        cotangent_ref[...].astype(jnp.float32).T, hidden, lambda index: pair[index], mixed, mixed_ref,
        out, gain, gate_up, down, waits, terms_ref, grad_ref, inner_ref,
    )


def descend_kernel(
    grad_query_ref, grad_local_ref, upper_ref, upper_grad_ref, upper_gain_ref, cosine_ref, sine_ref,
    mixed_ref, hidden_in_ref, pair_ref, gain_ref, qkv_ref, out_ref, gate_up_ref, down_ref,
    upper_terms_ref, grad_hidden_ref, terms_ref, grad_ref, inner_ref,
    out, gate_up, down, qkv, wide, sems,
):
    wait_qkv, *waits = brought(
        [(qkv_ref, qkv), (out_ref, out), (gate_up_ref, gate_up), (down_ref, down)], sems
    )
    wait_qkv()
    widen(wide, qkv)
    grad = project_back(
        grad_query_ref, grad_local_ref, upper_ref[...], upper_grad_ref[...], upper_gain_ref[...], wide,
        cosine_ref[...], sine_ref[...], upper_terms_ref,
    )
    grad_hidden_ref[...] = feed_back(
        grad, hidden_in_ref[...], lambda index: pair_ref[index], heads_mixed(mixed_ref), mixed_ref,
        out, gain_ref[...], gate_up, down, waits, terms_ref, grad_ref, inner_ref,
    )


def leave_kernel(
    grad_query_ref, grad_local_ref, current_ref, grad_hidden_ref, gain_ref, cosine_ref, sine_ref, qkv_ref,
    grad_in_ref, terms_ref, wide,
):
    widen(wide, qkv_ref)
    grad_in_ref[...] = project_back(
        grad_query_ref, grad_local_ref, current_ref[...].astype(jnp.float32).T, grad_hidden_ref[...], gain_ref[...], wide,
        cosine_ref[...], sine_ref[...], terms_ref,
    )


def weight_all_kernel(
    order_ref, low_one, low_two, high_one, high_two, high_one_in, high_two_in, out_ref,
    low, high, gathered, terms_0, terms_1, terms_2, sums_0, sums_1, sums_2, *refs
):
    terms, sums = (terms_0, terms_1, terms_2), (sums_0, sums_1, sums_2)
    landing = [refs[3 * chunk : 3 * chunk + 3] for chunk in range(3)]
    second_at, second_sum, third_at = refs[9:12], refs[12:15], refs[15:18]
    ring_send, ring_recv, second_send, second_recv, third_send, third_recv, low_send, low_recv, kept = refs[18:]
    section, at = here()
    rows = low.shape[0] // 2
    beside = (1 - section, at[0] * SIDE + at[1], at[2])
    barrier = pltpu.get_barrier_semaphore()
    devices = [device_at(section, at, axis, step) for axis in range(3) for step in range(1, SIDE)] + [beside]
    for device in devices:
        pl.semaphore_signal(barrier, inc=1, device_id=device, device_id_type=MESH)
    pl.semaphore_wait(barrier, len(devices))

    def local(layer, index):
        top, bottom = pl.ds(0, rows), pl.ds(rows, rows)
        source, target = (
            ((low_one, low_two)[layer], low.at[top]),
            ((high_one, high_two)[layer], high.at[top]),
            ((high_one_in, high_two_in)[layer], high.at[bottom]),
        )[index]
        return pltpu.make_async_copy(source, target, kept.at[index])

    def crossing(layer):
        return pltpu.make_async_remote_copy(
            src_ref=(low_two, low_one)[layer],
            dst_ref=low.at[pl.ds(rows, rows)],
            send_sem=low_send,
            recv_sem=low_recv,
            device_id=beside,
            device_id_type=MESH,
        )

    for layer in range(2):

        @pl.when(section == layer)
        def _(layer=layer):
            crossing(layer).start()
            for index in range(3):
                local(layer, index).start()

    width = order_ref.shape[0]
    blocks = 64
    tiles = out_ref.shape[1] // 3
    slab = width // 3

    def chunk_terms(chunk):
        def left(ref, start):
            part = order_ref[chunk * slab : (chunk + 1) * slab, :]
            return product_turned(part, ref[:, start : start + width]).astype(jnp.bfloat16)

        def put(term, tile):
            for index in range(3):
                row = index * tiles + tile
                gathered[pl.ds(row, blocks, stride=3 * tiles), :] = term[index * blocks : (index + 1) * blocks]

        normed_two = left(high, 640)
        for step in range(6):
            term = product(normed_two, high[:, 2560 + 512 * step : 3072 + 512 * step])
            for tile in range(4):
                put(term[:, 128 * tile : 128 * tile + 128], 12 + 4 * step + tile)
        branch = left(high, 1280)
        for step in range(3):
            term = product(branch, high[:, 5632 + 512 * step : 6144 + 512 * step])
            for tile in range(4):
                put(term[:, 128 * tile : 128 * tile + 128], 36 + 4 * step + tile)
        if chunk == 0:
            local(0, 0).wait()
            crossing(0).wait()
        first = product(left(low, 0), low[:, 640:1664])
        second = product(left(high, 0), high[:, 1920:2560])
        for tile in range(7):
            put(first[:, 128 * tile : 128 * tile + 128], tile)
        put(first[:, 896:] + second[:, :128], 7)
        for tile in range(1, 5):
            put(second[:, 128 * tile : 128 * tile + 128], 7 + tile)

        @pl.loop(0, blocks)
        def _(block):
            start = pl.multiple_of(block * (3 * tiles), 3 * tiles)
            y, x, z = lax.div(block, 16), lax.rem(lax.div(block, SIDE), SIDE), lax.rem(block, SIDE)
            terms[chunk][y, x, z] = gathered[pl.ds(start, 3 * tiles), :].astype(jnp.bfloat16)

    def plane(sub):
        return [axis for axis in range(3) if axis != LINES[sub][0]]

    def own(chunk, sub, coordinate, half):
        axis = LINES[sub][0]
        index = {axis: coordinate, plane(sub)[0]: pl.ds(2 * half, 2), plane(sub)[1]: slice(None)}
        return terms[chunk].at[index[0], index[1], index[2], pl.ds(sub * tiles, tiles)]

    flying = {}

    def message(chunk, sub, way, number, source):
        copy = pltpu.make_async_remote_copy(
            src_ref=source,
            dst_ref=landing[chunk][sub].at[3 * way + number],
            send_sem=ring_send.at[chunk, sub, way, number],
            recv_sem=ring_recv.at[chunk, sub, way, number],
            device_id=device_at(section, at, LINES[sub][0], STEPS[way][1]),
            device_id_type=MESH,
        )
        copy.start()
        flying[chunk, sub, way, number] = copy

    def add(target, parts):
        @pl.loop(0, 2 * SIDE)
        def _(index):
            place = (lax.div(index, SIDE), lax.rem(index, SIDE))
            total = parts[0][place].astype(jnp.float32)
            for part in parts[1:]:
                total = total + part[place].astype(jnp.float32)
            target[place] = total.astype(jnp.bfloat16)

    def ring_start(chunk):
        for number in range(2):
            for sub in range(3):
                for way, step in STEPS:
                    coordinate = shifted(at, LINES[sub][0], 2 * step if number == 0 else step)
                    message(chunk, sub, way, number, own(chunk, sub, coordinate, (number + way) % 2))

    def ring_pass(chunk):
        for sub in range(3):
            for way, step in STEPS:
                flying[chunk, sub, way, 0].wait_recv()
                passing = landing[chunk][sub].at[3 * way]
                add(passing, (passing, own(chunk, sub, shifted(at, LINES[sub][0], step), way)))
                message(chunk, sub, way, 2, passing)

    def ring_sum(chunk):
        for sub in range(3):
            for way in range(2):
                flying[chunk, sub, way, 1].wait_recv()
                flying[chunk, sub, way, 2].wait_recv()
            for half in range(2):
                found = landing[chunk][sub]
                add(
                    sums[sub].at[chunk, pl.ds(2 * half, 2)],
                    (
                        own(chunk, sub, at[LINES[sub][0]], half),
                        found.at[3 * half + 2],
                        found.at[3 * (1 - half) + 1],
                    ),
                )

    local(0, 1).wait()
    local(0, 2).wait()
    chunk_terms(0)
    ring_start(0)
    chunk_terms(1)
    ring_start(1)
    ring_pass(0)
    chunk_terms(2)
    ring_start(2)
    ring_pass(1)
    ring_sum(0)
    ring_pass(2)
    ring_sum(1)
    ring_sum(2)

    def direct(sub, axis, step, source, target, send, recv):
        copy = pltpu.make_async_remote_copy(
            src_ref=source,
            dst_ref=target,
            send_sem=send.at[sub, step - 1],
            recv_sem=recv.at[sub, step - 1],
            device_id=device_at(section, at, axis, step),
            device_id_type=MESH,
        )
        copy.start()
        return copy

    def part_of(sub, coordinate):
        if plane(sub)[0] == LINES[sub][1]:
            return sums[sub].at[:, coordinate]
        return sums[sub].at[:, :, coordinate]

    seconds, thirds = [], []
    for step in (2, 1, 3):
        for sub in range(3):
            axis = LINES[sub][1]
            seconds.append(
                direct(sub, axis, step, part_of(sub, shifted(at, axis, step)), second_at[sub].at[step - 1], second_send, second_recv)
            )
    for copy in seconds:
        copy.wait_recv()
    for sub in range(3):
        mine = part_of(sub, at[LINES[sub][1]])

        @pl.loop(0, 3 * SIDE)
        def _(index, sub=sub, mine=mine):
            place = (lax.div(index, SIDE), lax.rem(index, SIDE))
            total = mine[place].astype(jnp.float32)
            for step in range(SIDE - 1):
                total = total + second_at[sub][(step,) + place].astype(jnp.float32)
            second_sum[sub][place] = total.astype(jnp.bfloat16)

        axis = LINES[sub][2]
        for step in (2, 1, 3):
            thirds.append(
                direct(
                    sub, axis, step, second_sum[sub].at[:, shifted(at, axis, step)], third_at[sub].at[step - 1],
                    third_send, third_recv,
                )
            )
    for copy in thirds:
        copy.wait_recv()
    for sub in range(3):
        for chunk in range(3):
            total = second_sum[sub][chunk, at[LINES[sub][2]]].astype(jnp.float32)
            for step in range(SIDE - 1):
                total = total + third_at[sub][step, chunk].astype(jnp.float32)
            out_ref[chunk, sub * tiles : (sub + 1) * tiles, :] = total
    for copy in list(flying.values()) + seconds + thirds:
        copy.wait_send()


LINES = ((1, 0, 2), (2, 1, 0), (0, 2, 1))


def weight_all(order, low_one, low_two, high_one, high_two, high_one_in, high_two_in, collective_id):
    rows, kind = low_one.shape[0], low_one.dtype
    tiles = 6144 // 128
    block = (tiles, 128)
    vmem, held = pl.BlockSpec(memory_space=pltpu.VMEM), pl.BlockSpec(memory_space=pl.ANY)
    semaphore = pltpu.SemaphoreType.DMA
    count = SIDE - 1
    return pl.pallas_call(
        weight_all_kernel,
        out_shape=jax.ShapeDtypeStruct((3, 3 * tiles, 128), jnp.float32),
        in_specs=[vmem] + [held] * 6,
        out_specs=vmem,
        scratch_shapes=[
            pltpu.VMEM((2 * rows, low_one.shape[1]), kind),
            pltpu.VMEM((2 * rows, high_one.shape[1]), kind),
            pltpu.VMEM((64 * 3 * tiles, 128), jnp.float32),
        ]
        + [pltpu.VMEM((SIDE, SIDE, SIDE, 3 * tiles, 128), kind) for _ in range(3)]
        + [pltpu.VMEM((3, SIDE, SIDE) + block, kind) for _ in range(3)]
        + [pltpu.VMEM((6, 2, SIDE) + block, kind) for _ in range(9)]
        + [pltpu.VMEM((count, 3, SIDE) + block, kind) for _ in range(3)]
        + [pltpu.VMEM((3, SIDE) + block, kind) for _ in range(3)]
        + [pltpu.VMEM((count, 3) + block, kind) for _ in range(3)]
        + [semaphore(shape) for shape in ((3, 3, 2, 3), (3, count), (3, count)) for _ in range(2)]
        + [semaphore, semaphore, semaphore((3,))],
        compiler_params=pltpu.CompilerParams(
            collective_id=collective_id, has_side_effects=True, vmem_limit_bytes=VMEM_LIMIT
        ),
        cost_estimate=pl.CostEstimate(flops=4 * rows * 576 * 6144, bytes_accessed=1 << 24, transcendentals=0),
    )(order, low_one, low_two, high_one, high_two, high_one_in, high_two_in)


TERMS_LOW = 1664
TERMS_HIGH = 7168


def dense(kernel, arguments, hbm, results, scratch, flops):
    vmem = pl.BlockSpec(memory_space=pltpu.VMEM)
    kept = [vmem] * (len(arguments) - hbm) + [pl.BlockSpec(memory_space=pl.ANY)] * hbm
    size = sum(item.size * item.dtype.itemsize for item in arguments)
    return pl.pallas_call(
        kernel,
        out_shape=tuple(jax.ShapeDtypeStruct(shape, kind) for shape, kind in results),
        in_specs=kept,
        out_specs=tuple(vmem for _ in results),
        scratch_shapes=scratch,
        compiler_params=pltpu.CompilerParams(vmem_limit_bytes=VMEM_LIMIT),
        cost_estimate=pl.CostEstimate(flops=flops, bytes_accessed=size, transcendentals=0),
    )(*arguments)


def on_device(inputs, positions, attn_gain, w_qkv, w_out, ffn_gain, w_gate_up, w_down, cotangent):
    _, rows, width = inputs.shape
    section = lax.axis_index("section")
    place = lax.axis_index(("ctx", "fsdp"))
    half_kind, kind = jnp.bfloat16, jnp.float32
    lanes = 2 * HEAD_DIM
    columns = w_qkv.shape[2] * SIDE
    wide_rows = 128 * (HEADS + KV_HEADS)

    depth = lax.axis_index("fsdp")
    batch = depth // 2
    worked = place + section * (SIDE - 1 - 2 * depth)
    spots_k = lax.dynamic_index_in_dim(positions, batch, 0, keepdims=False)
    spots_q = lax.dynamic_slice_in_dim(spots_k, worked * rows, rows, 0)
    chunk_of = spots_k[::CHUNK] // CHUNK
    inverse = jnp.zeros_like(chunk_of).at[chunk_of].set(jnp.arange(chunk_of.shape[0], dtype=jnp.int32))
    spots = lax.dynamic_slice_in_dim(chunk_of, worked * 2, 2, 0)
    frequency = rope_base ** (-(jnp.arange(HEAD_DIM // 2, dtype=kind) * 2.0 / HEAD_DIM))
    angle = spots_q.astype(kind)[:, None] * frequency[None, :]
    cosine, sine = jnp.cos(angle), jnp.sin(angle)
    rest = jnp.ones((rows, HEAD_DIM), kind)
    cosine = jnp.concatenate([cosine, cosine, rest], axis=1)
    sine = jnp.concatenate([-sine, sine, 0.0 * rest], axis=1)

    local_gains = jnp.pad(jnp.concatenate([attn_gain, ffn_gain], axis=0), ((0, 6), (0, 0)))
    qkv_turned = w_qkv[0].T
    qkv_first, gains, current, given = first_weight(
        qkv_turned, local_gains, inputs.transpose(0, 2, 1), cotangent.transpose(0, 2, 1)
    )
    qkv_first = qkv_first.reshape(columns, width)

    shards = [w_out[0].T, w_gate_up[0], w_down[0].T, qkv_turned]
    gain_one = [gains[l, 0:1] for l in range(2)]
    gain_two = [gains[l, 1:2] for l in range(2)]

    query_like = ((KV_HEADS, 2, GROUP * CHUNK, lanes), half_kind)
    inner_like = ((KV_HEADS, 2, GROUP * CHUNK, 1), kind)
    local_like = ((KV_HEADS, 2, CHUNK, lanes), half_kind)
    state_like = ((rows, width), kind)
    pair_like = ((SIDE, rows, 2 * FF // SIDE), kind)
    low_like = ((rows, TERMS_LOW), half_kind)
    high_like = ((rows, TERMS_HIGH), half_kind)
    wide_scratch = pltpu.VMEM((wide_rows, width), half_kind)
    qkv_scratch = pltpu.VMEM((columns, width), half_kind)
    ffn_scratch = [
        pltpu.VMEM((width, width), half_kind),
        pltpu.VMEM((SIDE, width, 2 * FF // SIDE), half_kind),
        pltpu.VMEM((width, FF), half_kind),
    ]
    sems = pltpu.SemaphoreType.DMA((4,))
    qkv_flops = 2 * rows * width * wide_rows
    ffn_flops = 2 * rows * width * (width + 3 * FF)

    def attention(layer, query, local, shards):
        mixed, logsum, both, out, gate_up, down, *rest = attend_all(
            layer, inverse, spots, local, query, shards, layer
        )
        weights = [out.reshape(width, width), gate_up, down.reshape(width, FF)]
        return both, mixed, logsum, weights, [item.reshape(columns, width) for item in rest]

    def attention_back(layer, query, grad, logsum, inner, both, high):
        grad_query, grad_both, high_in = attend_back_all(
            layer, inverse, spots, chunk_of, query, grad, logsum, inner, both, high, 4 + layer
        )
        return grad_query, grad_both.reshape(KV_HEADS, rows, lanes), high_in

    query_one, local = dense(
        enter_kernel, (current, gain_one[0], cosine, sine, qkv_first), 0, (query_like, local_like), [wide_scratch], qkv_flops
    )
    both_one, mixed_one, logsum_one, weights_one, (qkv_second,) = attention(0, query_one, local, shards)
    hidden, pair, middle, query_two, local = dense(
        between_kernel,
        (mixed_one, current, gain_two[0], gain_one[1], cosine, sine, *weights_one, qkv_second),
        4,
        (state_like, pair_like, state_like, query_like, local_like),
        ffn_scratch + [qkv_scratch, wide_scratch, sems],
        ffn_flops + qkv_flops,
    )
    both_two, mixed_two, logsum_two, weights_two, _ = attention(1, query_two, local, shards[:3])
    result, grad_hidden, high_two, grad, inner = dense(
        top_kernel,
        (mixed_two, middle, given, gain_two[1], *weights_two),
        3,
        (state_like, state_like, high_like, query_like, inner_like),
        ffn_scratch + [sems],
        2 * ffn_flops,
    )
    earlier = lax.ppermute(
        result,
        ("section", "ctx", "fsdp"),
        [(64 + 4 * ctx + z, 64 + 4 * ctx + 3 - z) for ctx in range(16) for z in range(4)],
    )
    grad_query, grad_local, high_two_in = attention_back(1, query_two, grad, logsum_two, inner, both_two, high_two)
    low_two, grad_hidden, high_one, grad, inner = dense(
        descend_kernel,
        (
            grad_query, grad_local, middle, grad_hidden, gain_one[1], cosine, sine,
            mixed_one, hidden, pair, gain_two[0], qkv_second, *weights_one,
        ),
        4,
        (low_like, state_like, high_like, query_like, inner_like),
        ffn_scratch + [qkv_scratch, wide_scratch, sems],
        ffn_flops + qkv_flops,
    )
    grad_query, grad_local, high_one_in = attention_back(0, query_one, grad, logsum_one, inner, both_one, high_one)
    grad_in, low_one = dense(
        leave_kernel,
        (grad_query, grad_local, current, grad_hidden, gain_one[0], cosine, sine, qkv_first),
        0,
        (state_like, low_like),
        [wide_scratch],
        qkv_flops,
    )

    first = section == 0
    blocks = SIDE * SIDE * SIDE
    each = width // blocks
    total = columns + width + 3 * FF
    line = jnp.arange(width)
    order = (line[:, None] % blocks * each + line[:, None] // blocks == line[None, :]).astype(half_kind)
    summed = weight_all(order, low_one, low_two, high_one, high_two, high_one_in, high_two_in, 2)
    summed = summed.reshape(each, total)
    grad_qkv = summed[:, :columns]
    grad_out_weight = summed[:, columns : columns + width]
    grad_gate_up = summed[:, columns + width : columns + width + 2 * FF]
    grad_down = summed[:, columns + width + 2 * FF :].T

    qkv_own = jnp.where(
        first,
        lax.dynamic_slice_in_dim(qkv_first, place * each, each, 1),
        lax.dynamic_slice_in_dim(qkv_second, place * each, each, 1),
    )
    qkv_own = qkv_own.astype(kind).T
    gate_up_own = jnp.where(
        first,
        lax.dynamic_slice_in_dim(weights_one[1], place * each, each, 1),
        lax.dynamic_slice_in_dim(weights_two[1], place * each, each, 1),
    ).astype(kind)
    split = grad_gate_up.reshape(each, SIDE, -1).transpose(1, 0, 2)
    grad_gain_one = jnp.sum(qkv_own * grad_qkv, axis=1) / lax.dynamic_slice_in_dim(attn_gain[0], place * each, each, 0)
    grad_gain_two = jnp.sum(gate_up_own * split, axis=(0, 2)) / lax.dynamic_slice_in_dim(
        ffn_gain[0], place * each, each, 0
    )

    def index_of(core, ctx, z):
        return (core * SIDE * SIDE + ctx) * SIDE + z

    places = [(ctx, z) for ctx in range(SIDE * SIDE) for z in range(SIDE)]
    axes = ("section", "ctx", "fsdp")
    later = lax.ppermute(
        jnp.where(first, result, grad_in),
        axes,
        [(index_of(0, ctx, z), index_of(1, ctx, z)) for ctx, z in places]
        + [(index_of(1, ctx, z), index_of(0, ctx, SIDE - 1 - z)) for ctx, z in places],
    )
    mine = jnp.where(first, grad_in, later)
    other = jnp.where(first, later, earlier)
    ends = jnp.where(batch == 0, jnp.stack([mine, other]), jnp.stack([other, mine]))
    return (
        ends[None],
        grad_gain_one[None],
        grad_qkv[None],
        grad_out_weight[None],
        grad_gain_two[None],
        grad_gate_up[None],
        grad_down[None],
    )


def solution(mesh):
    placed = (
        P(None, ("ctx", "fsdp"), None),
        P(),
        P("section", None),
        P("section", None, "fsdp"),
        P("section", None, "fsdp"),
        P("section", None),
        P("section", None, "fsdp"),
        P("section", None, "fsdp"),
        P(None, ("ctx", "fsdp"), None),
    )
    return jax.shard_map(
        on_device,
        mesh=mesh,
        in_specs=placed,
        out_specs=(
            P("section", None, ("ctx", "fsdp"), None),
            P("section", ("ctx", "fsdp")),
            P("section", ("ctx", "fsdp"), None),
            P("section", ("ctx", "fsdp"), None),
            P("section", ("ctx", "fsdp")),
            P("section", ("ctx", "fsdp"), None),
            P("section", None, ("ctx", "fsdp")),
        ),
        check_vma=False,
    )
```

```python
import functools

import jax
import jax.numpy as jnp
from jax import lax
from jax.experimental import pallas as pl
from jax.experimental.pallas import tpu as pltpu
from jax.sharding import PartitionSpec as P

HEADS = 9
KV_HEADS = 3
GROUP = 3
HEAD_DIM = 64
FF = 1536
CHUNK = 64
BLOCK = 512
PER = BLOCK // CHUNK
MESH = pl.DeviceIdType.MESH
VMEM_LIMIT = 56 * 1024 * 1024

epsilon = 1e-05
rope_base = 100000.0
contract_last = (((1,), (1,)), ((), ()))
contract_first = (((0,), (0,)), ((), ()))

SIDE = 4


def here():
    ctx = lax.axis_index("ctx")
    return (lax.axis_index("section"), (ctx // SIDE, lax.rem(ctx, SIDE), lax.axis_index("fsdp")))


def shifted(at, axis, step):
    return lax.rem(at[axis] + (step + SIDE), SIDE)


def device_at(section, at, axis, step):
    moved = list(at)
    moved[axis] = shifted(at, axis, step)
    return (section, moved[0] * SIDE + moved[1], moved[2])


def pair_step(at):
    return 1 - 2 * lax.rem(at[2], 2)


SIDES = (SIDE, SIDE, 2)
STEPS = ((0, 1), (1, -1))


class Team:
    def __init__(self):
        self.section, self.at = here()
        w = lax.rem(self.at[2], 2)
        h = self.at[2] // 2
        self.h = lax.rem(h + self.section, 2)
        self.spot = (self.at[0], self.at[1], lax.rem(w + self.section, 2))

    def beside(self):
        return (1 - self.section, self.at[0] * SIDE + self.at[1], self.at[2])

    def shifted(self, axis, step):
        return lax.rem(self.spot[axis] + (step + SIDE), SIDES[axis])

    def moved(self, steps):
        y, x = (lax.rem(self.at[axis] + (steps[axis] + SIDE), SIDE) for axis in range(2))
        z = self.at[2] + (pair_step(self.at) if steps[2] % 2 else 0)
        return (self.section, y * SIDE + x, z)

    def device(self, axis, step):
        return self.moved(tuple(step if other == axis else 0 for other in range(3)))

    def enter(self):
        barrier = pltpu.get_barrier_semaphore()
        devices = [self.moved(steps) for steps in STRAIGHT]
        devices += [self.beside(), device_at(self.section, self.at, 2, -pair_step(self.at))]
        for device in devices:
            pl.semaphore_signal(barrier, inc=1, device_id=device, device_id_type=MESH)
        pl.semaphore_wait(barrier, len(devices))


def visible(shape, chunk, block):
    row = lax.broadcasted_iota(jnp.int32, shape, 0)
    column = lax.broadcasted_iota(jnp.int32, shape, 1)
    return block * BLOCK + column <= chunk * CHUNK + lax.rem(row, CHUNK)


STEPS_UNMASKED = 15


STRAIGHT = ((1, 0, 0), (2, 0, 0), (3, 0, 0), (0, 1, 0), (0, 2, 0), (0, 3, 0), (0, 0, 1))


class Exchange:
    def __init__(self, team, sems):
        self.team, self.sems = team, sems

    def send(self, source, target, device, kind, *index):
        send, recv = self.sems[kind]
        copy = pltpu.make_async_remote_copy(
            src_ref=source,
            dst_ref=target,
            send_sem=send.at[index],
            recv_sem=recv.at[index],
            device_id=device,
            device_id_type=MESH,
        )
        copy.start()
        return copy


class PartGather:
    def __init__(self, part, exchange, local_ref, keys):
        self.part, self.exchange, self.team = part, exchange, exchange.team
        self.local_ref, self.keys = local_ref, keys
        self.near, self.ring, self.side = [], {}, []

    def slab(self, unit, coordinate, w=slice(None)):
        y, x = (coordinate, slice(None)) if unit == 0 else (slice(None), coordinate)
        return self.keys.at[y, x, self.team.h, w, unit]

    def start_near(self):
        spot = self.team.spot
        for unit in range(2):
            for step in range(1, SIDE):
                steps = (0, step, 0) if unit == 0 else (step, 0, 0)
                place = self.keys.at[spot[0], spot[1], self.team.h, :, unit]
                self.near.append(
                    self.exchange.send(place, place, self.team.moved(steps), "near", self.part, unit, step - 1)
                )

    def message(self, unit, way, number, coordinate, w):
        place = self.slab(unit, coordinate, w)
        self.ring[unit, way, number] = self.exchange.send(
            place, place, self.team.device(unit, STEPS[way][1]), "ring", self.part, unit, way, number
        )

    def aside(self, unit, slot, coordinate):
        place = self.slab(unit, coordinate)
        self.side.append(
            self.exchange.send(place, place, self.team.beside(), "side", self.part, unit, slot)
        )

    def start_ring(self):
        for copy in self.near:
            copy.wait_recv()
        for number in range(2):
            for unit in range(2):
                for way, _ in STEPS:
                    self.message(unit, way, number, self.team.spot[unit], (number + way) % 2)
        for unit in range(2):
            self.aside(unit, 0, self.team.spot[unit])

    def pass_on(self):
        for unit in range(2):
            for way, step in STEPS:
                self.ring[unit, way, 0].wait_recv()
                self.message(unit, way, 2, self.team.shifted(unit, -step), way)

    def share(self):
        for unit in range(2):
            for way, step in STEPS:
                self.ring[unit, way, 1].wait_recv()
                self.aside(unit, 1 + way, self.team.shifted(unit, -step))
        for unit in range(2):
            for way, _ in STEPS:
                self.ring[unit, way, 2].wait_recv()
            self.aside(unit, 3, self.team.shifted(unit, 2))

    def finish(self):
        for copy in self.side:
            copy.wait_recv()

    def drain(self):
        for copy in self.near + list(self.ring.values()) + self.side:
            copy.wait_send()


class WeightGather:
    def __init__(self, owner, number, exchange, local_ref, out_ref):
        self.owner, self.number, self.exchange, self.team = owner, number, exchange, exchange.team
        self.local_ref, self.out_ref = local_ref, out_ref
        self.place = self.team.at[2]
        rows = local_ref.shape[0]
        middle = rows // 32 * 16
        if number % 2 == 0:
            middle = rows - middle
        self.rows = ((0, middle), (middle, rows))

    def each(self, body, roles=(0, 1)):
        for role in roles:

            @pl.when(self.team.section == (self.owner if role == 0 else 1 - self.owner))
            def _(role=role):
                body(role)

    def index(self, step):
        return lax.rem(self.place + (step + SIDE), SIDE)

    def message(self, role, way, number, start=True):
        low, high = self.rows[role]
        split = low + (high - low + 16) // 32 * 16
        low, high = (low, split) if (number + way) % 2 == 0 else (split, high)
        rows = pl.ds(low, high - low)
        spot = self.out_ref.at[self.place if number < 2 else self.index(-STEPS[way][1]), rows]
        source = self.local_ref.at[rows] if number < 2 and role == 0 else spot
        device = device_at(self.team.section, self.team.at, 2, STEPS[way][1])
        return self.copy(source, spot, device, "weight_ring", start, way, number)

    def aside(self, role, slot, start=True):
        if slot == 0:
            return self.copy(self.local_ref, self.out_ref.at[self.place], self.team.beside(), "weight_side", start, 0)
        low, high = self.rows[role]
        spot = self.out_ref.at[self.index((-1, 1, 2)[slot - 1]), pl.ds(low, high - low)]
        return self.copy(spot, spot, self.team.beside(), "weight_side", start, slot)

    def copy(self, source, target, device, kind, start, *index):
        send, recv = self.exchange.sems[kind]
        place = (self.number,) + index
        copy = pltpu.make_async_remote_copy(
            src_ref=source,
            dst_ref=target,
            send_sem=send.at[place],
            recv_sem=recv.at[place],
            device_id=device,
            device_id_type=MESH,
        )
        if start:
            copy.start()
        return copy

    def own(self):
        return pltpu.make_async_copy(
            self.local_ref, self.out_ref.at[self.place], self.exchange.sems["weight_own"].at[self.number]
        )

    def start_ring(self, role):
        for number in range(2):
            for way in range(2):
                self.message(role, way, number)

    def start(self):
        def body(role):
            self.own().start()
            self.aside(0, 0)
            self.start_ring(0)

        self.each(body, (0,))

    def start_beside(self):
        def body(role):
            self.aside(0, 0, False).wait_recv()
            self.start_ring(1)

        self.each(body, (1,))

    def pass_on(self):
        def body(role):
            for way in range(2):
                self.message(role, way, 0, False).wait_recv()
                self.message(role, way, 2)

        self.each(body)

    def hand(self):
        def body(role):
            for way in range(2):
                self.message(role, way, 1, False).wait_recv()
                self.aside(role, 1 + way)

        self.each(body)

    def share(self):
        def body(role):
            for way in range(2):
                self.message(role, way, 2, False).wait_recv()
            self.aside(role, 3)

        self.each(body)

    def finish(self):
        def body(role):
            for way in range(2):
                for number in range(3):
                    self.message(role, way, number, False).wait_send()
            for slot in range(1, 4):
                self.aside(role, slot, False).wait_send()
                self.aside(1 - role, slot, False).wait_recv()
            if role == 0:
                self.own().wait()
                self.aside(0, 0, False).wait_send()

        self.each(body)


EXP = jnp.exp


def key_block(inverse_ref, keys, block):
    pieces = []
    for index in range(PER):
        place = inverse_ref[block * PER + index]
        y = lax.shift_right_logical(place, 5)
        x, h, w, half = (
            lax.bitwise_and(lax.shift_right_logical(place, shift), mask) for shift, mask in ((3, 3), (2, 1), (1, 1), (0, 1))
        )
        pieces.append(keys[y, x, h, w, half])
    return jnp.concatenate(pieces, axis=0)


def schedule(spots_ref):
    return lax.shift_right_logical(spots_ref[0], 3), lax.shift_right_logical(spots_ref[1], 3)


def attend_all_kernel(
    owner, inverse_ref, spots_ref, local_ref, query_ref, *refs
):
    count = 4 if owner == 0 else 3
    shard_refs, refs = refs[:count], refs[count:]
    (mixed_ref, logsum_ref, both_ref), refs = refs[:3], refs[3:]
    whole_refs, refs = refs[:count], refs[count:]
    keys, (highest_at, mixed_at), refs = refs[:3], refs[3:5], refs[5:]
    sems = {
        "near": refs[0:2], "ring": refs[2:4], "side": refs[4:6],
        "weight_ring": refs[6:8], "weight_side": refs[8:10], "pair": refs[10:12], "weight_own": refs[12],
    }
    kept = refs[13]
    team = Team()
    team.enter()
    exchange = Exchange(team, sems)
    spot, h = team.spot, team.h
    parts = [PartGather(part, exchange, local_ref, keys[part]) for part in range(KV_HEADS)]
    weights = [
        WeightGather(owner if number < 3 else 1 - owner, number, exchange, shard_refs[number], whole_refs[number])
        for number in range(count)
    ]
    own = [
        pltpu.make_async_copy(local_ref.at[part], keys[part].at[spot[0], spot[1], h, spot[2]], kept.at[part])
        for part in range(KV_HEADS)
    ]
    saved = [
        pltpu.make_async_copy(keys[part], both_ref.at[part], kept.at[KV_HEADS + part]) for part in range(KV_HEADS)
    ]
    ends = schedule(spots_ref)

    def attend_scores(part, half, block):
        both = key_block(inverse_ref, keys[part], block)
        return lax.dot_general(
            query_ref[part, half], both, contract_last, preferred_element_type=jnp.float32
        )

    def attend_rest(part, scores, block, highest, mixed):
        both = key_block(inverse_ref, keys[part], block)
        higher = jnp.maximum(highest, jnp.broadcast_to(jnp.max(scores, axis=-1, keepdims=True), highest.shape))
        exponent = EXP(scores - jnp.concatenate([higher] * (BLOCK // 128), axis=1)).astype(jnp.bfloat16)
        values = jnp.where(is_lower(both.shape), jnp.bfloat16(1.0), both)
        return higher, jnp.dot(exponent, values, preferred_element_type=jnp.float32) + EXP(highest - higher) * mixed

    def attend_first(part):
        for half in range(2):
            scores = attend_scores(part, half, ends[half])
            scores = jnp.where(visible(scores.shape, spots_ref[half], ends[half]), scores, -1e30)
            highest, mixed = attend_rest(
                part, scores, ends[half], jnp.full((scores.shape[0], 128), -1e30, jnp.float32), jnp.zeros((scores.shape[0], 128), jnp.float32)
            )
            highest_at[half] = highest
            mixed_at[half] = mixed

    def attend_some(part, low, high):
        if True:
            size = high - low
            steps = [low + index for index in range(size)]
            halves = [jnp.where(step >= ends[0], 1, 0) for step in steps]
            blocks = [step - half * ends[0] for step, half in zip(steps, halves)]
            befores = [jnp.where(step == ends[0], 1, jnp.where(step == 0, 0, step + 1)) for step in steps]
            scores = attend_scores(part, halves[0], blocks[0])
            for index in range(size):
                later = attend_scores(part, halves[index + 1], blocks[index + 1]) if index + 1 < size else None
                before = befores[index]
                highest, mixed = attend_rest(part, scores, blocks[index], highest_at[before], mixed_at[before])
                highest_at[steps[index] + 2] = highest
                mixed_at[steps[index] + 2] = mixed
                scores = later

    def attend_last(part):
        last = (
            jnp.where(ends[0] == 0, 0, ends[0] + 1),
            jnp.where(ends[0] == STEPS_UNMASKED, 1, STEPS_UNMASKED + 1),
        )
        for half in range(2):
            mixed = mixed_at[last[half]]
            total = mixed[:, :1]
            mixed_ref[part, half] = mixed / total
            logsum_ref[part, half] = highest_at[last[half]][:, :1] + jnp.log(total)

    pairs = [
        exchange.send(
            local_ref.at[part], keys[part].at[spot[0], spot[1], h, spot[2]], team.device(2, 1), "pair", part
        )
        for part in range(KV_HEADS)
    ]
    for copy in own:
        copy.start()
    for weight in weights:
        weight.start()
    for part in range(KV_HEADS):
        own[part].wait()
        pairs[part].wait_recv()
        parts[part].start_near()
    parts[0].start_ring()
    for weight in weights:
        weight.start_beside()
    parts[0].pass_on()
    parts[1].start_ring()
    parts[0].share()
    parts[1].pass_on()
    parts[2].start_ring()
    parts[0].finish()
    saved[0].start()
    attend_first(0)
    attend_some(0, 0, 7)
    parts[1].share()
    parts[2].pass_on()
    attend_some(0, 7, 15)
    for weight in weights:
        weight.pass_on()
    attend_last(0)
    parts[1].finish()
    saved[1].start()
    attend_first(1)
    attend_some(1, 0, 7)
    parts[2].share()
    for weight in weights:
        weight.hand()
    attend_some(1, 7, 15)
    attend_last(1)
    parts[2].finish()
    saved[2].start()
    attend_first(2)
    for weight in weights:
        weight.share()
    attend_some(2, 0, 15)
    attend_last(2)
    for copy in pairs:
        copy.wait_send()
    for part in parts:
        part.drain()
    for weight in weights:
        weight.finish()
    for copy in saved:
        copy.wait()


def attend_all(owner, inverse, spots, local, query, shards, collective_id):
    groups, halves, rows, lanes = query.shape
    count = len(shards)
    keys = (SIDE, SIDE, 2, 2, 2, CHUNK, lanes)
    vmem, smem, held = (pl.BlockSpec(memory_space=space) for space in (pltpu.VMEM, pltpu.SMEM, pl.ANY))
    slots = STEPS_UNMASKED + 2
    scores = rows * BLOCK * slots * groups
    semaphore = pltpu.SemaphoreType.DMA
    return pl.pallas_call(
        functools.partial(attend_all_kernel, owner),
        out_shape=(
            jax.ShapeDtypeStruct((groups, halves, rows, lanes), jnp.float32),
            jax.ShapeDtypeStruct((groups, halves, rows, 1), jnp.float32),
            jax.ShapeDtypeStruct((groups,) + keys, local.dtype),
        )
        + tuple(jax.ShapeDtypeStruct((SIDE,) + item.shape, item.dtype) for item in shards),
        in_specs=[smem, smem, vmem, vmem] + [vmem] * count,
        out_specs=(vmem, vmem, held) + (held,) * count,
        scratch_shapes=[pltpu.VMEM(keys, local.dtype) for _ in range(groups)]
        + [
            pltpu.VMEM((slots, rows, lanes), jnp.float32),
            pltpu.VMEM((slots, rows, lanes), jnp.float32),
        ]
        + [semaphore(shape) for shape in ((3, 2, 3), (3, 2, 2, 3), (3, 2, 4), (count, 2, 3), (count, 4), (3,)) for _ in range(2)]
        + [semaphore((count,)), semaphore((2 * groups,))],
        compiler_params=pltpu.CompilerParams(
            collective_id=collective_id, has_side_effects=True, vmem_limit_bytes=VMEM_LIMIT
        ),
        cost_estimate=pl.CostEstimate(flops=4 * scores * lanes, bytes_accessed=128 * local.size, transcendentals=scores),
    )(inverse, spots, local, query, *shards)


class PartScatter:
    def __init__(self, part, exchange, terms, joined, landing, sums, near, pair, out_ref):
        self.part, self.exchange, self.team = part, exchange, exchange.team
        self.terms, self.joined, self.landing, self.sums = terms, joined, landing, sums
        self.near, self.pair, self.out_ref = near, pair, out_ref
        self.sides, self.rings, self.nears, self.pairs = [], [], [], []

    def swap(self):
        for unit in range(2):
            source = self.terms.at[:, :, 1 - self.team.h, :, unit]
            self.sides.append(
                self.exchange.send(source, self.joined.at[unit], self.team.beside(), "side", self.part, unit)
            )

    def send_ring(self):
        for unit in range(2):
            self.sides[unit].wait_recv()

            @pl.loop(0, SIDE * SIDE)
            def _(index, unit=unit):
                y, x = lax.div(index, SIDE), lax.rem(index, SIDE)
                own = self.terms[y, x, self.team.h, :, unit].astype(jnp.float32)
                other = self.joined[unit, y, x].astype(jnp.float32)
                self.joined[unit, y, x] = (own + other).astype(jnp.bfloat16)

            for step in (2, 1, 3):
                coordinate = self.team.shifted(unit, step)
                place = self.joined.at[unit, coordinate] if unit == 0 else self.joined.at[unit, :, coordinate]
                steps = (step, 0, 0) if unit == 0 else (0, step, 0)
                self.rings.append(
                    self.exchange.send(
                        place, self.landing.at[unit, step - 1], self.team.moved(steps), "ring", self.part, unit, step - 1
                    )
                )

    def send_near(self):
        for copy in self.rings:
            copy.wait_recv()
        for unit in range(2):
            mine = self.team.spot[unit]
            for index in range(SIDE):
                place = (unit, mine, index) if unit == 0 else (unit, index, mine)
                total = self.joined[place].astype(jnp.float32)
                for step in range(SIDE - 1):
                    total = total + self.landing[unit, step, index].astype(jnp.float32)
                self.sums[unit, index] = total.astype(jnp.bfloat16)
            for step in range(1, SIDE):
                steps = (0, step, 0) if unit == 0 else (step, 0, 0)
                self.nears.append(
                    self.exchange.send(
                        self.sums.at[unit, self.team.shifted(1 - unit, step)], self.near.at[unit, step - 1],
                        self.team.moved(steps), "near", self.part, unit, step - 1,
                    )
                )

    def send_pair(self):
        for copy in self.nears:
            copy.wait_recv()
        w = self.team.spot[2]
        for unit in range(2):
            mine = self.team.spot[1 - unit]
            for index in range(2):
                place = w if index == 0 else 1 - w
                total = self.sums[unit, mine, place].astype(jnp.float32)
                for step in range(SIDE - 1):
                    total = total + self.near[unit, step, place].astype(jnp.float32)
                if index == 0:
                    self.out_ref[self.part, unit] = total
                else:
                    self.pair[0, unit] = total.astype(jnp.bfloat16)
        self.pairs.append(
            self.exchange.send(self.pair.at[0], self.pair.at[1], self.team.device(2, 1), "pair", self.part)
        )

    def finish(self):
        self.pairs[0].wait_recv()
        for unit in range(2):
            self.out_ref[self.part, unit] = self.out_ref[self.part, unit] + self.pair[1, unit].astype(jnp.float32)
        for copy in self.sides + self.rings + self.nears + self.pairs:
            copy.wait_send()


def attend_back_all_kernel(
    layer, inverse_ref, spots_ref, chunk_ref, query_ref, grad_ref, logsum_ref, inner_ref, both_ref, terms_ref,
    grad_query_ref, out_ref, terms_in_ref, *refs
):
    keys, refs = refs[:3], refs[3:]
    terms, refs = refs[:3], refs[3:]
    buffers, refs = [refs[5 * part : 5 * part + 5] for part in range(3)], refs[15:]
    logsum_at, inner_at, query_at, grad_at, *refs = refs
    sems = {kind: refs[2 * index : 2 * index + 2] for index, kind in enumerate(("side", "ring", "near", "pair"))}
    kept = refs[8]
    terms_send, terms_recv = refs[9:]
    team = Team()
    brought_in = [pltpu.make_async_copy(both_ref.at[part], keys[part], kept.at[part]) for part in range(KV_HEADS)]
    for copy in brought_in:
        copy.start()
    team.enter()
    exchange = Exchange(team, sems)
    parts = [
        PartScatter(part, exchange, terms[part], *buffers[part], out_ref) for part in range(KV_HEADS)
    ]
    ends = schedule(spots_ref)
    for part in range(KV_HEADS):
        for half in range(2):
            logsum_at[part, half] = jnp.broadcast_to(logsum_ref[part, half], logsum_at.shape[2:])
            inner_at[part, half] = jnp.broadcast_to(inner_ref[part, half], inner_at.shape[2:])

    grad_at[STEPS_UNMASKED + 2] = jnp.zeros(grad_at.shape[1:], jnp.float32)

    def products(part, half, block):
        both = key_block(inverse_ref, keys[part], block)
        scores = lax.dot_general(query_ref[part, half], both, contract_last, preferred_element_type=jnp.float32)
        grad_weights = lax.dot_general(grad_ref[part, half], both, contract_last, preferred_element_type=jnp.float32)
        return scores, grad_weights

    def rest(part, slot, half, block, found, masked, before):
        scores, grad_weights = found
        both = key_block(inverse_ref, keys[part], block)
        logsum = jnp.concatenate([logsum_at[part, half]] * (BLOCK // 128), axis=1)
        inner = jnp.concatenate([inner_at[part, half]] * (BLOCK // 128), axis=1)
        probs = EXP(scores - logsum)
        if masked:
            probs = jnp.where(visible(scores.shape, spots_ref[half], block), probs, 0.0)
        grad_scores = (probs * (grad_weights - inner)).astype(jnp.bfloat16)
        grad_query = jnp.dot(grad_scores, both, preferred_element_type=jnp.float32)
        query_at[slot] = grad_query if before is None else grad_query + query_at[before]
        grad_at[slot] = lax.dot_general(
            jnp.concatenate([probs.astype(jnp.bfloat16), grad_scores], axis=0),
            jnp.concatenate([grad_ref[part, half], query_ref[part, half]], axis=0),
            contract_first,
            preferred_element_type=jnp.float32,
        ).reshape(PER, CHUNK, 2 * HEAD_DIM)

    def back_first(part):
        for half in range(2):
            rest(part, half, half, ends[half], products(part, half, ends[half]), True, None)

    def back_some(part, low, high):
        steps = list(range(low, high))
        halves = [jnp.where(step >= ends[0], 1, 0) for step in steps]
        blocks = [step - half * ends[0] for step, half in zip(steps, halves)]
        found = products(part, halves[0], blocks[0])
        for index, step in enumerate(steps):
            later = products(part, halves[index + 1], blocks[index + 1]) if index + 1 < len(steps) else None
            before = jnp.where(step == ends[0], 1, jnp.where(step == 0, 0, step + 1))
            rest(part, step + 2, halves[index], blocks[index], found, False, before)
            found = later

    def back_last(part):
        last = (
            jnp.where(ends[0] == 0, 0, ends[0] + 1),
            jnp.where(ends[0] == STEPS_UNMASKED, 1, STEPS_UNMASKED + 1),
        )
        for half in range(2):
            grad_query_ref[part, half] = query_at[last[half]]

        @pl.loop(0, SIDE * SIDE)
        def _(column):
            y, x = lax.div(column, SIDE), lax.rem(column, SIDE)
            for number in range(8):
                chunk = chunk_ref[8 * column + number]
                row = lax.bitwise_and(chunk, PER - 1)
                block = lax.shift_right_logical(chunk, 3)
                total = None
                for half in range(2):
                    slot = jnp.where(block == ends[half], half, 2 + half * ends[0] + block)
                    term = grad_at[jnp.where(block <= ends[half], slot, STEPS_UNMASKED + 2), row]
                    total = term if total is None else total + term
                terms[part][y, x, number // 4, number // 2 % 2, number % 2] = total.astype(jnp.bfloat16)

    crossing = pltpu.make_async_remote_copy(
        src_ref=terms_ref,
        dst_ref=terms_in_ref,
        send_sem=terms_send,
        recv_sem=terms_recv,
        device_id=team.beside(),
        device_id_type=MESH,
    )

    @pl.when(team.section != layer)
    def _():
        crossing.start()

    def begin(part):
        brought_in[part].wait()
        back_first(part)
        back_some(part, 0, 5)

    begin(0)
    back_some(0, 5, 15)
    back_last(0)
    parts[0].swap()
    begin(1)
    back_some(1, 5, 10)
    parts[0].send_ring()
    back_some(1, 10, 15)
    back_last(1)
    parts[1].swap()
    begin(2)
    back_some(2, 5, 10)
    parts[1].send_ring()
    back_some(2, 10, 15)
    back_last(2)
    parts[2].swap()
    parts[0].send_near()
    parts[2].send_ring()
    parts[0].send_pair()
    parts[1].send_near()
    parts[0].finish()
    parts[1].send_pair()
    parts[2].send_near()
    parts[1].finish()
    parts[2].send_pair()
    parts[2].finish()

    @pl.when(team.section != layer)
    def _():
        crossing.wait_send()

    @pl.when(team.section == layer)
    def _():
        crossing.wait_recv()


def attend_back_all(layer, inverse, spots, chunk_of, query, grad, logsum, inner, both, high, collective_id):
    groups, halves, rows, lanes = query.shape
    keys = both.shape[1:]
    kind = both.dtype
    block = (CHUNK, lanes)
    vmem, smem = (pl.BlockSpec(memory_space=space) for space in (pltpu.VMEM, pltpu.SMEM))
    slots = STEPS_UNMASKED + 2
    scores = rows * BLOCK * slots * groups
    semaphore = pltpu.SemaphoreType.DMA
    buffers = [
        pltpu.VMEM((2, SIDE, SIDE, 2) + block, kind),
        pltpu.VMEM((2, 3, SIDE, 2) + block, kind),
        pltpu.VMEM((2, SIDE, 2) + block, kind),
        pltpu.VMEM((2, 3, 2) + block, kind),
        pltpu.VMEM((2, 2) + block, kind),
    ]
    return pl.pallas_call(
        functools.partial(attend_back_all_kernel, layer),
        out_shape=(
            jax.ShapeDtypeStruct((groups, halves, rows, lanes), jnp.float32),
            jax.ShapeDtypeStruct((groups, 2) + block, jnp.float32),
            jax.ShapeDtypeStruct(high.shape, high.dtype),
        ),
        in_specs=[smem] * 3 + [vmem] * 4 + [pl.BlockSpec(memory_space=pl.ANY)] * 2,
        out_specs=(vmem, vmem, pl.BlockSpec(memory_space=pl.ANY)),
        scratch_shapes=[pltpu.VMEM(keys, kind) for _ in range(2 * groups)]
        + buffers * groups
        + [
            pltpu.VMEM((groups, halves, rows, lanes), jnp.float32),
            pltpu.VMEM((groups, halves, rows, lanes), jnp.float32),
            pltpu.VMEM((slots, rows, lanes), jnp.float32),
            pltpu.VMEM((slots + 1, PER) + block, jnp.float32),
        ]
        + [semaphore(shape) for shape in ((3, 2), (3, 2, 3), (3, 2, 3), (3,)) for _ in range(2)]
        + [semaphore((groups,)), semaphore, semaphore],
        compiler_params=pltpu.CompilerParams(
            collective_id=collective_id, has_side_effects=True, vmem_limit_bytes=VMEM_LIMIT
        ),
        cost_estimate=pl.CostEstimate(flops=10 * scores * lanes, bytes_accessed=4 * both.size, transcendentals=scores),
    )(inverse, spots, chunk_of, query, grad, logsum, inner, both, high)


def first_weight_kernel(
    local_ref, gains_ref, inputs_ref, cotangent_ref, out_ref, gains_out_ref, current_ref, given_ref,
    send, recv, side_send, side_recv, gain_send, gain_recv, token_send, token_recv, kept,
):
    rows = local_ref.shape[0]
    halves = (pl.ds(0, 128), pl.ds(128, rows - 128))
    section, at = here()
    place = at[2]
    beside = (1 - section, at[0] * SIDE + at[1], place)
    barrier = pltpu.get_barrier_semaphore()
    for device in (device_at(section, at, 2, 1), device_at(section, at, 2, -1), beside):
        pl.semaphore_signal(barrier, inc=1, device_id=device, device_id_type=MESH)
    pl.semaphore_wait(barrier, 3)
    own_gains = pltpu.make_async_copy(gains_ref, gains_out_ref.at[section], kept.at[0])
    own_gains.start()
    other_gains = pltpu.make_async_remote_copy(
        src_ref=gains_ref,
        dst_ref=gains_out_ref.at[section],
        send_sem=gain_send,
        recv_sem=gain_recv,
        device_id=beside,
        device_id_type=MESH,
    )
    other_gains.start()

    batch = place // 2
    partner = (section, at[0] * SIDE + at[1], SIDE - 1 - place)
    tokens = ((inputs_ref, current_ref), (cotangent_ref, given_ref))

    def crossing(number):
        source, target = tokens[number]
        return pltpu.make_async_remote_copy(
            src_ref=source.at[1 - batch],
            dst_ref=target,
            send_sem=token_send.at[number],
            recv_sem=token_recv.at[number],
            device_id=partner,
            device_id_type=MESH,
        )

    def staying(number):
        source, target = tokens[number]
        return pltpu.make_async_copy(source.at[batch], target, kept.at[2 + number])

    def aside(number, source):
        index = lax.rem(place + (0, 3, 1, 2)[number], SIDE)
        return pltpu.make_async_remote_copy(
            src_ref=out_ref.at[index] if source is None else source,
            dst_ref=out_ref.at[index],
            send_sem=side_send.at[number],
            recv_sem=side_recv.at[number],
            device_id=beside,
            device_id_type=MESH,
        )

    def message(way, number, step, index, half, source):
        spot = out_ref.at[index, halves[half]]
        return pltpu.make_async_remote_copy(
            src_ref=spot if source is None else source.at[halves[half]],
            dst_ref=spot,
            send_sem=send.at[way, number],
            recv_sem=recv.at[way, number],
            device_id=device_at(section, at, 2, step),
            device_id_type=MESH,
        )

    @pl.when(section == 0)
    def _():
        own = pltpu.make_async_copy(local_ref, out_ref.at[place], kept.at[1])
        own.start()
        for number in range(2):
            staying(number).start()
        flying = {}
        for number in range(2):
            for way, step in enumerate((1, -1)):
                flying[way, number] = message(way, number, step, place, (number + way) % 2, local_ref)
                flying[way, number].start()
        sides = [aside(0, local_ref)]
        sides[0].start()
        for way, step in enumerate((1, -1)):
            flying[way, 0].wait_recv()
            flying[way, 2] = message(way, 2, step, shifted(at, 2, -step), way, None)
            flying[way, 2].start()
        for way in range(2):
            flying[way, 1].wait_recv()
            sides.append(aside(1 + way, None))
            sides[-1].start()
        for way in range(2):
            flying[way, 2].wait_recv()
        sides.append(aside(3, None))
        sides[-1].start()
        for side in sides:
            side.wait_send()
        for way in range(2):
            for number in range(3):
                flying[way, number].wait_send()
        own.wait()
        for number in range(2):
            staying(number).wait()

    @pl.when(section == 1)
    def _():
        for number in range(2):
            crossing(number).start()
        for number in range(2):
            crossing(number).wait()
        for number in range(4):
            aside(number, None).wait_recv()

    own_gains.wait()
    other_gains.wait()


def first_weight(local, gains, inputs, cotangent):
    rows, columns = local.shape
    any_space = pl.BlockSpec(memory_space=pl.ANY)
    return pl.pallas_call(
        first_weight_kernel,
        out_shape=(
            jax.ShapeDtypeStruct((SIDE, rows, columns), local.dtype),
            jax.ShapeDtypeStruct((2,) + gains.shape, gains.dtype),
            jax.ShapeDtypeStruct(inputs.shape[1:], inputs.dtype),
            jax.ShapeDtypeStruct(cotangent.shape[1:], cotangent.dtype),
        ),
        in_specs=[pl.BlockSpec(memory_space=pltpu.VMEM)] * 4,
        out_specs=(any_space,) * 4,
        scratch_shapes=[
            pltpu.SemaphoreType.DMA((2, 3)),
            pltpu.SemaphoreType.DMA((2, 3)),
            pltpu.SemaphoreType.DMA((4,)),
            pltpu.SemaphoreType.DMA((4,)),
            pltpu.SemaphoreType.DMA,
            pltpu.SemaphoreType.DMA,
            pltpu.SemaphoreType.DMA((2,)),
            pltpu.SemaphoreType.DMA((2,)),
            pltpu.SemaphoreType.DMA((4,)),
        ],
        compiler_params=pltpu.CompilerParams(collective_id=3, has_side_effects=True),
        cost_estimate=pl.CostEstimate(flops=0, bytes_accessed=8 * local.size, transcendentals=0),
    )(local, gains, inputs, cotangent)


def normalize(values):
    factor = lax.rsqrt(jnp.mean(values * values, axis=-1, keepdims=True) + epsilon)
    return (values * factor, factor)


def norm_back(grad_unit, unit, factor):
    return factor * (grad_unit - unit * jnp.mean(grad_unit * unit, axis=-1, keepdims=True))


def product(left, right):
    return jnp.dot(left, right, preferred_element_type=jnp.float32)


def product_turned(left, right):
    return lax.dot_general(left, right, contract_last, preferred_element_type=jnp.float32)


def is_lower(shape):
    return lax.broadcasted_iota(jnp.int32, shape, len(shape) - 1) < HEAD_DIM


def turned(tile, cosine, sine):
    half = HEAD_DIM // 2
    lane = lax.broadcasted_iota(jnp.int32, tile.shape, 1)
    other = jnp.where(
        lax.rem(lane, HEAD_DIM) < half, pltpu.roll(tile, 128 - half, 1), pltpu.roll(tile, half, 1)
    )
    return tile * cosine + other * sine


def swapped(tile):
    return pltpu.roll(tile, HEAD_DIM, 1)


def head_rows(ref, head):
    group, index = head // GROUP, head % GROUP
    rows = slice(index * CHUNK, (index + 1) * CHUNK)
    return jnp.concatenate([ref[group, 0, rows, :], ref[group, 1, rows, :]], axis=0)


def put_head(ref, head, tile):
    group, index = head // GROUP, head % GROUP
    rows = slice(index * CHUNK, (index + 1) * CHUNK)
    ref[group, 0, rows, :] = tile[:CHUNK]
    ref[group, 1, rows, :] = tile[CHUNK:]


def widen(wide, qkv):
    for head in range(HEADS):
        wide[128 * head : 128 * head + 64, :] = qkv[64 * head : 64 * head + 64, :]
        wide[128 * head + 64 : 128 * head + 128, :] = jnp.zeros((64, wide.shape[1]), wide.dtype)
    for group in range(KV_HEADS):
        start = 128 * (HEADS + group)
        wide[start : start + 64, :] = qkv[576 + 64 * group : 640 + 64 * group, :]
        wide[start + 64 : start + 128, :] = qkv[768 + 64 * group : 832 + 64 * group, :]


def project(current, gain, wide, cosine, sine, query_ref, local_ref):
    unit, _ = normalize(current)
    projected = product_turned((unit * gain).astype(jnp.bfloat16), wide[...])
    for head in range(HEADS):
        tile = turned(projected[:, 128 * head : 128 * head + 128], cosine, sine) * HEAD_DIM ** (-0.5)
        put_head(query_ref, head, tile.astype(jnp.bfloat16))
    for group in range(KV_HEADS):
        start = 128 * (HEADS + group)
        tile = turned(projected[:, start : start + 128], cosine, sine).astype(jnp.bfloat16)
        local_ref[group, 0] = tile[:CHUNK]
        local_ref[group, 1] = tile[CHUNK:]


def project_back(grad_query_ref, grad_local_ref, current, grad_hidden, gain, wide, cosine, sine, terms_ref):
    lower = is_lower((2 * CHUNK, 128))
    tiles = []
    for head in range(HEADS):
        tile = jnp.where(lower, head_rows(grad_query_ref, head), 0.0)
        tiles.append(turned(tile, cosine, -sine) * HEAD_DIM ** (-0.5))
    for group in range(KV_HEADS):
        tiles.append(turned(grad_local_ref[group], cosine, -sine))
    grad_normed = product(
        jnp.concatenate([tile.astype(jnp.bfloat16) for tile in tiles], axis=1), wide[...]
    )
    unit, factor = normalize(current)
    key = tiles[HEADS:]
    pairs = [(tiles[2 * index], swapped(tiles[2 * index + 1])) for index in range(4)]
    pairs += [
        (tiles[8], swapped(key[0])),
        (key[1], swapped(key[2])),
        (swapped(key[0]), key[1]),
        (swapped(key[2]), jnp.zeros_like(key[2])),
    ]
    width = current.shape[1]
    terms_ref[:, :width] = (unit * gain).astype(jnp.bfloat16)
    for index, (low, high) in enumerate(pairs):
        terms_ref[:, 640 + 128 * index : 768 + 128 * index] = jnp.where(lower, low, high).astype(jnp.bfloat16)
    return grad_hidden + norm_back(grad_normed * gain, unit, factor)


def heads_mixed(mixed_ref):
    lower = is_lower((2 * CHUNK, 128))
    tiles = [head_rows(mixed_ref, head) for head in range(HEADS)]
    pairs = [jnp.where(lower, swapped(tiles[2 * i]), tiles[2 * i + 1]) for i in range(4)]
    pairs.append(swapped(tiles[8])[:, :HEAD_DIM])
    return jnp.concatenate([tile.astype(jnp.bfloat16) for tile in pairs], axis=1)


def feed_forward(current, mixed, out, gain, gate_up, down, waits):
    waits[0]()
    hidden = current + product_turned(mixed, out[...])
    unit, _ = normalize(hidden)
    normed = (unit * gain).astype(jnp.bfloat16)
    waits[1]()
    pair = [product(normed, gate_up[index]) for index in range(4)]
    act = [(pair[k] * jax.nn.sigmoid(pair[k]) * pair[k + 2]).astype(jnp.bfloat16) for k in range(2)]
    part = FF // 2
    waits[2]()
    result = hidden + (product_turned(act[0], down[:, :part]) + product_turned(act[1], down[:, part:]))
    return hidden, pair, result


def feed_back(grad_out, hidden, pair, mixed, mixed_ref, out, gain, gate_up, down, waits, terms_ref, grad_ref, inner_ref):
    part = FF // 2
    width = hidden.shape[1]
    branch = grad_out.astype(jnp.bfloat16)
    waits[2]()
    grad_act = product(branch, down[...])
    waits[1]()
    grad_normed = None
    for k in range(2):
        gate, upward = pair(k), pair(k + 2)
        squashed = jax.nn.sigmoid(gate)
        grad = grad_act[:, k * part : (k + 1) * part]
        grad_gate = (grad * upward * squashed * (1.0 + gate * (1.0 - squashed))).astype(jnp.bfloat16)
        grad_upward = (grad * (gate * squashed)).astype(jnp.bfloat16)
        terms_ref[:, 2560 + k * part : 2560 + (k + 1) * part] = grad_gate
        terms_ref[:, 2560 + (k + 2) * part : 2560 + (k + 3) * part] = grad_upward
        terms_ref[:, 5632 + k * part : 5632 + (k + 1) * part] = (gate * squashed * upward).astype(jnp.bfloat16)
        term = product_turned(grad_gate, gate_up[k]) + product_turned(grad_upward, gate_up[k + 2])
        grad_normed = term if grad_normed is None else grad_normed + term
    unit, factor = normalize(hidden)
    terms_ref[:, :width] = mixed
    terms_ref[:, 640 : 640 + width] = (unit * gain).astype(jnp.bfloat16)
    terms_ref[:, 1280 : 1280 + width] = branch
    grad_hidden = grad_out + norm_back(grad_normed * gain, unit, factor)
    grad_attn = grad_hidden.astype(jnp.bfloat16)
    terms_ref[:, 1920:2560] = jnp.concatenate(
        [jnp.zeros((2 * CHUNK, HEAD_DIM), jnp.float32), grad_hidden], axis=1
    ).astype(jnp.bfloat16)
    waits[0]()
    grad_mixed = product(grad_attn, out[...])
    lower = is_lower((2 * CHUNK, 128))
    for head in range(HEADS):
        start = 128 * (head // 2)
        if head == HEADS - 1:
            tile = jnp.concatenate([jnp.zeros((2 * CHUNK, HEAD_DIM), jnp.float32), grad_mixed[:, start:]], axis=1)
        else:
            tile = grad_mixed[:, start : start + 128]
            tile = jnp.where(lower, 0.0, tile if head % 2 else swapped(tile))
        tile = tile.astype(jnp.bfloat16)
        put_head(grad_ref, head, tile)
        inner = jnp.sum(tile.astype(jnp.float32) * head_rows(mixed_ref, head), axis=-1, keepdims=True)
        put_head(inner_ref, head, inner)
    return grad_hidden


def brought(pairs, sems):
    waits = []
    for index, (source, target) in enumerate(pairs):
        copy = pltpu.make_async_copy(source, target, sems.at[index])
        copy.start()
        waits.append(copy.wait)
    return waits


def once(waits):
    def first_only(wait):
        pending = [wait]

        def run():
            if pending:
                pending.pop()()

        return run

    return [first_only(wait) for wait in waits]


def enter_kernel(current_ref, gain_ref, cosine_ref, sine_ref, qkv_ref, query_ref, local_ref, wide):
    widen(wide, qkv_ref)
    project(
        current_ref[...].astype(jnp.float32).T, gain_ref[...], wide, cosine_ref[...], sine_ref[...], query_ref, local_ref
    )


def between_kernel(
    mixed_ref, current_ref, gain_ref, next_gain_ref, cosine_ref, sine_ref, out_ref, gate_up_ref, down_ref, qkv_ref,
    hidden_ref, pair_ref, next_ref, query_ref, local_ref,
    out, gate_up, down, qkv, wide, sems,
):
    *waits, wait_qkv = brought(
        [(out_ref, out), (gate_up_ref, gate_up), (down_ref, down), (qkv_ref, qkv)], sems
    )
    mixed = heads_mixed(mixed_ref)
    hidden, pair, result = feed_forward(
        current_ref[...].astype(jnp.float32).T, mixed, out, gain_ref[...], gate_up, down, waits
    )
    hidden_ref[...] = hidden
    for index in range(4):
        pair_ref[index] = pair[index]
    next_ref[...] = result
    wait_qkv()
    widen(wide, qkv)
    project(result, next_gain_ref[...], wide, cosine_ref[...], sine_ref[...], query_ref, local_ref)


def top_kernel(
    mixed_ref, current_ref, cotangent_ref, gain_ref, out_ref, gate_up_ref, down_ref,
    result_ref, grad_hidden_ref, terms_ref, grad_ref, inner_ref,
    out, gate_up, down, sems,
):
    waits = once(brought([(out_ref, out), (gate_up_ref, gate_up), (down_ref, down)], sems))
    mixed = heads_mixed(mixed_ref)
    gain = gain_ref[...]
    hidden, pair, result = feed_forward(current_ref[...], mixed, out, gain, gate_up, down, waits)
    result_ref[...] = result
    grad_hidden_ref[...] = feed_back(
        cotangent_ref[...].astype(jnp.float32).T, hidden, lambda index: pair[index], mixed, mixed_ref,
        out, gain, gate_up, down, waits, terms_ref, grad_ref, inner_ref,
    )


def descend_kernel(
    grad_query_ref, grad_local_ref, upper_ref, upper_grad_ref, upper_gain_ref, cosine_ref, sine_ref,
    mixed_ref, hidden_in_ref, pair_ref, gain_ref, qkv_ref, out_ref, gate_up_ref, down_ref,
    upper_terms_ref, grad_hidden_ref, terms_ref, grad_ref, inner_ref,
    out, gate_up, down, qkv, wide, sems,
):
    wait_qkv, *waits = brought(
        [(qkv_ref, qkv), (out_ref, out), (gate_up_ref, gate_up), (down_ref, down)], sems
    )
    wait_qkv()
    widen(wide, qkv)
    grad = project_back(
        grad_query_ref, grad_local_ref, upper_ref[...], upper_grad_ref[...], upper_gain_ref[...], wide,
        cosine_ref[...], sine_ref[...], upper_terms_ref,
    )
    grad_hidden_ref[...] = feed_back(
        grad, hidden_in_ref[...], lambda index: pair_ref[index], heads_mixed(mixed_ref), mixed_ref,
        out, gain_ref[...], gate_up, down, waits, terms_ref, grad_ref, inner_ref,
    )


def leave_kernel(
    grad_query_ref, grad_local_ref, current_ref, grad_hidden_ref, gain_ref, cosine_ref, sine_ref, qkv_ref,
    grad_in_ref, terms_ref, wide,
):
    widen(wide, qkv_ref)
    grad_in_ref[...] = project_back(
        grad_query_ref, grad_local_ref, current_ref[...].astype(jnp.float32).T, grad_hidden_ref[...], gain_ref[...], wide,
        cosine_ref[...], sine_ref[...], terms_ref,
    )


def weight_all_kernel(
    order_ref, low_one, low_two, high_one, high_two, high_one_in, high_two_in, out_ref,
    low, high, gathered, terms_0, terms_1, terms_2, sums_0, sums_1, sums_2, *refs
):
    terms, sums = (terms_0, terms_1, terms_2), (sums_0, sums_1, sums_2)
    landing = [refs[3 * chunk : 3 * chunk + 3] for chunk in range(3)]
    second_at, second_sum, third_at = refs[9:12], refs[12:15], refs[15:18]
    ring_send, ring_recv, second_send, second_recv, third_send, third_recv, low_send, low_recv, kept = refs[18:]
    section, at = here()
    rows = low.shape[0] // 2
    beside = (1 - section, at[0] * SIDE + at[1], at[2])
    barrier = pltpu.get_barrier_semaphore()
    devices = [device_at(section, at, axis, step) for axis in range(3) for step in range(1, SIDE)] + [beside]
    for device in devices:
        pl.semaphore_signal(barrier, inc=1, device_id=device, device_id_type=MESH)
    pl.semaphore_wait(barrier, len(devices))

    def local(layer, index):
        top, bottom = pl.ds(0, rows), pl.ds(rows, rows)
        source, target = (
            ((low_one, low_two)[layer], low.at[top]),
            ((high_one, high_two)[layer], high.at[top]),
            ((high_one_in, high_two_in)[layer], high.at[bottom]),
        )[index]
        return pltpu.make_async_copy(source, target, kept.at[index])

    def crossing(layer):
        return pltpu.make_async_remote_copy(
            src_ref=(low_two, low_one)[layer],
            dst_ref=low.at[pl.ds(rows, rows)],
            send_sem=low_send,
            recv_sem=low_recv,
            device_id=beside,
            device_id_type=MESH,
        )

    for layer in range(2):

        @pl.when(section == layer)
        def _(layer=layer):
            crossing(layer).start()
            for index in range(3):
                local(layer, index).start()

    width = order_ref.shape[0]
    blocks = 64
    tiles = out_ref.shape[1] // 3
    slab = width // 3

    def chunk_terms(chunk):
        def left(ref, start):
            part = order_ref[chunk * slab : (chunk + 1) * slab, :]
            return product_turned(part, ref[:, start : start + width]).astype(jnp.bfloat16)

        def put(term, tile):
            for index in range(3):
                row = index * tiles + tile
                gathered[pl.ds(row, blocks, stride=3 * tiles), :] = term[index * blocks : (index + 1) * blocks]

        normed_two = left(high, 640)
        for step in range(6):
            term = product(normed_two, high[:, 2560 + 512 * step : 3072 + 512 * step])
            for tile in range(4):
                put(term[:, 128 * tile : 128 * tile + 128], 12 + 4 * step + tile)
        branch = left(high, 1280)
        for step in range(3):
            term = product(branch, high[:, 5632 + 512 * step : 6144 + 512 * step])
            for tile in range(4):
                put(term[:, 128 * tile : 128 * tile + 128], 36 + 4 * step + tile)
        if chunk == 0:
            local(0, 0).wait()
            crossing(0).wait()
        first = product(left(low, 0), low[:, 640:1664])
        second = product(left(high, 0), high[:, 1920:2560])
        for tile in range(7):
            put(first[:, 128 * tile : 128 * tile + 128], tile)
        put(first[:, 896:] + second[:, :128], 7)
        for tile in range(1, 5):
            put(second[:, 128 * tile : 128 * tile + 128], 7 + tile)

        @pl.loop(0, blocks)
        def _(block):
            start = pl.multiple_of(block * (3 * tiles), 3 * tiles)
            y, x, z = lax.div(block, 16), lax.rem(lax.div(block, SIDE), SIDE), lax.rem(block, SIDE)
            terms[chunk][y, x, z] = gathered[pl.ds(start, 3 * tiles), :].astype(jnp.bfloat16)

    def plane(sub):
        return [axis for axis in range(3) if axis != LINES[sub][0]]

    def own(chunk, sub, coordinate, half):
        axis = LINES[sub][0]
        index = {axis: coordinate, plane(sub)[0]: pl.ds(2 * half, 2), plane(sub)[1]: slice(None)}
        return terms[chunk].at[index[0], index[1], index[2], pl.ds(sub * tiles, tiles)]

    flying = {}

    def message(chunk, sub, way, number, source):
        copy = pltpu.make_async_remote_copy(
            src_ref=source,
            dst_ref=landing[chunk][sub].at[3 * way + number],
            send_sem=ring_send.at[chunk, sub, way, number],
            recv_sem=ring_recv.at[chunk, sub, way, number],
            device_id=device_at(section, at, LINES[sub][0], STEPS[way][1]),
            device_id_type=MESH,
        )
        copy.start()
        flying[chunk, sub, way, number] = copy

    def add(target, parts):
        @pl.loop(0, 2 * SIDE)
        def _(index):
            place = (lax.div(index, SIDE), lax.rem(index, SIDE))
            total = parts[0][place].astype(jnp.float32)
            for part in parts[1:]:
                total = total + part[place].astype(jnp.float32)
            target[place] = total.astype(jnp.bfloat16)

    def ring_start(chunk):
        for number in range(2):
            for sub in range(3):
                for way, step in STEPS:
                    coordinate = shifted(at, LINES[sub][0], 2 * step if number == 0 else step)
                    message(chunk, sub, way, number, own(chunk, sub, coordinate, (number + way) % 2))

    def ring_pass(chunk):
        for sub in range(3):
            for way, step in STEPS:
                flying[chunk, sub, way, 0].wait_recv()
                passing = landing[chunk][sub].at[3 * way]
                add(passing, (passing, own(chunk, sub, shifted(at, LINES[sub][0], step), way)))
                message(chunk, sub, way, 2, passing)

    def ring_sum(chunk):
        for sub in range(3):
            for way in range(2):
                flying[chunk, sub, way, 1].wait_recv()
                flying[chunk, sub, way, 2].wait_recv()
            for half in range(2):
                found = landing[chunk][sub]
                add(
                    sums[sub].at[chunk, pl.ds(2 * half, 2)],
                    (
                        own(chunk, sub, at[LINES[sub][0]], half),
                        found.at[3 * half + 2],
                        found.at[3 * (1 - half) + 1],
                    ),
                )

    local(0, 1).wait()
    local(0, 2).wait()
    chunk_terms(0)
    ring_start(0)
    chunk_terms(1)
    ring_start(1)
    ring_pass(0)
    chunk_terms(2)
    ring_start(2)
    ring_pass(1)
    ring_sum(0)
    ring_pass(2)
    ring_sum(1)
    ring_sum(2)

    def direct(sub, axis, step, source, target, send, recv):
        copy = pltpu.make_async_remote_copy(
            src_ref=source,
            dst_ref=target,
            send_sem=send.at[sub, step - 1],
            recv_sem=recv.at[sub, step - 1],
            device_id=device_at(section, at, axis, step),
            device_id_type=MESH,
        )
        copy.start()
        return copy

    def part_of(sub, coordinate):
        if plane(sub)[0] == LINES[sub][1]:
            return sums[sub].at[:, coordinate]
        return sums[sub].at[:, :, coordinate]

    seconds, thirds = [], []
    for step in (2, 1, 3):
        for sub in range(3):
            axis = LINES[sub][1]
            seconds.append(
                direct(sub, axis, step, part_of(sub, shifted(at, axis, step)), second_at[sub].at[step - 1], second_send, second_recv)
            )
    for copy in seconds:
        copy.wait_recv()
    for sub in range(3):
        mine = part_of(sub, at[LINES[sub][1]])

        @pl.loop(0, 3 * SIDE)
        def _(index, sub=sub, mine=mine):
            place = (lax.div(index, SIDE), lax.rem(index, SIDE))
            total = mine[place].astype(jnp.float32)
            for step in range(SIDE - 1):
                total = total + second_at[sub][(step,) + place].astype(jnp.float32)
            second_sum[sub][place] = total.astype(jnp.bfloat16)

        axis = LINES[sub][2]
        for step in (2, 1, 3):
            thirds.append(
                direct(
                    sub, axis, step, second_sum[sub].at[:, shifted(at, axis, step)], third_at[sub].at[step - 1],
                    third_send, third_recv,
                )
            )
    for copy in thirds:
        copy.wait_recv()
    for sub in range(3):
        for chunk in range(3):
            total = second_sum[sub][chunk, at[LINES[sub][2]]].astype(jnp.float32)
            for step in range(SIDE - 1):
                total = total + third_at[sub][step, chunk].astype(jnp.float32)
            out_ref[chunk, sub * tiles : (sub + 1) * tiles, :] = total
    for copy in list(flying.values()) + seconds + thirds:
        copy.wait_send()


LINES = ((1, 0, 2), (2, 1, 0), (0, 2, 1))


def weight_all(order, low_one, low_two, high_one, high_two, high_one_in, high_two_in, collective_id):
    rows, kind = low_one.shape[0], low_one.dtype
    tiles = 6144 // 128
    block = (tiles, 128)
    vmem, held = pl.BlockSpec(memory_space=pltpu.VMEM), pl.BlockSpec(memory_space=pl.ANY)
    semaphore = pltpu.SemaphoreType.DMA
    count = SIDE - 1
    return pl.pallas_call(
        weight_all_kernel,
        out_shape=jax.ShapeDtypeStruct((3, 3 * tiles, 128), jnp.float32),
        in_specs=[vmem] + [held] * 6,
        out_specs=vmem,
        scratch_shapes=[
            pltpu.VMEM((2 * rows, low_one.shape[1]), kind),
            pltpu.VMEM((2 * rows, high_one.shape[1]), kind),
            pltpu.VMEM((64 * 3 * tiles, 128), jnp.float32),
        ]
        + [pltpu.VMEM((SIDE, SIDE, SIDE, 3 * tiles, 128), kind) for _ in range(3)]
        + [pltpu.VMEM((3, SIDE, SIDE) + block, kind) for _ in range(3)]
        + [pltpu.VMEM((6, 2, SIDE) + block, kind) for _ in range(9)]
        + [pltpu.VMEM((count, 3, SIDE) + block, kind) for _ in range(3)]
        + [pltpu.VMEM((3, SIDE) + block, kind) for _ in range(3)]
        + [pltpu.VMEM((count, 3) + block, kind) for _ in range(3)]
        + [semaphore(shape) for shape in ((3, 3, 2, 3), (3, count), (3, count)) for _ in range(2)]
        + [semaphore, semaphore, semaphore((3,))],
        compiler_params=pltpu.CompilerParams(
            collective_id=collective_id, has_side_effects=True, vmem_limit_bytes=VMEM_LIMIT
        ),
        cost_estimate=pl.CostEstimate(flops=4 * rows * 576 * 6144, bytes_accessed=1 << 24, transcendentals=0),
    )(order, low_one, low_two, high_one, high_two, high_one_in, high_two_in)


TERMS_LOW = 1664
TERMS_HIGH = 7168


def dense(kernel, arguments, hbm, results, scratch, flops):
    vmem = pl.BlockSpec(memory_space=pltpu.VMEM)
    kept = [vmem] * (len(arguments) - hbm) + [pl.BlockSpec(memory_space=pl.ANY)] * hbm
    size = sum(item.size * item.dtype.itemsize for item in arguments)
    return pl.pallas_call(
        kernel,
        out_shape=tuple(jax.ShapeDtypeStruct(shape, kind) for shape, kind in results),
        in_specs=kept,
        out_specs=tuple(vmem for _ in results),
        scratch_shapes=scratch,
        compiler_params=pltpu.CompilerParams(vmem_limit_bytes=VMEM_LIMIT),
        cost_estimate=pl.CostEstimate(flops=flops, bytes_accessed=size, transcendentals=0),
    )(*arguments)


def on_device(inputs, positions, attn_gain, w_qkv, w_out, ffn_gain, w_gate_up, w_down, cotangent):
    _, rows, width = inputs.shape
    section = lax.axis_index("section")
    place = lax.axis_index(("ctx", "fsdp"))
    half_kind, kind = jnp.bfloat16, jnp.float32
    lanes = 2 * HEAD_DIM
    columns = w_qkv.shape[2] * SIDE
    wide_rows = 128 * (HEADS + KV_HEADS)

    depth = lax.axis_index("fsdp")
    batch = depth // 2
    worked = place + section * (SIDE - 1 - 2 * depth)
    spots_k = lax.dynamic_index_in_dim(positions, batch, 0, keepdims=False)
    spots_q = lax.dynamic_slice_in_dim(spots_k, worked * rows, rows, 0)
    chunk_of = spots_k[::CHUNK] // CHUNK
    stored = jnp.arange(chunk_of.shape[0], dtype=jnp.int32)
    inverse = jnp.sum(jnp.where(chunk_of[:, None] == stored[None, :], stored[:, None], 0), axis=0)
    spots = lax.dynamic_slice_in_dim(chunk_of, worked * 2, 2, 0)
    frequency = rope_base ** (-(jnp.arange(HEAD_DIM // 2, dtype=kind) * 2.0 / HEAD_DIM))
    angle = spots_q.astype(kind)[:, None] * frequency[None, :]
    cosine, sine = jnp.cos(angle), jnp.sin(angle)
    rest = jnp.ones((rows, HEAD_DIM), kind)
    cosine = jnp.concatenate([cosine, cosine, rest], axis=1)
    sine = jnp.concatenate([-sine, sine, 0.0 * rest], axis=1)

    local_gains = jnp.pad(jnp.concatenate([attn_gain, ffn_gain], axis=0), ((0, 6), (0, 0)))
    qkv_turned = w_qkv[0].T
    qkv_first, gains, current, given = first_weight(
        qkv_turned, local_gains, inputs.transpose(0, 2, 1), cotangent.transpose(0, 2, 1)
    )
    qkv_first = qkv_first.reshape(columns, width)

    shards = [w_out[0].T, w_gate_up[0], w_down[0].T, qkv_turned]
    gain_one = [gains[l, 0:1] for l in range(2)]
    gain_two = [gains[l, 1:2] for l in range(2)]

    query_like = ((KV_HEADS, 2, GROUP * CHUNK, lanes), half_kind)
    inner_like = ((KV_HEADS, 2, GROUP * CHUNK, 1), kind)
    local_like = ((KV_HEADS, 2, CHUNK, lanes), half_kind)
    state_like = ((rows, width), kind)
    pair_like = ((SIDE, rows, 2 * FF // SIDE), kind)
    low_like = ((rows, TERMS_LOW), half_kind)
    high_like = ((rows, TERMS_HIGH), half_kind)
    wide_scratch = pltpu.VMEM((wide_rows, width), half_kind)
    qkv_scratch = pltpu.VMEM((columns, width), half_kind)
    ffn_scratch = [
        pltpu.VMEM((width, width), half_kind),
        pltpu.VMEM((SIDE, width, 2 * FF // SIDE), half_kind),
        pltpu.VMEM((width, FF), half_kind),
    ]
    sems = pltpu.SemaphoreType.DMA((4,))
    qkv_flops = 2 * rows * width * wide_rows
    ffn_flops = 2 * rows * width * (width + 3 * FF)

    def attention(layer, query, local, shards):
        mixed, logsum, both, out, gate_up, down, *rest = attend_all(
            layer, inverse, spots, local, query, shards, layer
        )
        weights = [out.reshape(width, width), gate_up, down.reshape(width, FF)]
        return both, mixed, logsum, weights, [item.reshape(columns, width) for item in rest]

    def attention_back(layer, query, grad, logsum, inner, both, high):
        grad_query, grad_both, high_in = attend_back_all(
            layer, inverse, spots, chunk_of, query, grad, logsum, inner, both, high, 4 + layer
        )
        return grad_query, grad_both.reshape(KV_HEADS, rows, lanes), high_in

    query_one, local = dense(
        enter_kernel, (current, gain_one[0], cosine, sine, qkv_first), 0, (query_like, local_like), [wide_scratch], qkv_flops
    )
    both_one, mixed_one, logsum_one, weights_one, (qkv_second,) = attention(0, query_one, local, shards)
    hidden, pair, middle, query_two, local = dense(
        between_kernel,
        (mixed_one, current, gain_two[0], gain_one[1], cosine, sine, *weights_one, qkv_second),
        4,
        (state_like, pair_like, state_like, query_like, local_like),
        ffn_scratch + [qkv_scratch, wide_scratch, sems],
        ffn_flops + qkv_flops,
    )
    both_two, mixed_two, logsum_two, weights_two, _ = attention(1, query_two, local, shards[:3])
    result, grad_hidden, high_two, grad, inner = dense(
        top_kernel,
        (mixed_two, middle, given, gain_two[1], *weights_two),
        3,
        (state_like, state_like, high_like, query_like, inner_like),
        ffn_scratch + [sems],
        2 * ffn_flops,
    )
    earlier = lax.ppermute(
        result,
        ("section", "ctx", "fsdp"),
        [(64 + 4 * ctx + z, 64 + 4 * ctx + 3 - z) for ctx in range(16) for z in range(4)],
    )
    grad_query, grad_local, high_two_in = attention_back(1, query_two, grad, logsum_two, inner, both_two, high_two)
    low_two, grad_hidden, high_one, grad, inner = dense(
        descend_kernel,
        (
            grad_query, grad_local, middle, grad_hidden, gain_one[1], cosine, sine,
            mixed_one, hidden, pair, gain_two[0], qkv_second, *weights_one,
        ),
        4,
        (low_like, state_like, high_like, query_like, inner_like),
        ffn_scratch + [qkv_scratch, wide_scratch, sems],
        ffn_flops + qkv_flops,
    )
    grad_query, grad_local, high_one_in = attention_back(0, query_one, grad, logsum_one, inner, both_one, high_one)
    grad_in, low_one = dense(
        leave_kernel,
        (grad_query, grad_local, current, grad_hidden, gain_one[0], cosine, sine, qkv_first),
        0,
        (state_like, low_like),
        [wide_scratch],
        qkv_flops,
    )

    first = section == 0
    blocks = SIDE * SIDE * SIDE
    each = width // blocks
    total = columns + width + 3 * FF
    line = jnp.arange(width)
    order = (line[:, None] % blocks * each + line[:, None] // blocks == line[None, :]).astype(half_kind)
    summed = weight_all(order, low_one, low_two, high_one, high_two, high_one_in, high_two_in, 2)
    summed = summed.reshape(each, total)
    grad_qkv = summed[:, :columns]
    grad_out_weight = summed[:, columns : columns + width]
    grad_gate_up = summed[:, columns + width : columns + width + 2 * FF]
    grad_down = summed[:, columns + width + 2 * FF :].T

    qkv_own = jnp.where(
        first,
        lax.dynamic_slice_in_dim(qkv_first, place * each, each, 1),
        lax.dynamic_slice_in_dim(qkv_second, place * each, each, 1),
    )
    qkv_own = qkv_own.astype(kind).T
    gate_up_own = jnp.where(
        first,
        lax.dynamic_slice_in_dim(weights_one[1], place * each, each, 1),
        lax.dynamic_slice_in_dim(weights_two[1], place * each, each, 1),
    ).astype(kind)
    split = grad_gate_up.reshape(each, SIDE, -1).transpose(1, 0, 2)
    grad_gain_one = jnp.sum(qkv_own * grad_qkv, axis=1) / lax.dynamic_slice_in_dim(attn_gain[0], place * each, each, 0)
    grad_gain_two = jnp.sum(gate_up_own * split, axis=(0, 2)) / lax.dynamic_slice_in_dim(
        ffn_gain[0], place * each, each, 0
    )

    def index_of(core, ctx, z):
        return (core * SIDE * SIDE + ctx) * SIDE + z

    places = [(ctx, z) for ctx in range(SIDE * SIDE) for z in range(SIDE)]
    axes = ("section", "ctx", "fsdp")
    later = lax.ppermute(
        jnp.where(first, result, grad_in),
        axes,
        [(index_of(0, ctx, z), index_of(1, ctx, z)) for ctx, z in places]
        + [(index_of(1, ctx, z), index_of(0, ctx, SIDE - 1 - z)) for ctx, z in places],
    )
    mine = jnp.where(first, grad_in, later)
    other = jnp.where(first, later, earlier)
    ends = jnp.where(batch == 0, jnp.stack([mine, other]), jnp.stack([other, mine]))
    return (
        ends[None],
        grad_gain_one[None],
        grad_qkv[None],
        grad_out_weight[None],
        grad_gain_two[None],
        grad_gate_up[None],
        grad_down[None],
    )


def solution(mesh):
    placed = (
        P(None, ("ctx", "fsdp"), None),
        P(),
        P("section", None),
        P("section", None, "fsdp"),
        P("section", None, "fsdp"),
        P("section", None),
        P("section", None, "fsdp"),
        P("section", None, "fsdp"),
        P(None, ("ctx", "fsdp"), None),
    )
    return jax.shard_map(
        on_device,
        mesh=mesh,
        in_specs=placed,
        out_specs=(
            P("section", None, ("ctx", "fsdp"), None),
            P("section", ("ctx", "fsdp")),
            P("section", ("ctx", "fsdp"), None),
            P("section", ("ctx", "fsdp"), None),
            P("section", ("ctx", "fsdp")),
            P("section", ("ctx", "fsdp"), None),
            P("section", None, ("ctx", "fsdp")),
        ),
        check_vma=False,
    )
```
